32 devices in a mesh: dp: 4 (over y, core), fsdp: 8 (over z, x).
Axes of the slice: x: 2, y: 2, z: 4, core: 2. Of those that a mesh axis runs over, the one named last changes fastest.
Arguments:
- tokens: bfloat16 [32, 1024, 768], P(('dp', 'fsdp')), may hold values from -6 to 6
- lengths: int32 [32], P(('dp', 'fsdp')), may hold values from 32 to 1024, as said below
- cotangent: bfloat16 [32, 1024, 768], P(('dp', 'fsdp')), may hold values from -6 to 6
- w_qkv: float32 [768, 2304], P(('dp', 'fsdp')), may hold values from -0.21875 to 0.21875
- m_qkv: float32 [768, 2304], P(('dp', 'fsdp')), may hold values from -0.00061035156 to 0.00061035156
- v_qkv: float32 [768, 2304], P(('dp', 'fsdp')), may hold values from 3.7117702e-09 to 5.927542e-08
- w_out: float32 [768, 768], P(('dp', 'fsdp')), may hold values from -1.25 to 1.25
- m_out: float32 [768, 768], P(('dp', 'fsdp')), may hold values from -0.00024414062 to 0.00024414062
- v_out: float32 [768, 768], P(('dp', 'fsdp')), may hold values from 5.6452776e-10 to 8.891313e-09
- w_up: float32 [768, 3072], P(('dp', 'fsdp')), may hold values from -0.21875 to 0.21875
- m_up: float32 [768, 3072], P(('dp', 'fsdp')), may hold values from -0.00061035156 to 0.00061035156
- v_up: float32 [768, 3072], P(('dp', 'fsdp')), may hold values from 3.7117702e-09 to 5.927542e-08
- w_down: float32 [3072, 768], P(('dp', 'fsdp')), may hold values from -0.109375 to 0.109375
- m_down: float32 [3072, 768], P(('dp', 'fsdp')), may hold values from -0.00061035156 to 0.00061035156
- v_down: float32 [3072, 768], P(('dp', 'fsdp')), may hold values from 3.7117702e-09 to 5.927542e-08
- packed: float32 [7680], P(('dp', 'fsdp')), may hold values from -0.8 to 3.2, as said below
- m_packed: float32 [7680], P(('dp', 'fsdp')), may hold values from -0.0024414062 to 0.0024414062
- v_packed: float32 [7680], P(('dp', 'fsdp')), may hold values from 5.927542e-08 to 9.45584e-07
Outputs:
- mixed: bfloat16 [32, 1024, 768], P(('dp', 'fsdp'))
- d_tokens: float32 [32, 1024, 768], P(('dp', 'fsdp'))
- grad_norm: float32 [], replicated
- new_w_qkv: float32 [768, 2304], P(('dp', 'fsdp'))
- new_m_qkv: float32 [768, 2304], P(('dp', 'fsdp'))
- new_v_qkv: float32 [768, 2304], P(('dp', 'fsdp'))
- new_w_out: float32 [768, 768], P(('dp', 'fsdp'))
- new_m_out: float32 [768, 768], P(('dp', 'fsdp'))
- new_v_out: float32 [768, 768], P(('dp', 'fsdp'))
- new_w_up: float32 [768, 3072], P(('dp', 'fsdp'))
- new_m_up: float32 [768, 3072], P(('dp', 'fsdp'))
- new_v_up: float32 [768, 3072], P(('dp', 'fsdp'))
- new_w_down: float32 [3072, 768], P(('dp', 'fsdp'))
- new_m_down: float32 [3072, 768], P(('dp', 'fsdp'))
- new_v_down: float32 [3072, 768], P(('dp', 'fsdp'))
- new_packed: float32 [7680], P(('dp', 'fsdp'))
- new_m_packed: float32 [7680], P(('dp', 'fsdp'))
- new_v_packed: float32 [7680], P(('dp', 'fsdp'))
The draws below stay inside these ranges and needn't reach their ends.
Inputs may be any that keep to these rules, and one draw needn't show every extreme that they name: `lengths`: each padded sequence has at least 32 live tokens; in every draw one sequence has all 1024. `packed`: gains are positive, biases of both signs.
All inputs are finite; a program needn't handle non-finite values.
Results may differ from the reference program's by a relative error of at most 0.01.
The reference program's roundings to bfloat16 on the way count: a program that leaves them out, or rounds other values in their place, can miss the bound.
Values may be sent and summed in bfloat16 or wider, within the bound.
A program may use at most 192 MiB of HBM per device.

```python
import math
import jax
import jax.numpy as jnp
from jax import lax

D = 768
FF = 3072
HEAD_DIM = 64
L = 1024
MIN_LEN = 32
STEP = 10
SEQS = 32
VEC = 7680
PARAMS = 7085568


def draw_lengths(key, part):
    key = jax.random.fold_in(key, 11)
    first_key, pick_key = jax.random.split(key)
    drawn = jax.random.randint(first_key, (SEQS,), MIN_LEN, L + 1)
    chosen = jax.random.randint(pick_key, (), 0, SEQS)
    return jnp.where(jnp.arange(SEQS) == chosen, L, drawn).astype(jnp.int32)


def draw_packed(key, part):
    key = jax.random.fold_in(key, 23)
    gain_key, bias_key = jax.random.split(key)
    ramp = jnp.arange(D, dtype=jnp.float32) / (D - 1)
    rising = 0.6 + 1.2 * ramp
    factors = 1.0 + 0.1 * jnp.clip(jax.random.normal(gain_key, (2, D), jnp.float32), -2.5, 2.5)
    biases = jnp.clip(0.2 * jax.random.normal(bias_key, (4 * D + FF,), jnp.float32), -0.8, 0.8)
    gains = rising[None, :] * factors
    return jnp.concatenate([gains[0], biases[:D], gains[1], biases[D:2 * D], biases[2 * D:4 * D], biases[4 * D:]]).astype(jnp.float32)


def levels(key, extent, cuts, least, top_value):
    loudness = 1.0
    for dim, blocks in cuts:
        steps = jax.random.uniform(jax.random.fold_in(jax.random.fold_in(key, 6), dim), (blocks,), jnp.float32, least / len(cuts), top_value / len(cuts))
        loudness = loudness * jnp.repeat(jnp.exp(steps), extent[dim] // blocks).reshape((-1,) + (1,) * (len(extent) - 1 - dim))
    return loudness


def bell_draw(key, extent, width, bound, cuts=(), kind=jnp.bfloat16):
    values = width * jax.random.normal(key, extent, jnp.float32)
    if cuts:
        values = values * levels(key, extent, cuts, -0.22, 0.18)
    return jnp.clip(values, -bound, bound).astype(kind)


def setup_inputs(seed: int = 0) -> dict:
    key_list = jax.random.split(jax.random.key(seed), 19)
    tokens = bell_draw(key_list[0], (SEQS, L, D), 1.0, 6.0, ((0, 32),))
    lengths = draw_lengths(jax.random.fold_in(key_list[18], 71), 0)
    cotangent = bell_draw(key_list[2], (SEQS, L, D), 1.0, 6.0, ((0, 32),))
    w_qkv = bell_draw(key_list[3], (D, 3 * D), D ** -0.5, 0.21875, ((0, 32),), jnp.float32)
    m_qkv = bell_draw(key_list[4], (D, 3 * D), (0.111 * PARAMS ** -0.5), 0.00061035156, ((0, 32),), jnp.float32)
    v_qkv = jnp.clip(jnp.exp(math.log(5.927541835148986e-08) - 2.77068578 * jax.random.uniform(key_list[5], (D, 3 * D), jnp.float32) ** levels(key_list[5], (D, 3 * D), ((0, 32),), -0.2, 0.2)), 3.711770224512634e-09, 5.927541835148986e-08)
    w_out = bell_draw(key_list[6], (D, D), (D // 32) ** -0.5, 1.25, ((0, 32),), jnp.float32)
    m_out = bell_draw(key_list[7], (D, D), (0.045 * PARAMS ** -0.5), 0.00024414062, ((0, 32),), jnp.float32)
    v_out = jnp.clip(jnp.exp(math.log(8.891312575087795e-09) - 2.7568404 * jax.random.uniform(key_list[8], (D, D), jnp.float32) ** levels(key_list[8], (D, D), ((0, 32),), -0.2, 0.2)), 5.645277578736341e-10, 8.891312575087795e-09)
    w_up = bell_draw(key_list[9], (D, FF), D ** -0.5, 0.21875, ((0, 32),), jnp.float32)
    m_up = bell_draw(key_list[10], (D, FF), (0.111 * PARAMS ** -0.5), 0.00061035156, ((0, 32),), jnp.float32)
    v_up = jnp.clip(jnp.exp(math.log(5.927541835148986e-08) - 2.77068578 * jax.random.uniform(key_list[11], (D, FF), jnp.float32) ** levels(key_list[11], (D, FF), ((0, 32),), -0.2, 0.2)), 3.711770224512634e-09, 5.927541835148986e-08)
    w_down = bell_draw(key_list[12], (FF, D), FF ** -0.5, 0.109375, ((0, 32),), jnp.float32)
    m_down = bell_draw(key_list[13], (FF, D), (0.111 * PARAMS ** -0.5), 0.00061035156, ((0, 32),), jnp.float32)
    v_down = jnp.clip(jnp.exp(math.log(5.927541835148986e-08) - 2.77068578 * jax.random.uniform(key_list[14], (FF, D), jnp.float32) ** levels(key_list[14], (FF, D), ((0, 32),), -0.2, 0.2)), 3.711770224512634e-09, 5.927541835148986e-08)
    packed = draw_packed(jax.random.fold_in(key_list[18], 71), 0)
    m_packed = bell_draw(key_list[16], (VEC,), (0.444 * PARAMS ** -0.5), 0.0024414062, ((0, 32),), jnp.float32)
    v_packed = jnp.clip(jnp.exp(math.log(9.455840199734666e-07) - 2.769608 * jax.random.uniform(key_list[17], (VEC,), jnp.float32) ** levels(key_list[17], (VEC,), ((0, 32),), -0.2, 0.2)), 5.927541835148986e-08, 9.455840199734666e-07)
    return {"tokens": tokens, "lengths": lengths, "cotangent": cotangent, "w_qkv": w_qkv, "m_qkv": m_qkv, "v_qkv": v_qkv, "w_out": w_out, "m_out": m_out, "v_out": v_out, "w_up": w_up, "m_up": m_up, "v_up": v_up, "w_down": w_down, "m_down": m_down, "v_down": v_down, "packed": packed, "m_packed": m_packed, "v_packed": v_packed}


EPS_NORM = 1e-05
NEG_FILL = -1000000000.0
CLIP_NORM = 1.0
BETA_ONE = 0.9
BETA_TWO = 0.95
ADAM_EPSILON = 1e-08
DECAY_RATE = 0.1
VECTOR_RATE = 0.2
HIGHEST = lax.Precision.HIGHEST

@jax.custom_vjp
def low(v):
    return lax.optimization_barrier(v.astype(jnp.bfloat16)).astype(jnp.float32)

@jax.custom_vjp
def low_back(v):
    return v

def low_keep(v):
    return (low(v), None)

def low_pass(kept, grad):
    return (grad,)

def back_keep(v):
    return (v, None)

def back_low(kept, grad):
    return (low(grad),)
low.defvjp(low_keep, low_pass)
low_back.defvjp(back_keep, back_low)

def round_both(value):
    return low(low_back(value))

def layer_norm(values, gain, shift):
    center = lax.optimization_barrier(jnp.mean(values, -1, keepdims=True))
    centered = values - center
    spread = lax.optimization_barrier(jnp.mean(centered * centered, -1, keepdims=True))
    return centered * lax.rsqrt(spread + EPS_NORM) * gain + shift

def smooth_gate(value):
    return jax.nn.gelu(value, approximate=True)

def layer(inputs, allowed, wqkv, wout, wup, wdown, vector):
    model_width = inputs.shape[1]
    head_count = model_width // HEAD_DIM
    seq_len = inputs.shape[0]
    vector = low(vector)
    gain_one = vector[:model_width]
    bias_one = vector[model_width:2 * model_width]
    gain_two = vector[2 * model_width:3 * model_width]
    bias_two = vector[3 * model_width:4 * model_width]
    bias_attn = vector[4 * model_width:5 * model_width]
    bias_down = vector[5 * model_width:6 * model_width]
    bias_up = vector[6 * model_width:]
    normed_one = low(layer_norm(inputs, gain_one, bias_one))
    qkv_all = round_both(jnp.dot(normed_one, low(wqkv), precision=HIGHEST))

    def head_split(block):
        return block.reshape(seq_len, head_count, HEAD_DIM).transpose(1, 0, 2)
    queries = head_split(qkv_all[:, :model_width])
    key_rows = head_split(qkv_all[:, model_width:2 * model_width])
    value_rows = head_split(qkv_all[:, 2 * model_width:])

    def one_head(operands):
        query_block, key_block, value_block = operands
        scores = jnp.einsum('qd,kd->qk', query_block, key_block, precision=HIGHEST) * HEAD_DIM ** (-0.5)
        scores = low_back(jnp.where(allowed, scores, NEG_FILL))
        row_top = lax.optimization_barrier(jnp.max(scores, -1, keepdims=True))
        expo = jnp.exp(scores - row_top)
        attn_probs = expo / lax.optimization_barrier(jnp.sum(expo, -1, keepdims=True))
        return jnp.einsum('qk,kd->qd', low(attn_probs), value_block, precision=HIGHEST)
    attended = lax.map(jax.checkpoint(one_head), (queries, key_rows, value_rows))
    attended = round_both(attended.transpose(1, 0, 2).reshape(seq_len, model_width))
    branch_attn = low_back(jnp.dot(attended, low(wout), precision=HIGHEST) + bias_attn)
    resid_one = inputs + branch_attn
    normed_two = low(layer_norm(resid_one, gain_two, bias_two))
    upper = low_back(jnp.dot(normed_two, low(wup), precision=HIGHEST) + bias_up)
    activ = low(smooth_gate(upper))
    return resid_one + jnp.dot(activ, low(wdown), precision=HIGHEST) + bias_down

def adam_step(weight, first_mom, second_mom, gradient, step_rate):
    first_new = BETA_ONE * first_mom + (1.0 - BETA_ONE) * gradient
    second_new = BETA_TWO * second_mom + (1.0 - BETA_TWO) * gradient * gradient
    fix_one = 1.0 - BETA_ONE ** STEP
    fix_two = 1.0 - BETA_TWO ** STEP
    update = first_new / fix_one / (jnp.sqrt(second_new / fix_two) + ADAM_EPSILON) + DECAY_RATE * weight
    return (weight - step_rate * update, first_new, second_new)

def reference(tokens, lengths, cotangent, w_qkv, m_qkv, v_qkv, w_out, m_out, v_out, w_up, m_up, v_up, w_down, m_down, v_down, packed, m_packed, v_packed):
    positions = jnp.arange(L, dtype=jnp.int32)
    causal = positions[:, None] >= positions[None, :]
    params = (w_qkv, w_out, w_up, w_down, packed)

    def one_sequence(totals, seq_entry):
        seq_tokens, seq_length, seq_cot = seq_entry
        live_rows = positions < seq_length
        allowed = causal & live_rows[None, :]

        def run(inputs, wqkv, wout, wup, wdown, vector):
            return layer(inputs, allowed, wqkv, wout, wup, wdown, vector)
        result, pull = jax.vjp(run, seq_tokens.astype(jnp.float32), *params)
        grads = pull(seq_cot.astype(jnp.float32) * live_rows[:, None].astype(jnp.float32))
        totals = jax.tree.map(jnp.add, totals, tuple(grads[1:]))
        return (totals, (result.astype(jnp.bfloat16), grads[0]))
    zeros = tuple((jnp.zeros_like(item) for item in params))
    totals, (mixed, d_tokens) = lax.scan(one_sequence, zeros, (tokens, lengths, cotangent))
    squares = jnp.float32(0.0) + sum((jnp.sum(item * item) for item in totals))
    grad_norm = jnp.sqrt(squares)
    factor = jnp.minimum(1.0, CLIP_NORM / (grad_norm + 1e-06))
    g_qkv, g_out, g_up, g_down, g_vec = [item * factor for item in totals]
    new_qkv = adam_step(w_qkv, m_qkv, v_qkv, g_qkv, D ** (-0.5))
    new_out = adam_step(w_out, m_out, v_out, g_out, D ** (-0.5))
    new_up = adam_step(w_up, m_up, v_up, g_up, D ** (-0.5))
    new_down = adam_step(w_down, m_down, v_down, g_down, FF ** (-0.5))
    new_vec = adam_step(packed, m_packed, v_packed, g_vec, VECTOR_RATE)
    return (mixed, d_tokens, grad_norm, new_qkv[0], new_qkv[1], new_qkv[2], new_out[0], new_out[1], new_out[2], new_up[0], new_up[1], new_up[2], new_down[0], new_down[1], new_down[2], new_vec[0], new_vec[1], new_vec[2])
```

```python
import functools

import jax
import jax.numpy as jnp
from jax import lax
from jax.experimental import pallas as pl
from jax.experimental.pallas import tpu as pltpu
from jax.sharding import PartitionSpec as P

D = 768
FF = 3072
HEAD_DIM = 64
STEP = 10
HD = 64
F32 = jnp.float32
BF = jnp.bfloat16
MESH = pl.DeviceIdType.MESH

EPS_NORM = 1e-05
CLIP_NORM = 1.0
BETA_ONE = 0.9
BETA_TWO = 0.95
ADAM_EPSILON = 1e-08
DECAY_RATE = 0.1
VECTOR_RATE = 0.2


def nt(a,b): return lax.dot_general(a,b,(((1,),(1,)),((),())),preferred_element_type=F32)
def nn(a,b): return jnp.dot(a,b,preferred_element_type=F32)
def head_mask(rows):
    lane=lax.broadcasted_iota(jnp.int32,(rows,128),1)
    return (lane<HD)
def half(x,h,scale=1.0):
    m=head_mask(x.shape[0]); m = m if h==0 else jnp.logical_not(m)
    return jnp.where(m,x*jnp.asarray(scale,x.dtype),jnp.zeros_like(x))

def attn_fwd_pair(q_ref,k_ref,v_ref,length,o_ref,oT_ref,lse_ref,QB):
    L=q_ref.shape[0]
    vT=v_ref[...].T
    for i in range(L//QB):
        nk=(i+1)*QB
        qs=q_ref[pl.ds(i*QB,QB),:]
        outs=[]
        jidx=lax.broadcasted_iota(jnp.int32,(nk,QB),0)
        lim=jnp.minimum(i*QB+1+lax.broadcasted_iota(jnp.int32,(1,QB),1),length)
        for h in range(2):
            s=nt(k_ref[pl.ds(0,nk),:],half(qs,h,0.125))
            s=jnp.where(jidx<lim,s,-1e9)
            m=jnp.max(s,0,keepdims=True)
            e=jnp.exp(s-m)
            l=jnp.sum(e,0,keepdims=True)
            oT=nn(vT[HD*h:HD*h+HD,:nk],e.astype(BF))
            outs.append(oT/l)
            lse_ref[pl.ds(h,1),pl.ds(i*QB,QB)]=m+jnp.log(l)
        oT=jnp.concatenate(outs,0)
        oT_ref[:,pl.ds(i*QB,QB)]=oT
        o_ref[pl.ds(i*QB,QB),:]=oT.T.astype(BF)

def attn_bwd_pair(q_ref,k_ref,v_ref,do_ref,oT_ref,lse_ref,length,dq_ref,dk_ref,dv_ref,dk_acc,dv_acc,QB):
    L=q_ref.shape[0]
    kT=k_ref[...].T
    for i in reversed(range(L//QB)):
        nk=(i+1)*QB
        sl=pl.ds(i*QB,QB)
        qs=q_ref[sl,:]; do=do_ref[sl,:]
        doT=do.astype(F32).T
        prod=doT*oT_ref[:,sl]
        live=(i*QB+lax.broadcasted_iota(jnp.int32,(1,QB),1))<length
        tri=lax.broadcasted_iota(jnp.int32,(QB,QB),0)<=lax.broadcasted_iota(jnp.int32,(QB,QB),1)
        dqs=[]
        k=k_ref[pl.ds(0,nk),:]; v=v_ref[pl.ds(0,nk),:]
        dk=None; dv=None
        for h in range(2):
            delta=jnp.sum(prod[HD*h:HD*h+HD],0,keepdims=True)
            lse=jnp.where(live,lse_ref[pl.ds(h,1),sl],1e30)
            qm=half(qs,h,0.125); dom=half(do,h)
            s=nt(k,qm)
            p=jnp.exp(s-lse)
            pd=jnp.where(tri,p[nk-QB:],0.0)
            p=pd if i==0 else jnp.concatenate([p[:nk-QB],pd],0)
            dp=nt(v,dom)
            ds=(p*(dp-delta)).astype(BF)
            a=nn(p.astype(BF),dom); b=nn(ds,qm)
            dv=a if dv is None else dv+a
            dk=b if dk is None else dk+b
            dqs.append(nn(kT[HD*h:HD*h+HD,:nk],ds))
        dq_ref[sl,:]=(jnp.concatenate(dqs,0)*0.125).T.astype(BF)
        if i==L//QB-1:
            dk_acc[...]=dk; dv_acc[...]=dv
        else:
            dk_acc[pl.ds(0,nk),:]+=dk; dv_acc[pl.ds(0,nk),:]+=dv
    dk_ref[...]=dk_acc[...].astype(BF); dv_ref[...]=dv_acc[...].astype(BF)

def fwd_call(qkv,length,QB=256):
    L=qkv.shape[0]; D=qkv.shape[1]//3; NP=D//128
    def k(len_ref,q,k_,v,o,oT,lse):
        attn_fwd_pair(q,k_,v,len_ref[0],o,oT,lse.at[0],QB)
    return pl.pallas_call(k,grid=(NP,),
      in_specs=[pl.BlockSpec(memory_space=pltpu.SMEM)]+[pl.BlockSpec((L,128),functools.partial(lambda off,p:(0,off+p),j*NP)) for j in range(3)],
      out_specs=[pl.BlockSpec((L,128),lambda p:(0,p)),pl.BlockSpec((128,L),lambda p:(p,0)),pl.BlockSpec((1,2,L),lambda p:(p,0,0))],
      out_shape=[jax.ShapeDtypeStruct((L,D),BF),jax.ShapeDtypeStruct((D,L),F32),jax.ShapeDtypeStruct((NP,2,L),F32)],
      compiler_params=pltpu.CompilerParams(vmem_limit_bytes=56*2**20),
      cost_estimate=pl.CostEstimate(flops=4*L*L*D//2,bytes_accessed=10*2**20,transcendentals=12*L*L//2))(length,qkv,qkv,qkv)
def bwd_call(qkv,do,oT,lse,length,QB=256):
    L=qkv.shape[0]; D=qkv.shape[1]//3; NP=D//128
    def k(len_ref,q,k_,v,do,oT,lse,dq,dk,dv,dka,dva):
        attn_bwd_pair(q,k_,v,do,oT,lse.at[0],len_ref[0],dq,dk,dv,dka,dva,QB)
    blk=pl.BlockSpec((L,128),lambda p:(0,p))
    return pl.pallas_call(k,grid=(NP,),
      in_specs=[pl.BlockSpec(memory_space=pltpu.SMEM)]+[pl.BlockSpec((L,128),functools.partial(lambda off,p:(0,off+p),j*NP)) for j in range(3)]+[blk,pl.BlockSpec((128,L),lambda p:(p,0)),pl.BlockSpec((1,2,L),lambda p:(p,0,0))],
      out_specs=[blk]*3,
      out_shape=[jax.ShapeDtypeStruct((L,D),BF)]*3,
      scratch_shapes=[pltpu.VMEM((L,128),F32)]*2,
      compiler_params=pltpu.CompilerParams(vmem_limit_bytes=56*2**20),
      cost_estimate=pl.CostEstimate(flops=10*L*L*D//2,bytes_accessed=14*2**20,transcendentals=12*L*L//2))(length,qkv,qkv,qkv,do,oT,lse)


class Place:
    def __init__(self, Z):
        dp=lax.axis_index("dp"); fs=lax.axis_index("fsdp")
        self.Z=Z; self.y=dp//2; self.c=dp%2; self.z=fs//2; self.x=fs%2
        self.nx=(dp,self.z*2+1-self.x)
        self.ny=((1-self.y)*2+self.c,fs)
        self.nc=(self.y*2+1-self.c,fs)
        self.me=self.piece(self.z)
        self.dp=dp; self.fs=fs
    def nz(self,z): return (self.dp,z*2+self.x)
    def piece(self,z,dx=0,dy=0,dc=0):
        y=self.y if dy==0 else 1-self.y
        x=self.x if dx==0 else 1-self.x
        c=self.c if dc==0 else 1-self.c
        return ((y*2+c)*self.Z+z)*2+x
    def slab(self,y,dc=0):
        c=self.c if dc==0 else 1-self.c
        return (y*2+c)*self.Z*2

def enter(pl_, Z):
    bar=pltpu.get_barrier_semaphore()
    def sig(d): pl.semaphore_signal(bar,inc=1,device_id=d,device_id_type=MESH)
    sig(pl_.nx); sig(pl_.ny); sig(pl_.nc)
    @pl.when(pl_.z>0)
    def _():
        sig(pl_.nz(pl_.z-1))
    @pl.when(pl_.z<Z-1)
    def _():
        sig(pl_.nz(pl_.z+1))
    n=3+(pl_.z>0).astype(jnp.int32)+(pl_.z<Z-1).astype(jnp.int32)
    pl.semaphore_wait(bar,n)

def rcopy(src,dst,ss,rs,dev):
    return pltpu.make_async_remote_copy(src_ref=src,dst_ref=dst,send_sem=ss,recv_sem=rs,device_id=dev,device_id_type=MESH)

def when(cond,fn):
    if cond is True: fn()
    else: pl.when(cond)(fn)

def gather_sems(NG,Z):
    D=pltpu.SemaphoreType.DMA
    return [D((NG*2*(Z-1),)),D((NG*2*(Z-1),)),
            D((NG*2*Z,)),D((NG*2*Z,)),
            D((NG*2*Z,)),D((NG*2*Z,)),
            D((NG*2,)),D((NG*2,))]

class Gather:
    def __init__(self,P,G,groups,sems):
        self.P=P; self.G=G; self.groups=groups; self.zs,self.zr,self.xs,self.xr,self.ys,self.yr,self.cs,self.cr=sems
    def _cp(self,idx,lo,n,ss,rs,dev):
        r=self.G.at[idx,:,pl.ds(lo,n)]
        return rcopy(r,r,ss,rs,dev)
    def zcp(self,g,d,t,zo,to):
        lo,n,_=self.groups[g]; i=(g*2+d)*(self.P.Z-1)+t
        return self._cp(self.P.piece(zo),lo,n,self.zs.at[i],self.zr.at[i],self.P.nz(to))
    def xfull(self,g,zo,arrive=0):
        lo,n,_=self.groups[g]; i=g*2*self.P.Z+zo
        return self._cp(self.P.piece(zo,dx=arrive),lo,n,self.xs.at[i],self.xr.at[i],self.P.nx)
    def yfull(self,g,zo,arrive=0):
        lo,n,_=self.groups[g]; i=g*2*self.P.Z+zo
        return self._cp(self.P.piece(zo,dy=arrive),lo,n,self.ys.at[i],self.yr.at[i],self.P.ny)
    def ydiag(self,g,zo,arrive=0):
        lo,n,a=self.groups[g]; i=g*2*self.P.Z+self.P.Z+zo
        return self._cp(self.P.piece(zo,dx=1,dy=arrive),lo,a,self.ys.at[i],self.yr.at[i],self.P.ny)
    def xdiag(self,g,zo,arrive=0):
        lo,n,a=self.groups[g]; i=g*2*self.P.Z+self.P.Z+zo
        return self._cp(self.P.piece(zo,dy=1,dx=arrive),lo+a,n-a,self.xs.at[i],self.xr.at[i],self.P.nx)
    def ccp(self,g,k,arrive=0):
        lo,n,_=self.groups[g]; Z=self.P.Z
        y=self.P.y if k==0 else 1-self.P.y
        r=self.G.at[pl.ds(self.P.slab(y,dc=arrive),2*Z),:,pl.ds(lo,n)]
        return rcopy(r,r,self.cs.at[g*2+k],self.cr.at[g*2+k],self.P.nc)
    def own(self,g):
        z=self.P.z; Z=self.P.Z
        when(z<Z-1,lambda: self.zcp(g,0,0,z,z+1).start())
        when(z>0,lambda: self.zcp(g,1,0,z,z-1).start())
        self.xfull(g,z).start(); self.yfull(g,z).start()
    def zarrive(self,g,t):
        z=self.P.z; Z=self.P.Z
        def below():
            zo=z-1-t
            self.zcp(g,0,t,zo,z).wait_recv()
            if t+1<Z-1:
                when(z<Z-1,lambda: self.zcp(g,0,t+1,zo,z+1).start())
            self.xfull(g,zo).start(); self.yfull(g,zo).start()
        def above():
            zo=z+1+t
            self.zcp(g,1,t,zo,z).wait_recv()
            if t+1<Z-1:
                when(z>0,lambda: self.zcp(g,1,t+1,zo,z-1).start())
            self.xfull(g,zo).start(); self.yfull(g,zo).start()
        when(z-1-t>=0,below); when(z+1+t<Z,above)
    def _diag(self,g,zo):
        self.xfull(g,zo,1).wait_recv(); self.ydiag(g,zo).start()
        self.yfull(g,zo,1).wait_recv(); self.xdiag(g,zo).start()
    def diag(self,g,t):
        z=self.P.z; Z=self.P.Z
        if t==0: self._diag(g,z)
        else:
            when(z-t>=0,lambda: self._diag(g,z-t))
            when(z+t<Z,lambda: self._diag(g,z+t))
    def corner(self,g):
        self.ccp(g,0).start()
        for zo in range(self.P.Z):
            self.ydiag(g,zo,1).wait_recv(); self.xdiag(g,zo,1).wait_recv()
        self.ccp(g,1).start()
    def sibling(self,g):
        self.ccp(g,0,1).wait_recv(); self.ccp(g,1,1).wait_recv()
    def drain(self,g):
        z=self.P.z; Z=self.P.Z
        for zo in range(Z):
            self.xfull(g,zo).wait_send(); self.yfull(g,zo).wait_send()
            self.xdiag(g,zo).wait_send(); self.ydiag(g,zo).wait_send()
        for k in range(2): self.ccp(g,k).wait_send()
        for t in range(Z-1):
            when(jnp.logical_and(z<Z-1,z-t>=0),lambda: self.zcp(g,0,t,z-t,z+1).wait_send())
            when(jnp.logical_and(z>0,z+t<=Z-1),lambda: self.zcp(g,1,t,z+t,z-1).wait_send())
    def events(self,g):
        Z=self.P.Z
        ev=[lambda: self.own(g)]
        for t in range(Z-1):
            ev.append(lambda t=t: self.zarrive(g,t))
            ev.append(lambda t=t: self.diag(g,t))
        ev.append(lambda: self.diag(g,Z-1))
        ev.append(lambda: self.corner(g))
        ev.append(lambda: self.sibling(g))
        return ev


def rs_sems(NG,Z):
    D=pltpu.SemaphoreType.DMA
    return [D((NG*2,)),D((NG*2,)),
            D((NG*3,)),D((NG*3,)),
            D((NG*2,)),D((NG*2,)),
            D((NG*2*Z,)),D((NG*2*Z,))]
def rs_bufs(groups,Z):
    V=lambda *s: pltpu.VMEM(s,BF)
    out=[]
    for lo,n,a in groups:
        out+=[V(2,Z,2,16,n),V(Z,2,16,a),V(Z,16,a),V(2,Z,16,n-a),V(Z,16,n-a),V(Z,16,n),V(Z,16,n)]
    return out
NB=7
class Scatter:
    def __init__(self,P,R,groups,bufs,sems):
        self.P=P; self.R=R; self.groups=groups
        self.b=[bufs[NB*g:NB*g+NB] for g in range(len(groups))]
        self.cs,self.cr,self.xs,self.xr,self.ys,self.yr,self.zs,self.zr=sems
    def row(self,dy=0,dc=0):
        y=self.P.y if dy==0 else 1-self.P.y
        c=self.P.c if dc==0 else 1-self.P.c
        return y*2+c
    def add(self,dst,src,z0=0,nz=None):
        def body(z,_):
            d=dst(z); s=src(z)
            d[...]=(d[...].astype(F32)+s[...].astype(F32)).astype(BF)
            return 0
        lax.fori_loop(0,self.P.Z,body,0)
    def ccp(self,g,k):
        lo,n,_=self.groups[g]
        return rcopy(self.R.at[self.row(k,1),:,:,:,pl.ds(lo,n)],self.b[g][0].at[k],self.cs.at[g*2+k],self.cr.at[g*2+k],self.P.nc)
    def x1(self,g,k):
        lo,n,a=self.groups[g]
        return rcopy(self.R.at[self.row(k),:,1-self.P.x,:,pl.ds(lo+a,n-a)],self.b[g][3].at[k],self.xs.at[g*3+k],self.xr.at[g*3+k],self.P.nx)
    def y1(self,g):
        lo,n,a=self.groups[g]
        return rcopy(self.R.at[self.row(1),:,:,:,pl.ds(lo,a)],self.b[g][1],self.ys.at[g*2],self.yr.at[g*2],self.P.ny)
    def x2(self,g):
        lo,n,a=self.groups[g]
        return rcopy(self.R.at[self.row(0),:,1-self.P.x,:,pl.ds(lo,a)],self.b[g][2],self.xs.at[g*3+2],self.xr.at[g*3+2],self.P.nx)
    def y2(self,g):
        lo,n,a=self.groups[g]
        return rcopy(self.R.at[self.row(1),:,self.P.x,:,pl.ds(lo+a,n-a)],self.b[g][4],self.ys.at[g*2+1],self.yr.at[g*2+1],self.P.ny)
    def zc(self,g,d,zo,to):
        lo,n,_=self.groups[g]; i=(g*2+d)*self.P.Z+zo
        return rcopy(self.R.at[self.row(0),zo,self.P.x,:,pl.ds(lo,n)],self.b[g][5+d].at[zo],self.zs.at[i],self.zr.at[i],self.P.nz(to))
    def s_c(self,g):
        self.ccp(g,1).start(); self.ccp(g,0).start()
    def a_c(self,g):
        lo,n,a=self.groups[g]; R=self.R; b=self.b[g][0]
        for k in (1,0):
            self.ccp(g,k).wait_recv()
            r=self.row(k)
            self.add(lambda z: R.at[r,z,:,:,pl.ds(lo,n)],lambda z: b.at[k,z])
            self.x1(g,k).start()
            if k==1: self.y1(g).start()
    def a_1(self,g):
        lo,n,a=self.groups[g]; R=self.R; B=self.b[g]; P=self.P
        self.y1(g).wait_recv()
        r=self.row(0)
        self.add(lambda z: R.at[r,z,:,:,pl.ds(lo,a)],lambda z: B[1].at[z])
        self.x2(g).start()
        for k in (1,0):
            self.x1(g,k).wait_recv()
            q=self.row(k)
            self.add(lambda z: R.at[q,z,P.x,:,pl.ds(lo+a,n-a)],lambda z: B[3].at[k,z])
            if k==1: self.y2(g).start()
    def a_2(self,g):
        lo,n,a=self.groups[g]; R=self.R; B=self.b[g]; P=self.P
        r=self.row(0)
        self.x2(g).wait_recv()
        self.add(lambda z: R.at[r,z,P.x,:,pl.ds(lo,a)],lambda z: B[2].at[z])
        self.y2(g).wait_recv()
        self.add(lambda z: R.at[r,z,P.x,:,pl.ds(lo+a,n-a)],lambda z: B[4].at[z])
    def zstep(self,g,t):
        lo,n,_=self.groups[g]; R=self.R; B=self.b[g]; P=self.P; Z=P.Z; z=P.z
        r=self.row(0)
        def acc(zo,buf):
            d=R.at[r,zo,P.x,:,pl.ds(lo,n)]
            d[...]=(d[...].astype(F32)+buf[zo].astype(F32)).astype(BF)
        def up():
            zo=Z-1-t
            @pl.when(z>0)
            def _():
                self.zc(g,0,zo,z).wait_recv()
                acc(zo,B[5])
            self.zc(g,0,zo,z+1).start()
        def down():
            zo=t
            @pl.when(z<Z-1)
            def _():
                self.zc(g,1,zo,z).wait_recv()
                acc(zo,B[6])
            self.zc(g,1,zo,z-1).start()
        when(z<Z-1-t,up); when(z>t,down)
    def final(self,g,out):
        lo,n,_=self.groups[g]; P=self.P; Z=P.Z; z=P.z; B=self.b[g]
        out[...]=self.R[self.row(0),z,P.x,:,pl.ds(lo,n)].astype(F32)
        @pl.when(z>0)
        def _():
            self.zc(g,0,z,z).wait_recv()
            out[...]+=B[5][z].astype(F32)
        @pl.when(z<Z-1)
        def _():
            self.zc(g,1,z,z).wait_recv()
            out[...]+=B[6][z].astype(F32)
    def drain(self,g):
        Z=self.P.Z; z=self.P.z
        for k in range(2):
            self.ccp(g,k).wait_send(); self.x1(g,k).wait_send()
        self.x2(g).wait_send(); self.y1(g).wait_send(); self.y2(g).wait_send()
        for t in range(Z-1):
            when(z<Z-1-t,lambda: self.zc(g,0,Z-1-t,z+1).wait_send())
            when(z>t,lambda: self.zc(g,1,t,z-1).wait_send())
    def events(self,g,out):
        ev=[lambda: self.s_c(g),lambda: self.a_c(g),lambda: self.a_1(g),lambda: self.a_2(g)]
        for t in range(self.P.Z-1): ev.append(lambda t=t: self.zstep(g,t))
        ev.append(lambda: self.final(g,out))
        return ev

def norm_sems(Z):
    D=pltpu.SemaphoreType.DMA
    return [D((3+Z,)),D((3+Z,))]
def norm_bufs(Z): return [pltpu.VMEM((4+Z,8,128),F32),pltpu.VMEM((3,8,128),F32)]
def all_sum(P,buf,got,ss,rs):
    Z=P.Z
    for i,dev in enumerate((P.nc,P.nx,P.ny)):
        cp=rcopy(buf.at[i],got.at[i],ss.at[i],rs.at[i],dev)
        cp.start(); cp.wait()
        buf[i+1]=buf[i]+got[i]
    buf[4+P.z]=buf[3]
    for t in range(Z):
        def send(): rcopy(buf.at[3],buf.at[4+P.z],ss.at[3+t],rs.at[3+P.z],P.nz(t)).start()
        when(P.z!=t,send)
    for t in range(Z):
        def wait():
            cp=rcopy(buf.at[3],buf.at[4+t],ss.at[3+t],rs.at[3+t],P.nz(t))
            cp.wait_send(); cp.wait_recv()
        when(P.z!=t,wait)
    tot=buf[4]
    for t in range(1,Z): tot=tot+buf[4+t]
    return tot
def enter_all(P,Z):
    bar=pltpu.get_barrier_semaphore()
    def sig(d): pl.semaphore_signal(bar,inc=1,device_id=d,device_id_type=MESH)
    sig(P.nx); sig(P.ny); sig(P.nc)
    for t in range(Z):
        when(P.z!=t,lambda: sig(P.nz(t)))
    pl.semaphore_wait(bar,3+Z-1)


def layer_norm(values, gain, shift):
    center = jnp.mean(values, -1, keepdims=True)
    centered = values - center
    spread = jnp.mean(centered * centered, -1, keepdims=True)
    return centered * lax.rsqrt(spread + EPS_NORM) * gain + shift


def smooth_gate(value):
    return jax.nn.gelu(value, approximate=True)


def adam_step(weight, first_mom, second_mom, gradient, step_rate):
    first_new = BETA_ONE * first_mom + (1.0 - BETA_ONE) * gradient
    second_new = BETA_TWO * second_mom + (1.0 - BETA_TWO) * gradient * gradient
    fix_one = 1.0 - BETA_ONE**STEP
    fix_two = 1.0 - BETA_TWO**STEP
    update = (
        first_new / fix_one / (jnp.sqrt(second_new / fix_two) + ADAM_EPSILON) + DECAY_RATE * weight
    )
    return (weight - step_rate * update, first_new, second_new)


VEC_COLS = 128
QKV_AT = 0
VEC_AT = 3456
OUT_AT = 3584
UP_AT = 4736
DOWN_AT = 9344
COLS = 13952
GROUPS = [(0, 3584, 1792), (3584, 5760, 2944), (9344, 4608, 2304)]


def pack24(block, parity):
    n = block.shape[1]
    main = lax.dynamic_slice(block, (8 * parity, 0), (16, n))
    rest = lax.dynamic_slice(block, (16 * (1 - parity), 0), (8, n))
    return jnp.concatenate([main, jnp.concatenate([rest[:, : n // 2], rest[:, n // 2 :]], 0)], 1)


def unpack24(piece, parity):
    n = piece.shape[1] * 2 // 3
    main = piece[:, :n]
    rest = jnp.concatenate([piece[:8, n:], piece[8:, n:]], 1)
    return jnp.where(
        parity == 0, jnp.concatenate([main, rest], 0), jnp.concatenate([rest, main], 0)
    )


def pack96(block):
    n = block.shape[1]
    return block.reshape(6, 16, n).transpose(1, 0, 2).reshape(16, 6 * n)


def unpack96(piece):
    n = piece.shape[1] // 6
    return piece.reshape(16, 6, n).transpose(1, 0, 2).reshape(96, n)


def pack_grad24(grad):
    n = grad.shape[1]
    pairs = grad.reshape(-1, 48, n)
    mid = pairs[:, 16:32]

    def rest(rows):
        return jnp.concatenate([rows[..., : n // 2], rows[..., n // 2 :]], 1)

    even = jnp.concatenate([pairs[:, :16], rest(mid[:, :8])], 2)
    odd = jnp.concatenate([pairs[:, 32:], rest(mid[:, 8:])], 2)
    return jnp.stack([even, odd], 1).reshape(-1, 16, 3 * n // 2).astype(BF)


def pack_grad96(grad):
    n = grad.shape[1]
    return grad.reshape(-1, 6, 16, n).transpose(0, 2, 1, 3).reshape(-1, 16, 6 * n).astype(BF)


def unpack_group(G, at, w_ref):
    n = w_ref.shape[1]
    h = n // 2

    def body(j, _):
        r = pl.multiple_of(j * 48, 16)
        w_ref[pl.ds(r, 16), :] = G[2 * j, :, pl.ds(at, n)]
        w_ref[pl.ds(r + 32, 16), :] = G[2 * j + 1, :, pl.ds(at, n)]
        a = G[2 * j, :, pl.ds(at + n, h)].astype(F32)
        b = G[2 * j + 1, :, pl.ds(at + n, h)].astype(F32)
        w_ref[pl.ds(r + 16, 16), pl.ds(0, h)] = jnp.concatenate([a[:8], b[:8]], 0).astype(BF)
        w_ref[pl.ds(r + 16, 16), pl.ds(h, h)] = jnp.concatenate([a[8:], b[8:]], 0).astype(BF)
        return 0

    lax.fori_loop(0, G.shape[0] // 2, body, 0)


def unpack_down(G, at, w_ref):
    n = w_ref.shape[1]

    def body(k, _):
        for r in range(6):
            w_ref[pl.ds(pl.multiple_of(k * 96 + 16 * r, 16), 16), :] = G[k, :, pl.ds(at + r * n, n)]
        return 0

    lax.fori_loop(0, G.shape[0], body, 0)


def gather_kernel(Z, own_ref, wqkv, wout, wup, wdown, vec, G, *sems):
    place = Place(Z)
    G[place.me] = own_ref[...]
    enter(place, Z)
    ga = Gather(place, G, GROUPS, sems)
    evs = [ga.events(g) for g in range(3)]
    n = len(evs[0])
    off = 2
    for s in range(n + 2 * off):
        for g in range(3):
            k = s - off * g
            if 0 <= k < n:
                evs[g][k]()
                if k == n - 1:
                    if g == 0:
                        unpack_group(G, QKV_AT, wqkv)
                        vec[...] = G[:, :, pl.ds(VEC_AT, VEC_COLS)]
                    if g == 1:
                        unpack_group(G, OUT_AT, wout)
                        unpack_group(G, UP_AT, wup)
                    if g == 2:
                        unpack_down(G, DOWN_AT, wdown)
    for g in range(3):
        ga.drain(g)


def gather_call(own, Z):
    pieces = 8 * Z
    vm = pl.BlockSpec(memory_space=pltpu.VMEM)
    return pl.pallas_call(
        functools.partial(gather_kernel, Z),
        out_shape=[
            jax.ShapeDtypeStruct((D, 3 * D), BF),
            jax.ShapeDtypeStruct((D, D), BF),
            jax.ShapeDtypeStruct((D, FF), BF),
            jax.ShapeDtypeStruct((FF, D), BF),
            jax.ShapeDtypeStruct((pieces, 16, VEC_COLS), BF),
        ],
        in_specs=[vm],
        out_specs=[vm] * 5,
        scratch_shapes=[pltpu.VMEM((pieces, 16, COLS), BF)] + gather_sems(3, Z),
        compiler_params=pltpu.CompilerParams(
            collective_id=1, has_side_effects=True, vmem_limit_bytes=60 * 2**20
        ),
        cost_estimate=pl.CostEstimate(flops=0, bytes_accessed=150 * 2**20, transcendentals=0),
    )(own)


def scatter_kernel(Z, r_qkv, r_vec, r_out, r_up, r_down, mask, out, nrm, R, *rest):
    bufs = rest[: NB * 3]
    sems = rest[NB * 3 : NB * 3 + 8]
    nb, got, ns, nr, isem = rest[NB * 3 + 8 :]
    place = Place(Z)

    def load(ref, at, i):
        return pltpu.make_async_copy(ref, R.at[:, :, :, :, pl.ds(at, ref.shape[4])], isem.at[i])

    cps = [
        [load(r_qkv, QKV_AT, 0), load(r_vec, VEC_AT, 1)],
        [load(r_out, OUT_AT, 2), load(r_up, UP_AT, 3)],
        [load(r_down, DOWN_AT, 4)],
    ]
    for c in reversed(cps):
        for d in c:
            d.start()
    enter_all(place, Z)
    sc = Scatter(place, R, GROUPS, bufs, sems)
    order = (2, 1, 0)
    evs = [sc.events(g, out.at[:, pl.ds(GROUPS[g][0], GROUPS[g][1])]) for g in order]
    n = len(evs[0])
    off = 2
    for s in range(n + 2 * off):
        for q in range(3):
            k = s - off * q
            if 0 <= k < n:
                if k == 0:
                    for d in cps[order[q]]:
                        d.wait()
                evs[q][k]()
    own = out[...]
    vec = out[:, pl.ds(VEC_AT, VEC_COLS)]
    masked = vec * mask[...]
    sq = jnp.sum(own * own) - jnp.sum(vec * vec) + jnp.sum(masked * masked)
    nb[0] = jnp.full((8, 128), 1.0, F32) * sq
    nrm[...] = all_sum(place, nb, got, ns, nr)
    for g in range(3):
        sc.drain(g)


def scatter_call(parts, mask, Z):
    parts = [p.reshape(4, Z, 2, 16, p.shape[2]) for p in parts]
    vm = pl.BlockSpec(memory_space=pltpu.VMEM)
    return pl.pallas_call(
        functools.partial(scatter_kernel, Z),
        out_shape=[jax.ShapeDtypeStruct((16, COLS), F32), jax.ShapeDtypeStruct((8, 128), F32)],
        in_specs=[pl.BlockSpec(memory_space=pl.ANY)] * 5 + [vm],
        out_specs=[vm] * 2,
        scratch_shapes=[pltpu.VMEM((4, Z, 2, 16, COLS), BF)]
        + rs_bufs(GROUPS, Z)
        + rs_sems(3, Z)
        + norm_bufs(Z)
        + norm_sems(Z)
        + [pltpu.SemaphoreType.DMA((5,))],
        compiler_params=pltpu.CompilerParams(
            collective_id=2, has_side_effects=True, vmem_limit_bytes=60 * 2**20
        ),
        cost_estimate=pl.CostEstimate(flops=0, bytes_accessed=150 * 2**20, transcendentals=0),
    )(*parts, mask)


def shards(
    sizes,
    tokens,
    lengths,
    cotangent,
    w_qkv,
    m_qkv,
    v_qkv,
    w_out,
    m_out,
    v_out,
    w_up,
    m_up,
    v_up,
    w_down,
    m_down,
    v_down,
    packed,
    m_packed,
    v_packed,
):
    seq_count, seq_len, model_width = tokens.shape
    row_count = seq_count * seq_len
    axes = ("dp", "fsdp")
    dp, fsdp = sizes
    direct = dp == 4 and fsdp % 2 == 0 and w_qkv.shape[0] == 24 and dp * fsdp * 24 == D
    Z = fsdp // 2
    vec_rows = packed.shape[0]
    if direct:
        parity = lax.axis_index("fsdp") % 2
        vec_piece = jnp.pad(packed.astype(BF), (0, 16 * VEC_COLS - vec_rows)).reshape(16, VEC_COLS)
        own = jnp.concatenate(
            [
                pack24(w_qkv.astype(BF), parity),
                vec_piece,
                pack24(w_out.astype(BF), parity),
                pack24(w_up.astype(BF), parity),
                pack96(w_down.astype(BF)),
            ],
            1,
        )
        wqkv_b, wout_b, wup_b, wdown_b, vec_all = gather_call(own, Z)
        vector_b = vec_all.reshape(-1, 16 * VEC_COLS)[:, :vec_rows].reshape(-1)
    else:
        wqkv_b, wout_b, wup_b, wdown_b, vector_b = [
            lax.all_gather(w.astype(BF), axes, axis=0, tiled=True)
            for w in (w_qkv, w_out, w_up, w_down, packed)
        ]
    vector = vector_b.astype(F32)
    gain_one = vector[:model_width]
    bias_one = vector[model_width : 2 * model_width]
    gain_two = vector[2 * model_width : 3 * model_width]
    bias_two = vector[3 * model_width : 4 * model_width]
    bias_attn = vector[4 * model_width : 5 * model_width]
    bias_down = vector[5 * model_width : 6 * model_width]
    bias_up = vector[6 * model_width :]
    positions = jnp.arange(seq_len, dtype=jnp.int32)
    live_rows = positions[None, :] < lengths[:, None]
    inputs = tokens.astype(F32).reshape(row_count, model_width)
    normed_one, norm_one_back = jax.vjp(layer_norm, inputs, gain_one, bias_one)
    normed_one_b = normed_one.astype(BF)
    qkv_all = jnp.dot(normed_one_b, wqkv_b, preferred_element_type=F32).astype(BF)
    attended_b, attended_t, log_total = fwd_call(qkv_all, lengths, 512)
    resid_one = inputs + jnp.dot(attended_b, wout_b, preferred_element_type=F32) + bias_attn
    normed_two, norm_two_back = jax.vjp(layer_norm, resid_one, gain_two, bias_two)
    normed_two_b = normed_two.astype(BF)
    upper = jnp.dot(normed_two_b, wup_b, preferred_element_type=F32) + bias_up
    activ, gate_back = jax.vjp(smooth_gate, upper)
    activ_b = activ.astype(BF)
    mixed = resid_one + jnp.dot(activ_b, wdown_b, preferred_element_type=F32) + bias_down
    mixed = mixed.reshape(seq_count, seq_len, model_width).astype(BF)
    grad_b = (
        (cotangent.astype(F32) * live_rows[:, :, None].astype(F32))
        .astype(BF)
        .reshape(row_count, model_width)
    )
    grad_full = grad_b.astype(F32)
    d_wdown = jnp.dot(activ_b.T, grad_b, preferred_element_type=F32)
    d_bias_down = jnp.sum(grad_full, 0)
    d_activ = jnp.dot(grad_b, wdown_b.T, preferred_element_type=F32)
    (d_upper,) = gate_back(d_activ)
    d_upper_b = d_upper.astype(BF)
    d_bias_up = jnp.sum(d_upper_b.astype(F32), 0)
    d_wup = jnp.dot(normed_two_b.T, d_upper_b, preferred_element_type=F32)
    d_normed_two = jnp.dot(d_upper_b, wup_b.T, preferred_element_type=F32)
    d_resid_norm, d_gain_two, d_bias_two = norm_two_back(d_normed_two)
    d_resid = grad_full + d_resid_norm
    d_branch_b = d_resid.astype(BF)
    d_bias_attn = jnp.sum(d_branch_b.astype(F32), 0)
    d_wout = jnp.dot(attended_b.T, d_branch_b, preferred_element_type=F32)
    d_attended_b = jnp.dot(d_branch_b, wout_b.T, preferred_element_type=F32).astype(BF)
    d_q, d_k, d_v = bwd_call(qkv_all, d_attended_b, attended_t, log_total, lengths)
    d_qkv_b = jnp.concatenate([d_q, d_k, d_v], 1)
    d_wqkv = jnp.dot(normed_one_b.T, d_qkv_b, preferred_element_type=F32)
    d_normed_one = jnp.dot(d_qkv_b, wqkv_b.T, preferred_element_type=F32)
    d_input_norm, d_gain_one, d_bias_one = norm_one_back(d_normed_one)
    d_tokens = (d_resid + d_input_norm).reshape(seq_count, seq_len, model_width)
    d_vector = jnp.concatenate(
        [d_gain_one, d_bias_one, d_gain_two, d_bias_two, d_bias_attn, d_bias_down, d_bias_up]
    )
    if direct:
        vec_parts = jnp.pad(
            d_vector.reshape(-1, vec_rows), ((0, 0), (0, 16 * VEC_COLS - vec_rows))
        ).reshape(-1, 16, VEC_COLS)
        flat = jnp.arange(16 * VEC_COLS).reshape(16, VEC_COLS)
        mask = (flat < vec_rows).astype(F32)
        own, norm_tile = scatter_call(
            [
                pack_grad24(d_wqkv),
                vec_parts.astype(BF),
                pack_grad24(d_wout),
                pack_grad24(d_wup),
                pack_grad96(d_wdown),
            ],
            mask,
            Z,
        )
        g_qkv = unpack24(own[:, QKV_AT:VEC_AT], parity)
        g_vec = own[:, VEC_AT:OUT_AT].reshape(-1)[:vec_rows]
        g_out = unpack24(own[:, OUT_AT:UP_AT], parity)
        g_up = unpack24(own[:, UP_AT:DOWN_AT], parity)
        g_down = unpack96(own[:, DOWN_AT:])
        grad_norm = jnp.sqrt(norm_tile[0, 0])
    else:
        g_qkv, g_out, g_up, g_down, g_vec = [
            lax.psum_scatter(g, axes, scatter_dimension=0, tiled=True)
            for g in (d_wqkv, d_wout, d_wup, d_wdown, d_vector)
        ]
        local_squares = sum(jnp.sum(g * g) for g in (g_qkv, g_out, g_up, g_down, g_vec))
        grad_norm = jnp.sqrt(lax.psum(local_squares, axes))
    factor = jnp.minimum(1.0, CLIP_NORM / (grad_norm + 1e-06))
    new_qkv = adam_step(w_qkv, m_qkv, v_qkv, g_qkv * factor, D ** (-0.5))
    new_out = adam_step(w_out, m_out, v_out, g_out * factor, D ** (-0.5))
    new_up = adam_step(w_up, m_up, v_up, g_up * factor, D ** (-0.5))
    new_down = adam_step(w_down, m_down, v_down, g_down * factor, FF ** (-0.5))
    new_vec = adam_step(packed, m_packed, v_packed, g_vec * factor, VECTOR_RATE)
    return (mixed, d_tokens, grad_norm) + new_qkv + new_out + new_up + new_down + new_vec


def solution(mesh):
    rows = P(("dp", "fsdp"), None)
    seqs = P(("dp", "fsdp"), None, None)
    flat = P(("dp", "fsdp"))
    in_specs = (seqs, flat, seqs) + (rows,) * 12 + (flat,) * 3
    out_specs = (seqs, seqs, P()) + (rows,) * 12 + (flat,) * 3
    sizes = (mesh.shape["dp"], mesh.shape["fsdp"])
    return jax.shard_map(
        functools.partial(shards, sizes),
        mesh=mesh,
        in_specs=in_specs,
        out_specs=out_specs,
        check_vma=False,
    )
```

```python
import functools

import jax
import jax.numpy as jnp
from jax import lax
from jax.experimental import pallas as pl
from jax.experimental.pallas import tpu as pltpu
from jax.sharding import PartitionSpec as P

D = 768
FF = 3072
HEAD_DIM = 64
STEP = 10
HD = 64
F32 = jnp.float32
BF = jnp.bfloat16
MESH = pl.DeviceIdType.MESH

EPS_NORM = 1e-05
CLIP_NORM = 1.0
BETA_ONE = 0.9
BETA_TWO = 0.95
ADAM_EPSILON = 1e-08
DECAY_RATE = 0.1
VECTOR_RATE = 0.2


def nt(a,b): return lax.dot_general(a,b,(((1,),(1,)),((),())),preferred_element_type=F32)
def nn(a,b): return jnp.dot(a,b,preferred_element_type=F32)
def head_mask(rows):
    lane=lax.broadcasted_iota(jnp.int32,(rows,128),1)
    return (lane<HD)
def half(x,h,scale=1.0):
    m=head_mask(x.shape[0]); m = m if h==0 else jnp.logical_not(m)
    return jnp.where(m,x*jnp.asarray(scale,x.dtype),jnp.zeros_like(x))

def attn_fwd_pair(q_ref,k_ref,v_ref,length,o_ref,oT_ref,lse_ref,QB,tick=None):
    L=q_ref.shape[0]
    vT=v_ref[...].T
    for i in range(L//QB):
        nk=(i+1)*QB
        qs=q_ref[pl.ds(i*QB,QB),:]
        outs=[]
        jidx=lax.broadcasted_iota(jnp.int32,(nk,QB),0)
        lim=jnp.minimum(i*QB+1+lax.broadcasted_iota(jnp.int32,(1,QB),1),length)
        for h in range(2):
            s=nt(k_ref[pl.ds(0,nk),:],half(qs,h,0.125))
            s=jnp.where(jidx<lim,s,-1e9)
            m=jnp.max(s,0,keepdims=True)
            e=jnp.exp(s-m)
            l=jnp.sum(e,0,keepdims=True)
            oT=nn(vT[HD*h:HD*h+HD,:nk],e.astype(BF))
            outs.append(oT/l)
            lse_ref[pl.ds(h,1),pl.ds(i*QB,QB)]=m+jnp.log(l)
            if tick is not None: tick(2*i+h)
        oT=jnp.concatenate(outs,0)
        oT_ref[:,pl.ds(i*QB,QB)]=oT
        o_ref[pl.ds(i*QB,QB),:]=oT.T.astype(BF)

def attn_bwd_pair(q_ref,k_ref,v_ref,do_ref,oT_ref,lse_ref,length,dq_ref,dk_ref,dv_ref,dk_acc,dv_acc,QB,tick=None):
    L=q_ref.shape[0]
    kT=k_ref[...].T
    for i in reversed(range(L//QB)):
        nk=(i+1)*QB
        sl=pl.ds(i*QB,QB)
        qs=q_ref[sl,:]; do=do_ref[sl,:]
        doT=do.astype(F32).T
        prod=doT*oT_ref[:,sl]
        live=(i*QB+lax.broadcasted_iota(jnp.int32,(1,QB),1))<length
        tri=lax.broadcasted_iota(jnp.int32,(QB,QB),0)<=lax.broadcasted_iota(jnp.int32,(QB,QB),1)
        dqs=[]
        k=k_ref[pl.ds(0,nk),:]; v=v_ref[pl.ds(0,nk),:]
        dk=None; dv=None
        for h in range(2):
            delta=jnp.sum(prod[HD*h:HD*h+HD],0,keepdims=True)
            lse=jnp.where(live,lse_ref[pl.ds(h,1),sl],1e30)
            qm=half(qs,h,0.125); dom=half(do,h)
            s=nt(k,qm)
            p=jnp.exp(s-lse)
            pd=jnp.where(tri,p[nk-QB:],0.0)
            p=pd if i==0 else jnp.concatenate([p[:nk-QB],pd],0)
            dp=nt(v,dom)
            ds=(p*(dp-delta)).astype(BF)
            a=nn(p.astype(BF),dom); b=nn(ds,qm)
            dv=a if dv is None else dv+a
            dk=b if dk is None else dk+b
            dqs.append(nn(kT[HD*h:HD*h+HD,:nk],ds))
        dq_ref[sl,:]=(jnp.concatenate(dqs,0)*0.125).T.astype(BF)
        if i==L//QB-1:
            dk_acc[...]=dk; dv_acc[...]=dv
        else:
            dk_acc[pl.ds(0,nk),:]+=dk; dv_acc[pl.ds(0,nk),:]+=dv
        if tick is not None: tick(L//QB-1-i)
    dk_ref[...]=dk_acc[...].astype(BF); dv_ref[...]=dv_acc[...].astype(BF)

def fwd_call(qkv,length,QB=256):
    L=qkv.shape[0]; D=qkv.shape[1]//3; NP=D//128
    def k(len_ref,q,k_,v,o,oT,lse):
        attn_fwd_pair(q,k_,v,len_ref[0],o,oT,lse.at[0],QB)
    return pl.pallas_call(k,grid=(NP,),
      in_specs=[pl.BlockSpec(memory_space=pltpu.SMEM)]+[pl.BlockSpec((L,128),functools.partial(lambda off,p:(0,off+p),j*NP)) for j in range(3)],
      out_specs=[pl.BlockSpec((L,128),lambda p:(0,p)),pl.BlockSpec((128,L),lambda p:(p,0)),pl.BlockSpec((1,2,L),lambda p:(p,0,0))],
      out_shape=[jax.ShapeDtypeStruct((L,D),BF),jax.ShapeDtypeStruct((D,L),F32),jax.ShapeDtypeStruct((NP,2,L),F32)],
      compiler_params=pltpu.CompilerParams(vmem_limit_bytes=56*2**20),
      cost_estimate=pl.CostEstimate(flops=4*L*L*D//2,bytes_accessed=10*2**20,transcendentals=12*L*L//2))(length,qkv,qkv,qkv)
def bwd_call(qkv,do,oT,lse,length,QB=256):
    L=qkv.shape[0]; D=qkv.shape[1]//3; NP=D//128
    def k(len_ref,q,k_,v,do,oT,lse,dq,dk,dv,dka,dva):
        attn_bwd_pair(q,k_,v,do,oT,lse.at[0],len_ref[0],dq,dk,dv,dka,dva,QB)
    blk=pl.BlockSpec((L,128),lambda p:(0,p))
    return pl.pallas_call(k,grid=(NP,),
      in_specs=[pl.BlockSpec(memory_space=pltpu.SMEM)]+[pl.BlockSpec((L,128),functools.partial(lambda off,p:(0,off+p),j*NP)) for j in range(3)]+[blk,pl.BlockSpec((128,L),lambda p:(p,0)),pl.BlockSpec((1,2,L),lambda p:(p,0,0))],
      out_specs=[blk]*3,
      out_shape=[jax.ShapeDtypeStruct((L,D),BF)]*3,
      scratch_shapes=[pltpu.VMEM((L,128),F32)]*2,
      compiler_params=pltpu.CompilerParams(vmem_limit_bytes=56*2**20),
      cost_estimate=pl.CostEstimate(flops=10*L*L*D//2,bytes_accessed=14*2**20,transcendentals=12*L*L//2))(length,qkv,qkv,qkv,do,oT,lse)


class Place:
    def __init__(self, Z):
        dp=lax.axis_index("dp"); fs=lax.axis_index("fsdp")
        self.Z=Z; self.y=dp//2; self.c=dp%2; self.z=fs//2; self.x=fs%2
        self.nx=(dp,self.z*2+1-self.x)
        self.ny=((1-self.y)*2+self.c,fs)
        self.nc=(self.y*2+1-self.c,fs)
        self.me=self.piece(self.z)
        self.dp=dp; self.fs=fs
    def nz(self,z): return (self.dp,z*2+self.x)
    def piece(self,z,dx=0,dy=0,dc=0):
        y=self.y if dy==0 else 1-self.y
        x=self.x if dx==0 else 1-self.x
        c=self.c if dc==0 else 1-self.c
        return (y*2+c,z,x)
    def slab(self,y,dc=0):
        c=self.c if dc==0 else 1-self.c
        return y*2+c

def rcopy(src,dst,ss,rs,dev):
    return pltpu.make_async_remote_copy(src_ref=src,dst_ref=dst,send_sem=ss,recv_sem=rs,device_id=dev,device_id_type=MESH)

def when(cond,fn):
    if cond is True: fn()
    else: pl.when(cond)(fn)

def gather_sems(NG,Z):
    D=pltpu.SemaphoreType.DMA
    return [D((NG*2*(Z-1),)),D((NG*2*(Z-1),)),
            D((NG*2*Z,)),D((NG*2*Z,)),
            D((NG*2*Z,)),D((NG*2*Z,)),
            D((NG*2,)),D((NG*2,))]

class Gather:
    def __init__(self,P,G,groups,sems):
        self.P=P; self.G=G; self.groups=groups; self.zs,self.zr,self.xs,self.xr,self.ys,self.yr,self.cs,self.cr=sems
    def _cp(self,idx,lo,n,ss,rs,dev):
        r=self.G.at[(*idx,slice(None),pl.ds(lo,n))]
        return rcopy(r,r,ss,rs,dev)
    def zcp(self,g,d,t,zo,to):
        lo,n,_=self.groups[g]; i=(g*2+d)*(self.P.Z-1)+t
        return self._cp(self.P.piece(zo),lo,n,self.zs.at[i],self.zr.at[i],self.P.nz(to))
    def xfull(self,g,zo,arrive=0):
        lo,n,_=self.groups[g]; i=g*2*self.P.Z+zo
        return self._cp(self.P.piece(zo,dx=arrive),lo,n,self.xs.at[i],self.xr.at[i],self.P.nx)
    def yfull(self,g,zo,arrive=0):
        lo,n,_=self.groups[g]; i=g*2*self.P.Z+zo
        return self._cp(self.P.piece(zo,dy=arrive),lo,n,self.ys.at[i],self.yr.at[i],self.P.ny)
    def ydiag(self,g,zo,arrive=0):
        lo,n,a=self.groups[g]; i=g*2*self.P.Z+self.P.Z+zo
        return self._cp(self.P.piece(zo,dx=1,dy=arrive),lo,a,self.ys.at[i],self.yr.at[i],self.P.ny)
    def xdiag(self,g,zo,arrive=0):
        lo,n,a=self.groups[g]; i=g*2*self.P.Z+self.P.Z+zo
        return self._cp(self.P.piece(zo,dy=1,dx=arrive),lo+a,n-a,self.xs.at[i],self.xr.at[i],self.P.nx)
    def ccp(self,g,k,arrive=0):
        lo,n,_=self.groups[g]
        y=self.P.y if k==0 else 1-self.P.y
        r=self.G.at[self.P.slab(y,dc=arrive),:,:,:,pl.ds(lo,n)]
        return rcopy(r,r,self.cs.at[g*2+k],self.cr.at[g*2+k],self.P.nc)
    def own(self,g):
        z=self.P.z; Z=self.P.Z
        when(z<Z-1,lambda: self.zcp(g,0,0,z,z+1).start())
        when(z>0,lambda: self.zcp(g,1,0,z,z-1).start())
        self.xfull(g,z).start(); self.yfull(g,z).start()
    def zarrive(self,g,t):
        z=self.P.z; Z=self.P.Z
        def below():
            zo=z-1-t
            self.zcp(g,0,t,zo,z).wait_recv()
            if t+1<Z-1:
                when(z<Z-1,lambda: self.zcp(g,0,t+1,zo,z+1).start())
            self.xfull(g,zo).start(); self.yfull(g,zo).start()
        def above():
            zo=z+1+t
            self.zcp(g,1,t,zo,z).wait_recv()
            if t+1<Z-1:
                when(z>0,lambda: self.zcp(g,1,t+1,zo,z-1).start())
            self.xfull(g,zo).start(); self.yfull(g,zo).start()
        when(z-1-t>=0,below); when(z+1+t<Z,above)
    def _diag(self,g,zo):
        self.xfull(g,zo,1).wait_recv(); self.ydiag(g,zo).start()
        self.yfull(g,zo,1).wait_recv(); self.xdiag(g,zo).start()
    def diag(self,g,t):
        z=self.P.z; Z=self.P.Z
        if t==0: self._diag(g,z)
        else:
            when(z-t>=0,lambda: self._diag(g,z-t))
            when(z+t<Z,lambda: self._diag(g,z+t))
    def corner(self,g):
        self.ccp(g,0).start()
        for zo in range(self.P.Z):
            self.ydiag(g,zo,1).wait_recv(); self.xdiag(g,zo,1).wait_recv()
        self.ccp(g,1).start()
    def sibling(self,g):
        self.ccp(g,0,1).wait_recv(); self.ccp(g,1,1).wait_recv()
    def drain(self,g):
        z=self.P.z; Z=self.P.Z
        for zo in range(Z):
            self.xfull(g,zo).wait_send(); self.yfull(g,zo).wait_send()
            self.xdiag(g,zo).wait_send(); self.ydiag(g,zo).wait_send()
        for k in range(2): self.ccp(g,k).wait_send()
        for t in range(Z-1):
            when(jnp.logical_and(z<Z-1,z-t>=0),lambda: self.zcp(g,0,t,z-t,z+1).wait_send())
            when(jnp.logical_and(z>0,z+t<=Z-1),lambda: self.zcp(g,1,t,z+t,z-1).wait_send())
    def events(self,g):
        Z=self.P.Z
        ev=[lambda: self.own(g)]
        for t in range(Z-1):
            ev.append(lambda t=t: self.zarrive(g,t))
            ev.append(lambda t=t: self.diag(g,t))
        ev.append(lambda: self.diag(g,Z-1))
        ev.append(lambda: self.corner(g))
        ev.append(lambda: self.sibling(g))
        return ev


SLOT = 1280
NB=7
def rs_sems(NG,Z):
    D=pltpu.SemaphoreType.DMA
    return [D((NG*2,)),D((NG*2,)),
            D((NG*3,)),D((NG*3,)),
            D((NG*2,)),D((NG*2,)),
            D((NG*2*Z,)),D((NG*2*Z,))]
def rs_bufs(Z):
    V=lambda *s: pltpu.VMEM(s,BF)
    h=640
    return [V(2,2,Z,2,16,SLOT),V(2,Z,2,16,h),V(2,Z,16,h),V(2,2,Z,16,h),V(2,Z,16,h),V(4,Z,16,SLOT),V(4,Z,16,SLOT)]
class Scatter:
    def __init__(self,P,R,groups,bufs,sems):
        self.P=P; self.R=R; self.groups=groups; self.bufs=bufs
        self.cs,self.cr,self.xs,self.xr,self.ys,self.yr,self.zs,self.zr=sems
    def buf(self,g,i,w):
        b=self.bufs[i]
        b=b.at[g%b.shape[0]]
        nd=len(b.shape)
        return b.at[(slice(None),)*(nd-1)+(pl.ds(0,w),)]
    def row(self,dy=0,dc=0):
        y=self.P.y if dy==0 else 1-self.P.y
        c=self.P.c if dc==0 else 1-self.P.c
        return y*2+c
    def add(self,dst,src):
        def body(z,_):
            d=dst(z); s=src(z)
            d[...]=(d[...].astype(F32)+s[...].astype(F32)).astype(BF)
            return 0
        lax.fori_loop(0,self.P.Z,body,0)
    def ccp(self,g,k):
        lo,n,_=self.groups[g]
        return rcopy(self.R.at[self.row(k,1),:,:,:,pl.ds(lo,n)],self.buf(g,0,n).at[k],self.cs.at[g*2+k],self.cr.at[g*2+k],self.P.nc)
    def x1(self,g,k):
        lo,n,a=self.groups[g]
        return rcopy(self.R.at[self.row(k),:,1-self.P.x,:,pl.ds(lo+a,n-a)],self.buf(g,3,n-a).at[k],self.xs.at[g*3+k],self.xr.at[g*3+k],self.P.nx)
    def y1(self,g):
        lo,n,a=self.groups[g]
        return rcopy(self.R.at[self.row(1),:,:,:,pl.ds(lo,a)],self.buf(g,1,a),self.ys.at[g*2],self.yr.at[g*2],self.P.ny)
    def x2(self,g):
        lo,n,a=self.groups[g]
        return rcopy(self.R.at[self.row(0),:,1-self.P.x,:,pl.ds(lo,a)],self.buf(g,2,a),self.xs.at[g*3+2],self.xr.at[g*3+2],self.P.nx)
    def y2(self,g):
        lo,n,a=self.groups[g]
        return rcopy(self.R.at[self.row(1),:,self.P.x,:,pl.ds(lo+a,n-a)],self.buf(g,4,n-a),self.ys.at[g*2+1],self.yr.at[g*2+1],self.P.ny)
    def zc(self,g,d,zo,to):
        lo,n,_=self.groups[g]; i=(g*2+d)*self.P.Z+zo
        return rcopy(self.R.at[self.row(0),zo,self.P.x,:,pl.ds(lo,n)],self.buf(g,5+d,n).at[zo],self.zs.at[i],self.zr.at[i],self.P.nz(to))
    def s_c(self,g):
        self.ccp(g,1).start(); self.ccp(g,0).start()
    def a_c(self,g):
        lo,n,a=self.groups[g]; R=self.R; b=self.buf(g,0,n)
        for k in (1,0):
            self.ccp(g,k).wait_recv()
            r=self.row(k)
            self.add(lambda z: R.at[r,z,:,:,pl.ds(lo,n)],lambda z: b.at[k,z])
            self.x1(g,k).start()
            if k==1: self.y1(g).start()
    def a_1(self,g):
        lo,n,a=self.groups[g]; R=self.R; P=self.P; B1=self.buf(g,1,a); B3=self.buf(g,3,n-a)
        self.y1(g).wait_recv()
        r=self.row(0)
        self.add(lambda z: R.at[r,z,:,:,pl.ds(lo,a)],lambda z: B1.at[z])
        for k in (1,0):
            self.x1(g,k).wait_recv()
            q=self.row(k)
            self.add(lambda z: R.at[q,z,P.x,:,pl.ds(lo+a,n-a)],lambda z: B3.at[k,z])
        self.x2(g).start()
        self.y2(g).start()
    def a_2(self,g):
        lo,n,a=self.groups[g]; R=self.R; P=self.P; B2=self.buf(g,2,a); B4=self.buf(g,4,n-a)
        r=self.row(0)
        self.x2(g).wait_recv()
        self.add(lambda z: R.at[r,z,P.x,:,pl.ds(lo,a)],lambda z: B2.at[z])
        self.y2(g).wait_recv()
        self.add(lambda z: R.at[r,z,P.x,:,pl.ds(lo+a,n-a)],lambda z: B4.at[z])
    def zstep(self,g,t):
        lo,n,_=self.groups[g]; R=self.R; P=self.P; Z=P.Z; z=P.z
        r=self.row(0)
        def acc(zo,b):
            d=R.at[r,zo,P.x,:,pl.ds(lo,n)]
            d[...]=(d[...].astype(F32)+b[zo].astype(F32)).astype(BF)
        def up():
            zo=Z-1-t
            @pl.when(z>0)
            def _():
                self.zc(g,0,zo,z).wait_recv()
                acc(zo,self.buf(g,5,n))
            self.zc(g,0,zo,z+1).start()
        def down():
            zo=t
            @pl.when(z<Z-1)
            def _():
                self.zc(g,1,zo,z).wait_recv()
                acc(zo,self.buf(g,6,n))
            self.zc(g,1,zo,z-1).start()
        when(z<Z-1-t,up); when(z>t,down)
    def final(self,g,out):
        lo,n,_=self.groups[g]; P=self.P; Z=P.Z; z=P.z
        out[...]=self.R[self.row(0),z,P.x,:,pl.ds(lo,n)].astype(F32)
        @pl.when(z>0)
        def _():
            self.zc(g,0,z,z).wait_recv()
            out[...]+=self.buf(g,5,n)[z].astype(F32)
        @pl.when(z<Z-1)
        def _():
            self.zc(g,1,z,z).wait_recv()
            out[...]+=self.buf(g,6,n)[z].astype(F32)
    def drain(self,g):
        Z=self.P.Z; z=self.P.z
        for k in range(2):
            self.ccp(g,k).wait_send(); self.x1(g,k).wait_send()
        self.x2(g).wait_send(); self.y1(g).wait_send(); self.y2(g).wait_send()
        for t in range(Z-1):
            when(z<Z-1-t,lambda: self.zc(g,0,Z-1-t,z+1).wait_send())
            when(z>t,lambda: self.zc(g,1,t,z-1).wait_send())
    def events(self,g,out):
        ev=[lambda: self.s_c(g),lambda: self.a_c(g),lambda: self.a_1(g),lambda: self.a_2(g)]
        for t in range(self.P.Z-1): ev.append(lambda t=t: self.zstep(g,t))
        ev.append(lambda: self.final(g,out))
        return ev

def norm_sems(Z):
    D=pltpu.SemaphoreType.DMA
    return [D((3+Z,)),D((3+Z,))]
def norm_bufs(Z): return [pltpu.VMEM((4+Z,8,128),F32),pltpu.VMEM((3,8,128),F32)]
def all_sum(P,buf,got,ss,rs):
    Z=P.Z
    for i,dev in enumerate((P.nc,P.nx,P.ny)):
        cp=rcopy(buf.at[i],got.at[i],ss.at[i],rs.at[i],dev)
        cp.start(); cp.wait()
        buf[i+1]=buf[i]+got[i]
    buf[4+P.z]=buf[3]
    for t in range(Z):
        def send(): rcopy(buf.at[3],buf.at[4+P.z],ss.at[3+t],rs.at[3+P.z],P.nz(t)).start()
        when(P.z!=t,send)
    for t in range(Z):
        def wait():
            cp=rcopy(buf.at[3],buf.at[4+t],ss.at[3+t],rs.at[3+t],P.nz(t))
            cp.wait_send(); cp.wait_recv()
        when(P.z!=t,wait)
    tot=buf[4]
    for t in range(1,Z): tot=tot+buf[4+t]
    return tot
def enter_all(P,Z):
    bar=pltpu.get_barrier_semaphore()
    def sig(d): pl.semaphore_signal(bar,inc=1,device_id=d,device_id_type=MESH)
    sig(P.nx); sig(P.ny); sig(P.nc)
    for t in range(Z):
        when(P.z!=t,lambda: sig(P.nz(t)))
    pl.semaphore_wait(bar,3+Z-1)


W3 = 768
CW = 1152
QKV_AT = 0
VEC_AT = 3456
VEC_COLS = 128
OUT_AT = 3584
DOWN_AT = 4736
UP_AT = 9344
COLS = 13952
GATHER = [(2304, 1280, 640), (0, 2304, 1152), (3584, 5760, 2944), (9344, 1152, 640), (10496, 1152, 512), (11648, 2304, 1152)]
SCATTER = ([(UP_AT + CW * c, CW, 640 if c % 2 else 512) for c in range(4)]
           + [(DOWN_AT + CW * c, CW, 640 if c % 2 else 512) for c in range(4)]
           + [(OUT_AT, CW, 512), (0, CW, 640), (CW, CW, 512), (2 * CW, 1280, 640)])

def al(v, m): return pl.multiple_of(v, m)

def third_cols(s): return [(D * j + 256 * s, 256) for j in range(3)]

def pack_rows(G, me, at, main, rest):
    G[(*me,slice(None),pl.ds(at,W3))]=main.astype(BF)
    parts=[jnp.concatenate([rest[:,256*s:256*s+128],rest[:,256*s+128:256*s+256]],0) for s in range(3)]
    G[(*me,slice(None),pl.ds(al(at+W3,128),W3//2))]=jnp.concatenate(parts,1).astype(BF)

def pack_own(place, G, wqkv, wout, wup, wdown, vec):
    me=place.me
    lo=al(8*place.x,8); ro=al(16*(1-place.x),8)
    def cols(w,cs):
        return [jnp.concatenate([w[pl.ds(a,n),pl.ds(c,k)] for c,k in cs],1) for a,n in ((lo,16),(ro,8))]
    for s in range(3): pack_rows(G,me,QKV_AT+CW*s,*cols(wqkv,third_cols(s)))
    pack_rows(G,me,OUT_AT,*cols(wout,[(0,W3)]))
    for c in range(4): pack_rows(G,me,UP_AT+CW*c,*cols(wup,[(W3*c,W3)]))
    for r in range(6):
        G[(*me,slice(None),pl.ds(DOWN_AT+r*D,D))]=wdown[pl.ds(16*r,16),:].astype(BF)
    G[(*me,slice(None),pl.ds(VEC_AT,VEC_COLS))]=vec[...]

def unpack24(G, at, dst):
    Z=G.shape[1]
    def body(j,_):
        r=al(j*48,16); d=j//Z; z=lax.rem(j,Z)
        dst[pl.ds(r,16),:]=G[d,z,0,:,pl.ds(al(at,128),W3)]
        dst[pl.ds(r+32,16),:]=G[d,z,1,:,pl.ds(al(at,128),W3)]
        a=G[d,z,0,:,pl.ds(al(at+W3,128),W3//2)].astype(F32)
        b=G[d,z,1,:,pl.ds(al(at+W3,128),W3//2)].astype(F32)
        parts=[]
        for s in range(3):
            q=slice(128*s,128*s+128)
            parts+=[jnp.concatenate([a[:8,q],b[:8,q]],0),jnp.concatenate([a[8:,q],b[8:,q]],0)]
        dst[pl.ds(r+16,16),:]=jnp.concatenate(parts,1).astype(BF)
        return 0
    lax.fori_loop(0,G.shape[0]*Z,body,0)

def pack24(G, at, src):
    Z=G.shape[1]
    def body(j,_):
        r=al(j*48,16); d=j//Z; z=lax.rem(j,Z)
        pack_rows(G,(d,z,0),al(at,128),src[pl.ds(r,16),:],src[pl.ds(al(r+16,8),8),:])
        pack_rows(G,(d,z,1),al(at,128),src[pl.ds(r+32,16),:],src[pl.ds(al(r+24,8),8),:])
        return 0
    lax.fori_loop(0,G.shape[0]*Z,body,0)

def unpack_down(G, c, dst):
    def body(k,_):
        for r in range(6):
            dst[pl.ds(al(k*96+16*r,16),16),:]=G[c,k//2,lax.rem(k,2),:,pl.ds(DOWN_AT+r*D,D)]
        return 0
    lax.fori_loop(0,2*G.shape[1],body,0)

def pack_down(G, c, src):
    def body(k,_):
        for r in range(6):
            G[c,k//2,lax.rem(k,2),:,pl.ds(DOWN_AT+r*D,D)]=src[pl.ds(al(k*96+16*r,16),16),:].astype(BF)
        return 0
    lax.fori_loop(0,2*G.shape[1],body,0)

def vec_shift(k): return (240*k)//128

def unpack_vec(G, V, V1):
    V[...]=jnp.zeros_like(V)
    Z=G.shape[1]
    for k in range(8*Z):
        V[pl.ds(vec_shift(k),3),:]+=G[k//(2*Z),k//2%Z,k%2,:,pl.ds(VEC_AT,VEC_COLS)].astype(F32)[0:3]
    for t in range(60):
        V1[:,pl.ds(128*t,128)]=V[pl.ds(t,1),:]

def pack_vec(G, V, V1):
    V[...]=jnp.zeros_like(V)
    for t in range(60):
        V[pl.ds(t,1),:]=V1[:,pl.ds(128*t,128)]
    Z=G.shape[1]
    for k in range(8*Z):
        G[k//(2*Z),k//2%Z,k%2,:,pl.ds(VEC_AT,VEC_COLS)]=V[pl.ds(vec_shift(k),16),:].astype(BF)

def norm_parts(x):
    c=x-jnp.mean(x,-1,keepdims=True)
    s=lax.rsqrt(jnp.mean(c*c,-1,keepdims=True)+EPS_NORM)
    return c*s,s

def norm_back(dx, xh, s):
    return s*(dx-jnp.mean(dx,-1,keepdims=True)-xh*jnp.mean(dx*xh,-1,keepdims=True))

def gelu_both(u):
    k0=0.7978845608028654; k1=0.044715
    u2=u*u
    t=jnp.tanh(k0*(u*(1.0+k1*u2)))
    h=0.5*(1.0+t)
    return u*h, h+(0.5*k0)*u*(1.0-t*t)*(1.0+(3.0*k1)*u2)

RB=256

RULES=((1,1,0),(2,3,1),(2,7,4))

class Clock:
    def __init__(self, places):
        self.times=places
        self.slots={}
        self.tail=[]
    def fill(self, events, deadlines):
        index={(n,s):i for i,(n,s,_) in enumerate(self.times)}
        times=[t for _,_,t in self.times]
        where={}
        last=0
        for time,key,fn in sorted(events,key=lambda e: e[0]):
            i=next((i for i,t in enumerate(times) if t>=time),len(times))
            where[key]=i
        for key,place in deadlines.items():
            where[key]=min(where[key],index[place])
        keys=sorted(where,key=lambda k:(k[0],k[1],-k[2]))
        prev=None
        for k in keys:
            if prev is not None and prev[:2]==k[:2]: where[k]=min(where[k],where[prev])
            prev=k
        fns={key:(time,fn) for time,key,fn in events}
        self.where=where
        self.order=[]
        for key in sorted(where,key=lambda k:(where[k],fns[k][0],k)):
            i=where[key]
            self.order.append(key)
            if i<len(times): self.slots.setdefault(self.times[i][:2],[]).append(fns[key][1])
            else: self.tail.append(fns[key][1])
    def at(self, name, step, count):
        for k in range(count):
            todo=self.slots.get((name,k))
            if todo:
                def run(todo=todo):
                    for f in todo: f()
                if isinstance(step,int):
                    if step==k: run()
                else: pl.when(step==k)(run)

def schedule(sched):
    p=[]
    t=[0.0]
    def add(name,step,dt):
        p.append((name,step,t[0])); t[0]+=dt
    for i in range(4): add("stat",i,0.5)
    t[0]=max(t[0],sched["first"])
    for i in range(3):
        add("third",i,0.6)
        for k in range(4): add("qkv",4*i+k,0.4)
        for pp in range(2):
            for k in range(4): add("af",8*i+4*pp+k,(0.8,0.8,1.4,1.4)[k])
    add("out",0,0.6)
    for k in range(4): add("ob",k,1.0)
    for c in range(4):
        add("chunk",c,1.0)
        for k in range(4): add("mr",4*c+k,1.35)
        for k in range(3): add("mw",3*c+k,0.6)
        for k in range(3): add("mu",3*c+k,0.6)
        add("mp",c,0.3)
    for k in range(4): add("bb",k,1.2)
    for k in range(3): add("bw",k,0.6)
    add("bp",0,0.3)
    for i in range(3):
        for pp in range(2):
            for k in range(4): add("ab",8*i+4*pp+k,0.9)
        for k in range(4): add("dh",4*i+k,0.5)
        if i==2:
            for k in range(4): add("ln",k,0.8)
        for k in range(3): add("dq",3*i+k,0.6)
        add("dp",i,0.3)
    return p

def mega_kernel(Z,sched,tok_h,cot_h,len_ref,wqkv_s,wout_s,wup_s,wdown_s,vec_s,
               mixed_o,dtok_o,own_o,nrm_o,
               G,tok,cot,F1,F2,F3,qkv,B1,B2,B3,hT,aT,oT,W0,W1,dW,lse,V,V1,dV1,dka,dva,own,nrm,dsem,*rest):
    gsems=rest[:8]; rbufs=rest[8:8+NB]; rsems=rest[8+NB:16+NB]; nb,got,ns,nr=rest[16+NB:]
    L=tok.shape[0]
    NBK=L//RB
    place=Place(Z)
    def dma(a,b,i):
        cp=pltpu.make_async_copy(a,b,dsem.at[i]); cp.start(); return cp
    ldt=dma(tok_h,tok,0); ldc=dma(cot_h,cot,1)
    pack_own(place,G,wqkv_s,wout_s,wup_s,wdown_s,vec_s)
    enter_all(place,Z)
    ga=Gather(place,G,GATHER,gsems)
    sc=Scatter(place,G,SCATTER,rbufs,rsems)
    clock=Clock(schedule(sched))
    events=[]; deadlines={}
    w=0.0
    for g,(lo,n,_) in enumerate(GATHER):
        d=sched["link"]*n/COLS
        ev=ga.events(g)
        for k,f in enumerate(ev):
            if k==0: time=max(0.0,w-sched["ahead"])
            else: time=w+sched["lat"]+d*min(k,len(ev)-2)/(len(ev)-2)+(sched["sib"] if k==len(ev)-1 else 0.0)
            events.append((time,("g",g,k),f))
        w+=d
    for g,place_ in enumerate((("third",0),("third",1),("out",0),("chunk",0),("chunk",1),("chunk",2))):
        deadlines[("g",g,9)]=place_
    tm={(n,s):t for n,s,t in clock.times}
    ready=[tm[("mp",c)] for c in range(4)]+[tm[("mp",3)]+sched["dgap"]*(k+1) for k in range(4)]+[tm[("bp",0)]]+[tm[("dp",i)] for i in range(3)]
    rt=sched["rs"]
    at_=[]
    for g,(lo,n,_) in enumerate(SCATTER):
        ev=sc.events(g,own.at[:,pl.ds(lo,n)])
        at_.append([])
        t=ready[g]
        for k,f in enumerate(ev):
            t=t+rt[k]
            if g: t=max(t,at_[g-1][k]+0.01)
            for back_,slot,first in RULES:
                if k==first and g>=back_: t=max(t,at_[g-back_][slot]+0.01)
            at_[g].append(t)
            events.append((t,("s",g,k),f))
    clock.fill(events,deadlines)
    index={(n,s):i for i,(n,s,_) in enumerate(clock.times)}
    after=[("mp",c) for c in range(4)]+[("mp",3)]*4+[("bp",0)]+[("dp",i) for i in range(3)]
    for g in range(len(SCATTER)): assert clock.where[("s",g,0)]>=index[after[g]]
    pos={k:i for i,k in enumerate(clock.order)}
    for g in range(len(SCATTER)):
        for back_,slot,first in RULES:
            if g>=back_: assert pos[("s",g-back_,slot)]<pos[("s",g,first)]
        for k in range(1,8): assert pos[("s",g,k-1)]<pos[("s",g,k)]
    def at(name,step,count): clock.at(name,step,count)
    def rows(i): return pl.ds(al(i*RB,RB),RB)
    length=len_ref[0]
    ldt.wait()
    xhat=F1; h1=B1; o=B3
    for i in range(4):
        at("stat",i,4)
        if i<NBK:
            xhat[rows(i),:]=norm_parts(tok[rows(i),:].astype(F32))[0]
    def third(i,_):
        s=lax.rem(i+2,3)
        at("third",i,3)
        @pl.when(i==0)
        def _():
            unpack_vec(G,V,V1)
            def first(j,_):
                h1[rows(j),:]=(xhat[rows(j),:]*V1[:,0:D]+V1[:,D:2*D]).astype(BF)
                return 0
            lax.fori_loop(0,NBK,first,0)
        unpack24(G,QKV_AT+CW*s,W0)
        def block(j,_):
            at("qkv",4*i+j,12)
            qkv[s,rows(j),:]=nn(h1[rows(j),:],W0[...]).astype(BF)
            return 0
        lax.fori_loop(0,NBK,block,0)
        def pair(pp,_):
            p=2*s+pp
            def col(j): return qkv.at[s,:,pl.ds(al(256*j+128*pp,128),128)]
            c=pl.ds(al(128*p,128),128)
            attn_fwd_pair(col(0),col(1),col(2),length,o.at[:,c],oT.at[c,:],lse.at[p],512,
                          tick=lambda k: at("af",8*i+4*pp+k,24))
            return 0
        lax.fori_loop(0,2,pair,0)
        return 0
    lax.fori_loop(0,3,third,0)
    at("out",0,1)
    unpack24(G,OUT_AT,W0)
    ldc.wait()
    r1=F1; mixed=F2; dh2=F3; h2=B1; h2T=hT
    def out_block(i,_):
        at("ob",i,4)
        sl=rows(i)
        r=tok[sl,:].astype(F32)+nn(o[sl,:],W0[...])+V1[:,4*D:5*D]
        r1[sl,:]=r
        mixed[sl,:]=r+V1[:,5*D:6*D]
        hb=(norm_parts(r)[0]*V1[:,2*D:3*D]+V1[:,3*D:4*D]).astype(BF)
        h2[sl,:]=hb
        h2T[:,sl]=hb.T
        pos_=i*RB+lax.broadcasted_iota(jnp.int32,(RB,D),0)
        cot[sl,:]=jnp.where(pos_<length,cot[sl,:],jnp.zeros((),BF))
        dh2[sl,:]=jnp.zeros((RB,D),F32)
        return 0
    lax.fori_loop(0,NBK,out_block,0)
    du_s=B2
    def chunk(c,_):
        at("chunk",c,4)
        for g,when_ in enumerate((0,0,0,0,1,2)):
            pl.when(c==when_)(lambda g=g: ga.drain(g))
        unpack24(G,UP_AT+CW*c,W0)
        unpack_down(G,c,W1)
        bu=V1[:,pl.ds(al(6*D+c*W3,128),W3)]
        def mrows(i,acc):
            at("mr",4*c+i,16)
            sl=rows(i)
            u=nn(h2[sl,:],W0[...])+bu
            a,slope=gelu_both(u)
            ab=a.astype(BF)
            mixed[sl,:]+=nn(ab,W1[...])
            aT[:,sl]=ab.T
            du=(nt(cot[sl,:],W1[...])*slope).astype(BF)
            du_s[sl,:]=du
            dh2[sl,:]+=nt(du,W0[...])
            return acc+jnp.sum(du.astype(F32),0,keepdims=True)
        s=lax.fori_loop(0,NBK,mrows,jnp.zeros((1,W3),F32))
        dV1[:,pl.ds(al(6*D+c*W3,128),W3)]=s
        def wrows(i,_):
            at("mw",3*c+i,12)
            dW[rows(i),:]=nn(aT[rows(i),:],cot[...])
            return 0
        lax.fori_loop(0,W3//RB,wrows,0)
        pack_down(G,c,dW)
        def urows(i,_):
            at("mu",3*c+i,12)
            dW[rows(i),:]=nn(h2T[rows(i),:],du_s[...])
            return 0
        lax.fori_loop(0,D//RB,urows,0)
        pack24(G,UP_AT+CW*c,dW)
        at("mp",c,4)
        return 0
    lax.fori_loop(0,FF//W3,chunk,0)
    mixed_b=B2
    def fin(i,_):
        mixed_b[rows(i),:]=mixed[rows(i),:].astype(BF)
        return 0
    lax.fori_loop(0,NBK,fin,0)
    outs=[dma(mixed_b,mixed_o,2)]
    unpack24(G,OUT_AT,W0)
    dr1=F3; dy=B3; do=B1
    def back(i,acc):
        at("bb",i,4)
        sl=rows(i)
        dh=dh2[sl,:]
        xh,s=norm_parts(r1[sl,:])
        g=cot[sl,:].astype(F32)
        dr=g+norm_back(dh*V1[:,2*D:3*D],xh,s)
        dr1[sl,:]=dr
        dyb=dr.astype(BF)
        dy[sl,:]=dyb
        do[sl,:]=nt(dyb,W0[...]).astype(BF)
        new=(dh*xh,dh,dyb.astype(F32),g)
        return tuple(a+jnp.sum(b,0,keepdims=True) for a,b in zip(acc,new))
    z1=jnp.zeros((1,D),F32)
    sums=lax.fori_loop(0,NBK,back,(z1,z1,z1,z1))
    for j,v in enumerate(sums): dV1[:,pl.ds((2+j)*D,D)]=v
    def orow(i,_):
        at("bw",i,3)
        dW[rows(i),:]=nn(oT[rows(i),:].astype(BF),dy[...])
        return 0
    lax.fori_loop(0,D//RB,orow,0)
    pack24(G,OUT_AT,dW)
    at("bp",0,1)
    h1T=hT; dqkv=B3; dh1=F2
    outs[0].wait()
    def again(i,_):
        sl=rows(i)
        hb=(norm_parts(tok[sl,:].astype(F32))[0]*V1[:,0:D]+V1[:,D:2*D]).astype(BF)
        h1T[:,sl]=hb.T
        dh1[sl,:]=jnp.zeros((RB,D),F32)
        return 0
    lax.fori_loop(0,NBK,again,0)
    def third_back(s,_):
        unpack24(G,QKV_AT+CW*s,W0)
        def pair(pp,_):
            p=2*s+pp
            def col(j): return qkv.at[s,:,pl.ds(al(256*j+128*pp,128),128)]
            def dcol(j): return dqkv.at[:,pl.ds(al(256*j+128*pp,128),128)]
            c=pl.ds(al(128*p,128),128)
            attn_bwd_pair(col(0),col(1),col(2),do.at[:,c],oT.at[c,:],lse.at[p],length,
                          dcol(0),dcol(1),dcol(2),dka,dva,256,tick=lambda k: at("ab",8*s+4*pp+k,24))
            return 0
        lax.fori_loop(0,2,pair,0)
        def drow(i,_):
            at("dh",4*s+i,12)
            dh1[rows(i),:]+=nt(dqkv[rows(i),:],W0[...])
            return 0
        lax.fori_loop(0,NBK,drow,0)
        @pl.when(s==2)
        def _():
            def lrow(i,acc):
                at("ln",i,4)
                sl=rows(i)
                dh=dh1[sl,:]
                xh,r=norm_parts(tok[sl,:].astype(F32))
                F1[sl,:]=dr1[sl,:]+norm_back(dh*V1[:,0:D],xh,r)
                return tuple(a+jnp.sum(b,0,keepdims=True) for a,b in zip(acc,(dh*xh,dh)))
            a,b=lax.fori_loop(0,NBK,lrow,(z1,z1))
            dV1[:,0:D]=a
            dV1[:,D:2*D]=b
            pack_vec(G,V,dV1)
        def qrow(i,_):
            at("dq",3*s+i,9)
            dW[rows(i),:]=nn(h1T[rows(i),:],dqkv[...])
            return 0
        lax.fori_loop(0,D//RB,qrow,0)
        pack24(G,QKV_AT+CW*s,dW)
        at("dp",s,3)
        return 0
    lax.fori_loop(0,3,third_back,0)
    outs=[dma(F1,dtok_o,3)]
    for f in clock.tail: f()
    flat=lax.broadcasted_iota(jnp.int32,(16,VEC_COLS),0)*VEC_COLS+lax.broadcasted_iota(jnp.int32,(16,VEC_COLS),1)
    start=lax.rem(240*((place.dp*Z+place.z)*2+place.x),128)
    vec=own[:,pl.ds(VEC_AT,VEC_COLS)]
    vec=jnp.where(jnp.logical_and(flat>=start,flat<start+240),vec,0.0)
    left=own[:,pl.ds(0,VEC_AT)]; right=own[:,pl.ds(OUT_AT,COLS-OUT_AT)]
    nb[0]=jnp.full((8,128),1.0,F32)*(jnp.sum(left*left)+jnp.sum(right*right)+jnp.sum(vec*vec))
    outs.append(dma(own,own_o,4))
    nrm[...]=all_sum(place,nb,got,ns,nr)
    outs.append(dma(nrm,nrm_o,5))
    for g in range(len(SCATTER)): sc.drain(g)
    for cp in outs: cp.wait()

SCHED=dict(first=14.0,link=57.0,ahead=4.0,lat=4.0,sib=2.0,dgap=1.5,rs=[0,1.8,4.5,3.0,1.5,2.0,2.0,2.0])
def mega_call(Z,tok,cot,length,wqkv,wout,wup,wdown,vec,sched=SCHED):
    L=tok.shape[0]; pieces=8*Z
    S=jax.ShapeDtypeStruct; V=pltpu.VMEM
    vm=pl.BlockSpec(memory_space=pltpu.VMEM); an=pl.BlockSpec(memory_space=pl.ANY); sm=pl.BlockSpec(memory_space=pltpu.SMEM)
    outs=[S((L,D),BF),S((L,D),F32),S((16,COLS),F32),S((8,128),F32)]
    f=lambda: V((L,D),F32)
    b=lambda: V((L,D),BF)
    scratch=[V((4,Z,2,16,COLS),BF),b(),b(),f(),f(),f(),V((3,L,D),BF),b(),b(),b(),V((D,L),BF),V((D,L),BF),V((D,L),F32),
             V((D,W3),BF),V((W3,D),BF),V((D,W3),F32),V((6,2,L),F32),V((80,128),F32),V((1,10*D),F32),V((1,10*D),F32),
             V((L,128),F32),V((L,128),F32),V((16,COLS),F32),V((8,128),F32),pltpu.SemaphoreType.DMA((6,))]
    return pl.pallas_call(functools.partial(mega_kernel,Z,sched),out_shape=outs,
        in_specs=[an,an,sm]+[vm]*5,out_specs=[an]*len(outs),
        scratch_shapes=scratch+gather_sems(len(GATHER),Z)+rs_bufs(Z)+rs_sems(len(SCATTER),Z)+norm_bufs(Z)+norm_sems(Z),
        compiler_params=pltpu.CompilerParams(collective_id=1,has_side_effects=True,vmem_limit_bytes=63*2**20),
        cost_estimate=pl.CostEstimate(flops=60*10**9,bytes_accessed=60*2**20,transcendentals=10**7))(tok,cot,length,wqkv,wout,wup,wdown,vec)


def adam_step(weight, first_mom, second_mom, gradient, step_rate):
    first_new = BETA_ONE * first_mom + (1.0 - BETA_ONE) * gradient
    second_new = BETA_TWO * second_mom + (1.0 - BETA_TWO) * gradient * gradient
    fix_one = 1.0 - BETA_ONE**STEP
    fix_two = 1.0 - BETA_TWO**STEP
    update = (
        first_new / fix_one / (jnp.sqrt(second_new / fix_two) + ADAM_EPSILON) + DECAY_RATE * weight
    )
    return (weight - step_rate * update, first_new, second_new)


def adam_kernel(par_ref, own, nrm, *refs):
    ins, outs = refs[:12], refs[12:]
    factor = jnp.minimum(1.0, CLIP_NORM / (jnp.sqrt(nrm[0:1, 0:1]) + 1e-06))
    main_at = al(8 * par_ref[0], 8)
    rest_at = al(16 * (1 - par_ref[0]), 8)

    def step(i, rows, cols, grad, rate):
        w, m, v = [r[rows, cols] for r in ins[3 * i : 3 * i + 3]]
        new = adam_step(w, m, v, grad * factor, rate)
        for r, a in zip(outs[3 * i : 3 * i + 3], new):
            r[rows, cols] = a

    def chunk(i, at, cols, rate):
        main = own[:, pl.ds(at, W3)]
        packed = own[:, pl.ds(at + W3, W3 // 2)]
        parts = []
        for s in range(3):
            parts += [packed[:8, 128 * s : 128 * s + 128], packed[8:, 128 * s : 128 * s + 128]]
        rest = jnp.concatenate(parts, 1)
        done = 0
        for c, n in cols:
            step(i, pl.ds(main_at, 16), pl.ds(c, n), main[:, done : done + n], rate)
            step(i, pl.ds(rest_at, 8), pl.ds(c, n), rest[:, done : done + n], rate)
            done += n

    for s in range(3):
        chunk(0, QKV_AT + CW * s, third_cols(s), D ** (-0.5))
    chunk(1, OUT_AT, [(0, W3)], D ** (-0.5))
    for c in range(4):
        chunk(2, UP_AT + CW * c, [(W3 * c, W3)], D ** (-0.5))
    for r in range(6):
        grad = own[:, pl.ds(DOWN_AT + r * D, D)]
        step(3, pl.ds(16 * r, 16), slice(None), grad, FF ** (-0.5))


def adam_call(parity, own, nrm, states):
    vm = pl.BlockSpec(memory_space=pltpu.VMEM)
    sm = pl.BlockSpec(memory_space=pltpu.SMEM)
    return pl.pallas_call(
        adam_kernel,
        out_shape=[jax.ShapeDtypeStruct(a.shape, F32) for a in states],
        in_specs=[sm, vm, vm] + [vm] * 12,
        out_specs=[vm] * 12,
        compiler_params=pltpu.CompilerParams(vmem_limit_bytes=40 * 2**20),
        cost_estimate=pl.CostEstimate(
            flops=10**7, bytes_accessed=8 * 2**20, transcendentals=10**6
        ),
    )(parity, own, nrm, *states)


def layer_norm(values, gain, shift):
    center = jnp.mean(values, -1, keepdims=True)
    centered = values - center
    spread = jnp.mean(centered * centered, -1, keepdims=True)
    return centered * lax.rsqrt(spread + EPS_NORM) * gain + shift


def smooth_gate(value):
    return jax.nn.gelu(value, approximate=True)


def plain_shards(tokens, lengths, cotangent, *state):
    w_qkv, m_qkv, v_qkv, w_out, m_out, v_out, w_up, m_up, v_up = state[:9]
    w_down, m_down, v_down, packed, m_packed, v_packed = state[9:]
    seq_count, seq_len, model_width = tokens.shape
    row_count = seq_count * seq_len
    axes = ("dp", "fsdp")
    wqkv_b, wout_b, wup_b, wdown_b, vector_b = [
        lax.all_gather(w.astype(BF), axes, axis=0, tiled=True)
        for w in (w_qkv, w_out, w_up, w_down, packed)
    ]
    vector = vector_b.astype(F32)
    gain_one, bias_one, gain_two, bias_two, bias_attn, bias_down = [
        vector[i * model_width : (i + 1) * model_width] for i in range(6)
    ]
    bias_up = vector[6 * model_width :]
    positions = jnp.arange(seq_len, dtype=jnp.int32)
    live_rows = positions[None, :] < lengths[:, None]
    inputs = tokens.astype(F32).reshape(row_count, model_width)
    normed_one, norm_one_back = jax.vjp(layer_norm, inputs, gain_one, bias_one)
    normed_one_b = normed_one.astype(BF)
    qkv_all = jnp.dot(normed_one_b, wqkv_b, preferred_element_type=F32).astype(BF)
    seqs = [slice(i * seq_len, (i + 1) * seq_len) for i in range(seq_count)]
    ahead = [fwd_call(qkv_all[s], lengths[i : i + 1], 512) for i, s in enumerate(seqs)]
    attended_b = jnp.concatenate([a[0] for a in ahead], 0)
    resid_one = inputs + jnp.dot(attended_b, wout_b, preferred_element_type=F32) + bias_attn
    normed_two, norm_two_back = jax.vjp(layer_norm, resid_one, gain_two, bias_two)
    normed_two_b = normed_two.astype(BF)
    upper = jnp.dot(normed_two_b, wup_b, preferred_element_type=F32) + bias_up
    activ, gate_back = jax.vjp(smooth_gate, upper)
    activ_b = activ.astype(BF)
    mixed = resid_one + jnp.dot(activ_b, wdown_b, preferred_element_type=F32) + bias_down
    mixed = mixed.reshape(seq_count, seq_len, model_width).astype(BF)
    grad_b = jnp.where(live_rows[:, :, None], cotangent, jnp.zeros((), BF))
    grad_b = grad_b.reshape(row_count, model_width)
    grad_full = grad_b.astype(F32)
    d_wdown = jnp.dot(activ_b.T, grad_b, preferred_element_type=F32)
    d_bias_down = jnp.sum(grad_full, 0)
    d_activ = jnp.dot(grad_b, wdown_b.T, preferred_element_type=F32)
    (d_upper,) = gate_back(d_activ)
    d_upper_b = d_upper.astype(BF)
    d_bias_up = jnp.sum(d_upper_b.astype(F32), 0)
    d_wup = jnp.dot(normed_two_b.T, d_upper_b, preferred_element_type=F32)
    d_normed_two = jnp.dot(d_upper_b, wup_b.T, preferred_element_type=F32)
    d_resid_norm, d_gain_two, d_bias_two = norm_two_back(d_normed_two)
    d_resid = grad_full + d_resid_norm
    d_branch_b = d_resid.astype(BF)
    d_bias_attn = jnp.sum(d_branch_b.astype(F32), 0)
    d_wout = jnp.dot(attended_b.T, d_branch_b, preferred_element_type=F32)
    d_attended_b = jnp.dot(d_branch_b, wout_b.T, preferred_element_type=F32).astype(BF)
    back = [
        bwd_call(qkv_all[s], d_attended_b[s], a[1], a[2], lengths[i : i + 1])
        for i, (s, a) in enumerate(zip(seqs, ahead))
    ]
    d_qkv_b = jnp.concatenate([jnp.concatenate(b, 1) for b in back], 0)
    d_wqkv = jnp.dot(normed_one_b.T, d_qkv_b, preferred_element_type=F32)
    d_normed_one = jnp.dot(d_qkv_b, wqkv_b.T, preferred_element_type=F32)
    d_input_norm, d_gain_one, d_bias_one = norm_one_back(d_normed_one)
    d_tokens = (d_resid + d_input_norm).reshape(seq_count, seq_len, model_width)
    d_vector = jnp.concatenate(
        [d_gain_one, d_bias_one, d_gain_two, d_bias_two, d_bias_attn, d_bias_down, d_bias_up]
    )
    owned = [
        lax.psum_scatter(g, axes, scatter_dimension=0, tiled=True)
        for g in (d_wqkv, d_wout, d_wup, d_wdown, d_vector)
    ]
    grad_norm = jnp.sqrt(lax.psum(sum(jnp.sum(g * g) for g in owned), axes))
    factor = jnp.minimum(1.0, CLIP_NORM / (grad_norm + 1e-06))
    rates = (D ** (-0.5), D ** (-0.5), D ** (-0.5), FF ** (-0.5), VECTOR_RATE)
    new = ()
    for i, (g, rate) in enumerate(zip(owned, rates)):
        new += adam_step(*state[3 * i : 3 * i + 3], g * factor, rate)
    return (mixed, d_tokens, grad_norm) + new


def direct_shards(Z, tokens, lengths, cotangent, *state):
    packed, m_packed, v_packed = state[12:]
    dp = lax.axis_index("dp")
    fsdp = lax.axis_index("fsdp")
    n = packed.shape[0]
    start = ((dp * 2 * Z + fsdp) * n) % VEC_COLS
    vec = lax.dynamic_update_slice(
        jnp.zeros((16 * VEC_COLS,), BF), packed.astype(BF), (start,)
    ).reshape(16, VEC_COLS)
    mixed, d_tokens, own, norm_tile = mega_call(
        Z, tokens[0], cotangent[0], lengths, state[0], state[3], state[6], state[9], vec
    )
    grad_norm = jnp.sqrt(norm_tile[0, 0])
    factor = jnp.minimum(1.0, CLIP_NORM / (grad_norm + 1e-06))
    parity = (fsdp % 2).astype(jnp.int32).reshape(1)
    new = adam_call(parity, own, norm_tile, state[:12])
    g_vec = lax.dynamic_slice(own[:, VEC_AT:OUT_AT].reshape(-1), (start,), (n,))
    new_vec = adam_step(packed, m_packed, v_packed, g_vec * factor, VECTOR_RATE)
    return (mixed[None], d_tokens[None], grad_norm) + tuple(new) + new_vec


def solution(mesh):
    rows = P(("dp", "fsdp"), None)
    seqs = P(("dp", "fsdp"), None, None)
    flat = P(("dp", "fsdp"))
    in_specs = (seqs, flat, seqs) + (rows,) * 12 + (flat,) * 3
    out_specs = (seqs, seqs, P()) + (rows,) * 12 + (flat,) * 3
    dp, fsdp = mesh.shape["dp"], mesh.shape["fsdp"]

    def shards(*args):
        tokens, w_qkv = args[0], args[3]
        fits = (
            dp == 4
            and fsdp == 8
            and tokens.shape[0] == 1
            and tokens.shape[1] == 1024
            and w_qkv.shape[0] * dp * fsdp == D
        )
        step = functools.partial(direct_shards, fsdp // 2) if fits else plain_shards
        return step(*args)

    return jax.shard_map(
        shards, mesh=mesh, in_specs=in_specs, out_specs=out_specs, check_vma=False
    )
```

```python
import functools

import jax
import jax.numpy as jnp
from jax import lax
from jax.experimental import pallas as pl
from jax.experimental.pallas import tpu as pltpu
from jax.sharding import PartitionSpec as P

D = 768
FF = 3072
HEAD_DIM = 64
STEP = 10
HD = 64
F32 = jnp.float32
BF = jnp.bfloat16
MESH = pl.DeviceIdType.MESH

EPS_NORM = 1e-05
CLIP_NORM = 1.0
BETA_ONE = 0.9
BETA_TWO = 0.95
ADAM_EPSILON = 1e-08
DECAY_RATE = 0.1
VECTOR_RATE = 0.2


def nt(a,b): return lax.dot_general(a,b,(((1,),(1,)),((),())),preferred_element_type=F32)
def nn(a,b): return jnp.dot(a,b,preferred_element_type=F32)
def head_mask(rows):
    lane=lax.broadcasted_iota(jnp.int32,(rows,128),1)
    return (lane<HD)
def half(x,h,scale=1.0):
    m=head_mask(x.shape[0]); m = m if h==0 else jnp.logical_not(m)
    return jnp.where(m,x*jnp.asarray(scale,x.dtype),jnp.zeros_like(x))

def attn_fwd_pair(q_ref,k_ref,v_ref,length,o_ref,oT_ref,lse_ref,QB,tick=None):
    L=q_ref.shape[0]
    vT=v_ref[...].T
    for i in range(L//QB):
        nk=(i+1)*QB
        qs=q_ref[pl.ds(i*QB,QB),:]
        if tick is not None: tick(i)
        outs=[]
        jidx=lax.broadcasted_iota(jnp.int32,(nk,QB),0)
        lim=jnp.minimum(i*QB+1+lax.broadcasted_iota(jnp.int32,(1,QB),1),length)
        for h in range(2):
            s=nt(k_ref[pl.ds(0,nk),:],half(qs,h,0.125))
            s=jnp.where(jidx<lim,s,-1e9)
            m=jnp.max(s,0,keepdims=True)
            e=jnp.exp(s-m)
            l=jnp.sum(e,0,keepdims=True)
            oT=nn(vT[HD*h:HD*h+HD,:nk],e.astype(BF))
            outs.append(oT/l)
            lse_ref[pl.ds(h,1),pl.ds(i*QB,QB)]=m+jnp.log(l)
        oT=jnp.concatenate(outs,0)
        oT_ref[:,pl.ds(i*QB,QB)]=oT
        o_ref[pl.ds(i*QB,QB),:]=oT.T.astype(BF)

def attn_bwd_pair(q_ref,k_ref,v_ref,do_ref,oT_ref,lse_ref,length,dq_ref,dk_ref,dv_ref,dk_acc,dv_acc,QB,tick=None):
    L=q_ref.shape[0]
    kT=k_ref[...].T
    for i in reversed(range(L//QB)):
        if tick is not None: tick(L//QB-1-i)
        nk=(i+1)*QB
        sl=pl.ds(i*QB,QB)
        qs=q_ref[sl,:]; do=do_ref[sl,:]
        doT=do.astype(F32).T
        prod=doT*oT_ref[:,sl]
        live=(i*QB+lax.broadcasted_iota(jnp.int32,(1,QB),1))<length
        tri=lax.broadcasted_iota(jnp.int32,(QB,QB),0)<=lax.broadcasted_iota(jnp.int32,(QB,QB),1)
        dqs=[]
        k=k_ref[pl.ds(0,nk),:]; v=v_ref[pl.ds(0,nk),:]
        dk=None; dv=None
        for h in range(2):
            delta=jnp.sum(prod[HD*h:HD*h+HD],0,keepdims=True)
            lse=jnp.where(live,lse_ref[pl.ds(h,1),sl],1e30)
            qm=half(qs,h,0.125); dom=half(do,h)
            s=nt(k,qm)
            p=jnp.exp(s-lse)
            pd=jnp.where(tri,p[nk-QB:],0.0)
            p=pd if i==0 else jnp.concatenate([p[:nk-QB],pd],0)
            dp=nt(v,dom)
            ds=(p*(dp-delta)).astype(BF)
            a=nn(p.astype(BF),dom); b=nn(ds,qm)
            dv=a if dv is None else dv+a
            dk=b if dk is None else dk+b
            dqs.append(nn(kT[HD*h:HD*h+HD,:nk],ds))
        dq_ref[sl,:]=(jnp.concatenate(dqs,0)*0.125).T.astype(BF)
        if i==L//QB-1:
            dk_acc[...]=dk; dv_acc[...]=dv
        else:
            dk_acc[pl.ds(0,nk),:]+=dk; dv_acc[pl.ds(0,nk),:]+=dv
    dk_ref[...]=dk_acc[...].astype(BF); dv_ref[...]=dv_acc[...].astype(BF)

def fwd_call(qkv,length,QB=256):
    L=qkv.shape[0]; D=qkv.shape[1]//3; NP=D//128
    def k(len_ref,q,k_,v,o,oT,lse):
        attn_fwd_pair(q,k_,v,len_ref[0],o,oT,lse.at[0],QB)
    return pl.pallas_call(k,grid=(NP,),
      in_specs=[pl.BlockSpec(memory_space=pltpu.SMEM)]+[pl.BlockSpec((L,128),functools.partial(lambda off,p:(0,off+p),j*NP)) for j in range(3)],
      out_specs=[pl.BlockSpec((L,128),lambda p:(0,p)),pl.BlockSpec((128,L),lambda p:(p,0)),pl.BlockSpec((1,2,L),lambda p:(p,0,0))],
      out_shape=[jax.ShapeDtypeStruct((L,D),BF),jax.ShapeDtypeStruct((D,L),F32),jax.ShapeDtypeStruct((NP,2,L),F32)],
      compiler_params=pltpu.CompilerParams(vmem_limit_bytes=56*2**20),
      cost_estimate=pl.CostEstimate(flops=4*L*L*D//2,bytes_accessed=10*2**20,transcendentals=12*L*L//2))(length,qkv,qkv,qkv)
def bwd_call(qkv,do,oT,lse,length,QB=256):
    L=qkv.shape[0]; D=qkv.shape[1]//3; NP=D//128
    def k(len_ref,q,k_,v,do,oT,lse,dq,dk,dv,dka,dva):
        attn_bwd_pair(q,k_,v,do,oT,lse.at[0],len_ref[0],dq,dk,dv,dka,dva,QB)
    blk=pl.BlockSpec((L,128),lambda p:(0,p))
    return pl.pallas_call(k,grid=(NP,),
      in_specs=[pl.BlockSpec(memory_space=pltpu.SMEM)]+[pl.BlockSpec((L,128),functools.partial(lambda off,p:(0,off+p),j*NP)) for j in range(3)]+[blk,pl.BlockSpec((128,L),lambda p:(p,0)),pl.BlockSpec((1,2,L),lambda p:(p,0,0))],
      out_specs=[blk]*3,
      out_shape=[jax.ShapeDtypeStruct((L,D),BF)]*3,
      scratch_shapes=[pltpu.VMEM((L,128),F32)]*2,
      compiler_params=pltpu.CompilerParams(vmem_limit_bytes=56*2**20),
      cost_estimate=pl.CostEstimate(flops=10*L*L*D//2,bytes_accessed=14*2**20,transcendentals=12*L*L//2))(length,qkv,qkv,qkv,do,oT,lse)


class Place:
    def __init__(self, Z):
        dp=lax.axis_index("dp"); fs=lax.axis_index("fsdp")
        self.Z=Z; self.y=dp//2; self.c=dp%2; self.z=fs//2; self.x=fs%2
        self.nx=(dp,self.z*2+1-self.x)
        self.ny=((1-self.y)*2+self.c,fs)
        self.nc=(self.y*2+1-self.c,fs)
        self.me=self.piece(self.z)
        self.dp=dp; self.fs=fs
    def nz(self,z): return (self.dp,z*2+self.x)
    def piece(self,z,dx=0,dy=0,dc=0):
        y=self.y if dy==0 else 1-self.y
        x=self.x if dx==0 else 1-self.x
        c=self.c if dc==0 else 1-self.c
        return (y*2+c,z,x)
    def slab(self,y,dc=0):
        c=self.c if dc==0 else 1-self.c
        return y*2+c

def rcopy(src,dst,ss,rs,dev):
    return pltpu.make_async_remote_copy(src_ref=src,dst_ref=dst,send_sem=ss,recv_sem=rs,device_id=dev,device_id_type=MESH)

def when(cond,fn):
    if cond is True: fn()
    else: pl.when(cond)(fn)

def gather_sems(NG,Z):
    D=pltpu.SemaphoreType.DMA
    return [D((NG*2*(Z-1),)),D((NG*2*(Z-1),)),
            D((NG*2*Z,)),D((NG*2*Z,)),
            D((NG*2*Z,)),D((NG*2*Z,)),
            D((NG*2,)),D((NG*2,))]

class Gather:
    def __init__(self,P,G,groups,sems):
        self.P=P; self.G=G; self.groups=groups; self.zs,self.zr,self.xs,self.xr,self.ys,self.yr,self.cs,self.cr=sems
    def _cp(self,idx,lo,n,ss,rs,dev):
        r=self.G.at[(*idx,slice(None),pl.ds(lo,n))]
        return rcopy(r,r,ss,rs,dev)
    def zcp(self,g,d,t,zo,to):
        lo,n,_=self.groups[g]; i=(g*2+d)*(self.P.Z-1)+t
        return self._cp(self.P.piece(zo),lo,n,self.zs.at[i],self.zr.at[i],self.P.nz(to))
    def xfull(self,g,zo,arrive=0):
        lo,n,_=self.groups[g]; i=g*2*self.P.Z+zo
        return self._cp(self.P.piece(zo,dx=arrive),lo,n,self.xs.at[i],self.xr.at[i],self.P.nx)
    def yfull(self,g,zo,arrive=0):
        lo,n,_=self.groups[g]; i=g*2*self.P.Z+zo
        return self._cp(self.P.piece(zo,dy=arrive),lo,n,self.ys.at[i],self.yr.at[i],self.P.ny)
    def ydiag(self,g,zo,arrive=0):
        lo,n,a=self.groups[g]; i=g*2*self.P.Z+self.P.Z+zo
        return self._cp(self.P.piece(zo,dx=1,dy=arrive),lo,a,self.ys.at[i],self.yr.at[i],self.P.ny)
    def xdiag(self,g,zo,arrive=0):
        lo,n,a=self.groups[g]; i=g*2*self.P.Z+self.P.Z+zo
        return self._cp(self.P.piece(zo,dy=1,dx=arrive),lo+a,n-a,self.xs.at[i],self.xr.at[i],self.P.nx)
    def ccp(self,g,k,arrive=0):
        lo,n,_=self.groups[g]
        y=self.P.y if k==0 else 1-self.P.y
        r=self.G.at[self.P.slab(y,dc=arrive),:,:,:,pl.ds(lo,n)]
        return rcopy(r,r,self.cs.at[g*2+k],self.cr.at[g*2+k],self.P.nc)
    def own(self,g):
        z=self.P.z; Z=self.P.Z
        when(z<Z-1,lambda: self.zcp(g,0,0,z,z+1).start())
        when(z>0,lambda: self.zcp(g,1,0,z,z-1).start())
        self.xfull(g,z).start(); self.yfull(g,z).start()
    def zarrive(self,g,t):
        z=self.P.z; Z=self.P.Z
        def below():
            zo=z-1-t
            self.zcp(g,0,t,zo,z).wait_recv()
            if t+1<Z-1:
                when(z<Z-1,lambda: self.zcp(g,0,t+1,zo,z+1).start())
            self.xfull(g,zo).start(); self.yfull(g,zo).start()
        def above():
            zo=z+1+t
            self.zcp(g,1,t,zo,z).wait_recv()
            if t+1<Z-1:
                when(z>0,lambda: self.zcp(g,1,t+1,zo,z-1).start())
            self.xfull(g,zo).start(); self.yfull(g,zo).start()
        when(z-1-t>=0,below); when(z+1+t<Z,above)
    def _diag(self,g,zo):
        self.xfull(g,zo,1).wait_recv(); self.ydiag(g,zo).start()
        self.yfull(g,zo,1).wait_recv(); self.xdiag(g,zo).start()
    def diag(self,g,t):
        z=self.P.z; Z=self.P.Z
        if t==0: self._diag(g,z)
        else:
            when(z-t>=0,lambda: self._diag(g,z-t))
            when(z+t<Z,lambda: self._diag(g,z+t))
    def corner(self,g):
        self.ccp(g,0).start()
        for zo in range(self.P.Z):
            self.ydiag(g,zo,1).wait_recv(); self.xdiag(g,zo,1).wait_recv()
        self.ccp(g,1).start()
    def sibling(self,g):
        self.ccp(g,0,1).wait_recv(); self.ccp(g,1,1).wait_recv()
    def drain(self,g):
        z=self.P.z; Z=self.P.Z
        for zo in range(Z):
            self.xfull(g,zo).wait_send(); self.yfull(g,zo).wait_send()
            self.xdiag(g,zo).wait_send(); self.ydiag(g,zo).wait_send()
        for k in range(2): self.ccp(g,k).wait_send()
        for t in range(Z-1):
            when(jnp.logical_and(z<Z-1,z-t>=0),lambda: self.zcp(g,0,t,z-t,z+1).wait_send())
            when(jnp.logical_and(z>0,z+t<=Z-1),lambda: self.zcp(g,1,t,z+t,z-1).wait_send())
    def events(self,g):
        Z=self.P.Z
        ev=[lambda: self.own(g)]
        for t in range(Z-1):
            ev.append(lambda t=t: self.zarrive(g,t))
            ev.append(lambda t=t: self.diag(g,t))
        ev.append(lambda: self.diag(g,Z-1))
        ev.append(lambda: self.corner(g))
        ev.append(lambda: self.sibling(g))
        return ev


SLOT = 1280
NB=7
def rs_sems(NG,Z):
    D=pltpu.SemaphoreType.DMA
    return [D((NG*2,)),D((NG*2,)),
            D((NG*3,)),D((NG*3,)),
            D((NG*2,)),D((NG*2,)),
            D((NG*2*Z,)),D((NG*2*Z,))]
def rs_bufs(Z):
    V=lambda *s: pltpu.VMEM(s,BF)
    h=640
    return [V(2,2,Z,2,16,SLOT),V(2,Z,2,16,h),V(2,Z,16,h),V(2,2,Z,16,h),V(2,Z,16,h),V(4,Z,16,SLOT),V(4,Z,16,SLOT)]
class Scatter:
    def __init__(self,P,R,groups,bufs,sems):
        self.P=P; self.R=R; self.groups=groups; self.bufs=bufs
        self.cs,self.cr,self.xs,self.xr,self.ys,self.yr,self.zs,self.zr=sems
    def buf(self,g,i,w):
        b=self.bufs[i]
        b=b.at[g%b.shape[0]]
        nd=len(b.shape)
        return b.at[(slice(None),)*(nd-1)+(pl.ds(0,w),)]
    def row(self,dy=0,dc=0):
        y=self.P.y if dy==0 else 1-self.P.y
        c=self.P.c if dc==0 else 1-self.P.c
        return y*2+c
    def add(self,dst,src):
        def body(z,_):
            d=dst(z); s=src(z)
            d[...]=d[...]+s[...]
            return 0
        lax.fori_loop(0,self.P.Z,body,0)
    def ccp(self,g,k):
        lo,n,_=self.groups[g]
        return rcopy(self.R.at[self.row(k,1),:,:,:,pl.ds(lo,n)],self.buf(g,0,n).at[k],self.cs.at[g*2+k],self.cr.at[g*2+k],self.P.nc)
    def x1(self,g,k):
        lo,n,a=self.groups[g]
        return rcopy(self.R.at[self.row(k),:,1-self.P.x,:,pl.ds(lo+a,n-a)],self.buf(g,3,n-a).at[k],self.xs.at[g*3+k],self.xr.at[g*3+k],self.P.nx)
    def y1(self,g):
        lo,n,a=self.groups[g]
        return rcopy(self.R.at[self.row(1),:,:,:,pl.ds(lo,a)],self.buf(g,1,a),self.ys.at[g*2],self.yr.at[g*2],self.P.ny)
    def x2(self,g):
        lo,n,a=self.groups[g]
        return rcopy(self.R.at[self.row(0),:,1-self.P.x,:,pl.ds(lo,a)],self.buf(g,2,a),self.xs.at[g*3+2],self.xr.at[g*3+2],self.P.nx)
    def y2(self,g):
        lo,n,a=self.groups[g]
        return rcopy(self.R.at[self.row(1),:,self.P.x,:,pl.ds(lo+a,n-a)],self.buf(g,4,n-a),self.ys.at[g*2+1],self.yr.at[g*2+1],self.P.ny)
    def zc(self,g,d,zo,to):
        lo,n,_=self.groups[g]; i=(g*2+d)*self.P.Z+zo
        return rcopy(self.R.at[self.row(0),zo,self.P.x,:,pl.ds(lo,n)],self.buf(g,5+d,n).at[zo],self.zs.at[i],self.zr.at[i],self.P.nz(to))
    def s_c(self,g):
        self.ccp(g,1).start(); self.ccp(g,0).start()
    def a_c(self,g):
        lo,n,a=self.groups[g]; R=self.R; b=self.buf(g,0,n)
        for k in (1,0):
            self.ccp(g,k).wait_recv()
            r=self.row(k)
            self.add(lambda z: R.at[r,z,:,:,pl.ds(lo,n)],lambda z: b.at[k,z])
            self.x1(g,k).start()
            if k==1: self.y1(g).start()
    def a_1(self,g):
        lo,n,a=self.groups[g]; R=self.R; P=self.P; B1=self.buf(g,1,a); B3=self.buf(g,3,n-a)
        self.y1(g).wait_recv()
        r=self.row(0)
        self.add(lambda z: R.at[r,z,:,:,pl.ds(lo,a)],lambda z: B1.at[z])
        for k in (1,0):
            self.x1(g,k).wait_recv()
            q=self.row(k)
            self.add(lambda z: R.at[q,z,P.x,:,pl.ds(lo+a,n-a)],lambda z: B3.at[k,z])
        self.x2(g).start()
        self.y2(g).start()
    def a_2(self,g):
        lo,n,a=self.groups[g]; R=self.R; P=self.P; B2=self.buf(g,2,a); B4=self.buf(g,4,n-a)
        r=self.row(0)
        self.x2(g).wait_recv()
        self.add(lambda z: R.at[r,z,P.x,:,pl.ds(lo,a)],lambda z: B2.at[z])
        self.y2(g).wait_recv()
        self.add(lambda z: R.at[r,z,P.x,:,pl.ds(lo+a,n-a)],lambda z: B4.at[z])
    def acc(self,g,zo,b):
        lo,n,_=self.groups[g]
        d=self.R.at[self.row(0),zo,self.P.x,:,pl.ds(lo,n)]
        d[...]=d[...]+b[zo]
    def zstep(self,g,h):
        n=self.groups[g][1]; Z=self.P.Z; z=self.P.z
        if h==0:
            def first():
                for zo in range(Z-1,0,-1): self.zc(g,0,zo,1).start()
            def last():
                for zo in range(Z-1): self.zc(g,1,zo,Z-2).start()
            when(z==0,first); when(z==Z-1,last)
            return
        def up():
            zo=Z-1-h+z
            self.zc(g,0,zo,z).wait_recv()
            self.acc(g,zo,self.buf(g,5,n))
            self.zc(g,0,zo,z+1).start()
        def down():
            zo=h-(Z-1)+z
            self.zc(g,1,zo,z).wait_recv()
            self.acc(g,zo,self.buf(g,6,n))
            self.zc(g,1,zo,z-1).start()
        when(jnp.logical_and(z>=1,z<=h),up)
        when(jnp.logical_and(z>=Z-1-h,z<=Z-2),down)
    def final(self,g,out):
        lo,n,_=self.groups[g]; P=self.P; Z=P.Z; z=P.z
        out[...]=self.R[self.row(0),z,P.x,:,pl.ds(lo,n)].astype(F32)
        @pl.when(z>0)
        def _():
            self.zc(g,0,z,z).wait_recv()
            out[...]+=self.buf(g,5,n)[z].astype(F32)
        @pl.when(z<Z-1)
        def _():
            self.zc(g,1,z,z).wait_recv()
            out[...]+=self.buf(g,6,n)[z].astype(F32)
    def drain(self,g):
        Z=self.P.Z; z=self.P.z
        for k in range(2):
            self.ccp(g,k).wait_send(); self.x1(g,k).wait_send()
        self.x2(g).wait_send(); self.y1(g).wait_send(); self.y2(g).wait_send()
        for zo in range(Z):
            when(z<zo,lambda: self.zc(g,0,zo,z+1).wait_send())
            when(z>zo,lambda: self.zc(g,1,zo,z-1).wait_send())
    def events(self,g,out):
        ev=[lambda: self.s_c(g),lambda: self.a_c(g),lambda: self.a_1(g),lambda: self.a_2(g)]
        for t in range(self.P.Z-1): ev.append(lambda t=t: self.zstep(g,t))
        ev.append(lambda: self.final(g,out))
        return ev

def norm_sems(Z):
    D=pltpu.SemaphoreType.DMA
    return [D((3+Z,)),D((3+Z,))]
def norm_bufs(Z): return [pltpu.VMEM((4+Z,8,128),F32),pltpu.VMEM((3,8,128),F32)]
def all_sum(P,buf,got,ss,rs):
    Z=P.Z
    for i,dev in enumerate((P.nc,P.nx,P.ny)):
        cp=rcopy(buf.at[i],got.at[i],ss.at[i],rs.at[i],dev)
        cp.start(); cp.wait()
        buf[i+1]=buf[i]+got[i]
    buf[4+P.z]=buf[3]
    for t in range(Z):
        def send(): rcopy(buf.at[3],buf.at[4+P.z],ss.at[3+t],rs.at[3+P.z],P.nz(t)).start()
        when(P.z!=t,send)
    for t in range(Z):
        def wait():
            cp=rcopy(buf.at[3],buf.at[4+t],ss.at[3+t],rs.at[3+t],P.nz(t))
            cp.wait_send(); cp.wait_recv()
        when(P.z!=t,wait)
    tot=buf[4]
    for t in range(1,Z): tot=tot+buf[4+t]
    return tot
def enter_all(P,Z):
    bar=pltpu.get_barrier_semaphore()
    def sig(d): pl.semaphore_signal(bar,inc=1,device_id=d,device_id_type=MESH)
    sig(P.nx); sig(P.ny); sig(P.nc)
    for t in range(Z):
        when(P.z!=t,lambda: sig(P.nz(t)))
    pl.semaphore_wait(bar,3+Z-1)


W3 = 768
CW = 1152
QKV_AT = 0
VEC_AT = 3456
VEC_COLS = 128
OUT_AT = 3584
DOWN_AT = 4736
UP_AT = 9344
COLS = 13952
GATHER = [(2304, 1280, 640), (0, 2304, 1152), (3584, 5760, 2944), (9344, 1152, 640), (10496, 1152, 512), (11648, 2304, 1152)]
SCATTER = ([(UP_AT + CW * c, CW, 640 if c % 2 else 512) for c in range(4)]
           + [(DOWN_AT + CW * c, CW, 640 if c % 2 else 512) for c in range(4)]
           + [(OUT_AT, CW, 512), (0, CW, 640), (CW, CW, 512), (2 * CW, 1280, 640)])

def al(v, m): return pl.multiple_of(v, m)

def third_cols(s): return [(D * j + 256 * s, 256) for j in range(3)]

def pack_rows(G, me, at, main, rest):
    G[(*me,slice(None),pl.ds(at,W3))]=main.astype(BF)
    parts=[jnp.concatenate([rest[:,256*s:256*s+128],rest[:,256*s+128:256*s+256]],0) for s in range(3)]
    G[(*me,slice(None),pl.ds(al(at+W3,128),W3//2))]=jnp.concatenate(parts,1).astype(BF)

def pack_own(place, G, wqkv, wout, wup, wdown, vec):
    me=place.me
    lo=al(8*place.x,8); ro=al(16*(1-place.x),8)
    def cols(w,cs):
        return [jnp.concatenate([w[pl.ds(a,n),pl.ds(c,k)] for c,k in cs],1) for a,n in ((lo,16),(ro,8))]
    for s in range(3): pack_rows(G,me,QKV_AT+CW*s,*cols(wqkv,third_cols(s)))
    pack_rows(G,me,OUT_AT,*cols(wout,[(0,W3)]))
    for c in range(4): pack_rows(G,me,UP_AT+CW*c,*cols(wup,[(W3*c,W3)]))
    for r in range(6):
        G[(*me,slice(None),pl.ds(DOWN_AT+r*D,D))]=wdown[pl.ds(16*r,16),:].astype(BF)
    G[(*me,slice(None),pl.ds(VEC_AT,VEC_COLS))]=vec[...]

def unpack24(G, at, dst):
    Z=G.shape[1]
    def body(j,_):
        r=al(j*48,16); d=j//Z; z=lax.rem(j,Z)
        dst[pl.ds(r,16),:]=G[d,z,0,:,pl.ds(al(at,128),W3)]
        dst[pl.ds(r+32,16),:]=G[d,z,1,:,pl.ds(al(at,128),W3)]
        a=G[d,z,0,:,pl.ds(al(at+W3,128),W3//2)].astype(F32)
        b=G[d,z,1,:,pl.ds(al(at+W3,128),W3//2)].astype(F32)
        parts=[]
        for s in range(3):
            q=slice(128*s,128*s+128)
            parts+=[jnp.concatenate([a[:8,q],b[:8,q]],0),jnp.concatenate([a[8:,q],b[8:,q]],0)]
        dst[pl.ds(r+16,16),:]=jnp.concatenate(parts,1).astype(BF)
        return 0
    lax.fori_loop(0,G.shape[0]*Z,body,0)

def pack24(G, at, src):
    Z=G.shape[1]
    def body(j,_):
        r=al(j*48,16); d=j//Z; z=lax.rem(j,Z)
        pack_rows(G,(d,z,0),al(at,128),src[pl.ds(r,16),:],src[pl.ds(al(r+16,8),8),:])
        pack_rows(G,(d,z,1),al(at,128),src[pl.ds(r+32,16),:],src[pl.ds(al(r+24,8),8),:])
        return 0
    lax.fori_loop(0,G.shape[0]*Z,body,0)

def unpack_down(G, c, dst):
    def body(k,_):
        for r in range(6):
            dst[pl.ds(al(k*96+16*r,16),16),:]=G[c,k//2,lax.rem(k,2),:,pl.ds(DOWN_AT+r*D,D)]
        return 0
    lax.fori_loop(0,2*G.shape[1],body,0)

def pack_down(G, c, src):
    def body(k,_):
        for r in range(6):
            G[c,k//2,lax.rem(k,2),:,pl.ds(DOWN_AT+r*D,D)]=src[pl.ds(al(k*96+16*r,16),16),:].astype(BF)
        return 0
    lax.fori_loop(0,2*G.shape[1],body,0)

def vec_shift(k): return (240*k)//128

def unpack_vec(G, V, V1):
    V[...]=jnp.zeros_like(V)
    Z=G.shape[1]
    for k in range(8*Z):
        V[pl.ds(vec_shift(k),3),:]+=G[k//(2*Z),k//2%Z,k%2,:,pl.ds(VEC_AT,VEC_COLS)].astype(F32)[0:3]
    for t in range(60):
        V1[:,pl.ds(128*t,128)]=V[pl.ds(t,1),:]

def pack_vec(G, V, V1):
    V[...]=jnp.zeros_like(V)
    for t in range(60):
        V[pl.ds(t,1),:]=V1[:,pl.ds(128*t,128)]
    Z=G.shape[1]
    for k in range(8*Z):
        G[k//(2*Z),k//2%Z,k%2,:,pl.ds(VEC_AT,VEC_COLS)]=V[pl.ds(vec_shift(k),16),:].astype(BF)

def norm_parts(x):
    c=x-jnp.mean(x,-1,keepdims=True)
    s=lax.rsqrt(jnp.mean(c*c,-1,keepdims=True)+EPS_NORM)
    return c*s,s

def norm_back(dx, xh, s):
    return s*(dx-jnp.mean(dx,-1,keepdims=True)-xh*jnp.mean(dx*xh,-1,keepdims=True))

def gelu_both(u):
    k0=0.7978845608028654; k1=0.044715
    u2=u*u
    t=jnp.tanh(k0*(u*(1.0+k1*u2)))
    h=0.5*(1.0+t)
    return u*h, h+(0.5*k0)*u*(1.0-t*t)*(1.0+(3.0*k1)*u2)

RB=256

RULES=((1,1,0),(2,3,1),(2,7,4))

def places():
    p=[("stat",i,0.6) for i in range(4)]
    for i in range(3):
        p.append(("third",i,0.6 if i else 2.0))
        p+=[("qkv",4*i+k,0.42) for k in range(4)]
        for pp in range(2): p+=[("af",4*i+2*pp+k,(1.2,2.4)[k]) for k in range(2)]
    p.append(("out",0,0.6))
    p+=[("ob",k,1.1) for k in range(4)]
    for c in range(4):
        p.append(("chunk",c,0.5))
        p+=[("mr",4*c+k,1.75) for k in range(4)]
        p+=[("mw",3*c+k,0.6+0.15*(k==2)) for k in range(3)]
        p+=[("mu",3*c+k,0.6+0.2*(k==2)) for k in range(3)]
        p.append(("mp",c,0.1))
    p.append(("fin",0,1.0))
    p+=[("bb",k,1.3) for k in range(4)]
    p+=[("bw",k,0.6+0.2*(k==2)) for k in range(3)]
    p.append(("bp",0,0.1))
    p+=[("ag",k,0.5) for k in range(4)]
    for i in range(3):
        for pp in range(2): p+=[("ab",8*i+4*pp+k,1.0) for k in range(4)]
        p+=[("dh",4*i+k,0.5) for k in range(4)]
        if i==2: p+=[("ln",k,0.9) for k in range(4)]
        p+=[("dq",3*i+k,0.6+0.2*(k==2)) for k in range(3)]
        p.append(("dp",i,0.1))
    return p

def ready_places():
    return [("mp",c) for c in range(4)]+[("mp",3)]*4+[("bp",0)]+[("dp",i) for i in range(3)]

def due_places():
    return [("third",0),("third",1),("out",0),("chunk",0),("chunk",1),("chunk",2)]

class Clock:
    def __init__(self, plan, ga, sc, own):
        names=[p[:2] for p in places()]
        index={p:i for i,p in enumerate(names)}
        fns={}
        for g in range(len(GATHER)):
            for k,f in enumerate(ga.events(g)): fns[(0,g,k)]=f
        for g,(lo,n,_) in enumerate(SCATTER):
            for k,f in enumerate(sc.events(g,own.at[:,pl.ds(lo,n)])): fns[(1,g,k)]=f
        check_plan(plan,set(fns),index)
        self.slots={}
        self.tail=[]
        for i,*key in plan:
            if i<len(names): self.slots.setdefault(names[i],[]).append(fns[tuple(key)])
            else: self.tail.append(fns[tuple(key)])
    def at(self, name, step, count):
        for k in range(count):
            todo=self.slots.get((name,k))
            if todo:
                def run(todo=todo):
                    for f in todo: f()
                if isinstance(step,int):
                    if step==k: run()
                else: pl.when(step==k)(run)

PLAN = (
    (0, 0, 0, 0), (2, 0, 0, 1), (3, 0, 1, 0), (3, 0, 0, 2), (4, 0, 0, 3), (4, 0, 0, 4), (4, 0, 1, 1), (4, 0, 0, 5),
    (4, 0, 0, 6), (4, 0, 1, 2), (4, 0, 1, 3), (4, 0, 0, 7), (4, 0, 0, 8), (4, 0, 1, 4), (4, 0, 2, 0), (4, 0, 0, 9),
    (4, 0, 1, 5), (5, 0, 1, 6), (10, 0, 2, 1), (10, 0, 1, 7), (11, 0, 1, 8), (12, 0, 2, 2), (12, 0, 2, 3),
    (13, 0, 1, 9), (20, 0, 2, 4), (20, 0, 2, 5), (24, 0, 4, 0), (24, 0, 2, 6), (27, 0, 4, 1), (28, 0, 2, 7),
    (28, 0, 3, 0), (29, 0, 3, 1), (30, 0, 3, 2), (30, 0, 3, 3), (30, 0, 2, 8), (30, 0, 4, 2), (30, 0, 3, 4),
    (30, 0, 3, 5), (30, 0, 4, 3), (30, 0, 4, 4), (30, 0, 3, 6), (30, 0, 4, 5), (30, 0, 5, 0), (31, 0, 3, 7),
    (31, 0, 2, 9), (31, 0, 5, 1), (32, 0, 3, 8), (33, 0, 4, 6), (34, 0, 5, 2), (35, 0, 4, 7), (36, 0, 3, 9),
    (39, 0, 5, 3), (40, 0, 4, 8), (41, 0, 5, 4), (42, 0, 4, 9), (43, 0, 5, 5), (47, 1, 0, 0), (49, 0, 5, 6),
    (49, 0, 5, 7), (50, 1, 0, 1), (53, 1, 0, 2), (54, 0, 5, 8), (58, 1, 0, 3), (59, 1, 1, 0), (60, 0, 5, 9),
    (61, 1, 0, 4), (63, 1, 1, 1), (66, 1, 0, 5), (67, 1, 1, 2), (70, 1, 0, 6), (72, 1, 2, 0), (72, 1, 1, 3),
    (72, 1, 1, 4), (74, 1, 2, 1), (75, 1, 1, 5), (76, 1, 0, 7), (78, 1, 2, 2), (81, 1, 2, 3), (81, 1, 2, 4),
    (82, 1, 1, 6), (83, 1, 3, 0), (86, 1, 2, 5), (87, 1, 3, 1), (87, 1, 4, 0), (88, 1, 2, 6), (88, 1, 1, 7),
    (89, 1, 4, 1), (90, 1, 5, 0), (90, 1, 2, 7), (94, 1, 3, 2), (97, 1, 4, 2), (99, 1, 3, 3), (100, 1, 3, 4),
    (100, 1, 4, 3), (100, 1, 5, 1), (101, 1, 6, 0), (103, 1, 3, 5), (103, 1, 6, 1), (103, 1, 7, 0), (103, 1, 4, 4),
    (105, 1, 5, 2), (107, 1, 3, 6), (108, 1, 4, 5), (109, 1, 6, 2), (110, 1, 5, 3), (110, 1, 7, 1), (110, 1, 8, 0),
    (111, 1, 4, 6), (112, 1, 3, 7), (112, 1, 5, 4), (113, 1, 6, 3), (113, 1, 8, 1), (114, 1, 4, 7), (114, 1, 6, 4),
    (115, 1, 5, 5), (115, 1, 9, 0), (116, 1, 7, 2), (116, 1, 6, 5), (117, 1, 5, 6), (119, 1, 6, 6), (120, 1, 8, 2),
    (120, 1, 7, 3), (121, 1, 9, 1), (122, 1, 5, 7), (122, 1, 7, 4), (124, 1, 8, 3), (125, 1, 7, 5), (126, 1, 6, 7),
    (126, 1, 8, 4), (128, 1, 10, 0), (128, 1, 9, 2), (128, 1, 8, 5), (130, 1, 7, 6), (131, 1, 8, 6),
    (131, 1, 10, 1), (132, 1, 7, 7), (134, 1, 10, 2), (134, 1, 8, 7), (137, 1, 9, 3), (137, 1, 9, 4),
    (139, 1, 9, 5), (141, 1, 10, 3), (143, 1, 9, 6), (148, 1, 11, 0), (148, 1, 10, 4), (148, 1, 10, 5),
    (148, 1, 10, 6), (148, 1, 9, 7), (149, 1, 11, 1), (149, 1, 10, 7), (149, 1, 11, 2), (149, 1, 11, 3),
    (149, 1, 11, 4), (149, 1, 11, 5), (149, 1, 11, 6), (149, 1, 11, 7),
)

def check_plan(plan, keys, index):
    pos={tuple(e[1:]):(e[0],j) for j,e in enumerate(plan)}
    assert set(pos)==keys and len(plan)==len(keys)
    assert all(a[0]<=b[0] for a,b in zip(plan,plan[1:]))
    last={0:9,1:7}
    for kind,g,k in keys:
        if k: assert pos[(kind,g,k-1)]<pos[(kind,g,k)]
    for g,p in enumerate(due_places()): assert pos[(0,g,9)][0]<=index[p]
    for g,p in enumerate(ready_places()):
        assert pos[(1,g,0)][0]>=index[p]
        for n,i,j in RULES:
            if g>=n: assert pos[(1,g-n,i)]<pos[(1,g,j)]

def mega_kernel(Z,plan,tok_h,cot_h,len_ref,wqkv_s,wout_s,wup_s,wdown_s,vec_s,
               mixed_o,dtok_o,own_o,nrm_o,
               G,tok,cot,F1,F2,F3,qkv,B1,B2,B3,hT,aT,oT,W0,W1,dW,lse,V,V1,dV1,dka,dva,own,nrm,dsem,*rest):
    gsems=rest[:8]; rbufs=rest[8:8+NB]; rsems=rest[8+NB:16+NB]; nb,got,ns,nr=rest[16+NB:]
    L=tok.shape[0]
    NBK=L//RB
    place=Place(Z)
    def dma(a,b,i):
        cp=pltpu.make_async_copy(a,b,dsem.at[i]); cp.start(); return cp
    ldt=dma(tok_h,tok,0); ldc=dma(cot_h,cot,1)
    pack_own(place,G,wqkv_s,wout_s,wup_s,wdown_s,vec_s)
    enter_all(place,Z)
    ga=Gather(place,G,GATHER,gsems)
    sc=Scatter(place,G,SCATTER,rbufs,rsems)
    clock=Clock(plan,ga,sc,own)
    def at(name,step,count): clock.at(name,step,count)
    def rows(i): return pl.ds(al(i*RB,RB),RB)
    length=len_ref[0]
    ldt.wait()
    xhat=F1; h1=B1; o=B3
    for i in range(4):
        at("stat",i,4)
        if i<NBK:
            xhat[rows(i),:]=norm_parts(tok[rows(i),:].astype(F32))[0]
    def third(i,_):
        s=lax.rem(i+2,3)
        at("third",i,3)
        @pl.when(i==0)
        def _():
            unpack_vec(G,V,V1)
            def first(j,_):
                h1[rows(j),:]=(xhat[rows(j),:]*V1[:,0:D]+V1[:,D:2*D]).astype(BF)
                return 0
            lax.fori_loop(0,NBK,first,0)
        unpack24(G,QKV_AT+CW*s,W0)
        def block(j,_):
            at("qkv",4*i+j,12)
            qkv[s,rows(j),:]=nn(h1[rows(j),:],W0[...]).astype(BF)
            return 0
        lax.fori_loop(0,NBK,block,0)
        def pair(pp,_):
            p=2*s+pp
            def col(j): return qkv.at[s,:,pl.ds(al(256*j+128*pp,128),128)]
            c=pl.ds(al(128*p,128),128)
            attn_fwd_pair(col(0),col(1),col(2),length,o.at[:,c],oT.at[c,:],lse.at[p],512,
                          tick=lambda k: at("af",4*i+2*pp+k,12))
            return 0
        lax.fori_loop(0,2,pair,0)
        return 0
    lax.fori_loop(0,3,third,0)
    at("out",0,1)
    unpack24(G,OUT_AT,W0)
    ldc.wait()
    r1=F1; mixed=F2; dh2=F3; h2=B1; h2T=hT
    def out_block(i,_):
        at("ob",i,4)
        sl=rows(i)
        r=tok[sl,:].astype(F32)+nn(o[sl,:],W0[...])+V1[:,4*D:5*D]
        r1[sl,:]=r
        mixed[sl,:]=r+V1[:,5*D:6*D]
        hb=(norm_parts(r)[0]*V1[:,2*D:3*D]+V1[:,3*D:4*D]).astype(BF)
        h2[sl,:]=hb
        h2T[:,sl]=hb.T
        pos_=i*RB+lax.broadcasted_iota(jnp.int32,(RB,D),0)
        cot[sl,:]=jnp.where(pos_<length,cot[sl,:],jnp.zeros((),BF))
        dh2[sl,:]=jnp.zeros((RB,D),F32)
        return 0
    lax.fori_loop(0,NBK,out_block,0)
    du_s=B2
    def chunk(c,_):
        at("chunk",c,4)
        for g,when_ in enumerate((0,0,0,0,1,2)):
            pl.when(c==when_)(lambda g=g: ga.drain(g))
        unpack24(G,UP_AT+CW*c,W0)
        unpack_down(G,c,W1)
        bu=V1[:,pl.ds(al(6*D+c*W3,128),W3)]
        def mrows(i,acc):
            at("mr",4*c+i,16)
            sl=rows(i)
            u=nn(h2[sl,:],W0[...])+bu
            a,slope=gelu_both(u)
            ab=a.astype(BF)
            mixed[sl,:]+=nn(ab,W1[...])
            aT[:,sl]=ab.T
            du=(nt(cot[sl,:],W1[...])*slope).astype(BF)
            du_s[sl,:]=du
            dh2[sl,:]+=nt(du,W0[...])
            return acc+jnp.sum(du.astype(F32),0,keepdims=True)
        s=lax.fori_loop(0,NBK,mrows,jnp.zeros((1,W3),F32))
        dV1[:,pl.ds(al(6*D+c*W3,128),W3)]=s
        def wrows(i,_):
            at("mw",3*c+i,12)
            dW[rows(i),:]=nn(aT[rows(i),:],cot[...])
            return 0
        lax.fori_loop(0,W3//RB,wrows,0)
        pack_down(G,c,dW)
        def urows(i,_):
            at("mu",3*c+i,12)
            dW[rows(i),:]=nn(h2T[rows(i),:],du_s[...])
            return 0
        lax.fori_loop(0,D//RB,urows,0)
        pack24(G,UP_AT+CW*c,dW)
        at("mp",c,4)
        return 0
    lax.fori_loop(0,FF//W3,chunk,0)
    at("fin",0,1)
    mixed_b=B2
    def fin(i,_):
        mixed_b[rows(i),:]=mixed[rows(i),:].astype(BF)
        return 0
    lax.fori_loop(0,NBK,fin,0)
    outs=[dma(mixed_b,mixed_o,2)]
    unpack24(G,OUT_AT,W0)
    dr1=F3; dy=B3; do=B1
    def back(i,acc):
        at("bb",i,4)
        sl=rows(i)
        dh=dh2[sl,:]
        xh,s=norm_parts(r1[sl,:])
        g=cot[sl,:].astype(F32)
        dr=g+norm_back(dh*V1[:,2*D:3*D],xh,s)
        dr1[sl,:]=dr
        dyb=dr.astype(BF)
        dy[sl,:]=dyb
        do[sl,:]=nt(dyb,W0[...]).astype(BF)
        new=(dh*xh,dh,dyb.astype(F32),g)
        return tuple(a+jnp.sum(b,0,keepdims=True) for a,b in zip(acc,new))
    z1=jnp.zeros((1,D),F32)
    sums=lax.fori_loop(0,NBK,back,(z1,z1,z1,z1))
    for j,v in enumerate(sums): dV1[:,pl.ds((2+j)*D,D)]=v
    def orow(i,_):
        at("bw",i,3)
        dW[rows(i),:]=nn(oT[rows(i),:].astype(BF),dy[...])
        return 0
    lax.fori_loop(0,D//RB,orow,0)
    pack24(G,OUT_AT,dW)
    at("bp",0,1)
    h1T=hT; dqkv=B3; dh1=F2
    outs[0].wait()
    def again(i,_):
        at("ag",i,4)
        sl=rows(i)
        hb=(norm_parts(tok[sl,:].astype(F32))[0]*V1[:,0:D]+V1[:,D:2*D]).astype(BF)
        h1T[:,sl]=hb.T
        dh1[sl,:]=jnp.zeros((RB,D),F32)
        return 0
    lax.fori_loop(0,NBK,again,0)
    def third_back(s,_):
        unpack24(G,QKV_AT+CW*s,W0)
        def pair(pp,_):
            p=2*s+pp
            def col(j): return qkv.at[s,:,pl.ds(al(256*j+128*pp,128),128)]
            def dcol(j): return dqkv.at[:,pl.ds(al(256*j+128*pp,128),128)]
            c=pl.ds(al(128*p,128),128)
            attn_bwd_pair(col(0),col(1),col(2),do.at[:,c],oT.at[c,:],lse.at[p],length,
                          dcol(0),dcol(1),dcol(2),dka,dva,256,tick=lambda k: at("ab",8*s+4*pp+k,24))
            return 0
        lax.fori_loop(0,2,pair,0)
        def drow(i,_):
            at("dh",4*s+i,12)
            dh1[rows(i),:]+=nt(dqkv[rows(i),:],W0[...])
            return 0
        lax.fori_loop(0,NBK,drow,0)
        @pl.when(s==2)
        def _():
            def lrow(i,acc):
                at("ln",i,4)
                sl=rows(i)
                dh=dh1[sl,:]
                xh,r=norm_parts(tok[sl,:].astype(F32))
                F1[sl,:]=dr1[sl,:]+norm_back(dh*V1[:,0:D],xh,r)
                return tuple(a+jnp.sum(b,0,keepdims=True) for a,b in zip(acc,(dh*xh,dh)))
            a,b=lax.fori_loop(0,NBK,lrow,(z1,z1))
            dV1[:,0:D]=a
            dV1[:,D:2*D]=b
            pack_vec(G,V,dV1)
        def qrow(i,_):
            at("dq",3*s+i,9)
            dW[rows(i),:]=nn(h1T[rows(i),:],dqkv[...])
            return 0
        lax.fori_loop(0,D//RB,qrow,0)
        pack24(G,QKV_AT+CW*s,dW)
        at("dp",s,3)
        return 0
    lax.fori_loop(0,3,third_back,0)
    outs=[dma(F1,dtok_o,3)]
    for f in clock.tail: f()
    flat=lax.broadcasted_iota(jnp.int32,(16,VEC_COLS),0)*VEC_COLS+lax.broadcasted_iota(jnp.int32,(16,VEC_COLS),1)
    start=lax.rem(240*((place.dp*Z+place.z)*2+place.x),128)
    vec=own[:,pl.ds(VEC_AT,VEC_COLS)]
    vec=jnp.where(jnp.logical_and(flat>=start,flat<start+240),vec,0.0)
    left=own[:,pl.ds(0,VEC_AT)]; right=own[:,pl.ds(OUT_AT,COLS-OUT_AT)]
    nb[0]=jnp.full((8,128),1.0,F32)*(jnp.sum(left*left)+jnp.sum(right*right)+jnp.sum(vec*vec))
    outs.append(dma(own,own_o,4))
    nrm[8:24,:]=vec
    nrm[0:8,:]=all_sum(place,nb,got,ns,nr)
    outs.append(dma(nrm,nrm_o,5))
    for g in range(len(SCATTER)): sc.drain(g)
    for cp in outs: cp.wait()

def mega_call(Z,tok,cot,length,wqkv,wout,wup,wdown,vec,plan=None):
    plan=PLAN if plan is None else plan
    L=tok.shape[0]; pieces=8*Z
    S=jax.ShapeDtypeStruct; V=pltpu.VMEM
    vm=pl.BlockSpec(memory_space=pltpu.VMEM); an=pl.BlockSpec(memory_space=pltpu.HBM); sm=pl.BlockSpec(memory_space=pltpu.SMEM)
    outs=[S((L,D),BF),S((L,D),F32),S((16,COLS),F32),S((24,128),F32)]
    f=lambda: V((L,D),F32)
    b=lambda: V((L,D),BF)
    scratch=[V((4,Z,2,16,COLS),BF),b(),b(),f(),f(),f(),V((3,L,D),BF),b(),b(),b(),V((D,L),BF),V((D,L),BF),V((D,L),F32),
             V((D,W3),BF),V((W3,D),BF),V((D,W3),F32),V((6,2,L),F32),V((80,128),F32),V((1,10*D),F32),V((1,10*D),F32),
             V((L,128),F32),V((L,128),F32),V((16,COLS),F32),V((24,128),F32),pltpu.SemaphoreType.DMA((6,))]
    return pl.pallas_call(functools.partial(mega_kernel,Z,plan),out_shape=outs,
        in_specs=[an,an,sm]+[vm]*5,out_specs=[an]*len(outs),
        scratch_shapes=scratch+gather_sems(len(GATHER),Z)+rs_bufs(Z)+rs_sems(len(SCATTER),Z)+norm_bufs(Z)+norm_sems(Z),
        compiler_params=pltpu.CompilerParams(collective_id=1,has_side_effects=True,vmem_limit_bytes=63*2**20),
        cost_estimate=pl.CostEstimate(flops=60*10**9,bytes_accessed=60*2**20,transcendentals=10**7))(tok,cot,length,wqkv,wout,wup,wdown,vec)


def adam_step(weight, first_mom, second_mom, gradient, step_rate):
    first_new = BETA_ONE * first_mom + (1.0 - BETA_ONE) * gradient
    second_new = BETA_TWO * second_mom + (1.0 - BETA_TWO) * gradient * gradient
    fix_one = 1.0 - BETA_ONE**STEP
    fix_two = 1.0 - BETA_TWO**STEP
    update = (
        first_new / fix_one / (jnp.sqrt(second_new / fix_two) + ADAM_EPSILON) + DECAY_RATE * weight
    )
    return (weight - step_rate * update, first_new, second_new)


def adam_kernel(par_ref, own_h, nrm_h, mixed_h, dtok_h, *refs):
    ins_h, outs_h = refs[:12], refs[12:24]
    own, nrm, *rest = refs[26:]
    ins, outs, mixed, dtok, sem = rest[:12], rest[12:24], rest[24], rest[25], rest[26]
    pairs = list(zip((own_h, nrm_h) + tuple(ins_h), (own, nrm) + tuple(ins)))
    loads = [pltpu.make_async_copy(a, b, sem.at[i]) for i, (a, b) in enumerate(pairs)]
    moves = [
        pltpu.make_async_copy(mixed_h, mixed, sem.at[14]),
        pltpu.make_async_copy(dtok_h, dtok, sem.at[15]),
    ]
    for cp in loads + moves:
        cp.start()
    for cp in loads:
        cp.wait()
    for cp in moves:
        cp.wait()
    moves = [
        pltpu.make_async_copy(mixed, refs[24], sem.at[14]),
        pltpu.make_async_copy(dtok, refs[25], sem.at[15]),
    ]
    for cp in moves:
        cp.start()
    factor = jnp.minimum(1.0, CLIP_NORM / (jnp.sqrt(nrm[0:1, 0:1]) + 1e-06))
    main_at = al(8 * par_ref[0], 8)
    rest_at = al(16 * (1 - par_ref[0]), 8)

    def step(i, rows, cols, grad, rate):
        w, m, v = [r[rows, cols] for r in ins[3 * i : 3 * i + 3]]
        new = adam_step(w, m, v, grad * factor, rate)
        for r, a in zip(outs[3 * i : 3 * i + 3], new):
            r[rows, cols] = a

    def chunk(i, at, cols, rate):
        main = own[:, pl.ds(at, W3)]
        packed = own[:, pl.ds(at + W3, W3 // 2)]
        parts = []
        for s in range(3):
            parts += [packed[:8, 128 * s : 128 * s + 128], packed[8:, 128 * s : 128 * s + 128]]
        rest = jnp.concatenate(parts, 1)
        done = 0
        for c, n in cols:
            step(i, pl.ds(main_at, 16), pl.ds(c, n), main[:, done : done + n], rate)
            step(i, pl.ds(rest_at, 8), pl.ds(c, n), rest[:, done : done + n], rate)
            done += n

    for s in range(3):
        chunk(0, QKV_AT + CW * s, third_cols(s), D ** (-0.5))
    chunk(1, OUT_AT, [(0, W3)], D ** (-0.5))
    for c in range(4):
        chunk(2, UP_AT + CW * c, [(W3 * c, W3)], D ** (-0.5))
    for r in range(6):
        grad = own[:, pl.ds(DOWN_AT + r * D, D)]
        step(3, pl.ds(16 * r, 16), slice(None), grad, FF ** (-0.5))
    stores = [pltpu.make_async_copy(a, b, sem.at[i]) for i, (a, b) in enumerate(zip(outs, outs_h))]
    for cp in stores:
        cp.start()
    for cp in stores + moves:
        cp.wait()


def adam_call(parity, own, nrm, mixed, d_tokens, states):
    hb = pl.BlockSpec(memory_space=pltpu.HBM)
    sm = pl.BlockSpec(memory_space=pltpu.SMEM)
    held = [pltpu.VMEM(a.shape, F32) for a in (own, nrm) + tuple(states) + tuple(states)]
    return pl.pallas_call(
        adam_kernel,
        out_shape=[jax.ShapeDtypeStruct(a.shape, a.dtype) for a in states + (mixed, d_tokens)],
        in_specs=[sm] + [hb] * 16,
        out_specs=[hb] * 14,
        scratch_shapes=held
        + [pltpu.VMEM(mixed.shape, BF), pltpu.VMEM(d_tokens.shape, F32)]
        + [pltpu.SemaphoreType.DMA((16,))],
        compiler_params=pltpu.CompilerParams(vmem_limit_bytes=63 * 2**20),
        cost_estimate=pl.CostEstimate(
            flops=10**7, bytes_accessed=8 * 2**20, transcendentals=10**6
        ),
    )(parity, own, nrm, mixed, d_tokens, *states)


def layer_norm(values, gain, shift):
    center = jnp.mean(values, -1, keepdims=True)
    centered = values - center
    spread = jnp.mean(centered * centered, -1, keepdims=True)
    return centered * lax.rsqrt(spread + EPS_NORM) * gain + shift


def smooth_gate(value):
    return jax.nn.gelu(value, approximate=True)


def plain_shards(tokens, lengths, cotangent, *state):
    w_qkv, m_qkv, v_qkv, w_out, m_out, v_out, w_up, m_up, v_up = state[:9]
    w_down, m_down, v_down, packed, m_packed, v_packed = state[9:]
    seq_count, seq_len, model_width = tokens.shape
    row_count = seq_count * seq_len
    axes = ("dp", "fsdp")
    wqkv_b, wout_b, wup_b, wdown_b, vector_b = [
        lax.all_gather(w.astype(BF), axes, axis=0, tiled=True)
        for w in (w_qkv, w_out, w_up, w_down, packed)
    ]
    vector = vector_b.astype(F32)
    gain_one, bias_one, gain_two, bias_two, bias_attn, bias_down = [
        vector[i * model_width : (i + 1) * model_width] for i in range(6)
    ]
    bias_up = vector[6 * model_width :]
    positions = jnp.arange(seq_len, dtype=jnp.int32)
    live_rows = positions[None, :] < lengths[:, None]
    inputs = tokens.astype(F32).reshape(row_count, model_width)
    normed_one, norm_one_back = jax.vjp(layer_norm, inputs, gain_one, bias_one)
    normed_one_b = normed_one.astype(BF)
    qkv_all = jnp.dot(normed_one_b, wqkv_b, preferred_element_type=F32).astype(BF)
    seqs = [slice(i * seq_len, (i + 1) * seq_len) for i in range(seq_count)]
    ahead = [fwd_call(qkv_all[s], lengths[i : i + 1], 512) for i, s in enumerate(seqs)]
    attended_b = jnp.concatenate([a[0] for a in ahead], 0)
    resid_one = inputs + jnp.dot(attended_b, wout_b, preferred_element_type=F32) + bias_attn
    normed_two, norm_two_back = jax.vjp(layer_norm, resid_one, gain_two, bias_two)
    normed_two_b = normed_two.astype(BF)
    upper = jnp.dot(normed_two_b, wup_b, preferred_element_type=F32) + bias_up
    activ, gate_back = jax.vjp(smooth_gate, upper)
    activ_b = activ.astype(BF)
    mixed = resid_one + jnp.dot(activ_b, wdown_b, preferred_element_type=F32) + bias_down
    mixed = mixed.reshape(seq_count, seq_len, model_width).astype(BF)
    grad_b = jnp.where(live_rows[:, :, None], cotangent, jnp.zeros((), BF))
    grad_b = grad_b.reshape(row_count, model_width)
    grad_full = grad_b.astype(F32)
    d_wdown = jnp.dot(activ_b.T, grad_b, preferred_element_type=F32)
    d_bias_down = jnp.sum(grad_full, 0)
    d_activ = jnp.dot(grad_b, wdown_b.T, preferred_element_type=F32)
    (d_upper,) = gate_back(d_activ)
    d_upper_b = d_upper.astype(BF)
    d_bias_up = jnp.sum(d_upper_b.astype(F32), 0)
    d_wup = jnp.dot(normed_two_b.T, d_upper_b, preferred_element_type=F32)
    d_normed_two = jnp.dot(d_upper_b, wup_b.T, preferred_element_type=F32)
    d_resid_norm, d_gain_two, d_bias_two = norm_two_back(d_normed_two)
    d_resid = grad_full + d_resid_norm
    d_branch_b = d_resid.astype(BF)
    d_bias_attn = jnp.sum(d_branch_b.astype(F32), 0)
    d_wout = jnp.dot(attended_b.T, d_branch_b, preferred_element_type=F32)
    d_attended_b = jnp.dot(d_branch_b, wout_b.T, preferred_element_type=F32).astype(BF)
    back = [
        bwd_call(qkv_all[s], d_attended_b[s], a[1], a[2], lengths[i : i + 1])
        for i, (s, a) in enumerate(zip(seqs, ahead))
    ]
    d_qkv_b = jnp.concatenate([jnp.concatenate(b, 1) for b in back], 0)
    d_wqkv = jnp.dot(normed_one_b.T, d_qkv_b, preferred_element_type=F32)
    d_normed_one = jnp.dot(d_qkv_b, wqkv_b.T, preferred_element_type=F32)
    d_input_norm, d_gain_one, d_bias_one = norm_one_back(d_normed_one)
    d_tokens = (d_resid + d_input_norm).reshape(seq_count, seq_len, model_width)
    d_vector = jnp.concatenate(
        [d_gain_one, d_bias_one, d_gain_two, d_bias_two, d_bias_attn, d_bias_down, d_bias_up]
    )
    owned = [
        lax.psum_scatter(g, axes, scatter_dimension=0, tiled=True)
        for g in (d_wqkv, d_wout, d_wup, d_wdown, d_vector)
    ]
    grad_norm = jnp.sqrt(lax.psum(sum(jnp.sum(g * g) for g in owned), axes))
    factor = jnp.minimum(1.0, CLIP_NORM / (grad_norm + 1e-06))
    rates = (D ** (-0.5), D ** (-0.5), D ** (-0.5), FF ** (-0.5), VECTOR_RATE)
    new = ()
    for i, (g, rate) in enumerate(zip(owned, rates)):
        new += adam_step(*state[3 * i : 3 * i + 3], g * factor, rate)
    return (mixed, d_tokens, grad_norm) + new


def direct_shards(Z, tokens, lengths, cotangent, *state):
    packed, m_packed, v_packed = state[12:]
    dp = lax.axis_index("dp")
    fsdp = lax.axis_index("fsdp")
    n = packed.shape[0]
    start = ((dp * 2 * Z + fsdp) * n) % VEC_COLS
    vec = lax.dynamic_update_slice(
        jnp.zeros((16 * VEC_COLS,), BF), packed.astype(BF), (start,)
    ).reshape(16, VEC_COLS)
    mixed, d_tokens, own, small = mega_call(
        Z, tokens[0], cotangent[0], lengths, state[0], state[3], state[6], state[9], vec
    )
    grad_norm = jnp.sqrt(small[0, 0])
    factor = jnp.minimum(1.0, CLIP_NORM / (grad_norm + 1e-06))
    parity = (fsdp % 2).astype(jnp.int32).reshape(1)
    *new, mixed, d_tokens = adam_call(parity, own, small, mixed, d_tokens, state[:12])
    g_vec = lax.dynamic_slice(small[8:].reshape(-1), (start,), (n,))
    new_vec = adam_step(packed, m_packed, v_packed, g_vec * factor, VECTOR_RATE)
    return (mixed[None], d_tokens[None], grad_norm) + tuple(new) + new_vec


def solution(mesh):
    rows = P(("dp", "fsdp"), None)
    seqs = P(("dp", "fsdp"), None, None)
    flat = P(("dp", "fsdp"))
    in_specs = (seqs, flat, seqs) + (rows,) * 12 + (flat,) * 3
    out_specs = (seqs, seqs, P()) + (rows,) * 12 + (flat,) * 3
    dp, fsdp = mesh.shape["dp"], mesh.shape["fsdp"]

    def shards(*args):
        tokens, w_qkv = args[0], args[3]
        fits = (
            dp == 4
            and fsdp == 8
            and tokens.shape[0] == 1
            and tokens.shape[1] == 1024
            and w_qkv.shape[0] * dp * fsdp == D
        )
        step = functools.partial(direct_shards, fsdp // 2) if fits else plain_shards
        return step(*args)

    return jax.shard_map(
        shards, mesh=mesh, in_specs=in_specs, out_specs=out_specs, check_vma=False
    )
```

```python
import functools

import jax
import jax.numpy as jnp
from jax import lax
from jax.experimental import pallas as pl
from jax.experimental.pallas import tpu as pltpu
from jax.sharding import PartitionSpec as P

D = 768
FF = 3072
HEAD_DIM = 64
STEP = 10
HD = 64
F32 = jnp.float32
BF = jnp.bfloat16
MESH = pl.DeviceIdType.MESH

EPS_NORM = 1e-05
CLIP_NORM = 1.0
BETA_ONE = 0.9
BETA_TWO = 0.95
ADAM_EPSILON = 1e-08
DECAY_RATE = 0.1
VECTOR_RATE = 0.2


def nt(a,b): return lax.dot_general(a,b,(((1,),(1,)),((),())),preferred_element_type=F32)
def nn(a,b): return jnp.dot(a,b,preferred_element_type=F32)
def head_mask(rows):
    lane=lax.broadcasted_iota(jnp.int32,(rows,128),1)
    return (lane<HD)
def half(x,h,scale=1.0):
    m=head_mask(x.shape[0]); m = m if h==0 else jnp.logical_not(m)
    return jnp.where(m,x*jnp.asarray(scale,x.dtype),jnp.zeros_like(x))

def attn_fwd_pair(q_ref,k_ref,v_ref,length,o_ref,oT_ref,lse_ref,QB):
    L=q_ref.shape[0]
    n=L//QB
    vT=v_ref[...].T
    lane=lax.broadcasted_iota(jnp.int32,(L,128),1)
    dead=jnp.where(lax.broadcasted_iota(jnp.int32,(L,128),0)<length,0.0,-1e9).astype(BF)
    keys=[jnp.where(lane==HD-HD*h,dead,k_ref[...]) for h in range(2)]
    ql=lax.broadcasted_iota(jnp.int32,(QB,128),1)
    tri=lax.broadcasted_iota(jnp.int32,(QB,QB),0)<=lax.broadcasted_iota(jnp.int32,(QB,QB),1)
    def scores(i,h):
        qh=jnp.where(ql==HD-HD*h,jnp.ones((),BF),half(q_ref[pl.ds(i*QB,QB),:],h,0.125))
        return nt(keys[h][:(i+1)*QB],qh)
    jobs=[(i,h) for i in range(n) for h in range(2)]
    now=scores(*jobs[0])
    outs=[]
    for x,(i,h) in enumerate(jobs):
        later=scores(*jobs[x+1]) if x+1<len(jobs) else None
        nk=(i+1)*QB
        s=jnp.where(tri,now[nk-QB:],-1e9)
        if i: s=jnp.concatenate([now[:nk-QB],s],0)
        m=jnp.max(s,0,keepdims=True)
        e=jnp.exp(s-m)
        l=jnp.sum(e,0,keepdims=True)
        outs.append(nn(vT[HD*h:HD*h+HD,:nk],e.astype(BF))/l)
        lse_ref[pl.ds(h,1),pl.ds(i*QB,QB)]=m+jnp.log(l)
        if h==1:
            oT=jnp.concatenate(outs,0); outs=[]
            oT_ref[:,pl.ds(i*QB,QB)]=oT
            o_ref[pl.ds(i*QB,QB),:]=oT.T.astype(BF)
        now=later

def attn_bwd_pair(q_ref,k_ref,v_ref,do_ref,oT_ref,lse_ref,length,dq_ref,dk_ref,dv_ref,dk_acc,dv_acc,QB,tick=None):
    L=q_ref.shape[0]
    n=L//QB
    kT=k_ref[...].T
    jobs=list(reversed(range(n)))
    tri=lax.broadcasted_iota(jnp.int32,(QB,2*QB),0)<=lax.rem(lax.broadcasted_iota(jnp.int32,(QB,2*QB),1),QB)
    def products(i):
        nk=(i+1)*QB; sl=pl.ds(i*QB,QB)
        q=q_ref[sl,:]; do=do_ref[sl,:]
        qm=jnp.concatenate([half(q,0,0.125),half(q,1,0.125)],0)
        dom=jnp.concatenate([half(do,0),half(do,1)],0)
        return nt(k_ref[pl.ds(0,nk),:],qm),nt(v_ref[pl.ds(0,nk),:],dom),qm,dom
    now=products(jobs[0])
    for x,i in enumerate(jobs):
        split=tick is not None and x==1
        later=products(jobs[x+1]) if x+1<n and not (tick is not None and x==0) else None
        if split:
            tick(1)
            now=products(i)
        nk=(i+1)*QB; sl=pl.ds(i*QB,QB)
        s,dp,qm,dom=now
        prod=do_ref[sl,:].astype(F32).T*oT_ref[:,sl]
        delta=jnp.concatenate([jnp.sum(prod[:HD],0,keepdims=True),jnp.sum(prod[HD:],0,keepdims=True)],1)
        live=(i*QB+lax.broadcasted_iota(jnp.int32,(1,QB),1))<length
        lse=jnp.concatenate([jnp.where(live,lse_ref[pl.ds(h,1),sl],1e30) for h in range(2)],1)
        p=jnp.exp(s-lse)
        pd=jnp.where(tri,p[nk-QB:],0.0)
        p=pd if i==0 else jnp.concatenate([p[:nk-QB],pd],0)
        ds=(p*(dp-delta)).astype(BF)
        dv=nn(p.astype(BF),dom); dk=nn(ds,qm)
        dq=[nn(kT[HD*h:HD*h+HD,:nk],ds[:,QB*h:QB*h+QB]) for h in range(2)]
        dq_ref[sl,:]=(jnp.concatenate(dq,0)*0.125).T.astype(BF)
        if i==n-1:
            dk_acc[...]=dk; dv_acc[...]=dv
        else:
            dk_acc[pl.ds(0,nk),:]+=dk; dv_acc[pl.ds(0,nk),:]+=dv
        now=later
    dk_ref[...]=dk_acc[...].astype(BF); dv_ref[...]=dv_acc[...].astype(BF)

def fwd_call(qkv,length,QB=256):
    L=qkv.shape[0]; D=qkv.shape[1]//3; NP=D//128
    def k(len_ref,q,k_,v,o,oT,lse):
        attn_fwd_pair(q,k_,v,len_ref[0],o,oT,lse.at[0],QB)
    return pl.pallas_call(k,grid=(NP,),
      in_specs=[pl.BlockSpec(memory_space=pltpu.SMEM)]+[pl.BlockSpec((L,128),functools.partial(lambda off,p:(0,off+p),j*NP)) for j in range(3)],
      out_specs=[pl.BlockSpec((L,128),lambda p:(0,p)),pl.BlockSpec((128,L),lambda p:(p,0)),pl.BlockSpec((1,2,L),lambda p:(p,0,0))],
      out_shape=[jax.ShapeDtypeStruct((L,D),BF),jax.ShapeDtypeStruct((D,L),F32),jax.ShapeDtypeStruct((NP,2,L),F32)],
      compiler_params=pltpu.CompilerParams(vmem_limit_bytes=56*2**20),
      cost_estimate=pl.CostEstimate(flops=4*L*L*D//2,bytes_accessed=10*2**20,transcendentals=12*L*L//2))(length,qkv,qkv,qkv)
def bwd_call(qkv,do,oT,lse,length,QB=256):
    L=qkv.shape[0]; D=qkv.shape[1]//3; NP=D//128
    def k(len_ref,q,k_,v,do,oT,lse,dq,dk,dv,dka,dva):
        attn_bwd_pair(q,k_,v,do,oT,lse.at[0],len_ref[0],dq,dk,dv,dka,dva,QB)
    blk=pl.BlockSpec((L,128),lambda p:(0,p))
    return pl.pallas_call(k,grid=(NP,),
      in_specs=[pl.BlockSpec(memory_space=pltpu.SMEM)]+[pl.BlockSpec((L,128),functools.partial(lambda off,p:(0,off+p),j*NP)) for j in range(3)]+[blk,pl.BlockSpec((128,L),lambda p:(p,0)),pl.BlockSpec((1,2,L),lambda p:(p,0,0))],
      out_specs=[blk]*3,
      out_shape=[jax.ShapeDtypeStruct((L,D),BF)]*3,
      scratch_shapes=[pltpu.VMEM((L,128),F32)]*2,
      compiler_params=pltpu.CompilerParams(vmem_limit_bytes=56*2**20),
      cost_estimate=pl.CostEstimate(flops=10*L*L*D//2,bytes_accessed=14*2**20,transcendentals=12*L*L//2))(length,qkv,qkv,qkv,do,oT,lse)


class Place:
    def __init__(self, Z):
        dp=lax.axis_index("dp"); fs=lax.axis_index("fsdp")
        self.Z=Z; self.y=dp//2; self.c=dp%2; self.z=fs//2; self.x=fs%2
        self.nx=(dp,self.z*2+1-self.x)
        self.ny=((1-self.y)*2+self.c,fs)
        self.nc=(self.y*2+1-self.c,fs)
        self.me=self.piece(self.z)
        self.dp=dp; self.fs=fs
    def nz(self,z): return (self.dp,z*2+self.x)
    def piece(self,z,dx=0,dy=0,dc=0):
        y=self.y if dy==0 else 1-self.y
        x=self.x if dx==0 else 1-self.x
        c=self.c if dc==0 else 1-self.c
        return (y*2+c,z,x)
    def slab(self,y,dc=0):
        c=self.c if dc==0 else 1-self.c
        return y*2+c

def rcopy(src,dst,ss,rs,dev):
    return pltpu.make_async_remote_copy(src_ref=src,dst_ref=dst,send_sem=ss,recv_sem=rs,device_id=dev,device_id_type=MESH)

def when(cond,fn):
    if cond is True: fn()
    else: pl.when(cond)(fn)

def gather_sems(NG,Z):
    D=pltpu.SemaphoreType.DMA
    return [D((NG*2*(Z-1),)),D((NG*2*(Z-1),)),
            D((NG*2*Z,)),D((NG*2*Z,)),
            D((NG*2*Z,)),D((NG*2*Z,)),
            D((NG*2,)),D((NG*2,))]

class Gather:
    def __init__(self,P,G,groups,sems):
        self.P=P; self.G=G; self.groups=groups; self.zs,self.zr,self.xs,self.xr,self.ys,self.yr,self.cs,self.cr=sems
    def _cp(self,idx,lo,n,ss,rs,dev):
        r=self.G.at[(*idx,slice(None),pl.ds(lo,n))]
        return rcopy(r,r,ss,rs,dev)
    def zcp(self,g,d,t,zo,to):
        lo,n,_=self.groups[g]; i=(g*2+d)*(self.P.Z-1)+t
        return self._cp(self.P.piece(zo),lo,n,self.zs.at[i],self.zr.at[i],self.P.nz(to))
    def xfull(self,g,zo,arrive=0):
        lo,n,_=self.groups[g]; i=g*2*self.P.Z+zo
        return self._cp(self.P.piece(zo,dx=arrive),lo,n,self.xs.at[i],self.xr.at[i],self.P.nx)
    def yfull(self,g,zo,arrive=0):
        lo,n,_=self.groups[g]; i=g*2*self.P.Z+zo
        return self._cp(self.P.piece(zo,dy=arrive),lo,n,self.ys.at[i],self.yr.at[i],self.P.ny)
    def ydiag(self,g,zo,arrive=0):
        lo,n,a=self.groups[g]; i=g*2*self.P.Z+self.P.Z+zo
        return self._cp(self.P.piece(zo,dx=1,dy=arrive),lo,a,self.ys.at[i],self.yr.at[i],self.P.ny)
    def xdiag(self,g,zo,arrive=0):
        lo,n,a=self.groups[g]; i=g*2*self.P.Z+self.P.Z+zo
        return self._cp(self.P.piece(zo,dy=1,dx=arrive),lo+a,n-a,self.xs.at[i],self.xr.at[i],self.P.nx)
    def ccp(self,g,k,arrive=0):
        lo,n,_=self.groups[g]
        y=self.P.y if k==0 else 1-self.P.y
        r=self.G.at[self.P.slab(y,dc=arrive),:,:,:,pl.ds(lo,n)]
        return rcopy(r,r,self.cs.at[g*2+k],self.cr.at[g*2+k],self.P.nc)
    def own(self,g):
        z=self.P.z; Z=self.P.Z
        when(z<Z-1,lambda: self.zcp(g,0,0,z,z+1).start())
        when(z>0,lambda: self.zcp(g,1,0,z,z-1).start())
        self.xfull(g,z).start(); self.yfull(g,z).start()
    def zarrive(self,g,t):
        z=self.P.z; Z=self.P.Z
        def below():
            zo=z-1-t
            self.zcp(g,0,t,zo,z).wait_recv()
            if t+1<Z-1:
                when(z<Z-1,lambda: self.zcp(g,0,t+1,zo,z+1).start())
            self.xfull(g,zo).start(); self.yfull(g,zo).start()
        def above():
            zo=z+1+t
            self.zcp(g,1,t,zo,z).wait_recv()
            if t+1<Z-1:
                when(z>0,lambda: self.zcp(g,1,t+1,zo,z-1).start())
            self.xfull(g,zo).start(); self.yfull(g,zo).start()
        when(z>t,below); when(z<Z-1-t,above)
    def _diag(self,g,zo):
        self.xfull(g,zo,1).wait_recv(); self.ydiag(g,zo).start()
        self.yfull(g,zo,1).wait_recv(); self.xdiag(g,zo).start()
    def diag(self,g,t):
        z=self.P.z; Z=self.P.Z
        if t==0: self._diag(g,z)
        else:
            when(z>=t,lambda: self._diag(g,z-t))
            when(z<Z-t,lambda: self._diag(g,z+t))
    def corner(self,g):
        self.ccp(g,0).start()
        for zo in range(self.P.Z):
            self.ydiag(g,zo,1).wait_recv(); self.xdiag(g,zo,1).wait_recv()
        self.ccp(g,1).start()
    def sibling(self,g):
        self.ccp(g,0,1).wait_recv(); self.ccp(g,1,1).wait_recv()
    def drain(self,g):
        z=self.P.z; Z=self.P.Z
        for zo in range(Z):
            self.xfull(g,zo).wait_send(); self.yfull(g,zo).wait_send()
            self.xdiag(g,zo).wait_send(); self.ydiag(g,zo).wait_send()
        for k in range(2): self.ccp(g,k).wait_send()
        for t in range(Z-1):
            when(jnp.logical_and(z<Z-1,z>=t),lambda: self.zcp(g,0,t,z-t,z+1).wait_send())
            when(jnp.logical_and(z>0,z<=Z-1-t),lambda: self.zcp(g,1,t,z+t,z-1).wait_send())
    def events(self,g):
        Z=self.P.Z
        ev=[lambda: self.own(g)]
        for t in range(Z-1):
            ev.append(lambda t=t: self.zarrive(g,t))
            ev.append(lambda t=t: self.diag(g,t))
        ev.append(lambda: self.diag(g,Z-1))
        ev.append(lambda: self.corner(g))
        ev.append(lambda: self.sibling(g))
        return ev


SLOT = 1152
NB=12
def rs_sems(NG,Z):
    D=pltpu.SemaphoreType.DMA
    return [D((NG*2,)),D((NG*2,)),
            D((NG*3,)),D((NG*3,)),
            D((NG*2,)),D((NG*2,)),
            D((NG*Z,)),D((NG*Z,))]
def rs_bufs(Z):
    V=lambda *s: pltpu.VMEM(s,BF)
    h=640
    v=128
    return [V(2,2,Z,2,16,SLOT),V(2,Z,2,16,h),V(2,Z,16,h),V(2,2,Z,16,h),V(2,Z,16,h),V(4,Z,16,SLOT),
            V(1,2,Z,2,16,v),V(1,Z,2,16,v),V(1,Z,16,v),V(1,2,Z,16,v),V(1,Z,16,v),V(1,Z,16,v)]
class Scatter:
    def __init__(self,P,R,groups,bufs,sems):
        self.P=P; self.R=R; self.groups=groups; self.bufs=bufs
        self.cs,self.cr,self.xs,self.xr,self.ys,self.yr,self.zs,self.zr=sems
    def buf(self,g,i,w):
        b=self.bufs[i+(NB//2 if g==len(self.groups)-1 else 0)]
        b=b.at[g%b.shape[0]]
        nd=len(b.shape)
        return b.at[(slice(None),)*(nd-1)+(pl.ds(0,w),)]
    def row(self,dy=0,dc=0):
        y=self.P.y if dy==0 else 1-self.P.y
        c=self.P.c if dc==0 else 1-self.P.c
        return y*2+c
    def add(self,dst,src):
        def body(z,_):
            d=dst(z); s=src(z)
            d[...]=d[...]+s[...]
            return 0
        lax.fori_loop(0,self.P.Z,body,0)
    def ccp(self,g,k):
        lo,n,_=self.groups[g]
        return rcopy(self.R.at[self.row(k,1),:,:,:,pl.ds(lo,n)],self.buf(g,0,n).at[k],self.cs.at[g*2+k],self.cr.at[g*2+k],self.P.nc)
    def x1(self,g,k):
        lo,n,a=self.groups[g]
        return rcopy(self.R.at[self.row(k),:,1-self.P.x,:,pl.ds(lo+a,n-a)],self.buf(g,3,n-a).at[k],self.xs.at[g*3+k],self.xr.at[g*3+k],self.P.nx)
    def y1(self,g):
        lo,n,a=self.groups[g]
        return rcopy(self.R.at[self.row(1),:,:,:,pl.ds(lo,a)],self.buf(g,1,a),self.ys.at[g*2],self.yr.at[g*2],self.P.ny)
    def x2(self,g):
        lo,n,a=self.groups[g]
        return rcopy(self.R.at[self.row(0),:,1-self.P.x,:,pl.ds(lo,a)],self.buf(g,2,a),self.xs.at[g*3+2],self.xr.at[g*3+2],self.P.nx)
    def y2(self,g):
        lo,n,a=self.groups[g]
        return rcopy(self.R.at[self.row(1),:,self.P.x,:,pl.ds(lo+a,n-a)],self.buf(g,4,n-a),self.ys.at[g*2+1],self.yr.at[g*2+1],self.P.ny)
    def zc(self,g,src,to):
        lo,n,_=self.groups[g]; Z=self.P.Z
        return rcopy(self.R.at[self.row(0),to,self.P.x,:,pl.ds(lo,n)],self.buf(g,5,n).at[src],self.zs.at[g*Z+to],self.zr.at[g*Z+src],self.P.nz(to))
    def both(self,g): return self.groups[g][1]>self.groups[g][2]
    def s_c(self,g):
        self.ccp(g,1).start(); self.ccp(g,0).start()
    def a_c(self,g):
        lo,n,a=self.groups[g]; R=self.R; b=self.buf(g,0,n)
        for k in (1,0):
            self.ccp(g,k).wait_recv()
            r=self.row(k)
            self.add(lambda z: R.at[r,z,:,:,pl.ds(lo,n)],lambda z: b.at[k,z])
            if self.both(g): self.x1(g,k).start()
            if k==1: self.y1(g).start()
    def a_1(self,g):
        lo,n,a=self.groups[g]; R=self.R; P=self.P; B1=self.buf(g,1,a)
        self.y1(g).wait_recv()
        r=self.row(0)
        self.add(lambda z: R.at[r,z,:,:,pl.ds(lo,a)],lambda z: B1.at[z])
        if self.both(g):
            B3=self.buf(g,3,n-a)
            for k in (1,0):
                self.x1(g,k).wait_recv()
                q=self.row(k)
                self.add(lambda z: R.at[q,z,P.x,:,pl.ds(lo+a,n-a)],lambda z: B3.at[k,z])
            self.y2(g).start()
        self.x2(g).start()
    def a_2(self,g):
        lo,n,a=self.groups[g]; R=self.R; P=self.P; Z=P.Z; B2=self.buf(g,2,a)
        r=self.row(0)
        self.x2(g).wait_recv()
        self.add(lambda z: R.at[r,z,P.x,:,pl.ds(lo,a)],lambda z: B2.at[z])
        if self.both(g):
            B4=self.buf(g,4,n-a)
            self.y2(g).wait_recv()
            self.add(lambda z: R.at[r,z,P.x,:,pl.ds(lo+a,n-a)],lambda z: B4.at[z])
        for d in range(Z-1,0,-1):
            when(P.z>=d,lambda: self.zc(g,P.z,P.z-d).start())
            when(P.z<Z-d,lambda: self.zc(g,P.z,P.z+d).start())
    def final(self,g,out):
        lo,n,_=self.groups[g]; P=self.P; Z=P.Z; z=P.z
        out[...]=self.R[self.row(0),z,P.x,:,pl.ds(lo,n)].astype(F32)
        for zo in range(Z):
            def take():
                self.zc(g,zo,z).wait_recv()
                out[...]+=self.buf(g,5,n)[zo].astype(F32)
            when(z!=zo,take)
    def drain(self,g):
        Z=self.P.Z; z=self.P.z
        for k in range(2):
            self.ccp(g,k).wait_send()
            if self.both(g): self.x1(g,k).wait_send()
        self.x2(g).wait_send(); self.y1(g).wait_send()
        if self.both(g): self.y2(g).wait_send()
        for zo in range(Z):
            when(z!=zo,lambda: self.zc(g,z,zo).wait_send())
    def events(self,g,out):
        return [lambda: self.s_c(g),lambda: self.a_c(g),lambda: self.a_1(g),lambda: self.a_2(g),lambda: self.final(g,out)]

def norm_sems(Z):
    D=pltpu.SemaphoreType.DMA
    return [D((8+Z,)),D((8+Z,))]
def norm_bufs(Z): return [pltpu.VMEM((8+Z,8,128),F32),pltpu.VMEM((2,8,128),F32)]
def cube(P):
    out=[]
    for d in range(1,8):
        dy,dc,dx=d//4,d//2%2,d%2
        y=1-P.y if dy else P.y
        c=1-P.c if dc else P.c
        x=1-P.x if dx else P.x
        out.append((y*4+c*2+x,(y*2+c,P.z*2+x)))
    return out
def all_sum(P,buf,got,ss,rs):
    Z=P.Z
    me=P.y*4+P.c*2+P.x
    buf[me]=got[0]
    def term(i,dev): return rcopy(got.at[0],buf.at[me],ss.at[i],rs.at[me],dev)
    def come(i): return rcopy(got.at[0],buf.at[i],ss.at[i],rs.at[i],P.nc)
    for i,dev in cube(P): term(i,dev).start()
    for i,dev in cube(P): come(i).wait_recv()
    tot=buf[0]
    for i in range(1,8): tot=tot+buf[i]
    got[1]=tot
    buf[8+P.z]=tot
    def line(src,to): return rcopy(got.at[1],buf.at[8+src],ss.at[8+to],rs.at[8+src],P.nz(to))
    for t in range(Z): when(P.z!=t,lambda: line(P.z,t).start())
    for t in range(Z): when(P.z!=t,lambda: line(t,P.z).wait_recv())
    tot=buf[8]
    for t in range(1,Z): tot=tot+buf[8+t]
    for i,dev in cube(P): term(i,dev).wait_send()
    for t in range(Z): when(P.z!=t,lambda: line(P.z,t).wait_send())
    return tot
def enter_all(P,Z):
    bar=pltpu.get_barrier_semaphore()
    def sig(d): pl.semaphore_signal(bar,inc=1,device_id=d,device_id_type=MESH)
    for _,d in cube(P): sig(d)
    for t in range(Z):
        when(P.z!=t,lambda: sig(P.nz(t)))
    pl.semaphore_wait(bar,7+Z-1)


W3 = 768
CW = 1152
QKV_AT = 0
VEC_AT = 3456
VEC_COLS = 128
OUT_AT = 3584
DOWN_AT = 4736
UP_AT = 9344
COLS = 13952
GATHER = [(2304, 1280, 640), (0, 2304, 1152), (3584, 5760, 2944), (9344, 1152, 640), (10496, 1152, 512), (11648, 2304, 1152)]
SCATTER = ([(UP_AT + CW * c, CW, 640 if c % 2 else 512) for c in range(4)]
           + [(DOWN_AT + CW * c, CW, 640 if c % 2 else 512) for c in range(4)]
           + [(OUT_AT, CW, 512), (0, CW, 640), (CW, CW, 512), (2 * CW, CW, 640), (VEC_AT, VEC_COLS, VEC_COLS)])

def al(v, m): return pl.multiple_of(v, m)

def third_cols(s): return [(D * j + 256 * s, 256) for j in range(3)]

def pack_rows(G, me, at, main, rest):
    G[(*me,slice(None),pl.ds(at,W3))]=main.astype(BF)
    parts=[jnp.concatenate([rest[:,256*s:256*s+128],rest[:,256*s+128:256*s+256]],0) for s in range(3)]
    G[(*me,slice(None),pl.ds(al(at+W3,128),W3//2))]=jnp.concatenate(parts,1).astype(BF)

def pack_own(place, G, wqkv, wout, wup, wdown, vec):
    me=place.me
    lo=al(8*place.x,8); ro=al(16*(1-place.x),8)
    def cols(w,cs):
        return [jnp.concatenate([w[pl.ds(a,n),pl.ds(c,k)] for c,k in cs],1) for a,n in ((lo,16),(ro,8))]
    for s in range(3): pack_rows(G,me,QKV_AT+CW*s,*cols(wqkv,third_cols(s)))
    pack_rows(G,me,OUT_AT,*cols(wout,[(0,W3)]))
    for c in range(4): pack_rows(G,me,UP_AT+CW*c,*cols(wup,[(W3*c,W3)]))
    for r in range(6):
        G[(*me,slice(None),pl.ds(DOWN_AT+r*D,D))]=wdown[pl.ds(16*r,16),:].astype(BF)
    G[(*me,slice(None),pl.ds(VEC_AT,VEC_COLS))]=vec[...]

def unpack24(G, at, dst):
    Z=G.shape[1]
    def body(j,_):
        r=al(j*48,16); d=j//Z; z=lax.rem(j,Z)
        dst[pl.ds(r,16),:]=G[d,z,0,:,pl.ds(al(at,128),W3)]
        dst[pl.ds(r+32,16),:]=G[d,z,1,:,pl.ds(al(at,128),W3)]
        a=G[d,z,0,:,pl.ds(al(at+W3,128),W3//2)].astype(F32)
        b=G[d,z,1,:,pl.ds(al(at+W3,128),W3//2)].astype(F32)
        parts=[]
        for s in range(3):
            q=slice(128*s,128*s+128)
            parts+=[jnp.concatenate([a[:8,q],b[:8,q]],0),jnp.concatenate([a[8:,q],b[8:,q]],0)]
        dst[pl.ds(r+16,16),:]=jnp.concatenate(parts,1).astype(BF)
        return 0
    lax.fori_loop(0,G.shape[0]*Z,body,0)

def pack24(G, at, src):
    Z=G.shape[1]
    def body(j,_):
        r=al(j*48,16); d=j//Z; z=lax.rem(j,Z)
        pack_rows(G,(d,z,0),al(at,128),src[pl.ds(r,16),:],src[pl.ds(al(r+16,8),8),:])
        pack_rows(G,(d,z,1),al(at,128),src[pl.ds(r+32,16),:],src[pl.ds(al(r+24,8),8),:])
        return 0
    lax.fori_loop(0,G.shape[0]*Z,body,0)

def unpack_down(G, c, dst):
    def body(k,_):
        for r in range(6):
            dst[pl.ds(al(k*96+16*r,16),16),:]=G[c,k//2,lax.rem(k,2),:,pl.ds(DOWN_AT+r*D,D)]
        return 0
    lax.fori_loop(0,2*G.shape[1],body,0)

def pack_down(G, c, src):
    def body(k,_):
        for r in range(6):
            G[c,k//2,lax.rem(k,2),:,pl.ds(DOWN_AT+r*D,D)]=src[pl.ds(al(k*96+16*r,16),16),:].astype(BF)
        return 0
    lax.fori_loop(0,2*G.shape[1],body,0)

def vec_shift(k): return (240*k)//128

def unpack_vec(G, V, V1):
    V[...]=jnp.zeros_like(V)
    Z=G.shape[1]
    for k in range(8*Z):
        V[pl.ds(vec_shift(k),3),:]+=G[k//(2*Z),k//2%Z,k%2,:,pl.ds(VEC_AT,VEC_COLS)].astype(F32)[0:3]
    for t in range(60):
        V1[:,pl.ds(128*t,128)]=V[pl.ds(t,1),:]

def pack_vec(G, V, V1):
    V[...]=jnp.zeros_like(V)
    for t in range(60):
        V[pl.ds(t,1),:]=V1[:,pl.ds(128*t,128)]
    Z=G.shape[1]
    for k in range(8*Z):
        G[k//(2*Z),k//2%Z,k%2,:,pl.ds(VEC_AT,VEC_COLS)]=V[pl.ds(vec_shift(k),16),:].astype(BF)

def norm_parts(x):
    c=x-jnp.mean(x,-1,keepdims=True)
    s=lax.rsqrt(jnp.mean(c*c,-1,keepdims=True)+EPS_NORM)
    return c*s,s

def norm_back(dx, xh, s):
    return s*(dx-jnp.mean(dx,-1,keepdims=True)-xh*jnp.mean(dx*xh,-1,keepdims=True))

def gelu_both(u):
    k0=0.7978845608028654; k1=0.044715
    u2=u*u
    t=jnp.tanh(k0*(u*(1.0+k1*u2)))
    h=0.5*(1.0+t)
    return u*h, h+(0.5*k0)*u*(1.0-t*t)*(1.0+(3.0*k1)*u2)

RB=256

RULES=((1,1,0),(2,3,1),(2,4,3))

def places():
    p=[("stat",i,0.6) for i in range(4)]
    for i in range(3):
        p.append(("third",i,0.6 if i else 2.0))
        p+=[("qkv",4*i+k,0.42) for k in range(4)]
        p+=[("af",2*i+pp,2.3) for pp in range(2)]
    p.append(("out",0,0.6))
    p+=[("ob",k,1.1) for k in range(4)]
    for c in range(4):
        p.append(("chunk",c,0.5))
        p+=[("mr",4*c+k,1.75) for k in range(4)]
        p+=[("mw",3*c+k,0.6+0.15*(k==2)) for k in range(3)]
        p+=[("mu",3*c+k,0.6+0.2*(k==2)) for k in range(3)]
        p.append(("mp",c,0.1))
    p.append(("fin",0,1.0))
    p+=[("bb",k,1.3) for k in range(4)]
    p+=[("bw",k,0.6+0.2*(k==2)) for k in range(3)]
    p.append(("bp",0,0.1))
    p+=[("ag",k,0.5) for k in range(4)]
    for i in range(3):
        for pp in range(2): p+=[("ab",4*i+2*pp+k,(1.6,2.1)[k]) for k in range(2)]
        p+=[("dq",3*i+k,0.6+0.2*(k==2)) for k in range(3)]
        p.append(("dp",i,0.1))
        p+=[("dh",4*i+k,0.5) for k in range(4)]
    p+=[("ln",k,0.9) for k in range(4)]
    p.append(("lp",0,0.3))
    return p

def ready_places():
    return [("mp",c) for c in range(4)]+[("mp",3)]*4+[("bp",0)]+[("dp",i) for i in range(3)]+[("lp",0)]

def due_places():
    return [("third",0),("third",1),("out",0),("chunk",0),("chunk",1),("chunk",2)]

class Clock:
    def __init__(self, plan, ga, sc, own):
        names=[p[:2] for p in places()]
        index={p:i for i,p in enumerate(names)}
        fns={}
        for g in range(len(GATHER)):
            for k,f in enumerate(ga.events(g)): fns[(0,g,k)]=f
        for g,(lo,n,_) in enumerate(SCATTER):
            for k,f in enumerate(sc.events(g,own.at[:,pl.ds(lo,n)])): fns[(1,g,k)]=f
        check_plan(plan,set(fns),index)
        self.slots={}
        self.tail=[]
        for i,*key in plan:
            if i<len(names): self.slots.setdefault(names[i],[]).append(fns[tuple(key)])
            else: self.tail.append(fns[tuple(key)])
    def at(self, name, step, count):
        for k in range(count):
            todo=self.slots.get((name,k))
            if todo:
                def run(todo=todo):
                    for f in todo: f()
                if isinstance(step,int):
                    if step==k: run()
                else: pl.when(step==k)(run)

PLAN = (
    (0, 0, 0, 0), (1, 0, 0, 1), (1, 0, 0, 2), (3, 0, 0, 3), (3, 0, 1, 0), (3, 0, 0, 4), (3, 0, 0, 5), (4, 0, 1, 1),
    (4, 0, 0, 6), (4, 0, 0, 7), (4, 0, 0, 8), (4, 0, 1, 2), (4, 0, 1, 3), (4, 0, 1, 4), (4, 0, 0, 9), (5, 0, 1, 5),
    (6, 0, 2, 0), (7, 0, 1, 6), (10, 0, 1, 7), (11, 0, 2, 1), (11, 0, 1, 8), (11, 0, 1, 9), (11, 0, 2, 2),
    (17, 0, 2, 3), (18, 0, 2, 4), (18, 0, 2, 5), (22, 0, 3, 0), (23, 0, 3, 1), (24, 0, 2, 6), (25, 0, 3, 2),
    (25, 0, 2, 7), (25, 0, 2, 8), (25, 0, 3, 3), (25, 0, 3, 4), (25, 0, 4, 0), (25, 0, 3, 5), (25, 0, 2, 9),
    (26, 0, 4, 1), (26, 0, 4, 2), (27, 0, 3, 6), (27, 0, 3, 7), (28, 0, 4, 3), (29, 0, 3, 8), (30, 0, 4, 4),
    (30, 0, 4, 5), (30, 0, 3, 9), (31, 0, 5, 0), (33, 0, 4, 6), (34, 0, 5, 1), (34, 0, 4, 7), (37, 0, 5, 2),
    (37, 0, 5, 3), (38, 0, 4, 8), (40, 0, 5, 4), (41, 0, 5, 5), (41, 1, 0, 0), (41, 0, 4, 9), (44, 0, 5, 6),
    (45, 1, 0, 1), (45, 0, 5, 7), (48, 0, 5, 8), (50, 1, 0, 2), (51, 0, 5, 9), (53, 1, 1, 0), (58, 1, 1, 1),
    (62, 1, 0, 3), (65, 1, 2, 0), (65, 1, 1, 2), (69, 1, 2, 1), (73, 1, 2, 2), (73, 1, 1, 3), (73, 1, 0, 4),
    (77, 1, 3, 0), (79, 1, 2, 3), (79, 1, 3, 1), (80, 1, 4, 0), (82, 1, 4, 1), (84, 1, 2, 4), (87, 1, 3, 2),
    (88, 1, 5, 0), (90, 1, 4, 2), (91, 1, 1, 4), (92, 1, 3, 3), (92, 1, 5, 1), (92, 1, 6, 0), (93, 1, 4, 3),
    (93, 1, 6, 1), (95, 1, 5, 2), (97, 1, 3, 4), (98, 1, 7, 0), (100, 1, 6, 2), (102, 1, 5, 3), (103, 1, 7, 1),
    (103, 1, 8, 0), (104, 1, 4, 4), (104, 1, 6, 3), (105, 1, 8, 1), (107, 1, 7, 2), (107, 1, 9, 0), (108, 1, 6, 4),
    (108, 1, 8, 2), (112, 1, 5, 4), (115, 1, 7, 3), (116, 1, 8, 3), (116, 1, 9, 1), (116, 1, 10, 0),
    (117, 1, 10, 1), (118, 1, 9, 2), (119, 1, 8, 4), (120, 1, 10, 2), (121, 1, 7, 4), (122, 1, 11, 0),
    (124, 1, 9, 3), (125, 1, 11, 1), (125, 1, 10, 3), (131, 1, 11, 2), (131, 1, 12, 0), (131, 1, 10, 4),
    (132, 1, 9, 4), (132, 1, 12, 1), (132, 1, 11, 3), (132, 1, 12, 2), (132, 1, 12, 3), (132, 1, 12, 4),
    (132, 1, 11, 4),
)

def check_plan(plan, keys, index):
    pos={tuple(e[1:]):(e[0],j) for j,e in enumerate(plan)}
    assert set(pos)==keys and len(plan)==len(keys)
    assert all(a[0]<=b[0] for a,b in zip(plan,plan[1:]))
    for kind,g,k in keys:
        if k: assert pos[(kind,g,k-1)]<pos[(kind,g,k)]
    for g,p in enumerate(due_places()): assert pos[(0,g,9)][0]<=index[p]
    for g,p in enumerate(ready_places()):
        assert pos[(1,g,0)][0]>=index[p]
        for n,i,j in RULES:
            if g>=n: assert pos[(1,g-n,i)]<pos[(1,g,j)]

def mega_kernel(Z,plan,tok_h,cot_h,len_ref,wqkv_s,wout_s,wup_s,wdown_s,vec_s,
               mixed_o,dtok_o,own_o,nrm_o,
               G,tok,cot,F1,F2,F3,qkv,B1,B2,B3,hT,aT,oT,W0,W1,dW,lse,V,V1,dV1,dka,dva,own,nrm,dsem,*rest):
    gsems=rest[:8]; rbufs=rest[8:8+NB]; rsems=rest[8+NB:16+NB]; nb,got,ns,nr=rest[16+NB:]
    L=tok.shape[0]
    NBK=L//RB
    place=Place(Z)
    def dma(a,b,i):
        cp=pltpu.make_async_copy(a,b,dsem.at[i]); cp.start(); return cp
    ldt=dma(tok_h,tok,0); ldc=dma(cot_h,cot,1)
    pack_own(place,G,wqkv_s,wout_s,wup_s,wdown_s,vec_s)
    enter_all(place,Z)
    ga=Gather(place,G,GATHER,gsems)
    sc=Scatter(place,G,SCATTER,rbufs,rsems)
    clock=Clock(plan,ga,sc,own)
    def at(name,step,count): clock.at(name,step,count)
    def rows(i): return pl.ds(al(i*RB,RB),RB)
    length=len_ref[0]
    ldt.wait()
    xhat=F1; h1=B1; o=B3
    for i in range(4):
        at("stat",i,4)
        if i<NBK:
            xhat[rows(i),:]=norm_parts(tok[rows(i),:].astype(F32))[0]
    def third(i,_):
        s=lax.rem(i+2,3)
        at("third",i,3)
        @pl.when(i==0)
        def _():
            unpack_vec(G,V,V1)
            def first(j,_):
                h1[rows(j),:]=(xhat[rows(j),:]*V1[:,0:D]+V1[:,D:2*D]).astype(BF)
                return 0
            lax.fori_loop(0,NBK,first,0)
        unpack24(G,QKV_AT+CW*s,W0)
        def block(j,_):
            at("qkv",4*i+j,12)
            qkv[s,rows(j),:]=nn(h1[rows(j),:],W0[...]).astype(BF)
            return 0
        lax.fori_loop(0,NBK,block,0)
        def pair(pp,_):
            p=2*s+pp
            def col(j): return qkv.at[s,:,pl.ds(al(256*j+128*pp,128),128)]
            c=pl.ds(al(128*p,128),128)
            at("af",2*i+pp,6)
            attn_fwd_pair(col(0),col(1),col(2),length,o.at[:,c],oT.at[c,:],lse.at[p],512)
            return 0
        lax.fori_loop(0,2,pair,0)
        return 0
    lax.fori_loop(0,3,third,0)
    at("out",0,1)
    unpack24(G,OUT_AT,W0)
    ldc.wait()
    r1=F1; mixed=F2; dh2=F3; h2=B1; h2T=hT
    def out_block(i,_):
        at("ob",i,4)
        sl=rows(i)
        r=tok[sl,:].astype(F32)+nn(o[sl,:],W0[...])+V1[:,4*D:5*D]
        r1[sl,:]=r
        mixed[sl,:]=r+V1[:,5*D:6*D]
        hb=(norm_parts(r)[0]*V1[:,2*D:3*D]+V1[:,3*D:4*D]).astype(BF)
        h2[sl,:]=hb
        h2T[:,sl]=hb.T
        pos_=i*RB+lax.broadcasted_iota(jnp.int32,(RB,D),0)
        cot[sl,:]=jnp.where(pos_<length,cot[sl,:],jnp.zeros((),BF))
        dh2[sl,:]=jnp.zeros((RB,D),F32)
        return 0
    lax.fori_loop(0,NBK,out_block,0)
    du_s=B2
    def chunk(c,_):
        at("chunk",c,4)
        for g,when_ in enumerate((0,0,0,0,1,2)):
            pl.when(c==when_)(lambda g=g: ga.drain(g))
        unpack24(G,UP_AT+CW*c,W0)
        unpack_down(G,c,W1)
        bu=V1[:,pl.ds(al(6*D+c*W3,128),W3)]
        def mrows(i,acc):
            at("mr",4*c+i,16)
            sl=rows(i)
            u=nn(h2[sl,:],W0[...])+bu
            a,slope=gelu_both(u)
            ab=a.astype(BF)
            mixed[sl,:]+=nn(ab,W1[...])
            aT[:,sl]=ab.T
            du=(nt(cot[sl,:],W1[...])*slope).astype(BF)
            du_s[sl,:]=du
            dh2[sl,:]+=nt(du,W0[...])
            return acc+jnp.sum(du.astype(F32),0,keepdims=True)
        s=lax.fori_loop(0,NBK,mrows,jnp.zeros((1,W3),F32))
        dV1[:,pl.ds(al(6*D+c*W3,128),W3)]=s
        def wrows(i,_):
            at("mw",3*c+i,12)
            dW[rows(i),:]=nn(aT[rows(i),:],cot[...])
            return 0
        lax.fori_loop(0,W3//RB,wrows,0)
        pack_down(G,c,dW)
        def urows(i,_):
            at("mu",3*c+i,12)
            dW[rows(i),:]=nn(h2T[rows(i),:],du_s[...])
            return 0
        lax.fori_loop(0,D//RB,urows,0)
        pack24(G,UP_AT+CW*c,dW)
        at("mp",c,4)
        return 0
    lax.fori_loop(0,FF//W3,chunk,0)
    at("fin",0,1)
    mixed_b=B2
    def fin(i,_):
        mixed_b[rows(i),:]=mixed[rows(i),:].astype(BF)
        return 0
    lax.fori_loop(0,NBK,fin,0)
    outs=[dma(mixed_b,mixed_o,2)]
    unpack24(G,OUT_AT,W0)
    dr1=F3; dy=B3; do=B1
    def back(i,acc):
        at("bb",i,4)
        sl=rows(i)
        dh=dh2[sl,:]
        xh,s=norm_parts(r1[sl,:])
        g=cot[sl,:].astype(F32)
        dr=g+norm_back(dh*V1[:,2*D:3*D],xh,s)
        dr1[sl,:]=dr
        dyb=dr.astype(BF)
        dy[sl,:]=dyb
        do[sl,:]=nt(dyb,W0[...]).astype(BF)
        new=(dh*xh,dh,dyb.astype(F32),g)
        return tuple(a+jnp.sum(b,0,keepdims=True) for a,b in zip(acc,new))
    z1=jnp.zeros((1,D),F32)
    sums=lax.fori_loop(0,NBK,back,(z1,z1,z1,z1))
    for j,v in enumerate(sums): dV1[:,pl.ds((2+j)*D,D)]=v
    def orow(i,_):
        at("bw",i,3)
        dW[rows(i),:]=nn(oT[rows(i),:].astype(BF),dy[...])
        return 0
    lax.fori_loop(0,D//RB,orow,0)
    pack24(G,OUT_AT,dW)
    at("bp",0,1)
    h1T=hT; dqkv=B3; dh1=F2
    outs[0].wait()
    def again(i,_):
        at("ag",i,4)
        sl=rows(i)
        hb=(norm_parts(tok[sl,:].astype(F32))[0]*V1[:,0:D]+V1[:,D:2*D]).astype(BF)
        h1T[:,sl]=hb.T
        dh1[sl,:]=jnp.zeros((RB,D),F32)
        return 0
    lax.fori_loop(0,NBK,again,0)
    def third_back(s,_):
        unpack24(G,QKV_AT+CW*s,W0)
        def pair(pp,_):
            p=2*s+pp
            at("ab",4*s+2*pp,12)
            def col(j): return qkv.at[s,:,pl.ds(al(256*j+128*pp,128),128)]
            def dcol(j): return dqkv.at[:,pl.ds(al(256*j+128*pp,128),128)]
            c=pl.ds(al(128*p,128),128)
            attn_bwd_pair(col(0),col(1),col(2),do.at[:,c],oT.at[c,:],lse.at[p],length,
                          dcol(0),dcol(1),dcol(2),dka,dva,256,tick=lambda k: at("ab",4*s+2*pp+k,12))
            return 0
        lax.fori_loop(0,2,pair,0)
        def qrow(i,_):
            at("dq",3*s+i,9)
            dW[rows(i),:]=nn(h1T[rows(i),:],dqkv[...])
            return 0
        lax.fori_loop(0,D//RB,qrow,0)
        pack24(G,QKV_AT+CW*s,dW)
        at("dp",s,3)
        def drow(i,_):
            at("dh",4*s+i,12)
            dh1[rows(i),:]+=nt(dqkv[rows(i),:],W0[...])
            return 0
        lax.fori_loop(0,NBK,drow,0)
        return 0
    lax.fori_loop(0,3,third_back,0)
    def lrow(i,acc):
        at("ln",i,4)
        sl=rows(i)
        dh=dh1[sl,:]
        xh,r=norm_parts(tok[sl,:].astype(F32))
        F1[sl,:]=dr1[sl,:]+norm_back(dh*V1[:,0:D],xh,r)
        return tuple(a+jnp.sum(b,0,keepdims=True) for a,b in zip(acc,(dh*xh,dh)))
    sums=lax.fori_loop(0,NBK,lrow,(z1,z1))
    for j,v in enumerate(sums): dV1[:,pl.ds(j*D,D)]=v
    pack_vec(G,V,dV1)
    at("lp",0,1)
    outs=[dma(F1,dtok_o,3)]
    for f in clock.tail: f()
    flat=lax.broadcasted_iota(jnp.int32,(16,VEC_COLS),0)*VEC_COLS+lax.broadcasted_iota(jnp.int32,(16,VEC_COLS),1)
    start=lax.rem(240*((place.dp*Z+place.z)*2+place.x),128)
    vec=own[:,pl.ds(VEC_AT,VEC_COLS)]
    vec=jnp.where(jnp.logical_and(flat>=start,flat<start+240),vec,0.0)
    left=own[:,pl.ds(0,VEC_AT)]; right=own[:,pl.ds(OUT_AT,COLS-OUT_AT)]
    got[0]=jnp.full((8,128),1.0,F32)*(jnp.sum(left*left)+jnp.sum(right*right)+jnp.sum(vec*vec))
    outs.append(dma(own,own_o,4))
    nrm[8:24,:]=vec
    nrm[0:8,:]=all_sum(place,nb,got,ns,nr)
    outs.append(dma(nrm,nrm_o,5))
    for g in range(len(SCATTER)): sc.drain(g)
    for cp in outs: cp.wait()

def mega_call(Z,tok,cot,length,wqkv,wout,wup,wdown,vec,plan=None):
    plan=PLAN if plan is None else plan
    L=tok.shape[0]; pieces=8*Z
    S=jax.ShapeDtypeStruct; V=pltpu.VMEM
    vm=pl.BlockSpec(memory_space=pltpu.VMEM); an=pl.BlockSpec(memory_space=pltpu.HBM); sm=pl.BlockSpec(memory_space=pltpu.SMEM)
    outs=[S((L,D),BF),S((L,D),F32),S((16,COLS),F32),S((24,128),F32)]
    f=lambda: V((L,D),F32)
    b=lambda: V((L,D),BF)
    scratch=[V((4,Z,2,16,COLS),BF),b(),b(),f(),f(),f(),V((3,L,D),BF),b(),b(),b(),V((D,L),BF),V((D,L),BF),V((D,L),F32),
             V((D,W3),BF),V((W3,D),BF),V((D,W3),F32),V((6,2,L),F32),V((80,128),F32),V((1,10*D),F32),V((1,10*D),F32),
             V((L,128),F32),V((L,128),F32),V((16,COLS),F32),V((24,128),F32),pltpu.SemaphoreType.DMA((6,))]
    return pl.pallas_call(functools.partial(mega_kernel,Z,plan),out_shape=outs,
        in_specs=[an,an,sm]+[vm]*5,out_specs=[an]*len(outs),
        scratch_shapes=scratch+gather_sems(len(GATHER),Z)+rs_bufs(Z)+rs_sems(len(SCATTER),Z)+norm_bufs(Z)+norm_sems(Z),
        compiler_params=pltpu.CompilerParams(collective_id=1,has_side_effects=True,vmem_limit_bytes=63*2**20),
        cost_estimate=pl.CostEstimate(flops=60*10**9,bytes_accessed=60*2**20,transcendentals=10**7))(tok,cot,length,wqkv,wout,wup,wdown,vec)


def adam_step(weight, first_mom, second_mom, gradient, step_rate):
    first_new = BETA_ONE * first_mom + (1.0 - BETA_ONE) * gradient
    second_new = BETA_TWO * second_mom + (1.0 - BETA_TWO) * gradient * gradient
    fix_one = 1.0 - BETA_ONE**STEP
    fix_two = 1.0 - BETA_TWO**STEP
    update = (
        first_new / fix_one / (jnp.sqrt(second_new / fix_two) + ADAM_EPSILON) + DECAY_RATE * weight
    )
    return (weight - step_rate * update, first_new, second_new)


def adam_kernel(par_ref, own_h, nrm_h, mixed_h, dtok_h, *refs):
    ins_h, outs_h = refs[:12], refs[12:24]
    own, nrm, *rest = refs[26:]
    ins, outs, mixed, dtok, sem = rest[:12], rest[12:24], rest[24], rest[25], rest[26]
    pairs = list(zip((own_h, nrm_h) + tuple(ins_h), (own, nrm) + tuple(ins)))
    loads = [pltpu.make_async_copy(a, b, sem.at[i]) for i, (a, b) in enumerate(pairs)]
    moves = [
        pltpu.make_async_copy(mixed_h, mixed, sem.at[14]),
        pltpu.make_async_copy(dtok_h, dtok, sem.at[15]),
    ]
    for cp in loads + moves:
        cp.start()
    for cp in loads:
        cp.wait()
    for cp in moves:
        cp.wait()
    moves = [
        pltpu.make_async_copy(mixed, refs[24], sem.at[14]),
        pltpu.make_async_copy(dtok, refs[25], sem.at[15]),
    ]
    for cp in moves:
        cp.start()
    factor = jnp.minimum(1.0, CLIP_NORM / (jnp.sqrt(nrm[0:1, 0:1]) + 1e-06))
    main_at = al(8 * par_ref[0], 8)
    rest_at = al(16 * (1 - par_ref[0]), 8)

    def step(i, rows, cols, grad, rate):
        w, m, v = [r[rows, cols] for r in ins[3 * i : 3 * i + 3]]
        new = adam_step(w, m, v, grad * factor, rate)
        for r, a in zip(outs[3 * i : 3 * i + 3], new):
            r[rows, cols] = a

    def chunk(i, at, cols, rate):
        main = own[:, pl.ds(at, W3)]
        packed = own[:, pl.ds(at + W3, W3 // 2)]
        parts = []
        for s in range(3):
            parts += [packed[:8, 128 * s : 128 * s + 128], packed[8:, 128 * s : 128 * s + 128]]
        rest = jnp.concatenate(parts, 1)
        done = 0
        for c, n in cols:
            step(i, pl.ds(main_at, 16), pl.ds(c, n), main[:, done : done + n], rate)
            step(i, pl.ds(rest_at, 8), pl.ds(c, n), rest[:, done : done + n], rate)
            done += n

    for s in range(3):
        chunk(0, QKV_AT + CW * s, third_cols(s), D ** (-0.5))
    chunk(1, OUT_AT, [(0, W3)], D ** (-0.5))
    for c in range(4):
        chunk(2, UP_AT + CW * c, [(W3 * c, W3)], D ** (-0.5))
    for r in range(6):
        grad = own[:, pl.ds(DOWN_AT + r * D, D)]
        step(3, pl.ds(16 * r, 16), slice(None), grad, FF ** (-0.5))
    stores = [pltpu.make_async_copy(a, b, sem.at[i]) for i, (a, b) in enumerate(zip(outs, outs_h))]
    for cp in stores:
        cp.start()
    for cp in stores + moves:
        cp.wait()


def adam_call(parity, own, nrm, mixed, d_tokens, states):
    hb = pl.BlockSpec(memory_space=pltpu.HBM)
    sm = pl.BlockSpec(memory_space=pltpu.SMEM)
    held = [pltpu.VMEM(a.shape, F32) for a in (own, nrm) + tuple(states) + tuple(states)]
    return pl.pallas_call(
        adam_kernel,
        out_shape=[jax.ShapeDtypeStruct(a.shape, a.dtype) for a in states + (mixed, d_tokens)],
        in_specs=[sm] + [hb] * 16,
        out_specs=[hb] * 14,
        scratch_shapes=held
        + [pltpu.VMEM(mixed.shape, BF), pltpu.VMEM(d_tokens.shape, F32)]
        + [pltpu.SemaphoreType.DMA((16,))],
        compiler_params=pltpu.CompilerParams(vmem_limit_bytes=63 * 2**20),
        cost_estimate=pl.CostEstimate(
            flops=10**7, bytes_accessed=8 * 2**20, transcendentals=10**6
        ),
    )(parity, own, nrm, mixed, d_tokens, *states)


def layer_norm(values, gain, shift):
    center = jnp.mean(values, -1, keepdims=True)
    centered = values - center
    spread = jnp.mean(centered * centered, -1, keepdims=True)
    return centered * lax.rsqrt(spread + EPS_NORM) * gain + shift


def smooth_gate(value):
    return jax.nn.gelu(value, approximate=True)


def plain_shards(tokens, lengths, cotangent, *state):
    w_qkv, m_qkv, v_qkv, w_out, m_out, v_out, w_up, m_up, v_up = state[:9]
    w_down, m_down, v_down, packed, m_packed, v_packed = state[9:]
    seq_count, seq_len, model_width = tokens.shape
    row_count = seq_count * seq_len
    axes = ("dp", "fsdp")
    wqkv_b, wout_b, wup_b, wdown_b, vector_b = [
        lax.all_gather(w.astype(BF), axes, axis=0, tiled=True)
        for w in (w_qkv, w_out, w_up, w_down, packed)
    ]
    vector = vector_b.astype(F32)
    gain_one, bias_one, gain_two, bias_two, bias_attn, bias_down = [
        vector[i * model_width : (i + 1) * model_width] for i in range(6)
    ]
    bias_up = vector[6 * model_width :]
    positions = jnp.arange(seq_len, dtype=jnp.int32)
    live_rows = positions[None, :] < lengths[:, None]
    inputs = tokens.astype(F32).reshape(row_count, model_width)
    normed_one, norm_one_back = jax.vjp(layer_norm, inputs, gain_one, bias_one)
    normed_one_b = normed_one.astype(BF)
    qkv_all = jnp.dot(normed_one_b, wqkv_b, preferred_element_type=F32).astype(BF)
    seqs = [slice(i * seq_len, (i + 1) * seq_len) for i in range(seq_count)]
    ahead = [fwd_call(qkv_all[s], lengths[i : i + 1], 512) for i, s in enumerate(seqs)]
    attended_b = jnp.concatenate([a[0] for a in ahead], 0)
    resid_one = inputs + jnp.dot(attended_b, wout_b, preferred_element_type=F32) + bias_attn
    normed_two, norm_two_back = jax.vjp(layer_norm, resid_one, gain_two, bias_two)
    normed_two_b = normed_two.astype(BF)
    upper = jnp.dot(normed_two_b, wup_b, preferred_element_type=F32) + bias_up
    activ, gate_back = jax.vjp(smooth_gate, upper)
    activ_b = activ.astype(BF)
    mixed = resid_one + jnp.dot(activ_b, wdown_b, preferred_element_type=F32) + bias_down
    mixed = mixed.reshape(seq_count, seq_len, model_width).astype(BF)
    grad_b = jnp.where(live_rows[:, :, None], cotangent, jnp.zeros((), BF))
    grad_b = grad_b.reshape(row_count, model_width)
    grad_full = grad_b.astype(F32)
    d_wdown = jnp.dot(activ_b.T, grad_b, preferred_element_type=F32)
    d_bias_down = jnp.sum(grad_full, 0)
    d_activ = jnp.dot(grad_b, wdown_b.T, preferred_element_type=F32)
    (d_upper,) = gate_back(d_activ)
    d_upper_b = d_upper.astype(BF)
    d_bias_up = jnp.sum(d_upper_b.astype(F32), 0)
    d_wup = jnp.dot(normed_two_b.T, d_upper_b, preferred_element_type=F32)
    d_normed_two = jnp.dot(d_upper_b, wup_b.T, preferred_element_type=F32)
    d_resid_norm, d_gain_two, d_bias_two = norm_two_back(d_normed_two)
    d_resid = grad_full + d_resid_norm
    d_branch_b = d_resid.astype(BF)
    d_bias_attn = jnp.sum(d_branch_b.astype(F32), 0)
    d_wout = jnp.dot(attended_b.T, d_branch_b, preferred_element_type=F32)
    d_attended_b = jnp.dot(d_branch_b, wout_b.T, preferred_element_type=F32).astype(BF)
    back = [
        bwd_call(qkv_all[s], d_attended_b[s], a[1], a[2], lengths[i : i + 1])
        for i, (s, a) in enumerate(zip(seqs, ahead))
    ]
    d_qkv_b = jnp.concatenate([jnp.concatenate(b, 1) for b in back], 0)
    d_wqkv = jnp.dot(normed_one_b.T, d_qkv_b, preferred_element_type=F32)
    d_normed_one = jnp.dot(d_qkv_b, wqkv_b.T, preferred_element_type=F32)
    d_input_norm, d_gain_one, d_bias_one = norm_one_back(d_normed_one)
    d_tokens = (d_resid + d_input_norm).reshape(seq_count, seq_len, model_width)
    d_vector = jnp.concatenate(
        [d_gain_one, d_bias_one, d_gain_two, d_bias_two, d_bias_attn, d_bias_down, d_bias_up]
    )
    owned = [
        lax.psum_scatter(g, axes, scatter_dimension=0, tiled=True)
        for g in (d_wqkv, d_wout, d_wup, d_wdown, d_vector)
    ]
    grad_norm = jnp.sqrt(lax.psum(sum(jnp.sum(g * g) for g in owned), axes))
    factor = jnp.minimum(1.0, CLIP_NORM / (grad_norm + 1e-06))
    rates = (D ** (-0.5), D ** (-0.5), D ** (-0.5), FF ** (-0.5), VECTOR_RATE)
    new = ()
    for i, (g, rate) in enumerate(zip(owned, rates)):
        new += adam_step(*state[3 * i : 3 * i + 3], g * factor, rate)
    return (mixed, d_tokens, grad_norm) + new


def direct_shards(Z, tokens, lengths, cotangent, *state):
    packed, m_packed, v_packed = state[12:]
    dp = lax.axis_index("dp")
    fsdp = lax.axis_index("fsdp")
    n = packed.shape[0]
    start = ((dp * 2 * Z + fsdp) * n) % VEC_COLS
    vec = lax.dynamic_update_slice(
        jnp.zeros((16 * VEC_COLS,), BF), packed.astype(BF), (start,)
    ).reshape(16, VEC_COLS)
    mixed, d_tokens, own, small = mega_call(
        Z, tokens[0], cotangent[0], lengths, state[0], state[3], state[6], state[9], vec
    )
    grad_norm = jnp.sqrt(small[0, 0])
    factor = jnp.minimum(1.0, CLIP_NORM / (grad_norm + 1e-06))
    parity = (fsdp % 2).astype(jnp.int32).reshape(1)
    *new, mixed, d_tokens = adam_call(parity, own, small, mixed, d_tokens, state[:12])
    g_vec = lax.dynamic_slice(small[8:].reshape(-1), (start,), (n,))
    new_vec = adam_step(packed, m_packed, v_packed, g_vec * factor, VECTOR_RATE)
    return (mixed[None], d_tokens[None], grad_norm) + tuple(new) + new_vec


def solution(mesh):
    rows = P(("dp", "fsdp"), None)
    seqs = P(("dp", "fsdp"), None, None)
    flat = P(("dp", "fsdp"))
    in_specs = (seqs, flat, seqs) + (rows,) * 12 + (flat,) * 3
    out_specs = (seqs, seqs, P()) + (rows,) * 12 + (flat,) * 3
    dp, fsdp = mesh.shape["dp"], mesh.shape["fsdp"]

    def shards(*args):
        tokens, w_qkv = args[0], args[3]
        fits = (
            dp == 4
            and fsdp == 8
            and tokens.shape[0] == 1
            and tokens.shape[1] == 1024
            and w_qkv.shape[0] * dp * fsdp == D
        )
        step = functools.partial(direct_shards, fsdp // 2) if fits else plain_shards
        return step(*args)

    return jax.shard_map(
        shards, mesh=mesh, in_specs=in_specs, out_specs=out_specs, check_vma=False
    )
```

```python
import functools

import jax
import jax.numpy as jnp
from jax import lax
from jax.experimental import pallas as pl
from jax.experimental.pallas import tpu as pltpu
from jax.sharding import PartitionSpec as P

D = 768
FF = 3072
HEAD_DIM = 64
STEP = 10
HD = 64
F32 = jnp.float32
BF = jnp.bfloat16
MESH = pl.DeviceIdType.MESH

EPS_NORM = 1e-05
CLIP_NORM = 1.0
BETA_ONE = 0.9
BETA_TWO = 0.95
ADAM_EPSILON = 1e-08
DECAY_RATE = 0.1
VECTOR_RATE = 0.2


def nt(a,b): return lax.dot_general(a,b,(((1,),(1,)),((),())),preferred_element_type=F32)
def nn(a,b): return jnp.dot(a,b,preferred_element_type=F32)
def head_mask(rows):
    lane=lax.broadcasted_iota(jnp.int32,(rows,128),1)
    return (lane<HD)
def half(x,h,scale=1.0):
    m=head_mask(x.shape[0]); m = m if h==0 else jnp.logical_not(m)
    return jnp.where(m,x*jnp.asarray(scale,x.dtype),jnp.zeros_like(x))

def attn_fwd_pair(q_ref,k_ref,v_ref,length,o_ref,oT_ref,lse_ref,QB):
    L=q_ref.shape[0]
    n=L//QB
    vT=v_ref[...].T
    lane=lax.broadcasted_iota(jnp.int32,(L,128),1)
    dead=jnp.where(lax.broadcasted_iota(jnp.int32,(L,128),0)<length,0.0,-1e9).astype(BF)
    keys=[jnp.where(lane==HD-HD*h,dead,k_ref[...]) for h in range(2)]
    ql=lax.broadcasted_iota(jnp.int32,(QB,128),1)
    tri=lax.broadcasted_iota(jnp.int32,(QB,QB),0)<=lax.broadcasted_iota(jnp.int32,(QB,QB),1)
    def scores(i,h):
        qh=jnp.where(ql==HD-HD*h,jnp.ones((),BF),half(q_ref[pl.ds(i*QB,QB),:],h,0.125))
        return nt(keys[h][:(i+1)*QB],qh)
    jobs=[(i,h) for i in range(n) for h in range(2)]
    now=scores(*jobs[0])
    outs=[]
    for x,(i,h) in enumerate(jobs):
        later=scores(*jobs[x+1]) if x+1<len(jobs) else None
        nk=(i+1)*QB
        s=jnp.where(tri,now[nk-QB:],-1e9)
        if i: s=jnp.concatenate([now[:nk-QB],s],0)
        m=jnp.max(s,0,keepdims=True)
        e=jnp.exp(s-m)
        l=jnp.sum(e,0,keepdims=True)
        outs.append(nn(vT[HD*h:HD*h+HD,:nk],e.astype(BF))/l)
        lse_ref[pl.ds(h,1),pl.ds(i*QB,QB)]=m+jnp.log(l)
        if h==1:
            oT=jnp.concatenate(outs,0); outs=[]
            oT_ref[:,pl.ds(i*QB,QB)]=oT
            o_ref[pl.ds(i*QB,QB),:]=oT.T.astype(BF)
        now=later

def attn_bwd_pair(q_ref,k_ref,v_ref,do_ref,oT_ref,lse_ref,length,dq_ref,dk_ref,dv_ref,dk_acc,dv_acc,QB,tick=None):
    L=q_ref.shape[0]
    n=L//QB
    kT=k_ref[...].T
    jobs=list(reversed(range(n)))
    tri=lax.broadcasted_iota(jnp.int32,(QB,2*QB),0)<=lax.rem(lax.broadcasted_iota(jnp.int32,(QB,2*QB),1),QB)
    def products(i):
        nk=(i+1)*QB; sl=pl.ds(i*QB,QB)
        q=q_ref[sl,:]; do=do_ref[sl,:]
        qm=jnp.concatenate([half(q,0,0.125),half(q,1,0.125)],0)
        dom=jnp.concatenate([half(do,0),half(do,1)],0)
        return nt(k_ref[pl.ds(0,nk),:],qm),nt(v_ref[pl.ds(0,nk),:],dom),qm,dom
    now=products(jobs[0])
    for x,i in enumerate(jobs):
        split=tick is not None and x==1
        later=products(jobs[x+1]) if x+1<n and not (tick is not None and x==0) else None
        if split:
            tick(1)
            now=products(i)
        nk=(i+1)*QB; sl=pl.ds(i*QB,QB)
        s,dp,qm,dom=now
        prod=do_ref[sl,:].astype(F32).T*oT_ref[:,sl]
        delta=jnp.concatenate([jnp.sum(prod[:HD],0,keepdims=True),jnp.sum(prod[HD:],0,keepdims=True)],1)
        live=(i*QB+lax.broadcasted_iota(jnp.int32,(1,QB),1))<length
        lse=jnp.concatenate([jnp.where(live,lse_ref[pl.ds(h,1),sl],1e30) for h in range(2)],1)
        p=jnp.exp(s-lse)
        pd=jnp.where(tri,p[nk-QB:],0.0)
        p=pd if i==0 else jnp.concatenate([p[:nk-QB],pd],0)
        ds=(p*(dp-delta)).astype(BF)
        dv=nn(p.astype(BF),dom); dk=nn(ds,qm)
        dq=[nn(kT[HD*h:HD*h+HD,:nk],ds[:,QB*h:QB*h+QB]) for h in range(2)]
        dq_ref[sl,:]=(jnp.concatenate(dq,0)*0.125).T.astype(BF)
        if i==n-1:
            dk_acc[...]=dk; dv_acc[...]=dv
        else:
            dk_acc[pl.ds(0,nk),:]+=dk; dv_acc[pl.ds(0,nk),:]+=dv
        now=later
    dk_ref[...]=dk_acc[...].astype(BF); dv_ref[...]=dv_acc[...].astype(BF)

def fwd_call(qkv,length,QB=256):
    L=qkv.shape[0]; D=qkv.shape[1]//3; NP=D//128
    def k(len_ref,q,k_,v,o,oT,lse):
        attn_fwd_pair(q,k_,v,len_ref[0],o,oT,lse.at[0],QB)
    return pl.pallas_call(k,grid=(NP,),
      in_specs=[pl.BlockSpec(memory_space=pltpu.SMEM)]+[pl.BlockSpec((L,128),functools.partial(lambda off,p:(0,off+p),j*NP)) for j in range(3)],
      out_specs=[pl.BlockSpec((L,128),lambda p:(0,p)),pl.BlockSpec((128,L),lambda p:(p,0)),pl.BlockSpec((1,2,L),lambda p:(p,0,0))],
      out_shape=[jax.ShapeDtypeStruct((L,D),BF),jax.ShapeDtypeStruct((D,L),F32),jax.ShapeDtypeStruct((NP,2,L),F32)],
      compiler_params=pltpu.CompilerParams(vmem_limit_bytes=56*2**20),
      cost_estimate=pl.CostEstimate(flops=4*L*L*D//2,bytes_accessed=10*2**20,transcendentals=12*L*L//2))(length,qkv,qkv,qkv)
def bwd_call(qkv,do,oT,lse,length,QB=256):
    L=qkv.shape[0]; D=qkv.shape[1]//3; NP=D//128
    def k(len_ref,q,k_,v,do,oT,lse,dq,dk,dv,dka,dva):
        attn_bwd_pair(q,k_,v,do,oT,lse.at[0],len_ref[0],dq,dk,dv,dka,dva,QB)
    blk=pl.BlockSpec((L,128),lambda p:(0,p))
    return pl.pallas_call(k,grid=(NP,),
      in_specs=[pl.BlockSpec(memory_space=pltpu.SMEM)]+[pl.BlockSpec((L,128),functools.partial(lambda off,p:(0,off+p),j*NP)) for j in range(3)]+[blk,pl.BlockSpec((128,L),lambda p:(p,0)),pl.BlockSpec((1,2,L),lambda p:(p,0,0))],
      out_specs=[blk]*3,
      out_shape=[jax.ShapeDtypeStruct((L,D),BF)]*3,
      scratch_shapes=[pltpu.VMEM((L,128),F32)]*2,
      compiler_params=pltpu.CompilerParams(vmem_limit_bytes=56*2**20),
      cost_estimate=pl.CostEstimate(flops=10*L*L*D//2,bytes_accessed=14*2**20,transcendentals=12*L*L//2))(length,qkv,qkv,qkv,do,oT,lse)


class Place:
    def __init__(self, Z):
        dp=lax.axis_index("dp"); fs=lax.axis_index("fsdp")
        self.Z=Z; self.y=dp//2; self.c=dp%2; self.z=fs//2; self.x=fs%2
        self.nx=(dp,self.z*2+1-self.x)
        self.ny=((1-self.y)*2+self.c,fs)
        self.nc=(self.y*2+1-self.c,fs)
        self.me=self.piece(self.z)
        self.dp=dp; self.fs=fs
    def nz(self,z): return (self.dp,z*2+self.x)
    def piece(self,z,dx=0,dy=0,dc=0):
        y=self.y if dy==0 else 1-self.y
        x=self.x if dx==0 else 1-self.x
        c=self.c if dc==0 else 1-self.c
        return (y*2+c,z,x)
    def slab(self,y,dc=0):
        c=self.c if dc==0 else 1-self.c
        return y*2+c

def rcopy(src,dst,ss,rs,dev):
    return pltpu.make_async_remote_copy(src_ref=src,dst_ref=dst,send_sem=ss,recv_sem=rs,device_id=dev,device_id_type=MESH)

def when(cond,fn):
    if cond is True: fn()
    else: pl.when(cond)(fn)

def gather_sems(NG,Z):
    D=pltpu.SemaphoreType.DMA
    return [D((NG*2*(Z-1),)),D((NG*2*(Z-1),)),
            D((NG*2*Z,)),D((NG*2*Z,)),
            D((NG*2*Z,)),D((NG*2*Z,)),
            D((NG*2,)),D((NG*2,)),
            D((NG*2*(Z-1),)),D((NG*2*(Z-1),))]

class Gather:
    def __init__(self,P,G,groups,sems):
        self.P=P; self.G=G; self.groups=groups
        self.zs,self.zr,self.xs,self.xr,self.ys,self.yr,self.cs,self.cr,self.fs,self.fr=sems
    def direct(self,g):
        lo,n,a,p,q=self.groups[g]
        return p+q==n
    def _cp(self,idx,lo,n,ss,rs,dev):
        r=self.G.at[(*idx,slice(None),pl.ds(lo,n))]
        return rcopy(r,r,ss,rs,dev)
    def zcp(self,g,d,t,zo,to):
        lo,n=self.groups[g][:2]; i=(g*2+d)*(self.P.Z-1)+t
        return self._cp(self.P.piece(zo),lo,n,self.zs.at[i],self.zr.at[i],self.P.nz(to))
    def zdiag(self,g,d,t,zo,to):
        lo,n,a,p,q=self.groups[g]; i=(g*2+d)*(self.P.Z-1)+t
        return self._cp(self.P.piece(zo,dx=1,dy=1),lo+p,n-p-q,self.fs.at[i],self.fr.at[i],self.P.nz(to))
    def xfull(self,g,zo,arrive=0):
        lo,n=self.groups[g][:2]; i=g*2*self.P.Z+zo
        return self._cp(self.P.piece(zo,dx=arrive),lo,n,self.xs.at[i],self.xr.at[i],self.P.nx)
    def yfull(self,g,zo,arrive=0):
        lo,n=self.groups[g][:2]; i=g*2*self.P.Z+zo
        return self._cp(self.P.piece(zo,dy=arrive),lo,n,self.ys.at[i],self.yr.at[i],self.P.ny)
    def ydiag(self,g,zo,near,arrive=0):
        lo,n,a,p,q=self.groups[g]; i=g*2*self.P.Z+self.P.Z+zo
        return self._cp(self.P.piece(zo,dx=1,dy=arrive),lo,a if near else p,self.ys.at[i],self.yr.at[i],self.P.ny)
    def xdiag(self,g,zo,near,arrive=0):
        lo,n,a,p,q=self.groups[g]; i=g*2*self.P.Z+self.P.Z+zo
        w=n-a if near else q
        return self._cp(self.P.piece(zo,dy=1,dx=arrive),lo+n-w,w,self.xs.at[i],self.xr.at[i],self.P.nx)
    def ccp(self,g,k,arrive=0):
        lo,n=self.groups[g][:2]
        y=self.P.y if k==0 else 1-self.P.y
        r=self.G.at[self.P.slab(y,dc=arrive),:,:,:,pl.ds(lo,n)]
        return rcopy(r,r,self.cs.at[g*2+k],self.cr.at[g*2+k],self.P.nc)
    def others(self,t,f):
        when(self.P.z>=t,lambda: f(self.P.z-t)); when(self.P.z<self.P.Z-t,lambda: f(self.P.z+t))
    def own(self,g):
        z=self.P.z; Z=self.P.Z
        self.xfull(g,z).start(); self.yfull(g,z).start()
        for t in range(Z-1 if self.direct(g) else 1):
            when(z<Z-1-t,lambda: self.zcp(g,0,t,z,z+1+t).start())
            when(z>t,lambda: self.zcp(g,1,t,z,z-1-t).start())
    def zarrive(self,g,t):
        z=self.P.z; Z=self.P.Z
        on=t+1<Z-1 and not self.direct(g)
        def below():
            zo=z-1-t
            self.zcp(g,0,t,zo,z).wait_recv()
            if on: when(z<Z-1,lambda: self.zcp(g,0,t+1,zo,z+1).start())
            self.xfull(g,zo).start(); self.yfull(g,zo).start()
        def above():
            zo=z+1+t
            self.zcp(g,1,t,zo,z).wait_recv()
            if on: when(z>0,lambda: self.zcp(g,1,t+1,zo,z-1).start())
            self.xfull(g,zo).start(); self.yfull(g,zo).start()
        when(z>t,below); when(z<Z-1-t,above)
    def diag(self,g,t):
        def pass_on(zo):
            self.xfull(g,zo,1).wait_recv(); self.ydiag(g,zo,t==0).start()
            self.yfull(g,zo,1).wait_recv(); self.xdiag(g,zo,t==0).start()
        if t==0: pass_on(self.P.z)
        else: self.others(t,pass_on)
    def line(self,g,t):
        z=self.P.z; Z=self.P.Z
        if t==0:
            self.ydiag(g,z,True,1).wait_recv(); self.xdiag(g,z,True,1).wait_recv()
            when(z<Z-1,lambda: self.zdiag(g,0,0,z,z+1).start())
            when(z>0,lambda: self.zdiag(g,1,0,z,z-1).start())
            return
        def below():
            self.zdiag(g,0,t-1,z-t,z).wait_recv()
            if t<Z-1: when(z<Z-1,lambda: self.zdiag(g,0,t,z-t,z+1).start())
        def above():
            self.zdiag(g,1,t-1,z+t,z).wait_recv()
            if t<Z-1: when(z>0,lambda: self.zdiag(g,1,t,z+t,z-1).start())
        when(z>=t,below); when(z<Z-t,above)
    def corner(self,g):
        self.ccp(g,0).start()
        if self.direct(g):
            self.ydiag(g,self.P.z,True,1).wait_recv(); self.xdiag(g,self.P.z,True,1).wait_recv()
        else: self.line(g,self.P.Z-1)
        def come(zo):
            self.ydiag(g,zo,False,1).wait_recv(); self.xdiag(g,zo,False,1).wait_recv()
        for t in range(1,self.P.Z): self.others(t,come)
        self.ccp(g,1).start()
    def sibling(self,g):
        self.ccp(g,0,1).wait_recv(); self.ccp(g,1,1).wait_recv()
    def drain(self,g):
        z=self.P.z; Z=self.P.Z
        def sent(zo,near):
            self.xfull(g,zo).wait_send(); self.yfull(g,zo).wait_send()
            self.xdiag(g,zo,near).wait_send(); self.ydiag(g,zo,near).wait_send()
        sent(z,True)
        for t in range(1,Z): self.others(t,lambda zo: sent(zo,False))
        for k in range(2): self.ccp(g,k).wait_send()
        for t in range(Z-1):
            if self.direct(g):
                when(z<Z-1-t,lambda: self.zcp(g,0,t,z,z+1+t).wait_send())
                when(z>t,lambda: self.zcp(g,1,t,z,z-1-t).wait_send())
                continue
            def up():
                self.zcp(g,0,t,z-t,z+1).wait_send(); self.zdiag(g,0,t,z-t,z+1).wait_send()
            def down():
                self.zcp(g,1,t,z+t,z-1).wait_send(); self.zdiag(g,1,t,z+t,z-1).wait_send()
            when(jnp.logical_and(z<Z-1,z>=t),up)
            when(jnp.logical_and(z>0,z<=Z-1-t),down)
    def events(self,g):
        Z=self.P.Z
        ev=[lambda: self.own(g)]
        for t in range(Z):
            if t<Z-1: ev.append(lambda t=t: self.zarrive(g,t))
            if t and not self.direct(g): ev.append(lambda t=t: self.line(g,t-1))
            ev.append(lambda t=t: self.diag(g,t))
        ev.append(lambda: self.corner(g))
        ev.append(lambda: self.sibling(g))
        return ev


SLOT = 1152
NB=12
def rs_sems(NG,Z):
    D=pltpu.SemaphoreType.DMA
    return [D((NG*2,)),D((NG*2,)),
            D((NG*3,)),D((NG*3,)),
            D((NG*2,)),D((NG*2,)),
            D((NG*Z,)),D((NG*Z,))]
def rs_bufs(Z):
    V=lambda *s: pltpu.VMEM(s,BF)
    h=640
    v=128
    return [V(2,2,Z,2,16,SLOT),V(2,Z,2,16,h),V(2,Z,16,h),V(2,2,Z,16,h),V(2,Z,16,h),V(4,Z,16,SLOT),
            V(1,2,Z,2,16,v),V(1,Z,2,16,v),V(1,Z,16,v),V(1,2,Z,16,v),V(1,Z,16,v),V(1,Z,16,v)]
class Scatter:
    def __init__(self,P,R,groups,bufs,sems):
        self.P=P; self.R=R; self.groups=groups; self.bufs=bufs
        self.cs,self.cr,self.xs,self.xr,self.ys,self.yr,self.zs,self.zr=sems
    def buf(self,g,i,w):
        b=self.bufs[i+(NB//2 if g==len(self.groups)-1 else 0)]
        b=b.at[g%b.shape[0]]
        nd=len(b.shape)
        return b.at[(slice(None),)*(nd-1)+(pl.ds(0,w),)]
    def row(self,dy=0,dc=0):
        y=self.P.y if dy==0 else 1-self.P.y
        c=self.P.c if dc==0 else 1-self.P.c
        return y*2+c
    def add(self,dst,src):
        def body(z,_):
            d=dst(z); s=src(z)
            d[...]=d[...]+s[...]
            return 0
        lax.fori_loop(0,self.P.Z,body,0)
    def ccp(self,g,k):
        lo,n,_=self.groups[g]
        return rcopy(self.R.at[self.row(k,1),:,:,:,pl.ds(lo,n)],self.buf(g,0,n).at[k],self.cs.at[g*2+k],self.cr.at[g*2+k],self.P.nc)
    def x1(self,g,k):
        lo,n,a=self.groups[g]
        return rcopy(self.R.at[self.row(k),:,1-self.P.x,:,pl.ds(lo+a,n-a)],self.buf(g,3,n-a).at[k],self.xs.at[g*3+k],self.xr.at[g*3+k],self.P.nx)
    def y1(self,g):
        lo,n,a=self.groups[g]
        return rcopy(self.R.at[self.row(1),:,:,:,pl.ds(lo,a)],self.buf(g,1,a),self.ys.at[g*2],self.yr.at[g*2],self.P.ny)
    def x2(self,g):
        lo,n,a=self.groups[g]
        return rcopy(self.R.at[self.row(0),:,1-self.P.x,:,pl.ds(lo,a)],self.buf(g,2,a),self.xs.at[g*3+2],self.xr.at[g*3+2],self.P.nx)
    def y2(self,g):
        lo,n,a=self.groups[g]
        return rcopy(self.R.at[self.row(1),:,self.P.x,:,pl.ds(lo+a,n-a)],self.buf(g,4,n-a),self.ys.at[g*2+1],self.yr.at[g*2+1],self.P.ny)
    def zc(self,g,src,to):
        lo,n,_=self.groups[g]; Z=self.P.Z
        return rcopy(self.R.at[self.row(0),to,self.P.x,:,pl.ds(lo,n)],self.buf(g,5,n).at[src],self.zs.at[g*Z+to],self.zr.at[g*Z+src],self.P.nz(to))
    def both(self,g): return self.groups[g][1]>self.groups[g][2]
    def s_c(self,g):
        self.ccp(g,1).start(); self.ccp(g,0).start()
    def a_c(self,g):
        lo,n,a=self.groups[g]; R=self.R; b=self.buf(g,0,n)
        for k in (1,0):
            self.ccp(g,k).wait_recv()
            r=self.row(k)
            self.add(lambda z: R.at[r,z,:,:,pl.ds(lo,n)],lambda z: b.at[k,z])
            if self.both(g): self.x1(g,k).start()
            if k==1: self.y1(g).start()
    def a_1(self,g):
        lo,n,a=self.groups[g]; R=self.R; P=self.P; B1=self.buf(g,1,a)
        self.y1(g).wait_recv()
        r=self.row(0)
        self.add(lambda z: R.at[r,z,:,:,pl.ds(lo,a)],lambda z: B1.at[z])
        if self.both(g):
            B3=self.buf(g,3,n-a)
            for k in (1,0):
                self.x1(g,k).wait_recv()
                q=self.row(k)
                self.add(lambda z: R.at[q,z,P.x,:,pl.ds(lo+a,n-a)],lambda z: B3.at[k,z])
            self.y2(g).start()
        self.x2(g).start()
    def a_2(self,g):
        lo,n,a=self.groups[g]; R=self.R; P=self.P; Z=P.Z; B2=self.buf(g,2,a)
        r=self.row(0)
        self.x2(g).wait_recv()
        self.add(lambda z: R.at[r,z,P.x,:,pl.ds(lo,a)],lambda z: B2.at[z])
        if self.both(g):
            B4=self.buf(g,4,n-a)
            self.y2(g).wait_recv()
            self.add(lambda z: R.at[r,z,P.x,:,pl.ds(lo+a,n-a)],lambda z: B4.at[z])
        for d in range(Z-1,0,-1):
            when(P.z>=d,lambda: self.zc(g,P.z,P.z-d).start())
            when(P.z<Z-d,lambda: self.zc(g,P.z,P.z+d).start())
    def final(self,g,out):
        lo,n,_=self.groups[g]; P=self.P; Z=P.Z; z=P.z
        out[...]=self.R[self.row(0),z,P.x,:,pl.ds(lo,n)].astype(F32)
        for zo in range(Z):
            def take():
                self.zc(g,zo,z).wait_recv()
                out[...]+=self.buf(g,5,n)[zo].astype(F32)
            when(z!=zo,take)
    def drain(self,g):
        Z=self.P.Z; z=self.P.z
        for k in range(2):
            self.ccp(g,k).wait_send()
            if self.both(g): self.x1(g,k).wait_send()
        self.x2(g).wait_send(); self.y1(g).wait_send()
        if self.both(g): self.y2(g).wait_send()
        for zo in range(Z):
            when(z!=zo,lambda: self.zc(g,z,zo).wait_send())
    def events(self,g,out):
        return [lambda: self.s_c(g),lambda: self.a_c(g),lambda: self.a_1(g),lambda: self.a_2(g),lambda: self.final(g,out)]

def norm_sems(Z):
    D=pltpu.SemaphoreType.DMA
    return [D((8*Z,)),D((8*Z,))]
def norm_bufs(Z): return [pltpu.VMEM((8*Z,8,128),F32),pltpu.VMEM((1,8,128),F32)]
def everyone(P):
    n=8*P.Z
    for k in range(1,n):
        i=lax.rem(P.dp*2*P.Z+P.fs+k,n)
        yield k,i,(i//(2*P.Z),lax.rem(i,2*P.Z))
def all_sum(P,buf,got,ss,rs):
    n=8*P.Z
    me=P.dp*2*P.Z+P.fs
    buf[me]=got[0]
    for k,i,dev in everyone(P):
        rcopy(got.at[0],buf.at[me],ss.at[k],rs.at[me],dev).start()
    for k,i,dev in everyone(P):
        rcopy(got.at[0],buf.at[i],ss.at[k],rs.at[i],dev).wait_recv()
    tot=buf[0]
    for i in range(1,n): tot=tot+buf[i]
    for k,i,dev in everyone(P):
        rcopy(got.at[0],buf.at[me],ss.at[k],rs.at[me],dev).wait_send()
    return tot
def announce(P,Z):
    bar=pltpu.get_barrier_semaphore()
    for _,_,d in everyone(P): pl.semaphore_signal(bar,inc=1,device_id=d,device_id_type=MESH)
    return bar


W3 = 768
CW = 1152
QKV_AT = 0
VEC_AT = 3456
VEC_COLS = 128
OUT_AT = 3584
DOWN_AT = 4736
UP_AT = 9344
COLS = 13952
GATHER = [(2304, 1280, 640, 640, 640), (0, 2304, 1152, 384, 384), (3584, 5760, 2944, 1024, 896),
          (9344, 1152, 640, 256, 128), (10496, 1152, 512, 128, 256), (11648, 2304, 1152, 384, 384)]
SCATTER = ([(UP_AT + CW * c, CW, 640 if c % 2 else 512) for c in range(4)]
           + [(DOWN_AT + CW * c, CW, 640 if c % 2 else 512) for c in range(4)]
           + [(OUT_AT, CW, 512), (0, CW, 640), (CW, CW, 512), (2 * CW, 640, 256), (2 * CW + 640, 512, 256), (VEC_AT, VEC_COLS, VEC_COLS)])

def al(v, m): return pl.multiple_of(v, m)

def third_cols(s): return [(D * j + 256 * s, 256) for j in range(3)]

def pack_rows(G, me, at, main, rest):
    G[(*me,slice(None),pl.ds(at,W3))]=main.astype(BF)
    parts=[jnp.concatenate([rest[:,256*s:256*s+128],rest[:,256*s+128:256*s+256]],0) for s in range(3)]
    G[(*me,slice(None),pl.ds(al(at+W3,128),W3//2))]=jnp.concatenate(parts,1).astype(BF)

def pack_own(place, G, wqkv, wout, wup, wdown, vec, first):
    me=place.me
    lo=al(8*place.x,8); ro=al(16*(1-place.x),8)
    def cols(w,cs):
        return [jnp.concatenate([w[pl.ds(a,n),pl.ds(c,k)] for c,k in cs],1) for a,n in ((lo,16),(ro,8))]
    for s in ((2,) if first else (0,1)): pack_rows(G,me,QKV_AT+CW*s,*cols(wqkv,third_cols(s)))
    if first:
        G[(*me,slice(None),pl.ds(VEC_AT,VEC_COLS))]=vec[...]
        return
    pack_rows(G,me,OUT_AT,*cols(wout,[(0,W3)]))
    for c in range(4): pack_rows(G,me,UP_AT+CW*c,*cols(wup,[(W3*c,W3)]))
    for r in range(6):
        G[(*me,slice(None),pl.ds(DOWN_AT+r*D,D))]=wdown[pl.ds(16*r,16),:].astype(BF)

def unpack24(G, at, dst):
    Z=G.shape[1]
    def body(j,_):
        r=al(j*48,16); d=j//Z; z=lax.rem(j,Z)
        dst[pl.ds(r,16),:]=G[d,z,0,:,pl.ds(al(at,128),W3)]
        dst[pl.ds(r+32,16),:]=G[d,z,1,:,pl.ds(al(at,128),W3)]
        a=G[d,z,0,:,pl.ds(al(at+W3,128),W3//2)].astype(F32)
        b=G[d,z,1,:,pl.ds(al(at+W3,128),W3//2)].astype(F32)
        parts=[]
        for s in range(3):
            q=slice(128*s,128*s+128)
            parts+=[jnp.concatenate([a[:8,q],b[:8,q]],0),jnp.concatenate([a[8:,q],b[8:,q]],0)]
        dst[pl.ds(r+16,16),:]=jnp.concatenate(parts,1).astype(BF)
        return 0
    lax.fori_loop(0,G.shape[0]*Z,body,0)

def pack24(G, at, src):
    Z=G.shape[1]
    def body(j,_):
        r=al(j*48,16); d=j//Z; z=lax.rem(j,Z)
        pack_rows(G,(d,z,0),al(at,128),src[pl.ds(r,16),:],src[pl.ds(al(r+16,8),8),:])
        pack_rows(G,(d,z,1),al(at,128),src[pl.ds(r+32,16),:],src[pl.ds(al(r+24,8),8),:])
        return 0
    lax.fori_loop(0,G.shape[0]*Z,body,0)

def unpack_down(G, c, dst):
    def body(k,_):
        for r in range(6):
            dst[pl.ds(al(k*96+16*r,16),16),:]=G[c,k//2,lax.rem(k,2),:,pl.ds(DOWN_AT+r*D,D)]
        return 0
    lax.fori_loop(0,2*G.shape[1],body,0)

def pack_down(G, c, src):
    def body(k,_):
        for r in range(6):
            G[c,k//2,lax.rem(k,2),:,pl.ds(DOWN_AT+r*D,D)]=src[pl.ds(al(k*96+16*r,16),16),:].astype(BF)
        return 0
    lax.fori_loop(0,2*G.shape[1],body,0)

def vec_shift(k): return (240*k)//128

def unpack_vec(G, V, V1):
    V[...]=jnp.zeros_like(V)
    Z=G.shape[1]
    for k in range(8*Z):
        V[pl.ds(vec_shift(k),3),:]+=G[k//(2*Z),k//2%Z,k%2,:,pl.ds(VEC_AT,VEC_COLS)].astype(F32)[0:3]
    for t in range(60):
        V1[:,pl.ds(128*t,128)]=V[pl.ds(t,1),:]

def pack_vec(G, V, V1):
    V[...]=jnp.zeros_like(V)
    for t in range(60):
        V[pl.ds(t,1),:]=V1[:,pl.ds(128*t,128)]
    Z=G.shape[1]
    for k in range(8*Z):
        G[k//(2*Z),k//2%Z,k%2,:,pl.ds(VEC_AT,VEC_COLS)]=V[pl.ds(vec_shift(k),16),:].astype(BF)

def norm_parts(x):
    c=x-jnp.mean(x,-1,keepdims=True)
    s=lax.rsqrt(jnp.mean(c*c,-1,keepdims=True)+EPS_NORM)
    return c*s,s

def norm_back(dx, xh, s):
    return s*(dx-jnp.mean(dx,-1,keepdims=True)-xh*jnp.mean(dx*xh,-1,keepdims=True))

def gelu_both(u):
    k0=0.7978845608028654; k1=0.044715
    u2=u*u
    t=jnp.tanh(k0*(u*(1.0+k1*u2)))
    h=0.5*(1.0+t)
    return u*h, h+(0.5*k0)*u*(1.0-t*t)*(1.0+(3.0*k1)*u2)

RB=256

RULES=((1,1,0),(2,3,1),(2,4,3))

def places():
    p=[("in",0,0.7),("in",1,0.8)]+[("stat",i,0.6) for i in range(4)]
    for i in range(3):
        p.append(("third",i,0.6 if i else 2.0))
        p+=[("qkv",4*i+k,0.42) for k in range(4)]
        p+=[("af",2*i+pp,2.3) for pp in range(2)]
    p.append(("out",0,0.6))
    p+=[("ob",k,1.1) for k in range(4)]
    for c in range(4):
        p.append(("chunk",c,0.5))
        p+=[("mr",4*c+k,1.7) for k in range(4)]
        p+=[("mw",3*c+k,0.6+0.15*(k==2)) for k in range(3)]
        p+=[("mu",3*c+k,0.6+0.2*(k==2)) for k in range(3)]
        p.append(("mp",c,0.1))
    p.append(("fin",0,1.0))
    p+=[("bb",k,1.3) for k in range(4)]
    p+=[("bw",k,0.6+0.2*(k==2)) for k in range(3)]
    p.append(("bp",0,0.4))
    for i in range(3):
        for pp in range(2): p+=[("ab",4*i+2*pp+k,(1.6,2.1)[k]) for k in range(2)]
        p+=[("dq",3*i+k,0.6+0.2*(k==2)) for k in range(3)]
        p.append(("dp",i,0.1))
        p+=[("dh",4*i+k,0.5) for k in range(4)]
    p+=[("ln",k,0.5+0.4*(k==3)) for k in range(4)]
    p.append(("lp",0,0.1))
    p+=[("lx",k,0.65) for k in range(4)]
    return p

def ready_places():
    return [("mp",c) for c in range(4)]+[("mp",3)]*4+[("bp",0)]+[("dp",i) for i in (0,1,2,2)]+[("lp",0)]

def due_places():
    return [("third",0),("third",1),("out",0),("chunk",0),("chunk",1),("chunk",2)]

class Clock:
    def __init__(self, plan, ga, sc, own):
        names=[p[:2] for p in places()]
        index={p:i for i,p in enumerate(names)}
        fns={}
        for g in range(len(GATHER)):
            for k,f in enumerate(ga.events(g)): fns[(0,g,k)]=f
        for g,(lo,n,_) in enumerate(SCATTER):
            for k,f in enumerate(sc.events(g,own.at[:,pl.ds(lo,n)])): fns[(1,g,k)]=f
        check_plan(plan,set(fns),index)
        self.slots={}
        self.tail=[]
        for i,*key in plan:
            if i<len(names): self.slots.setdefault(names[i],[]).append(fns[tuple(key)])
            else: self.tail.append(fns[tuple(key)])
    def at(self, name, step, count):
        for k in range(count):
            todo=self.slots.get((name,k))
            if todo:
                def run(todo=todo):
                    for f in todo: f()
                if isinstance(step,int):
                    if step==k: run()
                else: pl.when(step==k)(run)

PLAN = (
    (0, 0, 0, 0), (1, 0, 1, 0), (1, 0, 2, 0), (1, 0, 0, 1), (1, 0, 0, 2), (1, 0, 0, 3), (1, 0, 1, 1), (1, 0, 1, 2),
    (1, 0, 0, 4), (1, 0, 0, 5), (1, 0, 1, 3), (2, 0, 1, 4), (3, 0, 0, 6), (3, 0, 0, 7), (3, 0, 2, 1), (3, 0, 3, 0),
    (3, 0, 1, 5), (3, 0, 1, 6), (4, 0, 2, 2), (5, 0, 1, 7), (6, 0, 0, 8), (6, 0, 0, 9), (8, 0, 1, 8), (8, 0, 1, 9),
    (8, 0, 1, 10), (9, 0, 2, 3), (12, 0, 2, 4), (12, 0, 1, 11), (13, 0, 1, 12), (14, 0, 3, 1), (15, 0, 2, 5),
    (15, 0, 2, 6), (16, 0, 3, 2), (17, 0, 2, 7), (19, 0, 5, 0), (20, 0, 3, 3), (20, 0, 2, 8), (21, 0, 3, 4),
    (22, 0, 4, 0), (22, 0, 2, 9), (24, 0, 2, 10), (25, 0, 3, 5), (25, 0, 3, 6), (26, 0, 5, 1), (26, 0, 3, 7),
    (26, 0, 3, 8), (26, 0, 2, 11), (26, 0, 4, 1), (27, 0, 4, 2), (27, 0, 4, 3), (27, 0, 3, 9), (27, 0, 3, 10),
    (27, 0, 2, 12), (28, 0, 5, 2), (29, 0, 4, 4), (29, 0, 4, 5), (30, 0, 3, 11), (31, 0, 5, 3), (31, 0, 4, 6),
    (31, 0, 5, 4), (31, 0, 5, 5), (32, 0, 3, 12), (32, 0, 4, 7), (35, 0, 5, 6), (35, 0, 5, 7), (35, 0, 4, 8),
    (35, 0, 4, 9), (35, 0, 4, 10), (37, 0, 5, 8), (37, 0, 5, 9), (37, 0, 4, 11), (40, 0, 4, 12), (43, 1, 0, 0),
    (45, 0, 5, 10), (47, 1, 0, 1), (51, 0, 5, 11), (54, 1, 0, 2), (55, 1, 1, 0), (56, 0, 5, 12), (58, 1, 1, 1),
    (59, 1, 0, 3), (67, 1, 2, 0), (68, 1, 1, 2), (70, 1, 0, 4), (70, 1, 2, 1), (75, 1, 2, 2), (79, 1, 3, 0),
    (80, 1, 1, 3), (81, 1, 3, 1), (81, 1, 4, 0), (82, 1, 2, 3), (83, 1, 4, 1), (86, 1, 3, 2), (88, 1, 5, 0),
    (89, 1, 2, 4), (89, 1, 4, 2), (90, 1, 1, 4), (90, 1, 3, 3), (90, 1, 5, 1), (90, 1, 6, 0), (91, 1, 4, 3),
    (91, 1, 6, 1), (92, 1, 7, 0), (95, 1, 5, 2), (96, 1, 6, 2), (97, 1, 3, 4), (102, 1, 5, 3), (102, 1, 7, 1),
    (102, 1, 8, 0), (103, 1, 4, 4), (103, 1, 6, 3), (103, 1, 8, 1), (105, 1, 7, 2), (105, 1, 5, 4), (108, 1, 8, 2),
    (109, 1, 6, 4), (109, 1, 9, 0), (113, 1, 7, 3), (113, 1, 9, 1), (114, 1, 10, 0), (114, 1, 8, 3),
    (115, 1, 10, 1), (117, 1, 9, 2), (120, 1, 10, 2), (120, 1, 11, 0), (121, 1, 8, 4), (123, 1, 7, 4),
    (124, 1, 9, 3), (124, 1, 11, 1), (124, 1, 12, 0), (127, 1, 10, 3), (127, 1, 12, 1), (129, 1, 11, 2),
    (130, 1, 13, 0), (131, 1, 12, 2), (133, 1, 9, 4), (134, 1, 11, 3), (134, 1, 13, 1), (134, 1, 13, 2),
    (134, 1, 11, 4), (134, 1, 10, 4), (134, 1, 12, 3), (134, 1, 13, 3), (134, 1, 13, 4), (134, 1, 12, 4),
)

def check_plan(plan, keys, index):
    pos={tuple(e[1:]):(e[0],j) for j,e in enumerate(plan)}
    assert set(pos)==keys and len(plan)==len(keys)
    assert all(a[0]<=b[0] for a,b in zip(plan,plan[1:]))
    for kind,g,k in keys:
        if k: assert pos[(kind,g,k-1)]<pos[(kind,g,k)]
    assert pos[(0,0,0)][0]==0 and all(pos[(0,g,0)][0]>=1 for g in range(1,len(GATHER)))
    for g,p in enumerate(due_places()): assert max(v[0] for e,v in pos.items() if e[:2]==(0,g))<=index[p]
    for g,p in enumerate(ready_places()):
        assert pos[(1,g,0)][0]>=index[p]
        for n,i,j in RULES:
            if g>=n: assert pos[(1,g-n,i)]<pos[(1,g,j)]

def mega_kernel(Z,plan,tok_h,cot_h,len_ref,wqkv_s,wout_s,wup_s,wdown_s,vec_s,
               mixed_o,dtok_o,own_o,nrm_o,
               G,tok,cot,F1,F2,F3,qkv,B1,B2,B3,h1T,h2T,aT,oT,W0,W1,dW,lse,V,V1,dV1,dka,dva,own,nrm,dsem,*rest):
    gsems=rest[:10]; rbufs=rest[10:10+NB]; rsems=rest[10+NB:18+NB]; nb,got,ns,nr=rest[18+NB:]
    L=tok.shape[0]
    NBK=L//RB
    place=Place(Z)
    def dma(a,b,i):
        cp=pltpu.make_async_copy(a,b,dsem.at[i]); cp.start(); return cp
    ldt=dma(tok_h,tok,0); ldc=dma(cot_h,cot,1)
    bar=announce(place,Z)
    shards=(wqkv_s,wout_s,wup_s,wdown_s,vec_s)
    pack_own(place,G,*shards,True)
    pl.semaphore_wait(bar,8*Z-1)
    ga=Gather(place,G,GATHER,gsems)
    sc=Scatter(place,G,SCATTER,rbufs,rsems)
    clock=Clock(plan,ga,sc,own)
    def at(name,step,count): clock.at(name,step,count)
    def rows(i): return pl.ds(al(i*RB,RB),RB)
    length=len_ref[0]
    at("in",0,2)
    pack_own(place,G,*shards,False)
    at("in",1,2)
    F3[...]=jnp.zeros_like(F3)
    ldc.wait()
    dead=lax.broadcasted_iota(jnp.int32,(L,D),0)>=length
    cot[...]=jnp.where(dead,jnp.zeros((),BF),cot[...])
    ldt.wait()
    xhat=F1; h1=B1; o=B3
    for i in range(4):
        at("stat",i,4)
        if i<NBK:
            xhat[rows(i),:]=norm_parts(tok[rows(i),:].astype(F32))[0]
    def third(i,_):
        s=lax.rem(i+2,3)
        at("third",i,3)
        @pl.when(i==0)
        def _():
            unpack_vec(G,V,V1)
            def first(j,_):
                hb=(xhat[rows(j),:]*V1[:,0:D]+V1[:,D:2*D]).astype(BF)
                h1[rows(j),:]=hb
                h1T[:,rows(j)]=hb.T
                return 0
            lax.fori_loop(0,NBK,first,0)
        unpack24(G,QKV_AT+CW*s,W0)
        def block(j,_):
            at("qkv",4*i+j,12)
            qkv[s,rows(j),:]=nn(h1[rows(j),:],W0[...]).astype(BF)
            return 0
        lax.fori_loop(0,NBK,block,0)
        def pair(pp,_):
            p=2*s+pp
            def col(j): return qkv.at[s,:,pl.ds(al(256*j+128*pp,128),128)]
            c=pl.ds(al(128*p,128),128)
            at("af",2*i+pp,6)
            attn_fwd_pair(col(0),col(1),col(2),length,o.at[:,c],oT.at[c,:],lse.at[p],512)
            return 0
        lax.fori_loop(0,2,pair,0)
        return 0
    lax.fori_loop(0,3,third,0)
    at("out",0,1)
    unpack24(G,OUT_AT,W0)
    r1=F1; mixed=F2; dh2=F3; h2=B1
    def out_block(i,_):
        at("ob",i,4)
        sl=rows(i)
        r=tok[sl,:].astype(F32)+nn(o[sl,:],W0[...])+V1[:,4*D:5*D]
        r1[sl,:]=r
        mixed[sl,:]=r+V1[:,5*D:6*D]
        hb=(norm_parts(r)[0]*V1[:,2*D:3*D]+V1[:,3*D:4*D]).astype(BF)
        h2[sl,:]=hb
        h2T[:,sl]=hb.T
        return 0
    lax.fori_loop(0,NBK,out_block,0)
    du_s=B2
    def chunk(c,_):
        at("chunk",c,4)
        for g,when_ in enumerate((0,0,0,0,1,2)):
            pl.when(c==when_)(lambda g=g: ga.drain(g))
        unpack24(G,UP_AT+CW*c,W0)
        unpack_down(G,c,W1)
        bu=V1[:,pl.ds(al(6*D+c*W3,128),W3)]
        def mrows(i,acc):
            at("mr",4*c+i,16)
            sl=rows(i)
            u=nn(h2[sl,:],W0[...])+bu
            a,slope=gelu_both(u)
            ab=a.astype(BF)
            mixed[sl,:]+=nn(ab,W1[...])
            aT[:,sl]=ab.T
            du=(nt(cot[sl,:],W1[...])*slope).astype(BF)
            du_s[sl,:]=du
            dh2[sl,:]+=nt(du,W0[...])
            return acc+jnp.sum(du.astype(F32),0,keepdims=True)
        s=lax.fori_loop(0,NBK,mrows,jnp.zeros((1,W3),F32))
        dV1[:,pl.ds(al(6*D+c*W3,128),W3)]=s
        def wrows(i,_):
            at("mw",3*c+i,12)
            dW[rows(i),:]=nn(aT[rows(i),:],cot[...])
            return 0
        lax.fori_loop(0,W3//RB,wrows,0)
        pack_down(G,c,dW)
        def urows(i,_):
            at("mu",3*c+i,12)
            dW[rows(i),:]=nn(h2T[rows(i),:],du_s[...])
            return 0
        lax.fori_loop(0,D//RB,urows,0)
        pack24(G,UP_AT+CW*c,dW)
        at("mp",c,4)
        return 0
    lax.fori_loop(0,FF//W3,chunk,0)
    at("fin",0,1)
    mixed_b=B2
    def fin(i,_):
        mixed_b[rows(i),:]=mixed[rows(i),:].astype(BF)
        return 0
    lax.fori_loop(0,NBK,fin,0)
    outs=[dma(mixed_b,mixed_o,2)]
    unpack24(G,OUT_AT,W0)
    dr1=F3; dy=B3; do=B1
    def back(i,acc):
        at("bb",i,4)
        sl=rows(i)
        dh=dh2[sl,:]
        xh,s=norm_parts(r1[sl,:])
        g=cot[sl,:].astype(F32)
        dr=g+norm_back(dh*V1[:,2*D:3*D],xh,s)
        dr1[sl,:]=dr
        dyb=dr.astype(BF)
        dy[sl,:]=dyb
        do[sl,:]=nt(dyb,W0[...]).astype(BF)
        new=(dh*xh,dh,dyb.astype(F32),g)
        return tuple(a+jnp.sum(b,0,keepdims=True) for a,b in zip(acc,new))
    z1=jnp.zeros((1,D),F32)
    sums=lax.fori_loop(0,NBK,back,(z1,z1,z1,z1))
    for j,v in enumerate(sums): dV1[:,pl.ds((2+j)*D,D)]=v
    def orow(i,_):
        at("bw",i,3)
        dW[rows(i),:]=nn(oT[rows(i),:].astype(BF),dy[...])
        return 0
    lax.fori_loop(0,D//RB,orow,0)
    pack24(G,OUT_AT,dW)
    at("bp",0,1)
    dqkv=B3; dh1=F2
    outs[0].wait()
    dh1[...]=jnp.zeros_like(dh1)
    def third_back(s,_):
        unpack24(G,QKV_AT+CW*s,W0)
        def pair(pp,_):
            p=2*s+pp
            at("ab",4*s+2*pp,12)
            def col(j): return qkv.at[s,:,pl.ds(al(256*j+128*pp,128),128)]
            def dcol(j): return dqkv.at[:,pl.ds(al(256*j+128*pp,128),128)]
            c=pl.ds(al(128*p,128),128)
            attn_bwd_pair(col(0),col(1),col(2),do.at[:,c],oT.at[c,:],lse.at[p],length,
                          dcol(0),dcol(1),dcol(2),dka,dva,256,tick=lambda k: at("ab",4*s+2*pp+k,12))
            return 0
        lax.fori_loop(0,2,pair,0)
        def qrow(i,_):
            at("dq",3*s+i,9)
            dW[rows(i),:]=nn(h1T[rows(i),:],dqkv[...])
            return 0
        lax.fori_loop(0,D//RB,qrow,0)
        pack24(G,QKV_AT+CW*s,dW)
        at("dp",s,3)
        def drow(i,_):
            at("dh",4*s+i,12)
            dh1[rows(i),:]+=nt(dqkv[rows(i),:],W0[...])
            return 0
        lax.fori_loop(0,NBK,drow,0)
        return 0
    lax.fori_loop(0,3,third_back,0)
    def srow(i,acc):
        at("ln",i,4)
        sl=rows(i)
        dh=dh1[sl,:]
        xh,_=norm_parts(tok[sl,:].astype(F32))
        return tuple(a+jnp.sum(b,0,keepdims=True) for a,b in zip(acc,(dh*xh,dh)))
    sums=lax.fori_loop(0,NBK,srow,(z1,z1))
    for j,v in enumerate(sums): dV1[:,pl.ds(j*D,D)]=v
    pack_vec(G,V,dV1)
    at("lp",0,1)
    def lrow(i,_):
        at("lx",i,4)
        sl=rows(i)
        xh,r=norm_parts(tok[sl,:].astype(F32))
        F1[sl,:]=dr1[sl,:]+norm_back(dh1[sl,:]*V1[:,0:D],xh,r)
        return 0
    lax.fori_loop(0,NBK,lrow,0)
    outs=[dma(F1,dtok_o,3)]
    for f in clock.tail: f()
    flat=lax.broadcasted_iota(jnp.int32,(16,VEC_COLS),0)*VEC_COLS+lax.broadcasted_iota(jnp.int32,(16,VEC_COLS),1)
    start=lax.rem(240*((place.dp*Z+place.z)*2+place.x),128)
    vec=own[:,pl.ds(VEC_AT,VEC_COLS)]
    vec=jnp.where(jnp.logical_and(flat>=start,flat<start+240),vec,0.0)
    left=own[:,pl.ds(0,VEC_AT)]; right=own[:,pl.ds(OUT_AT,COLS-OUT_AT)]
    got[0]=jnp.full((8,128),1.0,F32)*(jnp.sum(left*left)+jnp.sum(right*right)+jnp.sum(vec*vec))
    outs.append(dma(own,own_o,4))
    nrm[8:24,:]=vec
    nrm[0:8,:]=all_sum(place,nb,got,ns,nr)
    outs.append(dma(nrm,nrm_o,5))
    for g in range(len(SCATTER)): sc.drain(g)
    for cp in outs: cp.wait()

def mega_call(Z,tok,cot,length,wqkv,wout,wup,wdown,vec,plan=None):
    plan=PLAN if plan is None else plan
    L=tok.shape[0]; pieces=8*Z
    S=jax.ShapeDtypeStruct; V=pltpu.VMEM
    vm=pl.BlockSpec(memory_space=pltpu.VMEM); an=pl.BlockSpec(memory_space=pltpu.HBM); sm=pl.BlockSpec(memory_space=pltpu.SMEM)
    outs=[S((L,D),BF),S((L,D),F32),S((16,COLS),F32),S((24,128),F32)]
    f=lambda: V((L,D),F32)
    b=lambda: V((L,D),BF)
    scratch=[V((4,Z,2,16,COLS),BF),b(),b(),f(),f(),f(),V((3,L,D),BF),b(),b(),b(),V((D,L),BF),V((D,L),BF),V((D,L),BF),V((D,L),F32),
             V((D,W3),BF),V((W3,D),BF),V((D,W3),F32),V((6,2,L),F32),V((80,128),F32),V((1,10*D),F32),V((1,10*D),F32),
             V((L,128),F32),V((L,128),F32),V((16,COLS),F32),V((24,128),F32),pltpu.SemaphoreType.DMA((6,))]
    return pl.pallas_call(functools.partial(mega_kernel,Z,plan),out_shape=outs,
        in_specs=[an,an,sm]+[vm]*5,out_specs=[an]*len(outs),
        scratch_shapes=scratch+gather_sems(len(GATHER),Z)+rs_bufs(Z)+rs_sems(len(SCATTER),Z)+norm_bufs(Z)+norm_sems(Z),
        compiler_params=pltpu.CompilerParams(collective_id=1,has_side_effects=True,vmem_limit_bytes=63*2**20),
        cost_estimate=pl.CostEstimate(flops=60*10**9,bytes_accessed=60*2**20,transcendentals=10**7))(tok,cot,length,wqkv,wout,wup,wdown,vec)


def adam_step(weight, first_mom, second_mom, gradient, step_rate):
    first_new = BETA_ONE * first_mom + (1.0 - BETA_ONE) * gradient
    second_new = BETA_TWO * second_mom + (1.0 - BETA_TWO) * gradient * gradient
    fix_one = 1.0 - BETA_ONE**STEP
    fix_two = 1.0 - BETA_TWO**STEP
    update = (
        first_new / fix_one / (jnp.sqrt(second_new / fix_two) + ADAM_EPSILON) + DECAY_RATE * weight
    )
    return (weight - step_rate * update, first_new, second_new)


def adam_kernel(par_ref, own_h, nrm_h, mixed_h, dtok_h, *refs):
    ins_h, outs_h = refs[:12], refs[12:24]
    own, nrm, *rest = refs[26:]
    ins, outs, mixed, dtok, sem = rest[:12], rest[12:24], rest[24], rest[25], rest[26]
    pairs = list(zip((own_h, nrm_h) + tuple(ins_h), (own, nrm) + tuple(ins)))
    loads = [pltpu.make_async_copy(a, b, sem.at[i]) for i, (a, b) in enumerate(pairs)]
    moves = [
        pltpu.make_async_copy(mixed_h, mixed, sem.at[14]),
        pltpu.make_async_copy(dtok_h, dtok, sem.at[15]),
    ]
    for cp in loads + moves:
        cp.start()
    for cp in loads:
        cp.wait()
    for cp in moves:
        cp.wait()
    moves = [
        pltpu.make_async_copy(mixed, refs[24], sem.at[14]),
        pltpu.make_async_copy(dtok, refs[25], sem.at[15]),
    ]
    for cp in moves:
        cp.start()
    factor = jnp.minimum(1.0, CLIP_NORM / (jnp.sqrt(nrm[0:1, 0:1]) + 1e-06))
    main_at = al(8 * par_ref[0], 8)
    rest_at = al(16 * (1 - par_ref[0]), 8)

    def step(i, rows, cols, grad, rate):
        w, m, v = [r[rows, cols] for r in ins[3 * i : 3 * i + 3]]
        new = adam_step(w, m, v, grad * factor, rate)
        for r, a in zip(outs[3 * i : 3 * i + 3], new):
            r[rows, cols] = a

    def chunk(i, at, cols, rate):
        main = own[:, pl.ds(at, W3)]
        packed = own[:, pl.ds(at + W3, W3 // 2)]
        parts = []
        for s in range(3):
            parts += [packed[:8, 128 * s : 128 * s + 128], packed[8:, 128 * s : 128 * s + 128]]
        rest = jnp.concatenate(parts, 1)
        done = 0
        for c, n in cols:
            step(i, pl.ds(main_at, 16), pl.ds(c, n), main[:, done : done + n], rate)
            step(i, pl.ds(rest_at, 8), pl.ds(c, n), rest[:, done : done + n], rate)
            done += n

    for s in range(3):
        chunk(0, QKV_AT + CW * s, third_cols(s), D ** (-0.5))
    chunk(1, OUT_AT, [(0, W3)], D ** (-0.5))
    for c in range(4):
        chunk(2, UP_AT + CW * c, [(W3 * c, W3)], D ** (-0.5))
    for r in range(6):
        grad = own[:, pl.ds(DOWN_AT + r * D, D)]
        step(3, pl.ds(16 * r, 16), slice(None), grad, FF ** (-0.5))
    stores = [pltpu.make_async_copy(a, b, sem.at[i]) for i, (a, b) in enumerate(zip(outs, outs_h))]
    for cp in stores:
        cp.start()
    for cp in stores + moves:
        cp.wait()


def adam_call(parity, own, nrm, mixed, d_tokens, states):
    hb = pl.BlockSpec(memory_space=pltpu.HBM)
    sm = pl.BlockSpec(memory_space=pltpu.SMEM)
    held = [pltpu.VMEM(a.shape, F32) for a in (own, nrm) + tuple(states) + tuple(states)]
    return pl.pallas_call(
        adam_kernel,
        out_shape=[jax.ShapeDtypeStruct(a.shape, a.dtype) for a in states + (mixed, d_tokens)],
        in_specs=[sm] + [hb] * 16,
        out_specs=[hb] * 14,
        scratch_shapes=held
        + [pltpu.VMEM(mixed.shape, BF), pltpu.VMEM(d_tokens.shape, F32)]
        + [pltpu.SemaphoreType.DMA((16,))],
        compiler_params=pltpu.CompilerParams(vmem_limit_bytes=63 * 2**20),
        cost_estimate=pl.CostEstimate(
            flops=10**7, bytes_accessed=8 * 2**20, transcendentals=10**6
        ),
    )(parity, own, nrm, mixed, d_tokens, *states)


def layer_norm(values, gain, shift):
    center = jnp.mean(values, -1, keepdims=True)
    centered = values - center
    spread = jnp.mean(centered * centered, -1, keepdims=True)
    return centered * lax.rsqrt(spread + EPS_NORM) * gain + shift


def smooth_gate(value):
    return jax.nn.gelu(value, approximate=True)


def plain_shards(tokens, lengths, cotangent, *state):
    w_qkv, m_qkv, v_qkv, w_out, m_out, v_out, w_up, m_up, v_up = state[:9]
    w_down, m_down, v_down, packed, m_packed, v_packed = state[9:]
    seq_count, seq_len, model_width = tokens.shape
    row_count = seq_count * seq_len
    axes = ("dp", "fsdp")
    wqkv_b, wout_b, wup_b, wdown_b, vector_b = [
        lax.all_gather(w.astype(BF), axes, axis=0, tiled=True)
        for w in (w_qkv, w_out, w_up, w_down, packed)
    ]
    vector = vector_b.astype(F32)
    gain_one, bias_one, gain_two, bias_two, bias_attn, bias_down = [
        vector[i * model_width : (i + 1) * model_width] for i in range(6)
    ]
    bias_up = vector[6 * model_width :]
    positions = jnp.arange(seq_len, dtype=jnp.int32)
    live_rows = positions[None, :] < lengths[:, None]
    inputs = tokens.astype(F32).reshape(row_count, model_width)
    normed_one, norm_one_back = jax.vjp(layer_norm, inputs, gain_one, bias_one)
    normed_one_b = normed_one.astype(BF)
    qkv_all = jnp.dot(normed_one_b, wqkv_b, preferred_element_type=F32).astype(BF)
    seqs = [slice(i * seq_len, (i + 1) * seq_len) for i in range(seq_count)]
    ahead = [fwd_call(qkv_all[s], lengths[i : i + 1], 512) for i, s in enumerate(seqs)]
    attended_b = jnp.concatenate([a[0] for a in ahead], 0)
    resid_one = inputs + jnp.dot(attended_b, wout_b, preferred_element_type=F32) + bias_attn
    normed_two, norm_two_back = jax.vjp(layer_norm, resid_one, gain_two, bias_two)
    normed_two_b = normed_two.astype(BF)
    upper = jnp.dot(normed_two_b, wup_b, preferred_element_type=F32) + bias_up
    activ, gate_back = jax.vjp(smooth_gate, upper)
    activ_b = activ.astype(BF)
    mixed = resid_one + jnp.dot(activ_b, wdown_b, preferred_element_type=F32) + bias_down
    mixed = mixed.reshape(seq_count, seq_len, model_width).astype(BF)
    grad_b = jnp.where(live_rows[:, :, None], cotangent, jnp.zeros((), BF))
    grad_b = grad_b.reshape(row_count, model_width)
    grad_full = grad_b.astype(F32)
    d_wdown = jnp.dot(activ_b.T, grad_b, preferred_element_type=F32)
    d_bias_down = jnp.sum(grad_full, 0)
    d_activ = jnp.dot(grad_b, wdown_b.T, preferred_element_type=F32)
    (d_upper,) = gate_back(d_activ)
    d_upper_b = d_upper.astype(BF)
    d_bias_up = jnp.sum(d_upper_b.astype(F32), 0)
    d_wup = jnp.dot(normed_two_b.T, d_upper_b, preferred_element_type=F32)
    d_normed_two = jnp.dot(d_upper_b, wup_b.T, preferred_element_type=F32)
    d_resid_norm, d_gain_two, d_bias_two = norm_two_back(d_normed_two)
    d_resid = grad_full + d_resid_norm
    d_branch_b = d_resid.astype(BF)
    d_bias_attn = jnp.sum(d_branch_b.astype(F32), 0)
    d_wout = jnp.dot(attended_b.T, d_branch_b, preferred_element_type=F32)
    d_attended_b = jnp.dot(d_branch_b, wout_b.T, preferred_element_type=F32).astype(BF)
    back = [
        bwd_call(qkv_all[s], d_attended_b[s], a[1], a[2], lengths[i : i + 1])
        for i, (s, a) in enumerate(zip(seqs, ahead))
    ]
    d_qkv_b = jnp.concatenate([jnp.concatenate(b, 1) for b in back], 0)
    d_wqkv = jnp.dot(normed_one_b.T, d_qkv_b, preferred_element_type=F32)
    d_normed_one = jnp.dot(d_qkv_b, wqkv_b.T, preferred_element_type=F32)
    d_input_norm, d_gain_one, d_bias_one = norm_one_back(d_normed_one)
    d_tokens = (d_resid + d_input_norm).reshape(seq_count, seq_len, model_width)
    d_vector = jnp.concatenate(
        [d_gain_one, d_bias_one, d_gain_two, d_bias_two, d_bias_attn, d_bias_down, d_bias_up]
    )
    owned = [
        lax.psum_scatter(g, axes, scatter_dimension=0, tiled=True)
        for g in (d_wqkv, d_wout, d_wup, d_wdown, d_vector)
    ]
    grad_norm = jnp.sqrt(lax.psum(sum(jnp.sum(g * g) for g in owned), axes))
    factor = jnp.minimum(1.0, CLIP_NORM / (grad_norm + 1e-06))
    rates = (D ** (-0.5), D ** (-0.5), D ** (-0.5), FF ** (-0.5), VECTOR_RATE)
    new = ()
    for i, (g, rate) in enumerate(zip(owned, rates)):
        new += adam_step(*state[3 * i : 3 * i + 3], g * factor, rate)
    return (mixed, d_tokens, grad_norm) + new


def direct_shards(Z, tokens, lengths, cotangent, *state):
    packed, m_packed, v_packed = state[12:]
    dp = lax.axis_index("dp")
    fsdp = lax.axis_index("fsdp")
    n = packed.shape[0]
    start = ((dp * 2 * Z + fsdp) * n) % VEC_COLS
    vec = lax.dynamic_update_slice(
        jnp.zeros((16 * VEC_COLS,), BF), packed.astype(BF), (start,)
    ).reshape(16, VEC_COLS)
    mixed, d_tokens, own, small = mega_call(
        Z, tokens[0], cotangent[0], lengths, state[0], state[3], state[6], state[9], vec
    )
    grad_norm = jnp.sqrt(small[0, 0])
    factor = jnp.minimum(1.0, CLIP_NORM / (grad_norm + 1e-06))
    parity = (fsdp % 2).astype(jnp.int32).reshape(1)
    *new, mixed, d_tokens = adam_call(parity, own, small, mixed, d_tokens, state[:12])
    g_vec = lax.dynamic_slice(small[8:].reshape(-1), (start,), (n,))
    new_vec = adam_step(packed, m_packed, v_packed, g_vec * factor, VECTOR_RATE)
    return (mixed[None], d_tokens[None], grad_norm) + tuple(new) + new_vec


def solution(mesh):
    rows = P(("dp", "fsdp"), None)
    seqs = P(("dp", "fsdp"), None, None)
    flat = P(("dp", "fsdp"))
    in_specs = (seqs, flat, seqs) + (rows,) * 12 + (flat,) * 3
    out_specs = (seqs, seqs, P()) + (rows,) * 12 + (flat,) * 3
    dp, fsdp = mesh.shape["dp"], mesh.shape["fsdp"]

    def shards(*args):
        tokens, w_qkv = args[0], args[3]
        fits = (
            dp == 4
            and fsdp == 8
            and tokens.shape[0] == 1
            and tokens.shape[1] == 1024
            and w_qkv.shape[0] * dp * fsdp == D
        )
        step = functools.partial(direct_shards, fsdp // 2) if fits else plain_shards
        return step(*args)

    return jax.shard_map(
        shards, mesh=mesh, in_specs=in_specs, out_specs=out_specs, check_vma=False
    )
```

```python
import functools

import jax
import jax.numpy as jnp
from jax import lax
from jax.experimental import pallas as pl
from jax.experimental.pallas import tpu as pltpu
from jax.sharding import PartitionSpec as P

D = 768
FF = 3072
HEAD_DIM = 64
STEP = 10
HD = 64
F32 = jnp.float32
BF = jnp.bfloat16
MESH = pl.DeviceIdType.MESH

EPS_NORM = 1e-05
CLIP_NORM = 1.0
BETA_ONE = 0.9
BETA_TWO = 0.95
ADAM_EPSILON = 1e-08
DECAY_RATE = 0.1
VECTOR_RATE = 0.2


def nt(a,b): return lax.dot_general(a,b,(((1,),(1,)),((),())),preferred_element_type=F32)
def nn(a,b): return jnp.dot(a,b,preferred_element_type=F32)
def head_mask(rows):
    lane=lax.broadcasted_iota(jnp.int32,(rows,128),1)
    return (lane<HD)
def half(x,h,scale=1.0):
    m=head_mask(x.shape[0]); m = m if h==0 else jnp.logical_not(m)
    return jnp.where(m,x*jnp.asarray(scale,x.dtype),jnp.zeros_like(x))

def attn_fwd_pair(q_ref,k_ref,v_ref,length,o_ref,oT_ref,lse_ref,QB):
    L=q_ref.shape[0]
    n=L//QB
    vT=v_ref[...].T
    lane=lax.broadcasted_iota(jnp.int32,(L,128),1)
    dead=jnp.where(lax.broadcasted_iota(jnp.int32,(L,128),0)<length,0.0,-1e9).astype(BF)
    keys=[jnp.where(lane==HD-HD*h,dead,k_ref[...]) for h in range(2)]
    ql=lax.broadcasted_iota(jnp.int32,(QB,128),1)
    tri=lax.broadcasted_iota(jnp.int32,(QB,QB),0)<=lax.broadcasted_iota(jnp.int32,(QB,QB),1)
    def scores(i,h):
        qh=jnp.where(ql==HD-HD*h,jnp.ones((),BF),half(q_ref[pl.ds(i*QB,QB),:],h,0.125))
        return nt(keys[h][:(i+1)*QB],qh)
    jobs=[(i,h) for i in range(n) for h in range(2)]
    now=scores(*jobs[0])
    outs=[]
    for x,(i,h) in enumerate(jobs):
        later=scores(*jobs[x+1]) if x+1<len(jobs) else None
        nk=(i+1)*QB
        s=jnp.where(tri,now[nk-QB:],-1e9)
        if i: s=jnp.concatenate([now[:nk-QB],s],0)
        m=jnp.max(s,0,keepdims=True)
        e=jnp.exp(s-m)
        l=jnp.sum(e,0,keepdims=True)
        outs.append(nn(vT[HD*h:HD*h+HD,:nk],e.astype(BF))/l)
        lse_ref[pl.ds(h,1),pl.ds(i*QB,QB)]=m+jnp.log(l)
        if h==1:
            oT=jnp.concatenate(outs,0); outs=[]
            oT_ref[:,pl.ds(i*QB,QB)]=oT
            o_ref[pl.ds(i*QB,QB),:]=oT.T.astype(BF)
        now=later

def attn_bwd_pair(q_ref,k_ref,v_ref,do_ref,oT_ref,lse_ref,length,dq_ref,dk_ref,dv_ref,dk_acc,dv_acc,QB,tick=None):
    L=q_ref.shape[0]
    n=L//QB
    kT=k_ref[...].T
    jobs=list(reversed(range(n)))
    tri=lax.broadcasted_iota(jnp.int32,(QB,2*QB),0)<=lax.rem(lax.broadcasted_iota(jnp.int32,(QB,2*QB),1),QB)
    def products(i):
        nk=(i+1)*QB; sl=pl.ds(i*QB,QB)
        q=q_ref[sl,:]; do=do_ref[sl,:]
        qm=jnp.concatenate([half(q,0,0.125),half(q,1,0.125)],0)
        dom=jnp.concatenate([half(do,0),half(do,1)],0)
        return nt(k_ref[pl.ds(0,nk),:],qm),nt(v_ref[pl.ds(0,nk),:],dom),qm,dom
    now=products(jobs[0])
    for x,i in enumerate(jobs):
        split=tick is not None and x==1
        later=products(jobs[x+1]) if x+1<n and not (tick is not None and x==0) else None
        if split:
            tick(1)
            now=products(i)
        nk=(i+1)*QB; sl=pl.ds(i*QB,QB)
        s,dp,qm,dom=now
        prod=do_ref[sl,:].astype(F32).T*oT_ref[:,sl]
        delta=jnp.concatenate([jnp.sum(prod[:HD],0,keepdims=True),jnp.sum(prod[HD:],0,keepdims=True)],1)
        live=(i*QB+lax.broadcasted_iota(jnp.int32,(1,QB),1))<length
        lse=jnp.concatenate([jnp.where(live,lse_ref[pl.ds(h,1),sl],1e30) for h in range(2)],1)
        p=jnp.exp(s-lse)
        pd=jnp.where(tri,p[nk-QB:],0.0)
        p=pd if i==0 else jnp.concatenate([p[:nk-QB],pd],0)
        ds=(p*(dp-delta)).astype(BF)
        dv=nn(p.astype(BF),dom); dk=nn(ds,qm)
        dq=[nn(kT[HD*h:HD*h+HD,:nk],ds[:,QB*h:QB*h+QB]) for h in range(2)]
        dq_ref[sl,:]=(jnp.concatenate(dq,0)*0.125).T.astype(BF)
        if i==n-1:
            dk_acc[...]=dk; dv_acc[...]=dv
        else:
            dk_acc[pl.ds(0,nk),:]+=dk; dv_acc[pl.ds(0,nk),:]+=dv
        now=later
    dk_ref[...]=dk_acc[...].astype(BF); dv_ref[...]=dv_acc[...].astype(BF)

def fwd_call(qkv,length,QB=256):
    L=qkv.shape[0]; D=qkv.shape[1]//3; NP=D//128
    def k(len_ref,q,k_,v,o,oT,lse):
        attn_fwd_pair(q,k_,v,len_ref[0],o,oT,lse.at[0],QB)
    return pl.pallas_call(k,grid=(NP,),
      in_specs=[pl.BlockSpec(memory_space=pltpu.SMEM)]+[pl.BlockSpec((L,128),functools.partial(lambda off,p:(0,off+p),j*NP)) for j in range(3)],
      out_specs=[pl.BlockSpec((L,128),lambda p:(0,p)),pl.BlockSpec((128,L),lambda p:(p,0)),pl.BlockSpec((1,2,L),lambda p:(p,0,0))],
      out_shape=[jax.ShapeDtypeStruct((L,D),BF),jax.ShapeDtypeStruct((D,L),F32),jax.ShapeDtypeStruct((NP,2,L),F32)],
      compiler_params=pltpu.CompilerParams(vmem_limit_bytes=56*2**20),
      cost_estimate=pl.CostEstimate(flops=4*L*L*D//2,bytes_accessed=10*2**20,transcendentals=12*L*L//2))(length,qkv,qkv,qkv)
def bwd_call(qkv,do,oT,lse,length,QB=256):
    L=qkv.shape[0]; D=qkv.shape[1]//3; NP=D//128
    def k(len_ref,q,k_,v,do,oT,lse,dq,dk,dv,dka,dva):
        attn_bwd_pair(q,k_,v,do,oT,lse.at[0],len_ref[0],dq,dk,dv,dka,dva,QB)
    blk=pl.BlockSpec((L,128),lambda p:(0,p))
    return pl.pallas_call(k,grid=(NP,),
      in_specs=[pl.BlockSpec(memory_space=pltpu.SMEM)]+[pl.BlockSpec((L,128),functools.partial(lambda off,p:(0,off+p),j*NP)) for j in range(3)]+[blk,pl.BlockSpec((128,L),lambda p:(p,0)),pl.BlockSpec((1,2,L),lambda p:(p,0,0))],
      out_specs=[blk]*3,
      out_shape=[jax.ShapeDtypeStruct((L,D),BF)]*3,
      scratch_shapes=[pltpu.VMEM((L,128),F32)]*2,
      compiler_params=pltpu.CompilerParams(vmem_limit_bytes=56*2**20),
      cost_estimate=pl.CostEstimate(flops=10*L*L*D//2,bytes_accessed=14*2**20,transcendentals=12*L*L//2))(length,qkv,qkv,qkv,do,oT,lse)


class Place:
    def __init__(self, Z):
        dp=lax.axis_index("dp"); fs=lax.axis_index("fsdp")
        self.Z=Z; self.y=dp//2; self.c=dp%2; self.z=fs//2; self.x=fs%2
        self.nx=(dp,self.z*2+1-self.x)
        self.ny=((1-self.y)*2+self.c,fs)
        self.nc=(self.y*2+1-self.c,fs)
        self.me=self.piece(self.z)
        self.dp=dp; self.fs=fs
    def nz(self,z): return (self.dp,z*2+self.x)
    def piece(self,z,dx=0,dy=0,dc=0):
        y=self.y if dy==0 else 1-self.y
        x=self.x if dx==0 else 1-self.x
        c=self.c if dc==0 else 1-self.c
        return (y*2+c,z,x)
    def slab(self,y,dc=0):
        c=self.c if dc==0 else 1-self.c
        return y*2+c

def rcopy(src,dst,ss,rs,dev):
    return pltpu.make_async_remote_copy(src_ref=src,dst_ref=dst,send_sem=ss,recv_sem=rs,device_id=dev,device_id_type=MESH)

def when(cond,fn):
    if cond is True: fn()
    else: pl.when(cond)(fn)

def gather_sems(NG,Z):
    D=pltpu.SemaphoreType.DMA
    return [D((NG*2*(Z-1),)),D((NG*2*(Z-1),)),
            D((NG*2*Z,)),D((NG*2*Z,)),
            D((NG*2*Z,)),D((NG*2*Z,)),
            D((NG*2,)),D((NG*2,)),
            D((NG*2*(Z-1),)),D((NG*2*(Z-1),))]

class Gather:
    def __init__(self,P,G,groups,sems):
        self.P=P; self.G=G; self.groups=groups
        self.zs,self.zr,self.xs,self.xr,self.ys,self.yr,self.cs,self.cr,self.fs,self.fr=sems
    def direct(self,g):
        lo,n,a,p,q=self.groups[g]
        return p+q==n
    def _cp(self,idx,lo,n,ss,rs,dev):
        r=self.G.at[(*idx,slice(None),pl.ds(lo,n))]
        return rcopy(r,r,ss,rs,dev)
    def zcp(self,g,d,t,zo,to):
        lo,n=self.groups[g][:2]; i=(g*2+d)*(self.P.Z-1)+t
        return self._cp(self.P.piece(zo),lo,n,self.zs.at[i],self.zr.at[i],self.P.nz(to))
    def zdiag(self,g,d,t,zo,to):
        lo,n,a,p,q=self.groups[g]; i=(g*2+d)*(self.P.Z-1)+t
        return self._cp(self.P.piece(zo,dx=1,dy=1),lo+p,n-p-q,self.fs.at[i],self.fr.at[i],self.P.nz(to))
    def xfull(self,g,zo,arrive=0):
        lo,n=self.groups[g][:2]; i=g*2*self.P.Z+zo
        return self._cp(self.P.piece(zo,dx=arrive),lo,n,self.xs.at[i],self.xr.at[i],self.P.nx)
    def yfull(self,g,zo,arrive=0):
        lo,n=self.groups[g][:2]; i=g*2*self.P.Z+zo
        return self._cp(self.P.piece(zo,dy=arrive),lo,n,self.ys.at[i],self.yr.at[i],self.P.ny)
    def ydiag(self,g,zo,near,arrive=0):
        lo,n,a,p,q=self.groups[g]; i=g*2*self.P.Z+self.P.Z+zo
        return self._cp(self.P.piece(zo,dx=1,dy=arrive),lo,a if near else p,self.ys.at[i],self.yr.at[i],self.P.ny)
    def xdiag(self,g,zo,near,arrive=0):
        lo,n,a,p,q=self.groups[g]; i=g*2*self.P.Z+self.P.Z+zo
        w=n-a if near else q
        return self._cp(self.P.piece(zo,dy=1,dx=arrive),lo+n-w,w,self.xs.at[i],self.xr.at[i],self.P.nx)
    def ccp(self,g,k,arrive=0):
        lo,n=self.groups[g][:2]
        y=self.P.y if k==0 else 1-self.P.y
        r=self.G.at[self.P.slab(y,dc=arrive),:,:,:,pl.ds(lo,n)]
        return rcopy(r,r,self.cs.at[g*2+k],self.cr.at[g*2+k],self.P.nc)
    def others(self,t,f):
        when(self.P.z>=t,lambda: f(self.P.z-t)); when(self.P.z<self.P.Z-t,lambda: f(self.P.z+t))
    def own(self,g):
        z=self.P.z; Z=self.P.Z
        self.xfull(g,z).start(); self.yfull(g,z).start()
        for t in range(Z-1 if self.direct(g) else 1):
            when(z<Z-1-t,lambda: self.zcp(g,0,t,z,z+1+t).start())
            when(z>t,lambda: self.zcp(g,1,t,z,z-1-t).start())
    def zarrive(self,g,t):
        z=self.P.z; Z=self.P.Z
        on=t+1<Z-1 and not self.direct(g)
        def below():
            zo=z-1-t
            self.zcp(g,0,t,zo,z).wait_recv()
            if on: when(z<Z-1,lambda: self.zcp(g,0,t+1,zo,z+1).start())
            self.xfull(g,zo).start(); self.yfull(g,zo).start()
        def above():
            zo=z+1+t
            self.zcp(g,1,t,zo,z).wait_recv()
            if on: when(z>0,lambda: self.zcp(g,1,t+1,zo,z-1).start())
            self.xfull(g,zo).start(); self.yfull(g,zo).start()
        when(z>t,below); when(z<Z-1-t,above)
    def diag(self,g,t):
        def pass_on(zo):
            self.xfull(g,zo,1).wait_recv(); self.ydiag(g,zo,t==0).start()
            self.yfull(g,zo,1).wait_recv(); self.xdiag(g,zo,t==0).start()
        if t==0: pass_on(self.P.z)
        else: self.others(t,pass_on)
    def line(self,g,t):
        z=self.P.z; Z=self.P.Z
        if t==0:
            self.ydiag(g,z,True,1).wait_recv(); self.xdiag(g,z,True,1).wait_recv()
            when(z<Z-1,lambda: self.zdiag(g,0,0,z,z+1).start())
            when(z>0,lambda: self.zdiag(g,1,0,z,z-1).start())
            return
        def below():
            self.zdiag(g,0,t-1,z-t,z).wait_recv()
            if t<Z-1: when(z<Z-1,lambda: self.zdiag(g,0,t,z-t,z+1).start())
        def above():
            self.zdiag(g,1,t-1,z+t,z).wait_recv()
            if t<Z-1: when(z>0,lambda: self.zdiag(g,1,t,z+t,z-1).start())
        when(z>=t,below); when(z<Z-t,above)
    def corner(self,g):
        self.ccp(g,0).start()
        if self.direct(g):
            self.ydiag(g,self.P.z,True,1).wait_recv(); self.xdiag(g,self.P.z,True,1).wait_recv()
        else: self.line(g,self.P.Z-1)
        def come(zo):
            self.ydiag(g,zo,False,1).wait_recv(); self.xdiag(g,zo,False,1).wait_recv()
        for t in range(1,self.P.Z): self.others(t,come)
        self.ccp(g,1).start()
    def sibling(self,g):
        self.ccp(g,0,1).wait_recv(); self.ccp(g,1,1).wait_recv()
    def drain(self,g):
        z=self.P.z; Z=self.P.Z
        def sent(zo,near):
            self.xfull(g,zo).wait_send(); self.yfull(g,zo).wait_send()
            self.xdiag(g,zo,near).wait_send(); self.ydiag(g,zo,near).wait_send()
        sent(z,True)
        for t in range(1,Z): self.others(t,lambda zo: sent(zo,False))
        for k in range(2): self.ccp(g,k).wait_send()
        for t in range(Z-1):
            if self.direct(g):
                when(z<Z-1-t,lambda: self.zcp(g,0,t,z,z+1+t).wait_send())
                when(z>t,lambda: self.zcp(g,1,t,z,z-1-t).wait_send())
                continue
            def up():
                self.zcp(g,0,t,z-t,z+1).wait_send(); self.zdiag(g,0,t,z-t,z+1).wait_send()
            def down():
                self.zcp(g,1,t,z+t,z-1).wait_send(); self.zdiag(g,1,t,z+t,z-1).wait_send()
            when(jnp.logical_and(z<Z-1,z>=t),up)
            when(jnp.logical_and(z>0,z<=Z-1-t),down)
    def events(self,g):
        Z=self.P.Z
        ev=[lambda: self.own(g)]
        for t in range(Z):
            if t<Z-1: ev.append(lambda t=t: self.zarrive(g,t))
            if t and not self.direct(g): ev.append(lambda t=t: self.line(g,t-1))
            ev.append(lambda t=t: self.diag(g,t))
        ev.append(lambda: self.corner(g))
        ev.append(lambda: self.sibling(g))
        return ev


SLOT = 1152
NB=12
def rs_sems(NG,Z):
    D=pltpu.SemaphoreType.DMA
    return [D((NG*2,)),D((NG*2,)),
            D((NG*3,)),D((NG*3,)),
            D((NG*2,)),D((NG*2,)),
            D((NG*Z,)),D((NG*Z,))]
def rs_bufs(Z):
    V=lambda *s: pltpu.VMEM(s,BF)
    h=640
    v=128
    return [V(2,2,Z,2,16,SLOT),V(2,Z,2,16,h),V(2,Z,16,h),V(2,2,Z,16,h),V(2,Z,16,h),V(4,Z,16,SLOT),
            V(1,2,Z,2,16,v),V(1,Z,2,16,v),V(1,Z,16,v),V(1,2,Z,16,v),V(1,Z,16,v),V(1,Z,16,v)]
class Scatter:
    def __init__(self,P,R,groups,bufs,sems):
        self.P=P; self.R=R; self.groups=groups; self.bufs=bufs
        self.cs,self.cr,self.xs,self.xr,self.ys,self.yr,self.zs,self.zr=sems
    def buf(self,g,i,w):
        b=self.bufs[i+(NB//2 if g==len(self.groups)-1 else 0)]
        b=b.at[g%b.shape[0]]
        nd=len(b.shape)
        return b.at[(slice(None),)*(nd-1)+(pl.ds(0,w),)]
    def row(self,dy=0,dc=0):
        y=self.P.y if dy==0 else 1-self.P.y
        c=self.P.c if dc==0 else 1-self.P.c
        return y*2+c
    def add(self,dst,src):
        def body(z,_):
            d=dst(z); s=src(z)
            d[...]=d[...]+s[...]
            return 0
        lax.fori_loop(0,self.P.Z,body,0)
    def ccp(self,g,k):
        lo,n,_=self.groups[g]
        return rcopy(self.R.at[self.row(k,1),:,:,:,pl.ds(lo,n)],self.buf(g,0,n).at[k],self.cs.at[g*2+k],self.cr.at[g*2+k],self.P.nc)
    def x1(self,g,k):
        lo,n,a=self.groups[g]
        return rcopy(self.R.at[self.row(k),:,1-self.P.x,:,pl.ds(lo+a,n-a)],self.buf(g,3,n-a).at[k],self.xs.at[g*3+k],self.xr.at[g*3+k],self.P.nx)
    def y1(self,g):
        lo,n,a=self.groups[g]
        return rcopy(self.R.at[self.row(1),:,:,:,pl.ds(lo,a)],self.buf(g,1,a),self.ys.at[g*2],self.yr.at[g*2],self.P.ny)
    def x2(self,g):
        lo,n,a=self.groups[g]
        return rcopy(self.R.at[self.row(0),:,1-self.P.x,:,pl.ds(lo,a)],self.buf(g,2,a),self.xs.at[g*3+2],self.xr.at[g*3+2],self.P.nx)
    def y2(self,g):
        lo,n,a=self.groups[g]
        return rcopy(self.R.at[self.row(1),:,self.P.x,:,pl.ds(lo+a,n-a)],self.buf(g,4,n-a),self.ys.at[g*2+1],self.yr.at[g*2+1],self.P.ny)
    def zc(self,g,src,to):
        lo,n,_=self.groups[g]; Z=self.P.Z
        return rcopy(self.R.at[self.row(0),to,self.P.x,:,pl.ds(lo,n)],self.buf(g,5,n).at[src],self.zs.at[g*Z+to],self.zr.at[g*Z+src],self.P.nz(to))
    def both(self,g): return self.groups[g][1]>self.groups[g][2]
    def s_c(self,g):
        self.ccp(g,1).start(); self.ccp(g,0).start()
    def a_c(self,g):
        lo,n,a=self.groups[g]; R=self.R; b=self.buf(g,0,n)
        for k in (1,0):
            self.ccp(g,k).wait_recv()
            r=self.row(k)
            self.add(lambda z: R.at[r,z,:,:,pl.ds(lo,n)],lambda z: b.at[k,z])
            if self.both(g): self.x1(g,k).start()
            if k==1: self.y1(g).start()
    def a_1(self,g):
        lo,n,a=self.groups[g]; R=self.R; P=self.P; B1=self.buf(g,1,a)
        self.y1(g).wait_recv()
        r=self.row(0)
        self.add(lambda z: R.at[r,z,:,:,pl.ds(lo,a)],lambda z: B1.at[z])
        if self.both(g):
            B3=self.buf(g,3,n-a)
            for k in (1,0):
                self.x1(g,k).wait_recv()
                q=self.row(k)
                self.add(lambda z: R.at[q,z,P.x,:,pl.ds(lo+a,n-a)],lambda z: B3.at[k,z])
            self.y2(g).start()
        self.x2(g).start()
    def a_2(self,g):
        lo,n,a=self.groups[g]; R=self.R; P=self.P; Z=P.Z; B2=self.buf(g,2,a)
        r=self.row(0)
        self.x2(g).wait_recv()
        self.add(lambda z: R.at[r,z,P.x,:,pl.ds(lo,a)],lambda z: B2.at[z])
        if self.both(g):
            B4=self.buf(g,4,n-a)
            self.y2(g).wait_recv()
            self.add(lambda z: R.at[r,z,P.x,:,pl.ds(lo+a,n-a)],lambda z: B4.at[z])
        for d in range(Z-1,0,-1):
            when(P.z>=d,lambda: self.zc(g,P.z,P.z-d).start())
            when(P.z<Z-d,lambda: self.zc(g,P.z,P.z+d).start())
    def final(self,g,out):
        lo,n,_=self.groups[g]; P=self.P; Z=P.Z; z=P.z
        out[...]=self.R[self.row(0),z,P.x,:,pl.ds(lo,n)].astype(F32)
        for zo in range(Z):
            def take():
                self.zc(g,zo,z).wait_recv()
                out[...]+=self.buf(g,5,n)[zo].astype(F32)
            when(z!=zo,take)
    def drain(self,g):
        Z=self.P.Z; z=self.P.z
        for k in range(2):
            self.ccp(g,k).wait_send()
            if self.both(g): self.x1(g,k).wait_send()
        self.x2(g).wait_send(); self.y1(g).wait_send()
        if self.both(g): self.y2(g).wait_send()
        for zo in range(Z):
            when(z!=zo,lambda: self.zc(g,z,zo).wait_send())
    def events(self,g,out):
        return [lambda: self.s_c(g),lambda: self.a_c(g),lambda: self.a_1(g),lambda: self.a_2(g),lambda: self.final(g,out)]

def norm_sems(Z):
    D=pltpu.SemaphoreType.DMA
    return [D((8*Z,)),D((8*Z,))]
def norm_bufs(Z): return [pltpu.VMEM((8*Z,8,128),F32),pltpu.VMEM((1,8,128),F32)]
def everyone(P):
    n=8*P.Z
    for k in range(1,n):
        i=lax.rem(P.dp*2*P.Z+P.fs+k,n)
        yield k,i,(i//(2*P.Z),lax.rem(i,2*P.Z))
def all_sum(P,buf,got,ss,rs):
    n=8*P.Z
    me=P.dp*2*P.Z+P.fs
    buf[me]=got[0]
    for k,i,dev in everyone(P):
        rcopy(got.at[0],buf.at[me],ss.at[k],rs.at[me],dev).start()
    for k,i,dev in everyone(P):
        rcopy(got.at[0],buf.at[i],ss.at[k],rs.at[i],dev).wait_recv()
    tot=buf[0]
    for i in range(1,n): tot=tot+buf[i]
    for k,i,dev in everyone(P):
        rcopy(got.at[0],buf.at[me],ss.at[k],rs.at[me],dev).wait_send()
    return tot
def announce(P,Z):
    bar=pltpu.get_barrier_semaphore()
    for _,_,d in everyone(P): pl.semaphore_signal(bar,inc=1,device_id=d,device_id_type=MESH)
    return bar


W3 = 768
CW = 1152
QKV_AT = 0
VEC_AT = 3456
VEC_COLS = 128
OUT_AT = 3584
DOWN_AT = 4736
UP_AT = 9344
COLS = 13952
GATHER = [(2304, 1280, 640, 640, 640), (0, 2304, 1152, 384, 384), (3584, 5760, 2944, 1024, 896),
          (9344, 1152, 640, 256, 128), (10496, 1152, 512, 128, 256), (11648, 2304, 1152, 384, 384)]
SCATTER = ([(UP_AT + CW * c, CW, 640 if c % 2 else 512) for c in range(4)]
           + [(DOWN_AT + CW * c, CW, 640 if c % 2 else 512) for c in range(4)]
           + [(OUT_AT, CW, 512), (0, CW, 640), (CW, CW, 512), (2 * CW, 640, 256), (2 * CW + 640, 512, 256), (VEC_AT, VEC_COLS, VEC_COLS)])

def al(v, m): return pl.multiple_of(v, m)

def third_cols(s): return [(D * j + 256 * s, 256) for j in range(3)]

def pack_rows(G, me, at, main, rest):
    G[(*me,slice(None),pl.ds(at,W3))]=main.astype(BF)
    parts=[jnp.concatenate([rest[:,256*s:256*s+128],rest[:,256*s+128:256*s+256]],0) for s in range(3)]
    G[(*me,slice(None),pl.ds(al(at+W3,128),W3//2))]=jnp.concatenate(parts,1).astype(BF)

def pack_own_vec(G, me, vec, wide, start):
    wide[...]=jnp.zeros_like(wide)
    wide[0:1,0:vec.shape[1]]=vec[...]
    n=3*VEC_COLS
    i=lax.broadcasted_iota(jnp.int32,(n,n),0); j=lax.broadcasted_iota(jnp.int32,(n,n),1)
    row=nn(wide[...].astype(BF),jnp.where(j==i+start,1.0,0.0).astype(BF))[0:1]
    parts=[row[:,VEC_COLS*k:VEC_COLS*k+VEC_COLS] for k in range(3)]+[jnp.zeros((13,VEC_COLS),F32)]
    G[(*me,slice(None),pl.ds(VEC_AT,VEC_COLS))]=jnp.concatenate(parts,0).astype(BF)

def pack_own(place, G, wqkv, wout, wup, wdown, vec, wide, start, first):
    me=place.me
    lo=al(8*place.x,8); ro=al(16*(1-place.x),8)
    def cols(w,cs):
        return [jnp.concatenate([w[pl.ds(a,n),pl.ds(c,k)] for c,k in cs],1) for a,n in ((lo,16),(ro,8))]
    for s in ((2,) if first else (0,1)): pack_rows(G,me,QKV_AT+CW*s,*cols(wqkv,third_cols(s)))
    if first:
        pack_own_vec(G,me,vec,wide,start)
        return
    pack_rows(G,me,OUT_AT,*cols(wout,[(0,W3)]))
    for c in range(4): pack_rows(G,me,UP_AT+CW*c,*cols(wup,[(W3*c,W3)]))
    for r in range(6):
        G[(*me,slice(None),pl.ds(DOWN_AT+r*D,D))]=wdown[pl.ds(16*r,16),:].astype(BF)

def unpack24(G, at, dst):
    Z=G.shape[1]
    def body(j,_):
        r=al(j*48,16); d=j//Z; z=lax.rem(j,Z)
        dst[pl.ds(r,16),:]=G[d,z,0,:,pl.ds(al(at,128),W3)]
        dst[pl.ds(r+32,16),:]=G[d,z,1,:,pl.ds(al(at,128),W3)]
        a=G[d,z,0,:,pl.ds(al(at+W3,128),W3//2)].astype(F32)
        b=G[d,z,1,:,pl.ds(al(at+W3,128),W3//2)].astype(F32)
        parts=[]
        for s in range(3):
            q=slice(128*s,128*s+128)
            parts+=[jnp.concatenate([a[:8,q],b[:8,q]],0),jnp.concatenate([a[8:,q],b[8:,q]],0)]
        dst[pl.ds(r+16,16),:]=jnp.concatenate(parts,1).astype(BF)
        return 0
    lax.fori_loop(0,G.shape[0]*Z,body,0)

def pack24(G, at, src):
    Z=G.shape[1]
    def body(j,_):
        r=al(j*48,16); d=j//Z; z=lax.rem(j,Z)
        pack_rows(G,(d,z,0),al(at,128),src[pl.ds(r,16),:],src[pl.ds(al(r+16,8),8),:])
        pack_rows(G,(d,z,1),al(at,128),src[pl.ds(r+32,16),:],src[pl.ds(al(r+24,8),8),:])
        return 0
    lax.fori_loop(0,G.shape[0]*Z,body,0)

def unpack_down(G, c, dst):
    def body(k,_):
        for r in range(6):
            dst[pl.ds(al(k*96+16*r,16),16),:]=G[c,k//2,lax.rem(k,2),:,pl.ds(DOWN_AT+r*D,D)]
        return 0
    lax.fori_loop(0,2*G.shape[1],body,0)

def pack_down(G, c, src):
    def body(k,_):
        for r in range(6):
            G[c,k//2,lax.rem(k,2),:,pl.ds(DOWN_AT+r*D,D)]=src[pl.ds(al(k*96+16*r,16),16),:].astype(BF)
        return 0
    lax.fori_loop(0,2*G.shape[1],body,0)

def vec_shift(k): return (240*k)//128

def unpack_vec(G, V, V1):
    V[...]=jnp.zeros_like(V)
    Z=G.shape[1]
    for k in range(8*Z):
        V[pl.ds(vec_shift(k),3),:]+=G[k//(2*Z),k//2%Z,k%2,:,pl.ds(VEC_AT,VEC_COLS)].astype(F32)[0:3]
    for t in range(60):
        V1[:,pl.ds(128*t,128)]=V[pl.ds(t,1),:]

def pack_vec(G, V, V1):
    V[...]=jnp.zeros_like(V)
    for t in range(60):
        V[pl.ds(t,1),:]=V1[:,pl.ds(128*t,128)]
    Z=G.shape[1]
    for k in range(8*Z):
        G[k//(2*Z),k//2%Z,k%2,:,pl.ds(VEC_AT,VEC_COLS)]=V[pl.ds(vec_shift(k),16),:].astype(BF)

def norm_parts(x):
    c=x-jnp.mean(x,-1,keepdims=True)
    s=lax.rsqrt(jnp.mean(c*c,-1,keepdims=True)+EPS_NORM)
    return c*s,s

def norm_back(dx, xh, s):
    return s*(dx-jnp.mean(dx,-1,keepdims=True)-xh*jnp.mean(dx*xh,-1,keepdims=True))

def gelu_both(u):
    k0=0.7978845608028654; k1=0.044715
    u2=u*u
    t=jnp.tanh(k0*(u*(1.0+k1*u2)))
    h=0.5*(1.0+t)
    return u*h, h+(0.5*k0)*u*(1.0-t*t)*(1.0+(3.0*k1)*u2)

RB=256

RULES=((1,1,0),(2,3,1),(2,4,3))

def places():
    p=[("in",0,0.7),("in",1,0.8)]+[("stat",i,0.6) for i in range(4)]
    for i in range(3):
        p.append(("third",i,0.6 if i else 2.0))
        p+=[("qkv",4*i+k,0.42) for k in range(4)]
        p+=[("af",2*i+pp,2.1) for pp in range(2)]
    p.append(("out",0,0.6))
    p+=[("ob",k,1.1) for k in range(4)]
    for c in range(4):
        p.append(("chunk",c,0.5))
        p+=[("mr",4*c+k,1.7) for k in range(4)]
        p+=[("mw",3*c+k,0.6+0.15*(k==2)) for k in range(3)]
        p+=[("mu",3*c+k,0.6+0.2*(k==2)) for k in range(3)]
        p.append(("mp",c,0.1))
    p.append(("fin",0,1.0))
    p+=[("bb",k,1.3) for k in range(4)]
    p+=[("bw",k,0.6+0.2*(k==2)) for k in range(3)]
    p.append(("bp",0,0.4))
    for i in range(3):
        for pp in range(2): p+=[("ab",4*i+2*pp+k,(1.6,2.1)[k]) for k in range(2)]
        p+=[("dq",3*i+k,0.6+0.2*(k==2)) for k in range(3)]
        p.append(("dp",i,0.1))
        p+=[("dh",4*i+k,0.5) for k in range(4)]
    p+=[("ln",k,0.35+0.4*(k==3)) for k in range(4)]
    p.append(("lp",0,0.1))
    p+=[("lx",k,0.45) for k in range(4)]
    return p

def ready_places():
    return [("mp",c) for c in range(4)]+[("mp",3)]*4+[("bp",0)]+[("dp",i) for i in (0,1,2,2)]+[("lp",0)]

def due_places():
    return [("third",0),("third",1),("out",0),("chunk",0),("chunk",1),("chunk",2)]

class Clock:
    def __init__(self, plan, ga, sc, own):
        names=[p[:2] for p in places()]
        index={p:i for i,p in enumerate(names)}
        fns={}
        for g in range(len(GATHER)):
            for k,f in enumerate(ga.events(g)): fns[(0,g,k)]=f
        for g,(lo,n,_) in enumerate(SCATTER):
            for k,f in enumerate(sc.events(g,own.at[:,pl.ds(lo,n)])): fns[(1,g,k)]=f
        check_plan(plan,set(fns),index)
        self.slots={}
        self.tail=[]
        for i,*key in plan:
            if i<len(names): self.slots.setdefault(names[i],[]).append(fns[tuple(key)])
            else: self.tail.append(fns[tuple(key)])
    def at(self, name, step, count):
        for k in range(count):
            todo=self.slots.get((name,k))
            if todo:
                def run(todo=todo):
                    for f in todo: f()
                if isinstance(step,int):
                    if step==k: run()
                else: pl.when(step==k)(run)

PLAN = (
    (0, 0, 0, 0), (1, 0, 1, 0), (1, 0, 2, 0), (1, 0, 0, 1), (1, 0, 0, 2), (1, 0, 0, 3), (1, 0, 1, 1), (1, 0, 1, 2),
    (1, 0, 0, 4), (1, 0, 0, 5), (1, 0, 1, 3), (1, 0, 1, 4), (2, 0, 0, 6), (2, 0, 0, 7), (3, 0, 2, 1), (3, 0, 3, 0),
    (3, 0, 1, 5), (3, 0, 1, 6), (4, 0, 2, 2), (5, 0, 1, 7), (6, 0, 0, 8), (6, 0, 0, 9), (8, 0, 1, 8), (8, 0, 1, 9),
    (8, 0, 1, 10), (9, 0, 2, 3), (12, 0, 2, 4), (12, 0, 1, 11), (13, 0, 1, 12), (14, 0, 3, 1), (15, 0, 2, 5),
    (15, 0, 2, 6), (16, 0, 3, 2), (17, 0, 2, 7), (19, 0, 5, 0), (20, 0, 3, 3), (20, 0, 2, 8), (21, 0, 3, 4),
    (22, 0, 4, 0), (22, 0, 2, 9), (24, 0, 2, 10), (25, 0, 3, 5), (25, 0, 3, 6), (26, 0, 5, 1), (26, 0, 3, 7),
    (26, 0, 3, 8), (26, 0, 2, 11), (26, 0, 4, 1), (27, 0, 4, 2), (27, 0, 4, 3), (27, 0, 3, 9), (27, 0, 2, 12),
    (27, 0, 3, 10), (28, 0, 5, 2), (29, 0, 4, 4), (29, 0, 4, 5), (30, 0, 3, 11), (31, 0, 5, 3), (31, 0, 5, 4),
    (31, 0, 5, 5), (31, 0, 4, 6), (32, 0, 3, 12), (32, 0, 4, 7), (35, 0, 5, 6), (35, 0, 5, 7), (35, 0, 4, 8),
    (35, 0, 4, 9), (35, 0, 4, 10), (37, 0, 5, 8), (37, 0, 5, 9), (37, 0, 4, 11), (40, 0, 4, 12), (43, 1, 0, 0),
    (45, 0, 5, 10), (47, 1, 0, 1), (51, 0, 5, 11), (54, 1, 0, 2), (56, 0, 5, 12), (57, 1, 1, 0), (59, 1, 0, 3),
    (59, 1, 1, 1), (67, 1, 2, 0), (69, 1, 1, 2), (70, 1, 0, 4), (70, 1, 2, 1), (75, 1, 2, 2), (79, 1, 3, 0),
    (80, 1, 1, 3), (81, 1, 3, 1), (81, 1, 4, 0), (82, 1, 2, 3), (83, 1, 4, 1), (86, 1, 3, 2), (88, 1, 5, 0),
    (89, 1, 2, 4), (89, 1, 4, 2), (90, 1, 1, 4), (90, 1, 3, 3), (90, 1, 5, 1), (90, 1, 6, 0), (91, 1, 4, 3),
    (91, 1, 6, 1), (92, 1, 7, 0), (95, 1, 5, 2), (97, 1, 3, 4), (98, 1, 6, 2), (102, 1, 5, 3), (102, 1, 7, 1),
    (102, 1, 8, 0), (103, 1, 4, 4), (103, 1, 6, 3), (103, 1, 8, 1), (105, 1, 5, 4), (105, 1, 7, 2), (108, 1, 8, 2),
    (109, 1, 6, 4), (109, 1, 9, 0), (113, 1, 7, 3), (113, 1, 9, 1), (114, 1, 8, 3), (114, 1, 10, 0),
    (115, 1, 10, 1), (117, 1, 9, 2), (120, 1, 11, 0), (120, 1, 10, 2), (121, 1, 8, 4), (124, 1, 7, 4),
    (124, 1, 9, 3), (124, 1, 11, 1), (124, 1, 12, 0), (127, 1, 10, 3), (127, 1, 12, 1), (129, 1, 11, 2),
    (130, 1, 13, 0), (131, 1, 12, 2), (133, 1, 9, 4), (134, 1, 11, 3), (134, 1, 13, 1), (134, 1, 13, 2),
    (134, 1, 11, 4), (134, 1, 10, 4), (134, 1, 12, 3), (134, 1, 13, 3), (134, 1, 13, 4), (134, 1, 12, 4),
)

def check_plan(plan, keys, index):
    pos={tuple(e[1:]):(e[0],j) for j,e in enumerate(plan)}
    assert set(pos)==keys and len(plan)==len(keys)
    assert all(a[0]<=b[0] for a,b in zip(plan,plan[1:]))
    for kind,g,k in keys:
        if k: assert pos[(kind,g,k-1)]<pos[(kind,g,k)]
    assert pos[(0,0,0)][0]==0 and all(pos[(0,g,0)][0]>=1 for g in range(1,len(GATHER)))
    for g,p in enumerate(due_places()): assert max(v[0] for e,v in pos.items() if e[:2]==(0,g))<=index[p]
    for g,p in enumerate(ready_places()):
        assert pos[(1,g,0)][0]>=index[p]
        for n,i,j in RULES:
            if g>=n: assert pos[(1,g-n,i)]<pos[(1,g,j)]

def mega_kernel(Z,plan,tok_h,cot_h,len_ref,wqkv_s,wout_s,wup_s,wdown_s,vec_s,
               mixed_o,dtok_o,own_o,nrm_o,place_o,
               G,tok,cot,F1,F2,F3,qkv,B1,B2,B3,h1T,h2T,aT,oT,W0,W1,dW,lse,V,V1,dV1,dka,dva,own,nrm,wide,dsem,*rest):
    gsems=rest[:10]; rbufs=rest[10:10+NB]; rsems=rest[10+NB:18+NB]; nb,got,ns,nr=rest[18+NB:]
    L=tok.shape[0]
    NBK=L//RB
    place=Place(Z)
    def dma(a,b,i):
        cp=pltpu.make_async_copy(a,b,dsem.at[i]); cp.start(); return cp
    ldt=dma(tok_h,tok,0); ldc=dma(cot_h,cot,1)
    bar=announce(place,Z)
    start=lax.rem(240*((place.dp*Z+place.z)*2+place.x),128)
    place_o[0]=place.x
    place_o[1]=start
    shards=(wqkv_s,wout_s,wup_s,wdown_s,vec_s,wide,start)
    pack_own(place,G,*shards,True)
    pl.semaphore_wait(bar,8*Z-1)
    ga=Gather(place,G,GATHER,gsems)
    sc=Scatter(place,G,SCATTER,rbufs,rsems)
    clock=Clock(plan,ga,sc,own)
    def at(name,step,count): clock.at(name,step,count)
    def rows(i): return pl.ds(al(i*RB,RB),RB)
    length=len_ref[0]
    at("in",0,2)
    pack_own(place,G,*shards,False)
    at("in",1,2)
    F3[...]=jnp.zeros_like(F3)
    ldc.wait()
    dead=lax.broadcasted_iota(jnp.int32,(L,D),0)>=length
    cot[...]=jnp.where(dead,jnp.zeros((),BF),cot[...])
    ldt.wait()
    xhat=F1; h1=B1; o=B3
    for i in range(4):
        at("stat",i,4)
        if i<NBK:
            xhat[rows(i),:]=norm_parts(tok[rows(i),:].astype(F32))[0]
    def third(i,_):
        s=lax.rem(i+2,3)
        at("third",i,3)
        @pl.when(i==0)
        def _():
            unpack_vec(G,V,V1)
            def first(j,_):
                hb=(xhat[rows(j),:]*V1[:,0:D]+V1[:,D:2*D]).astype(BF)
                h1[rows(j),:]=hb
                h1T[:,rows(j)]=hb.T
                return 0
            lax.fori_loop(0,NBK,first,0)
        unpack24(G,QKV_AT+CW*s,W0)
        def block(j,_):
            at("qkv",4*i+j,12)
            qkv[s,rows(j),:]=nn(h1[rows(j),:],W0[...]).astype(BF)
            return 0
        lax.fori_loop(0,NBK,block,0)
        def pair(pp,_):
            p=2*s+pp
            def col(j): return qkv.at[s,:,pl.ds(al(256*j+128*pp,128),128)]
            c=pl.ds(al(128*p,128),128)
            at("af",2*i+pp,6)
            attn_fwd_pair(col(0),col(1),col(2),length,o.at[:,c],oT.at[c,:],lse.at[p],512)
            return 0
        lax.fori_loop(0,2,pair,0)
        return 0
    lax.fori_loop(0,3,third,0)
    at("out",0,1)
    unpack24(G,OUT_AT,W0)
    r1=F1; mixed=F2; dh2=F3; h2=B1
    def out_block(i,_):
        at("ob",i,4)
        sl=rows(i)
        r=tok[sl,:].astype(F32)+nn(o[sl,:],W0[...])+V1[:,4*D:5*D]
        r1[sl,:]=r
        mixed[sl,:]=r+V1[:,5*D:6*D]
        hb=(norm_parts(r)[0]*V1[:,2*D:3*D]+V1[:,3*D:4*D]).astype(BF)
        h2[sl,:]=hb
        h2T[:,sl]=hb.T
        return 0
    lax.fori_loop(0,NBK,out_block,0)
    du_s=B2
    def chunk(c,_):
        at("chunk",c,4)
        for g,when_ in enumerate((0,0,0,0,1,2)):
            pl.when(c==when_)(lambda g=g: ga.drain(g))
        unpack24(G,UP_AT+CW*c,W0)
        unpack_down(G,c,W1)
        bu=V1[:,pl.ds(al(6*D+c*W3,128),W3)]
        def mrows(i,acc):
            at("mr",4*c+i,16)
            sl=rows(i)
            u=nn(h2[sl,:],W0[...])+bu
            a,slope=gelu_both(u)
            ab=a.astype(BF)
            mixed[sl,:]+=nn(ab,W1[...])
            aT[:,sl]=ab.T
            du=(nt(cot[sl,:],W1[...])*slope).astype(BF)
            du_s[sl,:]=du
            dh2[sl,:]+=nt(du,W0[...])
            return acc+jnp.sum(du.astype(F32),0,keepdims=True)
        s=lax.fori_loop(0,NBK,mrows,jnp.zeros((1,W3),F32))
        dV1[:,pl.ds(al(6*D+c*W3,128),W3)]=s
        def wrows(i,_):
            at("mw",3*c+i,12)
            dW[rows(i),:]=nn(aT[rows(i),:],cot[...])
            return 0
        lax.fori_loop(0,W3//RB,wrows,0)
        pack_down(G,c,dW)
        def urows(i,_):
            at("mu",3*c+i,12)
            dW[rows(i),:]=nn(h2T[rows(i),:],du_s[...])
            return 0
        lax.fori_loop(0,D//RB,urows,0)
        pack24(G,UP_AT+CW*c,dW)
        at("mp",c,4)
        return 0
    lax.fori_loop(0,FF//W3,chunk,0)
    at("fin",0,1)
    mixed_b=B2
    def fin(i,_):
        mixed_b[rows(i),:]=mixed[rows(i),:].astype(BF)
        return 0
    lax.fori_loop(0,NBK,fin,0)
    outs=[dma(mixed_b,mixed_o,2)]
    unpack24(G,OUT_AT,W0)
    dr1=F3; dy=B3; do=B1
    def back(i,acc):
        at("bb",i,4)
        sl=rows(i)
        dh=dh2[sl,:]
        xh,s=norm_parts(r1[sl,:])
        g=cot[sl,:].astype(F32)
        dr=g+norm_back(dh*V1[:,2*D:3*D],xh,s)
        dr1[sl,:]=dr
        dyb=dr.astype(BF)
        dy[sl,:]=dyb
        do[sl,:]=nt(dyb,W0[...]).astype(BF)
        new=(dh*xh,dh,dyb.astype(F32),g)
        return tuple(a+jnp.sum(b,0,keepdims=True) for a,b in zip(acc,new))
    z1=jnp.zeros((1,D),F32)
    sums=lax.fori_loop(0,NBK,back,(z1,z1,z1,z1))
    for j,v in enumerate(sums): dV1[:,pl.ds((2+j)*D,D)]=v
    def orow(i,_):
        at("bw",i,3)
        dW[rows(i),:]=nn(oT[rows(i),:].astype(BF),dy[...])
        return 0
    lax.fori_loop(0,D//RB,orow,0)
    pack24(G,OUT_AT,dW)
    at("bp",0,1)
    dqkv=B3; dh1=F2
    outs[0].wait()
    dh1[...]=jnp.zeros_like(dh1)
    def third_back(s,_):
        unpack24(G,QKV_AT+CW*s,W0)
        def pair(pp,_):
            p=2*s+pp
            at("ab",4*s+2*pp,12)
            def col(j): return qkv.at[s,:,pl.ds(al(256*j+128*pp,128),128)]
            def dcol(j): return dqkv.at[:,pl.ds(al(256*j+128*pp,128),128)]
            c=pl.ds(al(128*p,128),128)
            attn_bwd_pair(col(0),col(1),col(2),do.at[:,c],oT.at[c,:],lse.at[p],length,
                          dcol(0),dcol(1),dcol(2),dka,dva,256,tick=lambda k: at("ab",4*s+2*pp+k,12))
            return 0
        lax.fori_loop(0,2,pair,0)
        def qrow(i,_):
            at("dq",3*s+i,9)
            dW[rows(i),:]=nn(h1T[rows(i),:],dqkv[...])
            return 0
        lax.fori_loop(0,D//RB,qrow,0)
        pack24(G,QKV_AT+CW*s,dW)
        at("dp",s,3)
        def drow(i,_):
            at("dh",4*s+i,12)
            dh1[rows(i),:]+=nt(dqkv[rows(i),:],W0[...])
            return 0
        lax.fori_loop(0,NBK,drow,0)
        return 0
    lax.fori_loop(0,3,third_back,0)
    def srow(i,acc):
        at("ln",i,4)
        sl=rows(i)
        dh=dh1[sl,:]
        xh,_=norm_parts(tok[sl,:].astype(F32))
        return tuple(a+jnp.sum(b,0,keepdims=True) for a,b in zip(acc,(dh*xh,dh)))
    sums=lax.fori_loop(0,NBK,srow,(z1,z1))
    for j,v in enumerate(sums): dV1[:,pl.ds(j*D,D)]=v
    pack_vec(G,V,dV1)
    at("lp",0,1)
    def lrow(i,_):
        at("lx",i,4)
        sl=rows(i)
        xh,r=norm_parts(tok[sl,:].astype(F32))
        F1[sl,:]=dr1[sl,:]+norm_back(dh1[sl,:]*V1[:,0:D],xh,r)
        return 0
    lax.fori_loop(0,NBK,lrow,0)
    outs=[dma(F1,dtok_o,3)]
    for f in clock.tail: f()
    flat=lax.broadcasted_iota(jnp.int32,(16,VEC_COLS),0)*VEC_COLS+lax.broadcasted_iota(jnp.int32,(16,VEC_COLS),1)
    vec=own[:,pl.ds(VEC_AT,VEC_COLS)]
    vec=jnp.where(jnp.logical_and(flat>=start,flat<start+240),vec,0.0)
    left=own[:,pl.ds(0,VEC_AT)]; right=own[:,pl.ds(OUT_AT,COLS-OUT_AT)]
    got[0]=jnp.full((8,128),1.0,F32)*(jnp.sum(left*left)+jnp.sum(right*right)+jnp.sum(vec*vec))
    outs.append(dma(own,own_o,4))
    nrm[8:24,:]=vec
    nrm[0:8,:]=all_sum(place,nb,got,ns,nr)
    outs.append(dma(nrm,nrm_o,5))
    for g in range(len(SCATTER)): sc.drain(g)
    for cp in outs: cp.wait()

def mega_call(Z,tok,cot,length,wqkv,wout,wup,wdown,vec,plan=None):
    plan=PLAN if plan is None else plan
    L=tok.shape[0]; pieces=8*Z
    S=jax.ShapeDtypeStruct; V=pltpu.VMEM
    vm=pl.BlockSpec(memory_space=pltpu.VMEM); an=pl.BlockSpec(memory_space=pltpu.HBM); sm=pl.BlockSpec(memory_space=pltpu.SMEM)
    outs=[S((L,D),BF),S((L,D),F32),S((16,COLS),F32),S((24,128),F32),S((2,),jnp.int32)]
    f=lambda: V((L,D),F32)
    b=lambda: V((L,D),BF)
    scratch=[V((4,Z,2,16,COLS),BF),b(),b(),f(),f(),f(),V((3,L,D),BF),b(),b(),b(),V((D,L),BF),V((D,L),BF),V((D,L),BF),V((D,L),F32),
             V((D,W3),BF),V((W3,D),BF),V((D,W3),F32),V((6,2,L),F32),V((80,128),F32),V((1,10*D),F32),V((1,10*D),F32),
             V((L,128),F32),V((L,128),F32),V((16,COLS),F32),V((24,128),F32),V((8,3*VEC_COLS),F32),pltpu.SemaphoreType.DMA((6,))]
    return pl.pallas_call(functools.partial(mega_kernel,Z,plan),out_shape=outs,
        in_specs=[an,an,sm]+[vm]*5,out_specs=[an]*4+[sm],
        scratch_shapes=scratch+gather_sems(len(GATHER),Z)+rs_bufs(Z)+rs_sems(len(SCATTER),Z)+norm_bufs(Z)+norm_sems(Z),
        compiler_params=pltpu.CompilerParams(collective_id=1,has_side_effects=True,vmem_limit_bytes=63*2**20),
        cost_estimate=pl.CostEstimate(flops=60*10**9,bytes_accessed=60*2**20,transcendentals=10**7))(tok,cot,length,wqkv,wout,wup,wdown,vec)


def adam_step(weight, first_mom, second_mom, gradient, step_rate):
    first_new = BETA_ONE * first_mom + (1.0 - BETA_ONE) * gradient
    second_new = BETA_TWO * second_mom + (1.0 - BETA_TWO) * gradient * gradient
    fix_one = 1.0 - BETA_ONE**STEP
    fix_two = 1.0 - BETA_TWO**STEP
    update = (
        first_new / fix_one / (jnp.sqrt(second_new / fix_two) + ADAM_EPSILON) + DECAY_RATE * weight
    )
    return (weight - step_rate * update, first_new, second_new)


def adam_kernel(par_ref, own_h, nrm_h, mixed_h, dtok_h, *refs):
    ins_h, outs_h, moved, norm_ref = refs[:15], refs[15:30], refs[30:32], refs[32]
    own, nrm, *rest = refs[33:]
    ins, outs, (mixed, dtok, wide, sem) = rest[:15], rest[15:30], rest[30:]
    pairs = list(zip((own_h, nrm_h) + tuple(ins_h), (own, nrm) + tuple(ins)))
    loads = [pltpu.make_async_copy(a, b, sem.at[i]) for i, (a, b) in enumerate(pairs)]
    moves = [
        pltpu.make_async_copy(mixed_h, mixed, sem.at[32]),
        pltpu.make_async_copy(dtok_h, dtok, sem.at[33]),
    ]
    for cp in loads + moves:
        cp.start()
    loads[0].wait()
    loads[1].wait()
    stores = [pltpu.make_async_copy(a, b, sem.at[i]) for i, (a, b) in enumerate(zip(outs, outs_h), 17)]

    def take(i):
        for cp in loads[2 + 3 * i : 5 + 3 * i]:
            cp.wait()

    def give(i):
        for cp in stores[3 * i : 3 * i + 3]:
            cp.start()

    norm = jnp.sqrt(nrm[0:1, 0:1])
    norm_ref[0] = norm[0, 0]
    factor = jnp.minimum(1.0, CLIP_NORM / (norm + 1e-06))
    main_at = al(8 * par_ref[0], 8)
    rest_at = al(16 * (1 - par_ref[0]), 8)

    def step(i, rows, cols, grad, rate):
        w, m, v = [r[rows, cols] for r in ins[3 * i : 3 * i + 3]]
        new = adam_step(w, m, v, grad * factor, rate)
        for r, a in zip(outs[3 * i : 3 * i + 3], new):
            r[rows, cols] = a

    def chunk(i, at, cols, rate):
        main = own[:, pl.ds(at, W3)]
        packed = own[:, pl.ds(at + W3, W3 // 2)]
        parts = []
        for s in range(3):
            parts += [packed[:8, 128 * s : 128 * s + 128], packed[8:, 128 * s : 128 * s + 128]]
        rest = jnp.concatenate(parts, 1)
        done = 0
        for c, n in cols:
            step(i, pl.ds(main_at, 16), pl.ds(c, n), main[:, done : done + n], rate)
            step(i, pl.ds(rest_at, 8), pl.ds(c, n), rest[:, done : done + n], rate)
            done += n

    take(0)
    for s in range(3):
        chunk(0, QKV_AT + CW * s, third_cols(s), D ** (-0.5))
    for cp in moves:
        cp.wait()
    out_moves = [
        pltpu.make_async_copy(mixed, moved[0], sem.at[32]),
        pltpu.make_async_copy(dtok, moved[1], sem.at[33]),
    ]
    for cp in out_moves:
        cp.start()
    give(0)
    take(1)
    chunk(1, OUT_AT, [(0, W3)], D ** (-0.5))
    give(1)
    take(2)
    for c in range(4):
        chunk(2, UP_AT + CW * c, [(W3 * c, W3)], D ** (-0.5))
    give(2)
    take(3)
    for r in range(6):
        grad = own[:, pl.ds(DOWN_AT + r * D, D)]
        step(3, pl.ds(16 * r, 16), slice(None), grad, FF ** (-0.5))
    give(3)
    take(4)
    n = ins[12].shape[1]
    for k in range(3):
        wide[0:8, VEC_COLS * k : VEC_COLS * k + VEC_COLS] = jnp.broadcast_to(
            nrm[8 + k : 9 + k, :], (8, VEC_COLS)
        )
    width = 3 * VEC_COLS
    turned = pltpu.roll(wide[...], lax.rem(width - par_ref[1], width), 1)
    step(4, slice(None), slice(None), turned[0:1, :n], VECTOR_RATE)
    give(4)
    for cp in stores + out_moves:
        cp.wait()


def adam_call(parity, own, nrm, mixed, d_tokens, states):
    hb = pl.BlockSpec(memory_space=pltpu.HBM)
    sm = pl.BlockSpec(memory_space=pltpu.SMEM)
    held = [pltpu.VMEM(a.shape, F32) for a in (own, nrm) + tuple(states) + tuple(states)]
    return pl.pallas_call(
        adam_kernel,
        out_shape=[jax.ShapeDtypeStruct(a.shape, a.dtype) for a in states + (mixed, d_tokens)]
        + [jax.ShapeDtypeStruct((1,), F32)],
        in_specs=[sm] + [hb] * 19,
        out_specs=[hb] * 17 + [sm],
        scratch_shapes=held
        + [pltpu.VMEM(mixed.shape, BF), pltpu.VMEM(d_tokens.shape, F32)]
        + [pltpu.VMEM((8, 3 * VEC_COLS), F32)]
        + [pltpu.SemaphoreType.DMA((34,))],
        compiler_params=pltpu.CompilerParams(vmem_limit_bytes=63 * 2**20),
        cost_estimate=pl.CostEstimate(
            flops=10**7, bytes_accessed=8 * 2**20, transcendentals=10**6
        ),
    )(parity, own, nrm, mixed, d_tokens, *states)


def layer_norm(values, gain, shift):
    center = jnp.mean(values, -1, keepdims=True)
    centered = values - center
    spread = jnp.mean(centered * centered, -1, keepdims=True)
    return centered * lax.rsqrt(spread + EPS_NORM) * gain + shift


def smooth_gate(value):
    return jax.nn.gelu(value, approximate=True)


def plain_shards(tokens, lengths, cotangent, *state):
    w_qkv, m_qkv, v_qkv, w_out, m_out, v_out, w_up, m_up, v_up = state[:9]
    w_down, m_down, v_down, packed, m_packed, v_packed = state[9:]
    seq_count, seq_len, model_width = tokens.shape
    row_count = seq_count * seq_len
    axes = ("dp", "fsdp")
    wqkv_b, wout_b, wup_b, wdown_b, vector_b = [
        lax.all_gather(w.astype(BF), axes, axis=0, tiled=True)
        for w in (w_qkv, w_out, w_up, w_down, packed)
    ]
    vector = vector_b.astype(F32)
    gain_one, bias_one, gain_two, bias_two, bias_attn, bias_down = [
        vector[i * model_width : (i + 1) * model_width] for i in range(6)
    ]
    bias_up = vector[6 * model_width :]
    positions = jnp.arange(seq_len, dtype=jnp.int32)
    live_rows = positions[None, :] < lengths[:, None]
    inputs = tokens.astype(F32).reshape(row_count, model_width)
    normed_one, norm_one_back = jax.vjp(layer_norm, inputs, gain_one, bias_one)
    normed_one_b = normed_one.astype(BF)
    qkv_all = jnp.dot(normed_one_b, wqkv_b, preferred_element_type=F32).astype(BF)
    seqs = [slice(i * seq_len, (i + 1) * seq_len) for i in range(seq_count)]
    ahead = [fwd_call(qkv_all[s], lengths[i : i + 1], 512) for i, s in enumerate(seqs)]
    attended_b = jnp.concatenate([a[0] for a in ahead], 0)
    resid_one = inputs + jnp.dot(attended_b, wout_b, preferred_element_type=F32) + bias_attn
    normed_two, norm_two_back = jax.vjp(layer_norm, resid_one, gain_two, bias_two)
    normed_two_b = normed_two.astype(BF)
    upper = jnp.dot(normed_two_b, wup_b, preferred_element_type=F32) + bias_up
    activ, gate_back = jax.vjp(smooth_gate, upper)
    activ_b = activ.astype(BF)
    mixed = resid_one + jnp.dot(activ_b, wdown_b, preferred_element_type=F32) + bias_down
    mixed = mixed.reshape(seq_count, seq_len, model_width).astype(BF)
    grad_b = jnp.where(live_rows[:, :, None], cotangent, jnp.zeros((), BF))
    grad_b = grad_b.reshape(row_count, model_width)
    grad_full = grad_b.astype(F32)
    d_wdown = jnp.dot(activ_b.T, grad_b, preferred_element_type=F32)
    d_bias_down = jnp.sum(grad_full, 0)
    d_activ = jnp.dot(grad_b, wdown_b.T, preferred_element_type=F32)
    (d_upper,) = gate_back(d_activ)
    d_upper_b = d_upper.astype(BF)
    d_bias_up = jnp.sum(d_upper_b.astype(F32), 0)
    d_wup = jnp.dot(normed_two_b.T, d_upper_b, preferred_element_type=F32)
    d_normed_two = jnp.dot(d_upper_b, wup_b.T, preferred_element_type=F32)
    d_resid_norm, d_gain_two, d_bias_two = norm_two_back(d_normed_two)
    d_resid = grad_full + d_resid_norm
    d_branch_b = d_resid.astype(BF)
    d_bias_attn = jnp.sum(d_branch_b.astype(F32), 0)
    d_wout = jnp.dot(attended_b.T, d_branch_b, preferred_element_type=F32)
    d_attended_b = jnp.dot(d_branch_b, wout_b.T, preferred_element_type=F32).astype(BF)
    back = [
        bwd_call(qkv_all[s], d_attended_b[s], a[1], a[2], lengths[i : i + 1])
        for i, (s, a) in enumerate(zip(seqs, ahead))
    ]
    d_qkv_b = jnp.concatenate([jnp.concatenate(b, 1) for b in back], 0)
    d_wqkv = jnp.dot(normed_one_b.T, d_qkv_b, preferred_element_type=F32)
    d_normed_one = jnp.dot(d_qkv_b, wqkv_b.T, preferred_element_type=F32)
    d_input_norm, d_gain_one, d_bias_one = norm_one_back(d_normed_one)
    d_tokens = (d_resid + d_input_norm).reshape(seq_count, seq_len, model_width)
    d_vector = jnp.concatenate(
        [d_gain_one, d_bias_one, d_gain_two, d_bias_two, d_bias_attn, d_bias_down, d_bias_up]
    )
    owned = [
        lax.psum_scatter(g, axes, scatter_dimension=0, tiled=True)
        for g in (d_wqkv, d_wout, d_wup, d_wdown, d_vector)
    ]
    grad_norm = jnp.sqrt(lax.psum(sum(jnp.sum(g * g) for g in owned), axes))
    factor = jnp.minimum(1.0, CLIP_NORM / (grad_norm + 1e-06))
    rates = (D ** (-0.5), D ** (-0.5), D ** (-0.5), FF ** (-0.5), VECTOR_RATE)
    new = ()
    for i, (g, rate) in enumerate(zip(owned, rates)):
        new += adam_step(*state[3 * i : 3 * i + 3], g * factor, rate)
    return (mixed, d_tokens, grad_norm) + new


def direct_shards(Z, tokens, lengths, cotangent, *state):
    n = state[12].shape[0]
    vecs = tuple(v.reshape(1, n) for v in state[12:])
    mixed, d_tokens, own, small, place = mega_call(
        Z, tokens[0], cotangent[0], lengths, state[0], state[3], state[6], state[9], vecs[0]
    )
    *new, mixed, d_tokens, grad_norm = adam_call(
        place, own, small, mixed, d_tokens, state[:12] + vecs
    )
    new[12:] = [v.reshape(n) for v in new[12:]]
    return (mixed[None], d_tokens[None], grad_norm[0]) + tuple(new)


def solution(mesh):
    rows = P(("dp", "fsdp"), None)
    seqs = P(("dp", "fsdp"), None, None)
    flat = P(("dp", "fsdp"))
    in_specs = (seqs, flat, seqs) + (rows,) * 12 + (flat,) * 3
    out_specs = (seqs, seqs, P()) + (rows,) * 12 + (flat,) * 3
    dp, fsdp = mesh.shape["dp"], mesh.shape["fsdp"]

    def shards(*args):
        tokens, w_qkv = args[0], args[3]
        fits = (
            dp == 4
            and fsdp == 8
            and tokens.shape[0] == 1
            and tokens.shape[1] == 1024
            and w_qkv.shape[0] * dp * fsdp == D
        )
        step = functools.partial(direct_shards, fsdp // 2) if fits else plain_shards
        return step(*args)

    return jax.shard_map(
        shards, mesh=mesh, in_specs=in_specs, out_specs=out_specs, check_vma=False
    )
```

```python
import functools

import jax
import jax.numpy as jnp
from jax import lax
from jax.experimental import pallas as pl
from jax.experimental.pallas import tpu as pltpu
from jax.sharding import PartitionSpec as P

D = 768
FF = 3072
HEAD_DIM = 64
STEP = 10
HD = 64
F32 = jnp.float32
BF = jnp.bfloat16
MESH = pl.DeviceIdType.MESH

EPS_NORM = 1e-05
CLIP_NORM = 1.0
BETA_ONE = 0.9
BETA_TWO = 0.95
ADAM_EPSILON = 1e-08
DECAY_RATE = 0.1
VECTOR_RATE = 0.2


def nt(a,b): return lax.dot_general(a,b,(((1,),(1,)),((),())),preferred_element_type=F32)
def nn(a,b): return jnp.dot(a,b,preferred_element_type=F32)
def head_mask(rows):
    lane=lax.broadcasted_iota(jnp.int32,(rows,128),1)
    return (lane<HD)
def half(x,h,scale=1.0):
    m=head_mask(x.shape[0]); m = m if h==0 else jnp.logical_not(m)
    return jnp.where(m,x*jnp.asarray(scale,x.dtype),jnp.zeros_like(x))

def attn_fwd_pair(q_ref,k_ref,v_ref,length,o_ref,oT_ref,lse_ref,QB):
    L=q_ref.shape[0]
    n=L//QB
    vT=v_ref[...].T
    lane=lax.broadcasted_iota(jnp.int32,(L,128),1)
    dead=jnp.where(lax.broadcasted_iota(jnp.int32,(L,128),0)<length,0.0,-1e9).astype(BF)
    keys=[jnp.where(lane==HD-HD*h,dead,k_ref[...]) for h in range(2)]
    ql=lax.broadcasted_iota(jnp.int32,(QB,128),1)
    tri=lax.broadcasted_iota(jnp.int32,(QB,QB),0)<=lax.broadcasted_iota(jnp.int32,(QB,QB),1)
    def scores(i,h):
        qh=jnp.where(ql==HD-HD*h,jnp.ones((),BF),half(q_ref[pl.ds(i*QB,QB),:],h,0.125))
        return nt(keys[h][:(i+1)*QB],qh)
    jobs=[(i,h) for i in range(n) for h in range(2)]
    now=scores(*jobs[0])
    outs=[]
    for x,(i,h) in enumerate(jobs):
        later=scores(*jobs[x+1]) if x+1<len(jobs) else None
        nk=(i+1)*QB
        s=jnp.where(tri,now[nk-QB:],-1e9)
        if i: s=jnp.concatenate([now[:nk-QB],s],0)
        m=jnp.max(s,0,keepdims=True)
        e=jnp.exp(s-m)
        l=jnp.sum(e,0,keepdims=True)
        outs.append(nn(vT[HD*h:HD*h+HD,:nk],e.astype(BF))/l)
        lse_ref[pl.ds(h,1),pl.ds(i*QB,QB)]=m+jnp.log(l)
        if h==1:
            oT=jnp.concatenate(outs,0); outs=[]
            oT_ref[:,pl.ds(i*QB,QB)]=oT
            o_ref[pl.ds(i*QB,QB),:]=oT.T.astype(BF)
        now=later

def attn_bwd_pair(q_ref,k_ref,v_ref,do_ref,oT_ref,lse_ref,length,dq_ref,dk_ref,dv_ref,dk_acc,dv_acc,QB,tick=None):
    L=q_ref.shape[0]
    n=L//QB
    kT=k_ref[...].T
    jobs=list(reversed(range(n)))
    tri=lax.broadcasted_iota(jnp.int32,(QB,2*QB),0)<=lax.rem(lax.broadcasted_iota(jnp.int32,(QB,2*QB),1),QB)
    def products(i):
        nk=(i+1)*QB; sl=pl.ds(i*QB,QB)
        q=q_ref[sl,:]; do=do_ref[sl,:]
        qm=jnp.concatenate([half(q,0,0.125),half(q,1,0.125)],0)
        dom=jnp.concatenate([half(do,0),half(do,1)],0)
        return nt(k_ref[pl.ds(0,nk),:],qm),nt(v_ref[pl.ds(0,nk),:],dom),qm,dom
    now=products(jobs[0])
    for x,i in enumerate(jobs):
        split=tick is not None and x==1
        later=products(jobs[x+1]) if x+1<n and not (tick is not None and x==0) else None
        if split:
            tick(1)
            now=products(i)
        nk=(i+1)*QB; sl=pl.ds(i*QB,QB)
        s,dp,qm,dom=now
        prod=do_ref[sl,:].astype(F32).T*oT_ref[:,sl]
        delta=jnp.concatenate([jnp.sum(prod[:HD],0,keepdims=True),jnp.sum(prod[HD:],0,keepdims=True)],1)
        live=(i*QB+lax.broadcasted_iota(jnp.int32,(1,QB),1))<length
        lse=jnp.concatenate([jnp.where(live,lse_ref[pl.ds(h,1),sl],1e30) for h in range(2)],1)
        p=jnp.exp(s-lse)
        pd=jnp.where(tri,p[nk-QB:],0.0)
        p=pd if i==0 else jnp.concatenate([p[:nk-QB],pd],0)
        ds=(p*(dp-delta)).astype(BF)
        dv=nn(p.astype(BF),dom); dk=nn(ds,qm)
        dq=[nn(kT[HD*h:HD*h+HD,:nk],ds[:,QB*h:QB*h+QB]) for h in range(2)]
        dq_ref[sl,:]=(jnp.concatenate(dq,0)*0.125).T.astype(BF)
        if i==n-1:
            dk_acc[...]=dk; dv_acc[...]=dv
        else:
            dk_acc[pl.ds(0,nk),:]+=dk; dv_acc[pl.ds(0,nk),:]+=dv
        now=later
    dk_ref[...]=dk_acc[...].astype(BF); dv_ref[...]=dv_acc[...].astype(BF)

def fwd_call(qkv,length,QB=256):
    L=qkv.shape[0]; D=qkv.shape[1]//3; NP=D//128
    def k(len_ref,q,k_,v,o,oT,lse):
        attn_fwd_pair(q,k_,v,len_ref[0],o,oT,lse.at[0],QB)
    return pl.pallas_call(k,grid=(NP,),
      in_specs=[pl.BlockSpec(memory_space=pltpu.SMEM)]+[pl.BlockSpec((L,128),functools.partial(lambda off,p:(0,off+p),j*NP)) for j in range(3)],
      out_specs=[pl.BlockSpec((L,128),lambda p:(0,p)),pl.BlockSpec((128,L),lambda p:(p,0)),pl.BlockSpec((1,2,L),lambda p:(p,0,0))],
      out_shape=[jax.ShapeDtypeStruct((L,D),BF),jax.ShapeDtypeStruct((D,L),F32),jax.ShapeDtypeStruct((NP,2,L),F32)],
      compiler_params=pltpu.CompilerParams(vmem_limit_bytes=56*2**20),
      cost_estimate=pl.CostEstimate(flops=4*L*L*D//2,bytes_accessed=10*2**20,transcendentals=12*L*L//2))(length,qkv,qkv,qkv)
def bwd_call(qkv,do,oT,lse,length,QB=256):
    L=qkv.shape[0]; D=qkv.shape[1]//3; NP=D//128
    def k(len_ref,q,k_,v,do,oT,lse,dq,dk,dv,dka,dva):
        attn_bwd_pair(q,k_,v,do,oT,lse.at[0],len_ref[0],dq,dk,dv,dka,dva,QB)
    blk=pl.BlockSpec((L,128),lambda p:(0,p))
    return pl.pallas_call(k,grid=(NP,),
      in_specs=[pl.BlockSpec(memory_space=pltpu.SMEM)]+[pl.BlockSpec((L,128),functools.partial(lambda off,p:(0,off+p),j*NP)) for j in range(3)]+[blk,pl.BlockSpec((128,L),lambda p:(p,0)),pl.BlockSpec((1,2,L),lambda p:(p,0,0))],
      out_specs=[blk]*3,
      out_shape=[jax.ShapeDtypeStruct((L,D),BF)]*3,
      scratch_shapes=[pltpu.VMEM((L,128),F32)]*2,
      compiler_params=pltpu.CompilerParams(vmem_limit_bytes=56*2**20),
      cost_estimate=pl.CostEstimate(flops=10*L*L*D//2,bytes_accessed=14*2**20,transcendentals=12*L*L//2))(length,qkv,qkv,qkv,do,oT,lse)


class Place:
    def __init__(self, Z):
        dp=lax.axis_index("dp"); fs=lax.axis_index("fsdp")
        self.Z=Z; self.y=dp//2; self.c=dp%2; self.z=fs//2; self.x=fs%2
        self.nx=(dp,self.z*2+1-self.x)
        self.ny=((1-self.y)*2+self.c,fs)
        self.nc=(self.y*2+1-self.c,fs)
        self.me=self.piece(self.z)
        self.dp=dp; self.fs=fs
    def nz(self,z): return (self.dp,z*2+self.x)
    def piece(self,z,dx=0,dy=0,dc=0):
        y=self.y if dy==0 else 1-self.y
        x=self.x if dx==0 else 1-self.x
        c=self.c if dc==0 else 1-self.c
        return (y*2+c,z,x)
    def slab(self,y,dc=0):
        c=self.c if dc==0 else 1-self.c
        return y*2+c

def rcopy(src,dst,ss,rs,dev):
    return pltpu.make_async_remote_copy(src_ref=src,dst_ref=dst,send_sem=ss,recv_sem=rs,device_id=dev,device_id_type=MESH)

def when(cond,fn):
    if cond is True: fn()
    else: pl.when(cond)(fn)

def gather_sems(NG,Z):
    D=pltpu.SemaphoreType.DMA
    return [D((NG*2*(Z-1),)),D((NG*2*(Z-1),)),
            D((NG*2*Z,)),D((NG*2*Z,)),
            D((NG*2*Z,)),D((NG*2*Z,)),
            D((NG*2,)),D((NG*2,)),
            D((NG*2*(Z-1),)),D((NG*2*(Z-1),))]

class Gather:
    def __init__(self,P,G,groups,sems):
        self.P=P; self.G=G; self.groups=groups
        self.zs,self.zr,self.xs,self.xr,self.ys,self.yr,self.cs,self.cr,self.fs,self.fr=sems
    def direct(self,g):
        lo,n,a,p,q=self.groups[g]
        return p+q==n
    def _cp(self,idx,lo,n,ss,rs,dev):
        r=self.G.at[(*idx,slice(None),pl.ds(lo,n))]
        return rcopy(r,r,ss,rs,dev)
    def zcp(self,g,d,t,zo,to):
        lo,n=self.groups[g][:2]; i=(g*2+d)*(self.P.Z-1)+t
        return self._cp(self.P.piece(zo),lo,n,self.zs.at[i],self.zr.at[i],self.P.nz(to))
    def zdiag(self,g,d,t,zo,to):
        lo,n,a,p,q=self.groups[g]; i=(g*2+d)*(self.P.Z-1)+t
        return self._cp(self.P.piece(zo,dx=1,dy=1),lo+p,n-p-q,self.fs.at[i],self.fr.at[i],self.P.nz(to))
    def xfull(self,g,zo,arrive=0):
        lo,n=self.groups[g][:2]; i=g*2*self.P.Z+zo
        return self._cp(self.P.piece(zo,dx=arrive),lo,n,self.xs.at[i],self.xr.at[i],self.P.nx)
    def yfull(self,g,zo,arrive=0):
        lo,n=self.groups[g][:2]; i=g*2*self.P.Z+zo
        return self._cp(self.P.piece(zo,dy=arrive),lo,n,self.ys.at[i],self.yr.at[i],self.P.ny)
    def ydiag(self,g,zo,near,arrive=0):
        lo,n,a,p,q=self.groups[g]; i=g*2*self.P.Z+self.P.Z+zo
        return self._cp(self.P.piece(zo,dx=1,dy=arrive),lo,a if near else p,self.ys.at[i],self.yr.at[i],self.P.ny)
    def xdiag(self,g,zo,near,arrive=0):
        lo,n,a,p,q=self.groups[g]; i=g*2*self.P.Z+self.P.Z+zo
        w=n-a if near else q
        return self._cp(self.P.piece(zo,dy=1,dx=arrive),lo+n-w,w,self.xs.at[i],self.xr.at[i],self.P.nx)
    def ccp(self,g,k,arrive=0):
        lo,n=self.groups[g][:2]
        y=self.P.y if k==0 else 1-self.P.y
        r=self.G.at[self.P.slab(y,dc=arrive),:,:,:,pl.ds(lo,n)]
        return rcopy(r,r,self.cs.at[g*2+k],self.cr.at[g*2+k],self.P.nc)
    def others(self,t,f):
        when(self.P.z>=t,lambda: f(self.P.z-t)); when(self.P.z<self.P.Z-t,lambda: f(self.P.z+t))
    def own(self,g):
        z=self.P.z; Z=self.P.Z
        self.xfull(g,z).start(); self.yfull(g,z).start()
        for t in range(Z-1 if self.direct(g) else 1):
            when(z<Z-1-t,lambda: self.zcp(g,0,t,z,z+1+t).start())
            when(z>t,lambda: self.zcp(g,1,t,z,z-1-t).start())
    def zarrive(self,g,t):
        z=self.P.z; Z=self.P.Z
        on=t+1<Z-1 and not self.direct(g)
        def below():
            zo=z-1-t
            self.zcp(g,0,t,zo,z).wait_recv()
            if on: when(z<Z-1,lambda: self.zcp(g,0,t+1,zo,z+1).start())
            self.xfull(g,zo).start(); self.yfull(g,zo).start()
        def above():
            zo=z+1+t
            self.zcp(g,1,t,zo,z).wait_recv()
            if on: when(z>0,lambda: self.zcp(g,1,t+1,zo,z-1).start())
            self.xfull(g,zo).start(); self.yfull(g,zo).start()
        when(z>t,below); when(z<Z-1-t,above)
    def diag(self,g,t):
        def pass_on(zo):
            self.xfull(g,zo,1).wait_recv(); self.ydiag(g,zo,t==0).start()
            self.yfull(g,zo,1).wait_recv(); self.xdiag(g,zo,t==0).start()
        if t==0: pass_on(self.P.z)
        else: self.others(t,pass_on)
    def line(self,g,t):
        z=self.P.z; Z=self.P.Z
        if t==0:
            self.ydiag(g,z,True,1).wait_recv(); self.xdiag(g,z,True,1).wait_recv()
            when(z<Z-1,lambda: self.zdiag(g,0,0,z,z+1).start())
            when(z>0,lambda: self.zdiag(g,1,0,z,z-1).start())
            return
        def below():
            self.zdiag(g,0,t-1,z-t,z).wait_recv()
            if t<Z-1: when(z<Z-1,lambda: self.zdiag(g,0,t,z-t,z+1).start())
        def above():
            self.zdiag(g,1,t-1,z+t,z).wait_recv()
            if t<Z-1: when(z>0,lambda: self.zdiag(g,1,t,z+t,z-1).start())
        when(z>=t,below); when(z<Z-t,above)
    def corner(self,g):
        self.ccp(g,0).start()
        if self.direct(g):
            self.ydiag(g,self.P.z,True,1).wait_recv(); self.xdiag(g,self.P.z,True,1).wait_recv()
        else: self.line(g,self.P.Z-1)
        def come(zo):
            self.ydiag(g,zo,False,1).wait_recv(); self.xdiag(g,zo,False,1).wait_recv()
        for t in range(1,self.P.Z): self.others(t,come)
        self.ccp(g,1).start()
    def sibling(self,g):
        self.ccp(g,0,1).wait_recv(); self.ccp(g,1,1).wait_recv()
    def drain(self,g):
        z=self.P.z; Z=self.P.Z
        def sent(zo,near):
            self.xfull(g,zo).wait_send(); self.yfull(g,zo).wait_send()
            self.xdiag(g,zo,near).wait_send(); self.ydiag(g,zo,near).wait_send()
        sent(z,True)
        for t in range(1,Z): self.others(t,lambda zo: sent(zo,False))
        for k in range(2): self.ccp(g,k).wait_send()
        for t in range(Z-1):
            if self.direct(g):
                when(z<Z-1-t,lambda: self.zcp(g,0,t,z,z+1+t).wait_send())
                when(z>t,lambda: self.zcp(g,1,t,z,z-1-t).wait_send())
                continue
            def up():
                self.zcp(g,0,t,z-t,z+1).wait_send(); self.zdiag(g,0,t,z-t,z+1).wait_send()
            def down():
                self.zcp(g,1,t,z+t,z-1).wait_send(); self.zdiag(g,1,t,z+t,z-1).wait_send()
            when(jnp.logical_and(z<Z-1,z>=t),up)
            when(jnp.logical_and(z>0,z<=Z-1-t),down)
    def events(self,g):
        Z=self.P.Z
        ev=[lambda: self.own(g)]
        for t in range(Z):
            if t<Z-1: ev.append(lambda t=t: self.zarrive(g,t))
            if t and not self.direct(g): ev.append(lambda t=t: self.line(g,t-1))
            ev.append(lambda t=t: self.diag(g,t))
        ev.append(lambda: self.corner(g))
        ev.append(lambda: self.sibling(g))
        return ev


SLOT = 1152
NB=12
def rs_sems(NG,Z):
    D=pltpu.SemaphoreType.DMA
    return [D((NG*2,)),D((NG*2,)),
            D((NG*3,)),D((NG*3,)),
            D((NG*2,)),D((NG*2,)),
            D((NG*Z,)),D((NG*Z,))]
def rs_bufs(Z):
    V=lambda *s: pltpu.VMEM(s,BF)
    h=640
    v=128
    return [V(2,2,Z,2,16,SLOT),V(2,Z,2,16,h),V(2,Z,16,h),V(2,2,Z,16,h),V(2,Z,16,h),V(4,Z,16,SLOT),
            V(1,2,Z,2,16,v),V(1,Z,2,16,v),V(1,Z,16,v),V(1,2,Z,16,v),V(1,Z,16,v),V(1,Z,16,v)]
class Scatter:
    def __init__(self,P,R,groups,bufs,sems):
        self.P=P; self.R=R; self.groups=groups; self.bufs=bufs
        self.cs,self.cr,self.xs,self.xr,self.ys,self.yr,self.zs,self.zr=sems
    def buf(self,g,i,w):
        b=self.bufs[i+(NB//2 if g==len(self.groups)-1 else 0)]
        b=b.at[g%b.shape[0]]
        nd=len(b.shape)
        return b.at[(slice(None),)*(nd-1)+(pl.ds(0,w),)]
    def row(self,dy=0,dc=0):
        y=self.P.y if dy==0 else 1-self.P.y
        c=self.P.c if dc==0 else 1-self.P.c
        return y*2+c
    def add(self,dst,src):
        def body(z,_):
            d=dst(z); s=src(z)
            d[...]=d[...]+s[...]
            return 0
        lax.fori_loop(0,self.P.Z,body,0)
    def ccp(self,g,k):
        lo,n,_=self.groups[g]
        return rcopy(self.R.at[self.row(k,1),:,:,:,pl.ds(lo,n)],self.buf(g,0,n).at[k],self.cs.at[g*2+k],self.cr.at[g*2+k],self.P.nc)
    def x1(self,g,k):
        lo,n,a=self.groups[g]
        return rcopy(self.R.at[self.row(k),:,1-self.P.x,:,pl.ds(lo+a,n-a)],self.buf(g,3,n-a).at[k],self.xs.at[g*3+k],self.xr.at[g*3+k],self.P.nx)
    def y1(self,g):
        lo,n,a=self.groups[g]
        return rcopy(self.R.at[self.row(1),:,:,:,pl.ds(lo,a)],self.buf(g,1,a),self.ys.at[g*2],self.yr.at[g*2],self.P.ny)
    def x2(self,g):
        lo,n,a=self.groups[g]
        return rcopy(self.R.at[self.row(0),:,1-self.P.x,:,pl.ds(lo,a)],self.buf(g,2,a),self.xs.at[g*3+2],self.xr.at[g*3+2],self.P.nx)
    def y2(self,g):
        lo,n,a=self.groups[g]
        return rcopy(self.R.at[self.row(1),:,self.P.x,:,pl.ds(lo+a,n-a)],self.buf(g,4,n-a),self.ys.at[g*2+1],self.yr.at[g*2+1],self.P.ny)
    def zc(self,g,src,to):
        lo,n,_=self.groups[g]; Z=self.P.Z
        return rcopy(self.R.at[self.row(0),to,self.P.x,:,pl.ds(lo,n)],self.buf(g,5,n).at[src],self.zs.at[g*Z+to],self.zr.at[g*Z+src],self.P.nz(to))
    def both(self,g): return self.groups[g][1]>self.groups[g][2]
    def s_c(self,g):
        self.ccp(g,1).start(); self.ccp(g,0).start()
    def a_c(self,g):
        lo,n,a=self.groups[g]; R=self.R; b=self.buf(g,0,n)
        for k in (1,0):
            self.ccp(g,k).wait_recv()
            r=self.row(k)
            self.add(lambda z: R.at[r,z,:,:,pl.ds(lo,n)],lambda z: b.at[k,z])
            if self.both(g): self.x1(g,k).start()
            if k==1: self.y1(g).start()
    def a_1(self,g):
        lo,n,a=self.groups[g]; R=self.R; P=self.P; B1=self.buf(g,1,a)
        self.y1(g).wait_recv()
        r=self.row(0)
        self.add(lambda z: R.at[r,z,:,:,pl.ds(lo,a)],lambda z: B1.at[z])
        if self.both(g):
            B3=self.buf(g,3,n-a)
            for k in (1,0):
                self.x1(g,k).wait_recv()
                q=self.row(k)
                self.add(lambda z: R.at[q,z,P.x,:,pl.ds(lo+a,n-a)],lambda z: B3.at[k,z])
            self.y2(g).start()
        self.x2(g).start()
    def a_2(self,g):
        lo,n,a=self.groups[g]; R=self.R; P=self.P; Z=P.Z; B2=self.buf(g,2,a)
        r=self.row(0)
        self.x2(g).wait_recv()
        self.add(lambda z: R.at[r,z,P.x,:,pl.ds(lo,a)],lambda z: B2.at[z])
        if self.both(g):
            B4=self.buf(g,4,n-a)
            self.y2(g).wait_recv()
            self.add(lambda z: R.at[r,z,P.x,:,pl.ds(lo+a,n-a)],lambda z: B4.at[z])
        for d in range(Z-1,0,-1):
            when(P.z>=d,lambda: self.zc(g,P.z,P.z-d).start())
            when(P.z<Z-d,lambda: self.zc(g,P.z,P.z+d).start())
    def final(self,g,out):
        lo,n,_=self.groups[g]; P=self.P; Z=P.Z; z=P.z
        out[...]=self.R[self.row(0),z,P.x,:,pl.ds(lo,n)].astype(F32)
        for zo in range(Z):
            def take():
                self.zc(g,zo,z).wait_recv()
                out[...]+=self.buf(g,5,n)[zo].astype(F32)
            when(z!=zo,take)
    def drain(self,g):
        Z=self.P.Z; z=self.P.z
        for k in range(2):
            self.ccp(g,k).wait_send()
            if self.both(g): self.x1(g,k).wait_send()
        self.x2(g).wait_send(); self.y1(g).wait_send()
        if self.both(g): self.y2(g).wait_send()
        for zo in range(Z):
            when(z!=zo,lambda: self.zc(g,z,zo).wait_send())
    def events(self,g,out):
        return [lambda: self.s_c(g),lambda: self.a_c(g),lambda: self.a_1(g),lambda: self.a_2(g),lambda: self.final(g,out)]

def norm_sems(Z):
    D=pltpu.SemaphoreType.DMA
    return [D((8*Z,)),D((8*Z,))]
def norm_bufs(Z): return [pltpu.VMEM((8*Z,8,128),F32),pltpu.VMEM((1,8,128),F32)]
def everyone(P):
    n=8*P.Z
    for k in range(1,n):
        i=lax.rem(P.dp*2*P.Z+P.fs+k,n)
        yield k,i,(i//(2*P.Z),lax.rem(i,2*P.Z))
def all_sum(P,buf,got,ss,rs):
    n=8*P.Z
    me=P.dp*2*P.Z+P.fs
    buf[me]=got[0]
    for k,i,dev in everyone(P):
        rcopy(got.at[0],buf.at[me],ss.at[k],rs.at[me],dev).start()
    for k,i,dev in everyone(P):
        rcopy(got.at[0],buf.at[i],ss.at[k],rs.at[i],dev).wait_recv()
    tot=buf[0]
    for i in range(1,n): tot=tot+buf[i]
    for k,i,dev in everyone(P):
        rcopy(got.at[0],buf.at[me],ss.at[k],rs.at[me],dev).wait_send()
    return tot
def announce(P,Z):
    bar=pltpu.get_barrier_semaphore()
    for _,_,d in everyone(P): pl.semaphore_signal(bar,inc=1,device_id=d,device_id_type=MESH)
    return bar


W3 = 768
CW = 1152
QKV_AT = 0
VEC_AT = 3456
VEC_COLS = 128
OUT_AT = 3584
DOWN_AT = 4736
UP_AT = 9344
COLS = 13952
GATHER = [(2304, 1280, 640, 640, 640), (0, 2304, 1152, 384, 384), (3584, 5760, 2944, 1024, 896),
          (9344, 1152, 640, 256, 128), (10496, 1152, 512, 128, 256), (11648, 2304, 1152, 384, 384)]
SCATTER = ([(UP_AT + CW * c, CW, 640 if c % 2 else 512) for c in range(4)]
           + [(DOWN_AT + CW * c, CW, 640 if c % 2 else 512) for c in range(4)]
           + [(OUT_AT, CW, 512), (0, CW, 640), (CW, CW, 512), (2 * CW, 640, 256), (2 * CW + 640, 512, 256), (VEC_AT, VEC_COLS, VEC_COLS)])

def al(v, m): return pl.multiple_of(v, m)

def third_cols(s): return [(D * j + 256 * s, 256) for j in range(3)]

def pack_rows(G, me, at, main, rest):
    G[(*me,slice(None),pl.ds(at,W3))]=main.astype(BF)
    parts=[jnp.concatenate([rest[:,256*s:256*s+128],rest[:,256*s+128:256*s+256]],0) for s in range(3)]
    G[(*me,slice(None),pl.ds(al(at+W3,128),W3//2))]=jnp.concatenate(parts,1).astype(BF)

def pack_own_vec(G, me, vec, wide, start):
    wide[...]=jnp.zeros_like(wide)
    wide[0:1,0:vec.shape[1]]=vec[...]
    n=3*VEC_COLS
    i=lax.broadcasted_iota(jnp.int32,(n,n),0); j=lax.broadcasted_iota(jnp.int32,(n,n),1)
    row=nn(wide[...].astype(BF),jnp.where(j==i+start,1.0,0.0).astype(BF))[0:1]
    parts=[row[:,VEC_COLS*k:VEC_COLS*k+VEC_COLS] for k in range(3)]+[jnp.zeros((13,VEC_COLS),F32)]
    G[(*me,slice(None),pl.ds(VEC_AT,VEC_COLS))]=jnp.concatenate(parts,0).astype(BF)

def pack_own(place, G, wqkv, wout, wup, wdown, vec, wide, start, first):
    me=place.me
    lo=al(8*place.x,8); ro=al(16*(1-place.x),8)
    def cols(w,cs):
        return [jnp.concatenate([w[pl.ds(a,n),pl.ds(c,k)] for c,k in cs],1) for a,n in ((lo,16),(ro,8))]
    for s in ((2,) if first else (0,1)): pack_rows(G,me,QKV_AT+CW*s,*cols(wqkv,third_cols(s)))
    if first:
        pack_own_vec(G,me,vec,wide,start)
        return
    pack_rows(G,me,OUT_AT,*cols(wout,[(0,W3)]))
    for c in range(4): pack_rows(G,me,UP_AT+CW*c,*cols(wup,[(W3*c,W3)]))
    for r in range(6):
        G[(*me,slice(None),pl.ds(DOWN_AT+r*D,D))]=wdown[pl.ds(16*r,16),:].astype(BF)

def unpack24(G, at, dst):
    Z=G.shape[1]
    def body(j,_):
        r=al(j*48,16); d=j//Z; z=lax.rem(j,Z)
        dst[pl.ds(r,16),:]=G[d,z,0,:,pl.ds(al(at,128),W3)]
        dst[pl.ds(r+32,16),:]=G[d,z,1,:,pl.ds(al(at,128),W3)]
        a=G[d,z,0,:,pl.ds(al(at+W3,128),W3//2)].astype(F32)
        b=G[d,z,1,:,pl.ds(al(at+W3,128),W3//2)].astype(F32)
        parts=[]
        for s in range(3):
            q=slice(128*s,128*s+128)
            parts+=[jnp.concatenate([a[:8,q],b[:8,q]],0),jnp.concatenate([a[8:,q],b[8:,q]],0)]
        dst[pl.ds(r+16,16),:]=jnp.concatenate(parts,1).astype(BF)
        return 0
    lax.fori_loop(0,G.shape[0]*Z,body,0)

def pack24(G, at, src):
    Z=G.shape[1]
    def body(j,_):
        r=al(j*48,16); d=j//Z; z=lax.rem(j,Z)
        pack_rows(G,(d,z,0),al(at,128),src[pl.ds(r,16),:],src[pl.ds(al(r+16,8),8),:])
        pack_rows(G,(d,z,1),al(at,128),src[pl.ds(r+32,16),:],src[pl.ds(al(r+24,8),8),:])
        return 0
    lax.fori_loop(0,G.shape[0]*Z,body,0)

def unpack_down(G, c, dst):
    def body(k,_):
        for r in range(6):
            dst[pl.ds(al(k*96+16*r,16),16),:]=G[c,k//2,lax.rem(k,2),:,pl.ds(DOWN_AT+r*D,D)]
        return 0
    lax.fori_loop(0,2*G.shape[1],body,0)

def pack_down(G, c, src):
    def body(k,_):
        for r in range(6):
            G[c,k//2,lax.rem(k,2),:,pl.ds(DOWN_AT+r*D,D)]=src[pl.ds(al(k*96+16*r,16),16),:].astype(BF)
        return 0
    lax.fori_loop(0,2*G.shape[1],body,0)

def vec_shift(k): return (240*k)//128

def unpack_vec(G, V, V1):
    V[...]=jnp.zeros_like(V)
    Z=G.shape[1]
    for k in range(8*Z):
        V[pl.ds(vec_shift(k),3),:]+=G[k//(2*Z),k//2%Z,k%2,:,pl.ds(VEC_AT,VEC_COLS)].astype(F32)[0:3]
    for t in range(60):
        V1[:,pl.ds(128*t,128)]=V[pl.ds(t,1),:]

def pack_vec(G, V, V1):
    V[...]=jnp.zeros_like(V)
    for t in range(60):
        V[pl.ds(t,1),:]=V1[:,pl.ds(128*t,128)]
    Z=G.shape[1]
    for k in range(8*Z):
        G[k//(2*Z),k//2%Z,k%2,:,pl.ds(VEC_AT,VEC_COLS)]=V[pl.ds(vec_shift(k),16),:].astype(BF)

def norm_parts(x):
    c=x-jnp.mean(x,-1,keepdims=True)
    s=lax.rsqrt(jnp.mean(c*c,-1,keepdims=True)+EPS_NORM)
    return c*s,s

def norm_back(dx, xh, s):
    return s*(dx-jnp.mean(dx,-1,keepdims=True)-xh*jnp.mean(dx*xh,-1,keepdims=True))

def gelu_both(u):
    k0=0.7978845608028654; k1=0.044715
    u2=u*u
    t=jnp.tanh(k0*(u*(1.0+k1*u2)))
    h=0.5*(1.0+t)
    return u*h, h+(0.5*k0)*u*(1.0-t*t)*(1.0+(3.0*k1)*u2)

RB=256

RULES=((1,1,0),(2,3,1),(2,4,3))

def places():
    p=[("in",0,0.7),("in",1,0.8)]+[("stat",i,0.6) for i in range(4)]
    for i in range(3):
        p.append(("third",i,0.6 if i else 2.0))
        p+=[("qkv",4*i+k,0.42) for k in range(4)]
        p+=[("af",2*i+pp,2.1) for pp in range(2)]
    p.append(("out",0,0.6))
    p+=[("ob",k,1.1) for k in range(4)]
    for c in range(4):
        p.append(("chunk",c,0.5))
        p+=[("mr",4*c+k,1.7) for k in range(4)]
        p+=[("mw",3*c+k,0.6+0.15*(k==2)) for k in range(3)]
        p+=[("mu",3*c+k,0.6+0.2*(k==2)) for k in range(3)]
        p.append(("mp",c,0.1))
    p.append(("fin",0,1.0))
    p+=[("bb",k,1.3) for k in range(4)]
    p+=[("bw",k,0.6+0.2*(k==2)) for k in range(3)]
    p.append(("bp",0,0.4))
    for i in range(3):
        for pp in range(2): p+=[("ab",4*i+2*pp+k,(1.6,2.1)[k]) for k in range(2)]
        p+=[("dq",3*i+k,0.6+0.2*(k==2)) for k in range(3)]
        p.append(("dp",i,0.1))
        p+=[("dh",4*i+k,0.5) for k in range(4)]
    p+=[("ln",k,0.35+0.4*(k==3)) for k in range(4)]
    p.append(("lp",0,0.1))
    p+=[("lx",k,0.45) for k in range(4)]
    return p

def ready_places():
    return [("mp",c) for c in range(4)]+[("mp",3)]*4+[("bp",0)]+[("dp",i) for i in (0,1,2,2)]+[("lp",0)]

def due_places():
    return [("third",0),("third",1),("out",0),("chunk",0),("chunk",1),("chunk",2)]

class Clock:
    def __init__(self, plan, ga, sc, own):
        names=[p[:2] for p in places()]
        index={p:i for i,p in enumerate(names)}
        fns={}
        for g in range(len(GATHER)):
            for k,f in enumerate(ga.events(g)): fns[(0,g,k)]=f
        for g,(lo,n,_) in enumerate(SCATTER):
            for k,f in enumerate(sc.events(g,own.at[:,pl.ds(lo,n)])): fns[(1,g,k)]=f
        check_plan(plan,set(fns),index)
        self.slots={}
        self.tail=[]
        for i,*key in plan:
            if i<len(names): self.slots.setdefault(names[i],[]).append(fns[tuple(key)])
            else: self.tail.append(fns[tuple(key)])
    def at(self, name, step, count):
        for k in range(count):
            todo=self.slots.get((name,k))
            if todo:
                def run(todo=todo):
                    for f in todo: f()
                if isinstance(step,int):
                    if step==k: run()
                else: pl.when(step==k)(run)

PLAN = (
    (0, 0, 0, 0), (1, 0, 1, 0), (1, 0, 2, 0), (1, 0, 0, 1), (1, 0, 0, 2), (1, 0, 0, 3), (1, 0, 1, 1), (1, 0, 1, 2),
    (1, 0, 0, 4), (1, 0, 0, 5), (1, 0, 1, 3), (1, 0, 1, 4), (2, 0, 0, 6), (2, 0, 0, 7), (3, 0, 2, 1), (3, 0, 3, 0),
    (3, 0, 1, 5), (3, 0, 1, 6), (4, 0, 2, 2), (5, 0, 1, 7), (6, 0, 0, 8), (6, 0, 0, 9), (8, 0, 1, 8), (8, 0, 1, 9),
    (8, 0, 1, 10), (9, 0, 2, 3), (12, 0, 2, 4), (12, 0, 1, 11), (13, 0, 1, 12), (14, 0, 3, 1), (15, 0, 2, 5),
    (15, 0, 2, 6), (16, 0, 3, 2), (17, 0, 2, 7), (19, 0, 5, 0), (20, 0, 3, 3), (20, 0, 2, 8), (21, 0, 3, 4),
    (22, 0, 4, 0), (22, 0, 2, 9), (24, 0, 2, 10), (25, 0, 3, 5), (25, 0, 3, 6), (26, 0, 5, 1), (26, 0, 3, 7),
    (26, 0, 3, 8), (26, 0, 2, 11), (26, 0, 4, 1), (27, 0, 4, 2), (27, 0, 4, 3), (27, 0, 3, 9), (27, 0, 2, 12),
    (27, 0, 3, 10), (28, 0, 5, 2), (29, 0, 4, 4), (29, 0, 4, 5), (30, 0, 3, 11), (31, 0, 5, 3), (31, 0, 5, 4),
    (31, 0, 5, 5), (31, 0, 4, 6), (32, 0, 3, 12), (32, 0, 4, 7), (35, 0, 5, 6), (35, 0, 5, 7), (35, 0, 4, 8),
    (35, 0, 4, 9), (35, 0, 4, 10), (37, 0, 5, 8), (37, 0, 5, 9), (37, 0, 4, 11), (40, 0, 4, 12), (43, 1, 0, 0),
    (45, 0, 5, 10), (47, 1, 0, 1), (51, 0, 5, 11), (54, 1, 0, 2), (56, 0, 5, 12), (57, 1, 1, 0), (59, 1, 0, 3),
    (59, 1, 1, 1), (67, 1, 2, 0), (69, 1, 1, 2), (70, 1, 0, 4), (70, 1, 2, 1), (75, 1, 2, 2), (79, 1, 3, 0),
    (80, 1, 1, 3), (81, 1, 3, 1), (81, 1, 4, 0), (82, 1, 2, 3), (83, 1, 4, 1), (86, 1, 3, 2), (88, 1, 5, 0),
    (89, 1, 2, 4), (89, 1, 4, 2), (90, 1, 1, 4), (90, 1, 3, 3), (90, 1, 5, 1), (90, 1, 6, 0), (91, 1, 4, 3),
    (91, 1, 6, 1), (92, 1, 7, 0), (95, 1, 5, 2), (97, 1, 3, 4), (98, 1, 6, 2), (102, 1, 5, 3), (102, 1, 7, 1),
    (102, 1, 8, 0), (103, 1, 4, 4), (103, 1, 6, 3), (103, 1, 8, 1), (105, 1, 5, 4), (105, 1, 7, 2), (108, 1, 8, 2),
    (109, 1, 6, 4), (109, 1, 9, 0), (113, 1, 7, 3), (113, 1, 9, 1), (114, 1, 8, 3), (114, 1, 10, 0),
    (115, 1, 10, 1), (117, 1, 9, 2), (120, 1, 11, 0), (120, 1, 10, 2), (121, 1, 8, 4), (124, 1, 7, 4),
    (124, 1, 9, 3), (124, 1, 11, 1), (124, 1, 12, 0), (127, 1, 10, 3), (127, 1, 12, 1), (129, 1, 11, 2),
    (130, 1, 13, 0), (131, 1, 12, 2), (133, 1, 9, 4), (134, 1, 11, 3), (134, 1, 13, 1), (134, 1, 13, 2),
    (134, 1, 11, 4), (134, 1, 10, 4), (134, 1, 12, 3), (134, 1, 13, 3), (134, 1, 13, 4), (134, 1, 12, 4),
)

def check_plan(plan, keys, index):
    pos={tuple(e[1:]):(e[0],j) for j,e in enumerate(plan)}
    assert set(pos)==keys and len(plan)==len(keys)
    assert all(a[0]<=b[0] for a,b in zip(plan,plan[1:]))
    for kind,g,k in keys:
        if k: assert pos[(kind,g,k-1)]<pos[(kind,g,k)]
    assert pos[(0,0,0)][0]==0 and all(pos[(0,g,0)][0]>=1 for g in range(1,len(GATHER)))
    for g,p in enumerate(due_places()): assert max(v[0] for e,v in pos.items() if e[:2]==(0,g))<=index[p]
    for g,p in enumerate(ready_places()):
        assert pos[(1,g,0)][0]>=index[p]
        for n,i,j in RULES:
            if g>=n: assert pos[(1,g-n,i)]<pos[(1,g,j)]

def mega_kernel(Z,plan,tok_h,cot_h,len_ref,wqkv_s,wout_s,wup_s,wdown_s,vec_s,
               mixed_o,dtok_o,own_o,nrm_o,place_o,
               G,tok,cot,F1,F2,F3,qkv,B1,B2,B3,h1T,h2T,aT,oT,W0,W1,dW,lse,V,V1,dV1,dka,dva,own,nrm,wide,dsem,*rest):
    gsems=rest[:10]; rbufs=rest[10:10+NB]; rsems=rest[10+NB:18+NB]; nb,got,ns,nr=rest[18+NB:]
    L=tok.shape[0]
    NBK=L//RB
    place=Place(Z)
    def dma(a,b,i):
        cp=pltpu.make_async_copy(a,b,dsem.at[i]); cp.start(); return cp
    ldt=dma(tok_h,tok,0); ldc=dma(cot_h,cot,1)
    bar=announce(place,Z)
    start=lax.rem(240*((place.dp*Z+place.z)*2+place.x),128)
    place_o[0]=place.x
    place_o[1]=start
    shards=(wqkv_s,wout_s,wup_s,wdown_s,vec_s,wide,start)
    pack_own(place,G,*shards,True)
    pl.semaphore_wait(bar,8*Z-1)
    ga=Gather(place,G,GATHER,gsems)
    sc=Scatter(place,G,SCATTER,rbufs,rsems)
    clock=Clock(plan,ga,sc,own)
    def at(name,step,count): clock.at(name,step,count)
    def rows(i): return pl.ds(al(i*RB,RB),RB)
    length=len_ref[0]
    at("in",0,2)
    pack_own(place,G,*shards,False)
    at("in",1,2)
    F3[...]=jnp.zeros_like(F3)
    ldc.wait()
    dead=lax.broadcasted_iota(jnp.int32,(L,D),0)>=length
    cot[...]=jnp.where(dead,jnp.zeros((),BF),cot[...])
    ldt.wait()
    xhat=F1; h1=B1; o=B3
    for i in range(4):
        at("stat",i,4)
        if i<NBK:
            xhat[rows(i),:]=norm_parts(tok[rows(i),:].astype(F32))[0]
    def third(i,_):
        s=lax.rem(i+2,3)
        at("third",i,3)
        @pl.when(i==0)
        def _():
            unpack_vec(G,V,V1)
            def first(j,_):
                hb=(xhat[rows(j),:]*V1[:,0:D]+V1[:,D:2*D]).astype(BF)
                h1[rows(j),:]=hb
                h1T[:,rows(j)]=hb.T
                return 0
            lax.fori_loop(0,NBK,first,0)
        unpack24(G,QKV_AT+CW*s,W0)
        def block(j,_):
            at("qkv",4*i+j,12)
            qkv[s,rows(j),:]=nn(h1[rows(j),:],W0[...]).astype(BF)
            return 0
        lax.fori_loop(0,NBK,block,0)
        def pair(pp,_):
            p=2*s+pp
            def col(j): return qkv.at[s,:,pl.ds(al(256*j+128*pp,128),128)]
            c=pl.ds(al(128*p,128),128)
            at("af",2*i+pp,6)
            attn_fwd_pair(col(0),col(1),col(2),length,o.at[:,c],oT.at[c,:],lse.at[p],512)
            return 0
        lax.fori_loop(0,2,pair,0)
        return 0
    lax.fori_loop(0,3,third,0)
    at("out",0,1)
    unpack24(G,OUT_AT,W0)
    r1=F1; mixed=F2; dh2=F3; h2=B1
    def out_block(i,_):
        at("ob",i,4)
        sl=rows(i)
        r=tok[sl,:].astype(F32)+nn(o[sl,:],W0[...])+V1[:,4*D:5*D]
        r1[sl,:]=r
        mixed[sl,:]=r+V1[:,5*D:6*D]
        hb=(norm_parts(r)[0]*V1[:,2*D:3*D]+V1[:,3*D:4*D]).astype(BF)
        h2[sl,:]=hb
        h2T[:,sl]=hb.T
        return 0
    lax.fori_loop(0,NBK,out_block,0)
    du_s=B2
    def chunk(c,_):
        at("chunk",c,4)
        for g,when_ in enumerate((0,0,0,0,1,2)):
            pl.when(c==when_)(lambda g=g: ga.drain(g))
        unpack24(G,UP_AT+CW*c,W0)
        unpack_down(G,c,W1)
        bu=V1[:,pl.ds(al(6*D+c*W3,128),W3)]
        def mrows(i,acc):
            at("mr",4*c+i,16)
            sl=rows(i)
            u=nn(h2[sl,:],W0[...])+bu
            a,slope=gelu_both(u)
            ab=a.astype(BF)
            mixed[sl,:]+=nn(ab,W1[...])
            aT[:,sl]=ab.T
            du=(nt(cot[sl,:],W1[...])*slope).astype(BF)
            du_s[sl,:]=du
            dh2[sl,:]+=nt(du,W0[...])
            return acc+jnp.sum(du.astype(F32),0,keepdims=True)
        s=lax.fori_loop(0,NBK,mrows,jnp.zeros((1,W3),F32))
        dV1[:,pl.ds(al(6*D+c*W3,128),W3)]=s
        def wrows(i,_):
            at("mw",3*c+i,12)
            dW[rows(i),:]=nn(aT[rows(i),:],cot[...])
            return 0
        lax.fori_loop(0,W3//RB,wrows,0)
        pack_down(G,c,dW)
        def urows(i,_):
            at("mu",3*c+i,12)
            dW[rows(i),:]=nn(h2T[rows(i),:],du_s[...])
            return 0
        lax.fori_loop(0,D//RB,urows,0)
        pack24(G,UP_AT+CW*c,dW)
        at("mp",c,4)
        return 0
    lax.fori_loop(0,FF//W3,chunk,0)
    at("fin",0,1)
    mixed_b=B2
    def fin(i,_):
        mixed_b[rows(i),:]=mixed[rows(i),:].astype(BF)
        return 0
    lax.fori_loop(0,NBK,fin,0)
    outs=[dma(mixed_b,mixed_o,2)]
    unpack24(G,OUT_AT,W0)
    dr1=F3; dy=B3; do=B1
    def back(i,acc):
        at("bb",i,4)
        sl=rows(i)
        dh=dh2[sl,:]
        xh,s=norm_parts(r1[sl,:])
        g=cot[sl,:].astype(F32)
        dr=g+norm_back(dh*V1[:,2*D:3*D],xh,s)
        dr1[sl,:]=dr
        dyb=dr.astype(BF)
        dy[sl,:]=dyb
        do[sl,:]=nt(dyb,W0[...]).astype(BF)
        new=(dh*xh,dh,dyb.astype(F32),g)
        return tuple(a+jnp.sum(b,0,keepdims=True) for a,b in zip(acc,new))
    z1=jnp.zeros((1,D),F32)
    sums=lax.fori_loop(0,NBK,back,(z1,z1,z1,z1))
    for j,v in enumerate(sums): dV1[:,pl.ds((2+j)*D,D)]=v
    def orow(i,_):
        at("bw",i,3)
        dW[rows(i),:]=nn(oT[rows(i),:].astype(BF),dy[...])
        return 0
    lax.fori_loop(0,D//RB,orow,0)
    pack24(G,OUT_AT,dW)
    at("bp",0,1)
    dqkv=B3; dh1=F2
    outs[0].wait()
    dh1[...]=jnp.zeros_like(dh1)
    def third_back(s,_):
        unpack24(G,QKV_AT+CW*s,W0)
        def pair(pp,_):
            p=2*s+pp
            at("ab",4*s+2*pp,12)
            def col(j): return qkv.at[s,:,pl.ds(al(256*j+128*pp,128),128)]
            def dcol(j): return dqkv.at[:,pl.ds(al(256*j+128*pp,128),128)]
            c=pl.ds(al(128*p,128),128)
            attn_bwd_pair(col(0),col(1),col(2),do.at[:,c],oT.at[c,:],lse.at[p],length,
                          dcol(0),dcol(1),dcol(2),dka,dva,256,tick=lambda k: at("ab",4*s+2*pp+k,12))
            return 0
        lax.fori_loop(0,2,pair,0)
        def qrow(i,_):
            at("dq",3*s+i,9)
            dW[rows(i),:]=nn(h1T[rows(i),:],dqkv[...])
            return 0
        lax.fori_loop(0,D//RB,qrow,0)
        pack24(G,QKV_AT+CW*s,dW)
        at("dp",s,3)
        def drow(i,_):
            at("dh",4*s+i,12)
            dh1[rows(i),:]+=nt(dqkv[rows(i),:],W0[...])
            return 0
        lax.fori_loop(0,NBK,drow,0)
        return 0
    lax.fori_loop(0,3,third_back,0)
    def srow(i,acc):
        at("ln",i,4)
        sl=rows(i)
        dh=dh1[sl,:]
        xh,_=norm_parts(tok[sl,:].astype(F32))
        return tuple(a+jnp.sum(b,0,keepdims=True) for a,b in zip(acc,(dh*xh,dh)))
    sums=lax.fori_loop(0,NBK,srow,(z1,z1))
    for j,v in enumerate(sums): dV1[:,pl.ds(j*D,D)]=v
    pack_vec(G,V,dV1)
    at("lp",0,1)
    def lrow(i,_):
        at("lx",i,4)
        sl=rows(i)
        xh,r=norm_parts(tok[sl,:].astype(F32))
        F1[sl,:]=dr1[sl,:]+norm_back(dh1[sl,:]*V1[:,0:D],xh,r)
        return 0
    lax.fori_loop(0,NBK,lrow,0)
    outs=[dma(F1,dtok_o,3)]
    for f in clock.tail: f()
    flat=lax.broadcasted_iota(jnp.int32,(16,VEC_COLS),0)*VEC_COLS+lax.broadcasted_iota(jnp.int32,(16,VEC_COLS),1)
    vec=own[:,pl.ds(VEC_AT,VEC_COLS)]
    vec=jnp.where(jnp.logical_and(flat>=start,flat<start+240),vec,0.0)
    left=own[:,pl.ds(0,VEC_AT)]; right=own[:,pl.ds(OUT_AT,COLS-OUT_AT)]
    got[0]=jnp.full((8,128),1.0,F32)*(jnp.sum(left*left)+jnp.sum(right*right)+jnp.sum(vec*vec))
    outs.append(dma(own,own_o,4))
    nrm[8:24,:]=vec
    nrm[0:8,:]=all_sum(place,nb,got,ns,nr)
    outs.append(dma(nrm,nrm_o,5))
    for g in range(len(SCATTER)): sc.drain(g)
    for cp in outs: cp.wait()

def mega_call(Z,tok,cot,length,wqkv,wout,wup,wdown,vec,plan=None):
    plan=PLAN if plan is None else plan
    L=tok.shape[0]; pieces=8*Z
    S=jax.ShapeDtypeStruct; V=pltpu.VMEM
    vm=pl.BlockSpec(memory_space=pltpu.VMEM); an=pl.BlockSpec(memory_space=pltpu.HBM); sm=pl.BlockSpec(memory_space=pltpu.SMEM)
    outs=[S((L,D),BF),S((L,D),F32),S((16,COLS),F32),S((24,128),F32),S((2,),jnp.int32)]
    f=lambda: V((L,D),F32)
    b=lambda: V((L,D),BF)
    scratch=[V((4,Z,2,16,COLS),BF),b(),b(),f(),f(),f(),V((3,L,D),BF),b(),b(),b(),V((D,L),BF),V((D,L),BF),V((D,L),BF),V((D,L),F32),
             V((D,W3),BF),V((W3,D),BF),V((D,W3),F32),V((6,2,L),F32),V((80,128),F32),V((1,10*D),F32),V((1,10*D),F32),
             V((L,128),F32),V((L,128),F32),V((16,COLS),F32),V((24,128),F32),V((8,3*VEC_COLS),F32),pltpu.SemaphoreType.DMA((6,))]
    return pl.pallas_call(functools.partial(mega_kernel,Z,plan),out_shape=outs,
        in_specs=[an,an,sm]+[vm]*5,out_specs=[an]*4+[sm],
        scratch_shapes=scratch+gather_sems(len(GATHER),Z)+rs_bufs(Z)+rs_sems(len(SCATTER),Z)+norm_bufs(Z)+norm_sems(Z),
        compiler_params=pltpu.CompilerParams(collective_id=1,has_side_effects=True,vmem_limit_bytes=63*2**20),
        cost_estimate=pl.CostEstimate(flops=60*10**9,bytes_accessed=60*2**20,transcendentals=10**7))(tok,cot,length,wqkv,wout,wup,wdown,vec)


def adam_step(weight, first_mom, second_mom, gradient, step_rate):
    first_new = BETA_ONE * first_mom + (1.0 - BETA_ONE) * gradient
    second_new = BETA_TWO * second_mom + (1.0 - BETA_TWO) * gradient * gradient
    fix_one = 1.0 - BETA_ONE**STEP
    fix_two = 1.0 - BETA_TWO**STEP
    update = (
        first_new / fix_one / (jnp.sqrt(second_new / fix_two) + ADAM_EPSILON) + DECAY_RATE * weight
    )
    return (weight - step_rate * update, first_new, second_new)


def adam_kernel(par_ref, own_h, nrm_h, mixed_h, dtok_h, *refs):
    ins_h, outs_h, moved, norm_ref = refs[:15], refs[15:30], refs[30:32], refs[32]
    own, nrm, *rest = refs[33:]
    ins, outs, (mixed, dtok, wide, sem) = rest[:15], rest[15:30], rest[30:]
    pairs = list(zip((own_h, nrm_h) + tuple(ins_h), (own, nrm) + tuple(ins)))
    loads = [pltpu.make_async_copy(a, b, sem.at[i]) for i, (a, b) in enumerate(pairs)]
    moves = [
        pltpu.make_async_copy(mixed_h, mixed, sem.at[32]),
        pltpu.make_async_copy(dtok_h, dtok, sem.at[33]),
    ]
    for cp in moves + loads:
        cp.start()
    out_moves = [
        pltpu.make_async_copy(mixed, moved[0], sem.at[32]),
        pltpu.make_async_copy(dtok, moved[1], sem.at[33]),
    ]
    for cp, out in zip(moves, out_moves):
        cp.wait()
        out.start()
    loads[0].wait()
    loads[1].wait()
    stores = [pltpu.make_async_copy(a, b, sem.at[i]) for i, (a, b) in enumerate(zip(outs, outs_h), 17)]

    def take(i):
        for cp in loads[2 + 3 * i : 5 + 3 * i]:
            cp.wait()

    def give(i):
        for cp in stores[3 * i : 3 * i + 3]:
            cp.start()

    norm = jnp.sqrt(nrm[0:1, 0:1])
    norm_ref[0] = norm[0, 0]
    factor = jnp.minimum(1.0, CLIP_NORM / (norm + 1e-06))
    main_at = al(8 * par_ref[0], 8)
    rest_at = al(16 * (1 - par_ref[0]), 8)

    def step(i, rows, cols, grad, rate):
        w, m, v = [r[rows, cols] for r in ins[3 * i : 3 * i + 3]]
        new = adam_step(w, m, v, grad * factor, rate)
        for r, a in zip(outs[3 * i : 3 * i + 3], new):
            r[rows, cols] = a

    def chunk(i, at, cols, rate):
        main = own[:, pl.ds(at, W3)]
        packed = own[:, pl.ds(at + W3, W3 // 2)]
        parts = []
        for s in range(3):
            parts += [packed[:8, 128 * s : 128 * s + 128], packed[8:, 128 * s : 128 * s + 128]]
        rest = jnp.concatenate(parts, 1)
        done = 0
        for c, n in cols:
            step(i, pl.ds(main_at, 16), pl.ds(c, n), main[:, done : done + n], rate)
            step(i, pl.ds(rest_at, 8), pl.ds(c, n), rest[:, done : done + n], rate)
            done += n

    take(0)
    for s in range(3):
        chunk(0, QKV_AT + CW * s, third_cols(s), D ** (-0.5))
    give(0)
    take(1)
    chunk(1, OUT_AT, [(0, W3)], D ** (-0.5))
    give(1)
    take(2)
    for c in range(4):
        chunk(2, UP_AT + CW * c, [(W3 * c, W3)], D ** (-0.5))
    give(2)
    take(3)
    for r in range(6):
        grad = own[:, pl.ds(DOWN_AT + r * D, D)]
        step(3, pl.ds(16 * r, 16), slice(None), grad, FF ** (-0.5))
    give(3)
    take(4)
    n = ins[12].shape[1]
    for k in range(3):
        wide[0:8, VEC_COLS * k : VEC_COLS * k + VEC_COLS] = jnp.broadcast_to(
            nrm[8 + k : 9 + k, :], (8, VEC_COLS)
        )
    width = 3 * VEC_COLS
    turned = pltpu.roll(wide[...], lax.rem(width - par_ref[1], width), 1)
    step(4, slice(None), slice(None), turned[0:1, :n], VECTOR_RATE)
    give(4)
    for cp in stores + out_moves:
        cp.wait()


def adam_call(parity, own, nrm, mixed, d_tokens, states):
    hb = pl.BlockSpec(memory_space=pltpu.HBM)
    sm = pl.BlockSpec(memory_space=pltpu.SMEM)
    held = [pltpu.VMEM(a.shape, F32) for a in (own, nrm) + tuple(states) + tuple(states)]
    return pl.pallas_call(
        adam_kernel,
        out_shape=[jax.ShapeDtypeStruct(a.shape, a.dtype) for a in states + (mixed, d_tokens)]
        + [jax.ShapeDtypeStruct((1,), F32)],
        in_specs=[sm] + [hb] * 19,
        out_specs=[hb] * 17 + [sm],
        scratch_shapes=held
        + [pltpu.VMEM(mixed.shape, BF), pltpu.VMEM(d_tokens.shape, F32)]
        + [pltpu.VMEM((8, 3 * VEC_COLS), F32)]
        + [pltpu.SemaphoreType.DMA((34,))],
        compiler_params=pltpu.CompilerParams(vmem_limit_bytes=63 * 2**20),
        cost_estimate=pl.CostEstimate(
            flops=10**7, bytes_accessed=8 * 2**20, transcendentals=10**6
        ),
    )(parity, own, nrm, mixed, d_tokens, *states)


def layer_norm(values, gain, shift):
    center = jnp.mean(values, -1, keepdims=True)
    centered = values - center
    spread = jnp.mean(centered * centered, -1, keepdims=True)
    return centered * lax.rsqrt(spread + EPS_NORM) * gain + shift


def smooth_gate(value):
    return jax.nn.gelu(value, approximate=True)


def plain_shards(tokens, lengths, cotangent, *state):
    w_qkv, m_qkv, v_qkv, w_out, m_out, v_out, w_up, m_up, v_up = state[:9]
    w_down, m_down, v_down, packed, m_packed, v_packed = state[9:]
    seq_count, seq_len, model_width = tokens.shape
    row_count = seq_count * seq_len
    axes = ("dp", "fsdp")
    wqkv_b, wout_b, wup_b, wdown_b, vector_b = [
        lax.all_gather(w.astype(BF), axes, axis=0, tiled=True)
        for w in (w_qkv, w_out, w_up, w_down, packed)
    ]
    vector = vector_b.astype(F32)
    gain_one, bias_one, gain_two, bias_two, bias_attn, bias_down = [
        vector[i * model_width : (i + 1) * model_width] for i in range(6)
    ]
    bias_up = vector[6 * model_width :]
    positions = jnp.arange(seq_len, dtype=jnp.int32)
    live_rows = positions[None, :] < lengths[:, None]
    inputs = tokens.astype(F32).reshape(row_count, model_width)
    normed_one, norm_one_back = jax.vjp(layer_norm, inputs, gain_one, bias_one)
    normed_one_b = normed_one.astype(BF)
    qkv_all = jnp.dot(normed_one_b, wqkv_b, preferred_element_type=F32).astype(BF)
    seqs = [slice(i * seq_len, (i + 1) * seq_len) for i in range(seq_count)]
    ahead = [fwd_call(qkv_all[s], lengths[i : i + 1], 512) for i, s in enumerate(seqs)]
    attended_b = jnp.concatenate([a[0] for a in ahead], 0)
    resid_one = inputs + jnp.dot(attended_b, wout_b, preferred_element_type=F32) + bias_attn
    normed_two, norm_two_back = jax.vjp(layer_norm, resid_one, gain_two, bias_two)
    normed_two_b = normed_two.astype(BF)
    upper = jnp.dot(normed_two_b, wup_b, preferred_element_type=F32) + bias_up
    activ, gate_back = jax.vjp(smooth_gate, upper)
    activ_b = activ.astype(BF)
    mixed = resid_one + jnp.dot(activ_b, wdown_b, preferred_element_type=F32) + bias_down
    mixed = mixed.reshape(seq_count, seq_len, model_width).astype(BF)
    grad_b = jnp.where(live_rows[:, :, None], cotangent, jnp.zeros((), BF))
    grad_b = grad_b.reshape(row_count, model_width)
    grad_full = grad_b.astype(F32)
    d_wdown = jnp.dot(activ_b.T, grad_b, preferred_element_type=F32)
    d_bias_down = jnp.sum(grad_full, 0)
    d_activ = jnp.dot(grad_b, wdown_b.T, preferred_element_type=F32)
    (d_upper,) = gate_back(d_activ)
    d_upper_b = d_upper.astype(BF)
    d_bias_up = jnp.sum(d_upper_b.astype(F32), 0)
    d_wup = jnp.dot(normed_two_b.T, d_upper_b, preferred_element_type=F32)
    d_normed_two = jnp.dot(d_upper_b, wup_b.T, preferred_element_type=F32)
    d_resid_norm, d_gain_two, d_bias_two = norm_two_back(d_normed_two)
    d_resid = grad_full + d_resid_norm
    d_branch_b = d_resid.astype(BF)
    d_bias_attn = jnp.sum(d_branch_b.astype(F32), 0)
    d_wout = jnp.dot(attended_b.T, d_branch_b, preferred_element_type=F32)
    d_attended_b = jnp.dot(d_branch_b, wout_b.T, preferred_element_type=F32).astype(BF)
    back = [
        bwd_call(qkv_all[s], d_attended_b[s], a[1], a[2], lengths[i : i + 1])
        for i, (s, a) in enumerate(zip(seqs, ahead))
    ]
    d_qkv_b = jnp.concatenate([jnp.concatenate(b, 1) for b in back], 0)
    d_wqkv = jnp.dot(normed_one_b.T, d_qkv_b, preferred_element_type=F32)
    d_normed_one = jnp.dot(d_qkv_b, wqkv_b.T, preferred_element_type=F32)
    d_input_norm, d_gain_one, d_bias_one = norm_one_back(d_normed_one)
    d_tokens = (d_resid + d_input_norm).reshape(seq_count, seq_len, model_width)
    d_vector = jnp.concatenate(
        [d_gain_one, d_bias_one, d_gain_two, d_bias_two, d_bias_attn, d_bias_down, d_bias_up]
    )
    owned = [
        lax.psum_scatter(g, axes, scatter_dimension=0, tiled=True)
        for g in (d_wqkv, d_wout, d_wup, d_wdown, d_vector)
    ]
    grad_norm = jnp.sqrt(lax.psum(sum(jnp.sum(g * g) for g in owned), axes))
    factor = jnp.minimum(1.0, CLIP_NORM / (grad_norm + 1e-06))
    rates = (D ** (-0.5), D ** (-0.5), D ** (-0.5), FF ** (-0.5), VECTOR_RATE)
    new = ()
    for i, (g, rate) in enumerate(zip(owned, rates)):
        new += adam_step(*state[3 * i : 3 * i + 3], g * factor, rate)
    return (mixed, d_tokens, grad_norm) + new


def direct_shards(Z, tokens, lengths, cotangent, *state):
    n = state[12].shape[0]
    vecs = tuple(v.reshape(1, n) for v in state[12:])
    mixed, d_tokens, own, small, place = mega_call(
        Z, tokens[0], cotangent[0], lengths, state[0], state[3], state[6], state[9], vecs[0]
    )
    *new, mixed, d_tokens, grad_norm = adam_call(
        place, own, small, mixed, d_tokens, state[:12] + vecs
    )
    new[12:] = [v.reshape(n) for v in new[12:]]
    return (mixed[None], d_tokens[None], grad_norm[0]) + tuple(new)


def solution(mesh):
    rows = P(("dp", "fsdp"), None)
    seqs = P(("dp", "fsdp"), None, None)
    flat = P(("dp", "fsdp"))
    in_specs = (seqs, flat, seqs) + (rows,) * 12 + (flat,) * 3
    out_specs = (seqs, seqs, P()) + (rows,) * 12 + (flat,) * 3
    dp, fsdp = mesh.shape["dp"], mesh.shape["fsdp"]

    def shards(*args):
        tokens, w_qkv = args[0], args[3]
        fits = (
            dp == 4
            and fsdp == 8
            and tokens.shape[0] == 1
            and tokens.shape[1] == 1024
            and w_qkv.shape[0] * dp * fsdp == D
        )
        step = functools.partial(direct_shards, fsdp // 2) if fits else plain_shards
        return step(*args)

    return jax.shard_map(
        shards, mesh=mesh, in_specs=in_specs, out_specs=out_specs, check_vma=False
    )
```
